32 devices in a mesh: freq: 4 (over z), lat: 2 (over x), lon: 4 (over y, core).
Axes of the slice: x: 2, y: 2, z: 4, core: 2. Of those that a mesh axis runs over, the one named last changes fastest.
Arguments:
- direction: float32 [3, 32, 256, 2048], P(None, 'freq', 'lat', 'lon'), may hold values from -6 to 6
- base_flow: float32 [2, 32, 256, 2048], P(None, 'freq', 'lat', 'lon'), may hold values from -2 to 2
- water_depth: float32 [256, 2048], P('lat', 'lon'), may hold values from 0.5 to 2
- drag_factor: float32 [256, 2048], P('lat', 'lon'), may hold values from 0.2 to 2
- wet_mask: int32 [256, 2048], P('lat', 'lon'), may hold values 0 or 1
Outputs:
- result: float32 [3, 32, 256, 2048], P(None, 'freq', 'lat', 'lon')
The draws below stay inside these ranges and needn't reach their ends.
All inputs are finite; a program needn't handle non-finite values. No bound on the sum of `wet_mask` on one device may be relied on, other than what follows from the above.
Results may differ from the reference program's by a relative error of at most 0.000071.
Values sent between devices are 32-bit elements; how exact they have to be, the bound alone decides.
No kernel may reach another device: no remote copies, remote signals or barrier semaphores. Data moves between devices by JAX's collectives and lax.ppermute only.
A program may use at most 128 MiB of HBM per device.

```python
import math
import jax
import jax.numpy as jnp
from jax import lax

NCON = 16
NTIME = 256
NLAT = 256
NLON = 2048


def set_ends(result, own_key, least, largest):
    shape = result.shape
    place = [jax.random.randint(jax.random.fold_in(own_key, axis), (), 0, shape[axis]) for axis in range(len(shape))]
    result = result.at[tuple(place)].set(least)
    longest = shape.index(max(shape))
    place[longest] = (place[longest] + 1) % shape[longest]
    return result.at[tuple(place)].set(largest)


def levels(own_key, shape, pieces, least, largest):
    def one(position, shards_of):
        draws = jax.random.uniform(jax.random.fold_in(jax.random.fold_in(own_key, 6), position), (shards_of,), jnp.float32, least / len(pieces), largest / len(pieces))
        return jnp.repeat(jnp.exp(draws), shape[position] // shards_of).reshape((-1,) + (1,) * (len(shape) - position - 1))

    gain = one(*pieces[0])
    for cut in pieces[1:]:
        gain = gain * one(*cut)
    return gain


def scatter_about(stream_key, dims, scale, bound, pieces=(), kind=jnp.bfloat16):
    entries = jax.random.normal(stream_key, dims, jnp.float32) * scale
    if len(pieces) > 0:
        entries = levels(stream_key, dims, pieces, -0.22, 0.18) * entries
    return jnp.clip(entries, min=-bound, max=bound).astype(kind)


def setup_inputs(seed: int = 0) -> dict:
    keys = jax.random.split(jax.random.key(seed), 6)
    return {
        "direction": scatter_about(keys[0], (3, 2 * NCON, NLAT, NLON), 1.0, 6.0, ((1, 4), (2, 2), (3, 4)), jnp.float32),
        "base_flow": scatter_about(keys[1], (2, 2 * NCON, NLAT, NLON), 0.3, 2.0, ((1, 4), (2, 2), (3, 4)), jnp.float32),
        "water_depth": jnp.clip(jnp.exp(math.log(2.0) - 1.3862944 * jax.random.uniform(keys[2], (NLAT, NLON), jnp.float32) ** levels(keys[2], (NLAT, NLON), ((0, 2), (1, 4)), -0.2, 0.2)), 0.5, 2.0),
        "drag_factor": jnp.clip(jnp.exp(math.log(2.0) - 2.3025851 * jax.random.uniform(keys[3], (NLAT, NLON), jnp.float32) ** levels(keys[3], (NLAT, NLON), ((0, 2), (1, 4)), -0.2, 0.2)), 0.2, 2.0),
        "wet_mask": set_ends((jax.random.randint(keys[4], (NLAT, NLON), 0, 4) < 3).astype(jnp.int32), jax.random.fold_in(keys[4], 1), 0, 1),
    }


LINEAR_DRAG = 0.5
GRAVITY = 1.0
OMEGA_STEP = 0.25
SPEED_SOFT = 0.01

def samples_table(sample_count, constituents):
    sample_index = jnp.arange(sample_count, dtype=jnp.int32)
    harmonic = jnp.arange(1, constituents + 1, dtype=jnp.int32)
    wrapped_turns = sample_index[:, None] * harmonic[None, :] % sample_count
    phase_angle = wrapped_turns.astype(jnp.float32) * (2.0 * math.pi / sample_count)
    table = jnp.stack([jnp.cos(phase_angle), jnp.sin(phase_angle)], axis=2)
    return table.reshape(sample_count, 2 * constituents)

def rotation_of(row_index, total_rows):
    return 0.5 + (row_index.astype(jnp.float32) + 0.5) / total_rows

def tendency(values, angular):
    cos_sin = values.reshape((values.shape[0] // 2, 2) + values.shape[1:])
    moved = jnp.stack([angular * cos_sin[:, 1], -angular * cos_sin[:, 0]], axis=1)
    return moved.reshape(values.shape)

def linear_residual(extended, tile_rows, tile_cols, angular, rotation):

    def neighbour(plane, row_step, col_step):
        return extended[plane, :, 1 + row_step:1 + row_step + tile_rows, 1 + col_step:1 + col_step + tile_cols]
    height = neighbour(0, 0, 0)
    east = neighbour(1, 0, 0)
    north = neighbour(2, 0, 0)
    res_height = tendency(height, angular) + neighbour(3, 0, 0) - neighbour(3, 0, -1) + neighbour(4, 0, 0) - neighbour(4, -1, 0)
    north_mean = 0.25 * (north + neighbour(2, 0, 1) + neighbour(2, -1, 0) + neighbour(2, -1, 1))
    east_mean = 0.25 * (east + neighbour(1, 0, -1) + neighbour(1, 1, 0) + neighbour(1, 1, -1))
    res_east = tendency(east, angular) + LINEAR_DRAG * east - rotation * north_mean + GRAVITY * (neighbour(0, 0, 1) - height)
    res_north = tendency(north, angular) + LINEAR_DRAG * north + rotation * east_mean + GRAVITY * (neighbour(0, 1, 0) - height)
    return jnp.stack([res_height, res_east, res_north])

def friction_row(row_block, drag_row, table):
    highest = lax.Precision.HIGHEST
    series = jnp.einsum('tc,fcn->ftn', table, row_block, precision=highest)
    base_east, base_north, step_east, step_north = (series[0], series[1], series[2], series[3])
    magnitude = jnp.sqrt(base_east * base_east + base_north * base_north + SPEED_SOFT)
    projected = (base_east * step_east + base_north * step_north) / magnitude
    force_east = drag_row * (magnitude * step_east + base_east * projected)
    force_north = drag_row * (magnitude * step_north + base_north * projected)
    forces = jnp.stack([force_east, force_north])
    analysed = jnp.einsum('tc,ftn->fcn', table, forces, precision=highest) * (2.0 / table.shape[0])
    drag_rate = drag_row * lax.optimization_barrier(jnp.mean(magnitude, axis=0))
    return (analysed, drag_rate)

def precondition(residual, angular, rotation, drag_rate):
    shaped = residual.reshape((3, residual.shape[1] // 2, 2) + residual.shape[2:])
    cos_part = shaped[:, :, 0]
    sin_part = shaped[:, :, 1]
    height_cos = -sin_part[0] / angular
    height_sin = cos_part[0] / angular
    real_rate = drag_rate + LINEAR_DRAG
    det_real = real_rate * real_rate - angular * angular + rotation * rotation
    det_imag = 2.0 * real_rate * angular
    det_norm = det_real * det_real + det_imag * det_imag
    inv_real = det_real / det_norm
    inv_imag = -det_imag / det_norm
    east_re = cos_part[1]
    east_im = -sin_part[1]
    north_re = cos_part[2]
    north_im = -sin_part[2]
    num_east_re = real_rate * east_re - angular * east_im + rotation * north_re
    num_east_im = real_rate * east_im + angular * east_re + rotation * north_im
    num_north_re = -rotation * east_re + real_rate * north_re - angular * north_im
    num_north_im = -rotation * east_im + real_rate * north_im + angular * north_re
    east_out_re = num_east_re * inv_real - num_east_im * inv_imag
    east_out_im = num_east_re * inv_imag + num_east_im * inv_real
    north_out_re = num_north_re * inv_real - num_north_im * inv_imag
    north_out_im = num_north_re * inv_imag + num_north_im * inv_real
    cosines = jnp.stack([height_cos, east_out_re, north_out_re])
    sines = jnp.stack([height_sin, -east_out_im, -north_out_im])
    return jnp.stack([cosines, sines], axis=2).reshape(residual.shape)

def extend_grid(planes):
    wrapped = jnp.concatenate([planes[..., -1:], planes, planes[..., :1]], axis=-1)
    return jnp.pad(wrapped, ((0, 0), (0, 0), (1, 1), (0, 0)))

def reference(direction, base_flow, water_depth, drag_factor, wet_mask):
    wet_cells = wet_mask.astype(jnp.float32)
    height = direction[0] * wet_cells
    east = direction[1] * wet_cells
    north = direction[2] * wet_cells
    planes = jnp.stack([height, east, north, water_depth * east, water_depth * north])
    extended = extend_grid(planes)
    angular = OMEGA_STEP * jnp.arange(1, NCON + 1, dtype=jnp.float32)
    rotation = rotation_of(jnp.arange(NLAT, dtype=jnp.int32), NLAT)
    linear_part = linear_residual(extended, NLAT, NLON, angular[:, None, None], rotation[:, None])
    table = samples_table(NTIME, NCON)
    flows = jnp.concatenate([base_flow, jnp.stack([east, north])], axis=0)

    def one_row(items):
        return friction_row(items[0], items[1], table)
    friction, drag_rate = lax.map(one_row, (jnp.moveaxis(flows, 2, 0), drag_factor))
    friction = jnp.moveaxis(friction, 0, 2)
    residual = (linear_part + jnp.concatenate([jnp.zeros_like(friction[:1]), friction], axis=0)) * wet_cells
    return precondition(residual, angular[:, None, None], rotation[:, None], drag_rate)
```

```python
import math

import jax
import jax.numpy as jnp
import ml_dtypes
import numpy as np
from jax import lax
from jax.experimental import pallas as pl
from jax.experimental.pallas import tpu as pltpu
from jax.sharding import PartitionSpec as P

NCON = 16
NTIME = 256
LANES = 128
SUB = 8

LINEAR_DRAG = 0.5
GRAVITY = 1.0
OMEGA_STEP = 0.25
SPEED_SOFT = 0.01
CHUNKS = 4
VMEM_BYTES = 48 * 1024 * 1024


def split_table():
    sample = np.arange(NTIME)[:, None]
    harmonic = np.arange(1, NCON + 1)[None, :]
    phase = (sample * harmonic % NTIME) * (2.0 * math.pi / NTIME)
    table = np.stack([np.cos(phase), np.sin(phase)], axis=2).reshape(NTIME, 2 * NCON)
    table = table.astype(np.float32)
    high = table.astype(ml_dtypes.bfloat16)
    low = (table - high.astype(np.float32)).astype(ml_dtypes.bfloat16)
    return high, low


def split_value(value):
    high = value.astype(jnp.bfloat16)
    low = (value - high.astype(jnp.float32)).astype(jnp.bfloat16)
    return high, low


def friction_kernel(groups, coefs, synth_ref, analyse_ref, flows_ref, out_ref):
    width = 2 * LANES
    columns = 2 * NCON

    def body(step, carry):
        tile = step * 2
        loaded = []
        for source in range(groups):
            pair = [flows_ref[source, tile], flows_ref[source, tile + 1]]
            loaded.append(jnp.concatenate(pair, axis=1))
        series = []
        for field in range(4):
            rows = slice(field * coefs, (field + 1) * coefs)
            values = jnp.concatenate([part[rows] for part in loaded], axis=0)
            high, low = split_value(values)
            operand = jnp.concatenate([high, low, high], axis=0)
            series.append(
                jnp.dot(synth_ref[...], operand, preferred_element_type=jnp.float32)
            )
        base_east, base_north, step_east, step_north = series
        square = base_east * base_east + base_north * base_north + SPEED_SOFT
        inverse = lax.rsqrt(square)
        speed = square * inverse
        projected = (base_east * step_east + base_north * step_north) * inverse
        forces = (
            speed * step_east + base_east * projected,
            speed * step_north + base_north * projected,
        )
        mean = jnp.sum(speed, axis=0, keepdims=True) * (1.0 / NTIME)
        analysed = []
        for force in forces:
            high, low = split_value(force)
            both = jnp.dot(analyse_ref[...], high, preferred_element_type=jnp.float32)
            rest = jnp.dot(
                analyse_ref[:columns, :], low, preferred_element_type=jnp.float32
            )
            analysed.append(both[:columns] + both[columns:] + rest)
        for part in range(2):
            lanes = slice(part * LANES, (part + 1) * LANES)
            for target in range(groups):
                rows = slice(target * coefs, (target + 1) * coefs)
                block = jnp.concatenate(
                    [analysed[0][rows, lanes], analysed[1][rows, lanes]], axis=0
                )
                start = pl.multiple_of((tile + part) * 2 * coefs, SUB)
                out_ref[target, 0, pl.ds(start, 2 * coefs), :] = block
                out_ref[target, 0, pl.ds(SUB * 2 * coefs + tile + part, 1), :] = mean[:, lanes]
        return carry

    lax.fori_loop(0, SUB // 2, body, 0)


def friction_call(flows, groups, coefs):
    tiles = flows.shape[1]
    rows = flows.shape[2]
    high, low = split_table()
    synth = np.concatenate([high, high, low], axis=1)
    scale = 2.0 / NTIME
    analyse = np.concatenate([high.T, low.T], axis=0).astype(np.float32) * scale
    analyse = analyse.astype(ml_dtypes.bfloat16)
    out_rows = SUB * (2 * coefs + 1)
    cells = groups * tiles * LANES
    return pl.pallas_call(
        lambda *refs: friction_kernel(groups, coefs, *refs),
        out_shape=jax.ShapeDtypeStruct((groups, tiles // SUB, out_rows, LANES), jnp.float32),
        grid=(tiles // SUB,),
        in_specs=[
            pl.BlockSpec(synth.shape, lambda i: (0, 0)),
            pl.BlockSpec(analyse.shape, lambda i: (0, 0)),
            pl.BlockSpec((groups, SUB, rows, LANES), lambda i: (0, i, 0, 0)),
        ],
        out_specs=pl.BlockSpec((groups, 1, out_rows, LANES), lambda i: (0, i, 0, 0)),
        compiler_params=pltpu.CompilerParams(vmem_limit_bytes=VMEM_BYTES),
        cost_estimate=pl.CostEstimate(
            flops=2 * cells * NTIME * 96 * 6 // 4, bytes_accessed=cells * 128, transcendentals=0
        ),
        name="friction",
    )(jnp.asarray(synth), jnp.asarray(analyse), flows)


def finish_kernel(coefs, lane_tiles, scalars_ref, first_block, refs):
    direction_ref, wet_ref, depth_ref, drag_ref, edge_ref, slab_ref, back_ref, out_ref = refs
    columns = lane_tiles * LANES
    wet = wet_ref[...].astype(jnp.float32)
    depth = depth_ref[...]
    drag = drag_ref[...]
    lane = lax.broadcasted_iota(jnp.int32, (SUB, columns), 1)
    sub = lax.broadcasted_iota(jnp.int32, (SUB, columns), 0)
    block = (first_block + pl.program_id(0)) * SUB
    row = (block + sub).astype(jnp.float32)
    rotation = 0.5 + (row + scalars_ref[0] + 0.5) * scalars_ref[1]

    def wide(slab):
        return jnp.concatenate([slab] * lane_tiles, axis=1)

    def west(value, slab):
        return jnp.where(lane == 0, wide(slab), pltpu.roll(value, 1, 1))

    def east_of(value, slab):
        return jnp.where(lane == columns - 1, wide(slab), pltpu.roll(value, columns - 1, 1))

    def above(value, edge):
        return jnp.where(sub == 0, edge, pltpu.roll(value, 1, 0))

    def below(value, edge):
        return jnp.where(sub == SUB - 1, edge, pltpu.roll(value, SUB - 1, 0))

    group_tiles = []
    for lane_tile in range(lane_tiles):
        rows = []
        for r in range(SUB):
            tile = r * lane_tiles + lane_tile
            start = (tile % SUB) * 2 * coefs
            rows.append(back_ref[tile // SUB, start : start + 2 * coefs, :])
        group_tiles.append(jnp.swapaxes(jnp.stack(rows, axis=0), 0, 1))
    friction = [
        jnp.concatenate([part[index] for part in group_tiles], axis=1) * drag
        for index in range(2 * coefs)
    ]
    speed = []
    for lane_tile in range(lane_tiles):
        rows = []
        for r in range(SUB):
            tile = r * lane_tiles + lane_tile
            at = SUB * 2 * coefs + tile % SUB
            rows.append(back_ref[tile // SUB, at : at + 1, :])
        speed.append(jnp.concatenate(rows, axis=0))
    real_rate = drag * jnp.concatenate(speed, axis=1) + LINEAR_DRAG

    for k in range(coefs // 2):
        angular = scalars_ref[2 + k]
        residual = []
        planes = []
        for part in range(2):
            c = 2 * k + part
            planes.append([direction_ref[p, c] * wet for p in range(3)])
        for part in range(2):
            c = 2 * k + part
            height, east, north = planes[part]
            other = planes[1 - part]
            signed = angular if part == 0 else -angular
            east_flux = depth * east
            north_flux = depth * north
            north_up = above(north, edge_ref[0, 0, c : c + 1])
            flux_up = above(north_flux, edge_ref[0, 1, c : c + 1])
            height_down = below(height, edge_ref[0, 2, c : c + 1])
            east_down = below(east, edge_ref[0, 3, c : c + 1])
            res_height = (
                signed * other[0]
                + east_flux
                - west(east_flux, slab_ref[2, c])
                + north_flux
                - flux_up
            )
            north_mean = 0.25 * (
                north
                + east_of(north, slab_ref[4, c])
                + north_up
                + east_of(north_up, slab_ref[5, c])
            )
            east_mean = 0.25 * (
                east
                + west(east, slab_ref[0, c])
                + east_down
                + west(east_down, slab_ref[1, c])
            )
            res_east = (
                signed * other[1]
                + LINEAR_DRAG * east
                - rotation * north_mean
                + GRAVITY * (east_of(height, slab_ref[3, c]) - height)
            )
            res_north = (
                signed * other[2]
                + LINEAR_DRAG * north
                + rotation * east_mean
                + GRAVITY * (height_down - height)
            )
            residual.append(
                (
                    res_height * wet,
                    (res_east + friction[c]) * wet,
                    (res_north + friction[coefs + c]) * wet,
                )
            )
        cos_part, sin_part = residual
        inverse_angular = 1.0 / (angular + jnp.zeros((SUB, columns), jnp.float32))
        out_ref[0, 2 * k] = -sin_part[0] * inverse_angular
        out_ref[0, 2 * k + 1] = cos_part[0] * inverse_angular
        det_real = real_rate * real_rate - angular * angular + rotation * rotation
        det_imag = 2.0 * real_rate * angular
        inverse_norm = 1.0 / (det_real * det_real + det_imag * det_imag)
        inv_real = det_real * inverse_norm
        inv_imag = -det_imag * inverse_norm
        east_re, north_re = cos_part[1], cos_part[2]
        east_im, north_im = -sin_part[1], -sin_part[2]
        num_east_re = real_rate * east_re - angular * east_im + rotation * north_re
        num_east_im = real_rate * east_im + angular * east_re + rotation * north_im
        num_north_re = -rotation * east_re + real_rate * north_re - angular * north_im
        num_north_im = -rotation * east_im + real_rate * north_im + angular * north_re
        out_ref[1, 2 * k] = num_east_re * inv_real - num_east_im * inv_imag
        out_ref[1, 2 * k + 1] = -(num_east_re * inv_imag + num_east_im * inv_real)
        out_ref[2, 2 * k] = num_north_re * inv_real - num_north_im * inv_imag
        out_ref[2, 2 * k + 1] = -(num_north_re * inv_imag + num_north_im * inv_real)


def finish_call(scalars, direction, wet_mask, depth, drag, edges, slabs, back, result, start, blocks):
    coefs = direction.shape[1]
    columns = direction.shape[3]
    lane_tiles = columns // LANES

    def kernel(scalars_ref, *refs):
        if result is not None:
            refs = refs[:7] + refs[8:]
        finish_kernel(coefs, lane_tiles, scalars_ref, start, refs)

    flat = pl.BlockSpec((SUB, columns), lambda i: (start + i, 0))
    planes = pl.BlockSpec((3, coefs, SUB, columns), lambda i: (0, 0, start + i, 0))
    in_specs = [
        pl.BlockSpec(memory_space=pltpu.SMEM),
        planes,
        flat,
        flat,
        flat,
        pl.BlockSpec((1, 4, coefs, columns), lambda i: (start + i, 0, 0, 0)),
        pl.BlockSpec((6, coefs, SUB, LANES), lambda i: (0, 0, start + i, 0)),
        pl.BlockSpec((lane_tiles,) + back.shape[1:], lambda i: (i, 0, 0)),
    ]
    operands = [scalars, direction, wet_mask, depth, drag, edges, slabs, back]
    aliases = {}
    if result is not None:
        in_specs.append(pl.BlockSpec(memory_space=pl.ANY))
        operands.append(result)
        aliases = {8: 0}
    return pl.pallas_call(
        kernel,
        out_shape=jax.ShapeDtypeStruct(direction.shape, jnp.float32),
        grid=(blocks,),
        in_specs=in_specs,
        out_specs=planes,
        input_output_aliases=aliases,
        compiler_params=pltpu.CompilerParams(vmem_limit_bytes=VMEM_BYTES),
        cost_estimate=pl.CostEstimate(
            flops=0, bytes_accessed=blocks * SUB * columns * coefs * 36, transcendentals=0
        ),
        name="finish",
    )(*operands)


def shifted(block, axis, step, wrap):
    count = lax.axis_size(axis)
    pairs = [
        (i, (i + step) % count) for i in range(count) if wrap or 0 <= i + step < count
    ]
    return lax.ppermute(block, axis, pairs)


def halo(direction, wet, depth):
    height, east, north = direction[0], direction[1], direction[2]
    rows = direction.shape[2]
    last = north[:, SUB - 1 :: SUB] * wet[SUB - 1 :: SUB]
    up = jnp.stack([last, last * depth[SUB - 1 :: SUB]])
    first = wet[::SUB]
    down = jnp.stack([height[:, ::SUB] * first, east[:, ::SUB] * first])
    from_above = shifted(up[:, :, -1:], "lat", 1, False)
    from_below = shifted(down[:, :, :1], "lat", -1, False)
    up = jnp.concatenate([from_above, up[:, :, :-1]], axis=2)
    down = jnp.concatenate([down[:, :, 1:], from_below], axis=2)
    edges = jnp.moveaxis(jnp.concatenate([up, down], axis=0), 2, 0)
    wet_last = wet[:, -1]
    east_col = east[:, :, -1] * wet_last
    east_below = jnp.concatenate([east_col[:, 1:], from_below[1, :, :, -1]], axis=1)
    north_col = north[:, :, 0] * wet[:, 0]
    north_above = jnp.concatenate([from_above[0, :, :, 0], north_col[:, :-1]], axis=1)
    to_right = jnp.stack([east_col, east_below, east_col * depth[:, -1]])
    to_left = jnp.stack([height[:, :, 0] * wet[:, 0], north_col, north_above])
    cols = jnp.concatenate(
        [shifted(to_right, "lon", 1, True), shifted(to_left, "lon", -1, True)], axis=0
    )
    slabs = jnp.broadcast_to(cols[:, :, :, None], cols.shape + (LANES,))
    return edges, slabs


def exchange(block):
    return lax.all_to_all(block, "freq", split_axis=0, concat_axis=0, tiled=True)


def local(direction, base_flow, water_depth, drag_factor, wet_mask):
    coefs, tile_rows, tile_cols = direction.shape[1:]
    groups = lax.axis_size("freq")
    member = lax.axis_index("freq")
    lat_place = lax.axis_index("lat")
    total_rows = tile_rows * lax.axis_size("lat")
    lane_tiles = tile_cols // LANES
    wet = wet_mask.astype(jnp.float32)
    angular = OMEGA_STEP * (
        member * (coefs // 2) + jnp.arange(coefs // 2, dtype=jnp.int32) + 1
    ).astype(jnp.float32)
    row_start = (lat_place * tile_rows).astype(jnp.float32)
    scalars = jnp.concatenate(
        [jnp.stack([row_start, jnp.float32(1.0 / total_rows)]), angular]
    )
    edges, slabs = halo(direction, wet, water_depth)
    rows = tile_rows // CHUNKS
    band = rows // groups
    result = None
    for chunk in range(CHUNKS):
        span = slice(chunk * rows, (chunk + 1) * rows)
        flows = jnp.concatenate([base_flow[:, :, span], direction[1:, :, span]], axis=0)
        flows = flows.reshape(4, coefs, groups, band, lane_tiles, LANES)
        flows = flows.transpose(2, 3, 4, 0, 1, 5)
        flows = flows.reshape(groups, band * lane_tiles, 4 * coefs, LANES)
        flows = exchange(flows)
        back = friction_call(flows, groups, coefs)
        back = exchange(back)
        back = back.reshape((-1,) + back.shape[2:])
        result = finish_call(
            scalars, direction, wet_mask, water_depth, drag_factor, edges, slabs, back,
            result, chunk * rows // SUB, rows // SUB,
        )
    return result


def solution(mesh):
    placed = (
        P(None, "freq", "lat", "lon"),
        P(None, "freq", "lat", "lon"),
        P("lat", "lon"),
        P("lat", "lon"),
        P("lat", "lon"),
    )
    return jax.shard_map(
        local, mesh=mesh, in_specs=placed, out_specs=P(None, "freq", "lat", "lon"), check_vma=False
    )
```

```python
import math

import jax
import jax.numpy as jnp
import ml_dtypes
import numpy as np
from jax import lax
from jax.experimental import pallas as pl
from jax.experimental.pallas import tpu as pltpu
from jax.sharding import PartitionSpec as P

NCON = 16
NTIME = 256
LANES = 128
SUB = 8

LINEAR_DRAG = 0.5
GRAVITY = 1.0
OMEGA_STEP = 0.25
SPEED_SOFT = 0.01
VMEM_BYTES = 48 * 1024 * 1024


def split_table():
    sample = np.arange(NTIME)[:, None]
    harmonic = np.arange(1, NCON + 1)[None, :]
    phase = (sample * harmonic % NTIME) * (2.0 * math.pi / NTIME)
    table = np.stack([np.cos(phase), np.sin(phase)], axis=2).reshape(NTIME, 2 * NCON)
    table = table.astype(np.float32)
    high = table.astype(ml_dtypes.bfloat16)
    low = (table - high.astype(np.float32)).astype(ml_dtypes.bfloat16)
    return high, low


def split_value(value):
    high = value.astype(jnp.bfloat16)
    low = (value - high.astype(jnp.float32)).astype(jnp.bfloat16)
    return high, low


def friction_kernel(groups, coefs, place_ref, synth_ref, analyse_ref, *refs):
    flow_refs, out_refs = refs[:groups], refs[groups:]
    columns = 2 * NCON

    def body(step, carry):
        tile = step * 2
        loaded = []
        for source in range(groups):
            pair = [flow_refs[source][tile], flow_refs[source][tile + 1]]
            loaded.append(jnp.concatenate(pair, axis=1))
        series = []
        for field in range(4):
            rows = slice(field * coefs, (field + 1) * coefs)
            values = jnp.concatenate([part[rows] for part in loaded], axis=0)
            high, low = split_value(values)
            operand = jnp.concatenate([high, low, high], axis=0)
            series.append(
                jnp.dot(synth_ref[0], operand, preferred_element_type=jnp.float32)
            )
        base_east, base_north, step_east, step_north = series
        square = base_east * base_east + base_north * base_north + SPEED_SOFT
        inverse = lax.rsqrt(square)
        speed = square * inverse
        projected = (base_east * step_east + base_north * step_north) * inverse
        forces = (
            speed * step_east + base_east * projected,
            speed * step_north + base_north * projected,
        )
        mean = jnp.sum(speed, axis=0, keepdims=True) * (1.0 / NTIME)
        analysed = []
        for force in forces:
            high, low = split_value(force)
            both = jnp.dot(analyse_ref[0], high, preferred_element_type=jnp.float32)
            rest = jnp.dot(
                analyse_ref[0, :columns, :], low, preferred_element_type=jnp.float32
            )
            analysed.append(both[:columns] + both[columns:] + rest)
        for part in range(2):
            lanes = slice(part * LANES, (part + 1) * LANES)
            for target in range(groups):
                rows = slice(target * coefs, (target + 1) * coefs)
                block = jnp.concatenate(
                    [analysed[0][rows, lanes], analysed[1][rows, lanes]], axis=0
                )
                start = pl.multiple_of((tile + part) * 2 * coefs, SUB)
                out_refs[target][0, pl.ds(start, 2 * coefs), :] = block
                at = SUB * 2 * coefs + tile + part
                out_refs[target][0, pl.ds(at, 1), :] = mean[:, lanes]
        return carry

    lax.fori_loop(0, SUB // 2, body, 0)


def placed_tables(groups, coefs):
    high, low = split_table()
    synth, analyse = [], []
    for member in range(groups):
        sources = [(member - step) % groups for step in range(groups)]
        targets = [(member + step) % groups for step in range(groups)]
        source = np.concatenate([np.arange(coefs) + m * coefs for m in sources])
        target = np.concatenate([np.arange(coefs) + m * coefs for m in targets])
        synth.append(np.concatenate([high[:, source], high[:, source], low[:, source]], axis=1))
        both = np.concatenate([high[:, target].T, low[:, target].T], axis=0)
        analyse.append((both.astype(np.float32) * (2.0 / NTIME)).astype(ml_dtypes.bfloat16))
    return np.stack(synth), np.stack(analyse)


def friction_call(place, flows, coefs):
    groups = len(flows)
    tiles, rows = flows[0].shape[:2]
    synth, analyse = placed_tables(groups, coefs)
    out_rows = SUB * (2 * coefs + 1)
    cells = groups * tiles * LANES
    grid_spec = pltpu.PrefetchScalarGridSpec(
        num_scalar_prefetch=1,
        grid=(tiles // SUB,),
        in_specs=[
            pl.BlockSpec((1,) + synth.shape[1:], lambda i, place: (place[0], 0, 0)),
            pl.BlockSpec((1,) + analyse.shape[1:], lambda i, place: (place[0], 0, 0)),
        ]
        + [pl.BlockSpec((SUB, rows, LANES), lambda i, place: (i, 0, 0))] * groups,
        out_specs=[pl.BlockSpec((1, out_rows, LANES), lambda i, place: (i, 0, 0))] * groups,
    )
    out = jax.ShapeDtypeStruct((tiles // SUB, out_rows, LANES), jnp.float32)
    return pl.pallas_call(
        lambda *refs: friction_kernel(groups, coefs, *refs),
        out_shape=[out] * groups,
        grid_spec=grid_spec,
        compiler_params=pltpu.CompilerParams(vmem_limit_bytes=VMEM_BYTES),
        cost_estimate=pl.CostEstimate(
            flops=cells * NTIME * 512, bytes_accessed=cells * 128, transcendentals=0
        ),
        name="friction",
    )(place, jnp.asarray(synth), jnp.asarray(analyse), *flows)


def finish_kernel(coefs, lane_tiles, blocks_ref, scalars_ref, refs):
    direction_ref, wet_ref, depth_ref, drag_ref, edge_ref, slab_ref, back_ref, out_ref = refs
    columns = lane_tiles * LANES
    wet = wet_ref[...].astype(jnp.float32)
    depth = depth_ref[...]
    drag = drag_ref[...]
    lane = lax.broadcasted_iota(jnp.int32, (SUB, columns), 1)
    sub = lax.broadcasted_iota(jnp.int32, (SUB, columns), 0)
    block = blocks_ref[pl.program_id(0)] * SUB
    row = (block + sub).astype(jnp.float32)
    rotation = 0.5 + (row + scalars_ref[0] + 0.5) * scalars_ref[1]

    def wide(slab):
        return jnp.concatenate([slab] * lane_tiles, axis=1)

    def west(value, slab):
        return jnp.where(lane == 0, wide(slab), pltpu.roll(value, 1, 1))

    def east_of(value, slab):
        return jnp.where(lane == columns - 1, wide(slab), pltpu.roll(value, columns - 1, 1))

    def above(value, edge):
        return jnp.where(sub == 0, edge, pltpu.roll(value, 1, 0))

    def below(value, edge):
        return jnp.where(sub == SUB - 1, edge, pltpu.roll(value, SUB - 1, 0))

    group_tiles = []
    for lane_tile in range(lane_tiles):
        rows = []
        for r in range(SUB):
            tile = r * lane_tiles + lane_tile
            start = (tile % SUB) * 2 * coefs
            rows.append(back_ref[tile // SUB, start : start + 2 * coefs, :])
        group_tiles.append(jnp.swapaxes(jnp.stack(rows, axis=0), 0, 1))
    friction = [
        jnp.concatenate([part[index] for part in group_tiles], axis=1) * drag
        for index in range(2 * coefs)
    ]
    speed = []
    for lane_tile in range(lane_tiles):
        rows = []
        for r in range(SUB):
            tile = r * lane_tiles + lane_tile
            at = SUB * 2 * coefs + tile % SUB
            rows.append(back_ref[tile // SUB, at : at + 1, :])
        speed.append(jnp.concatenate(rows, axis=0))
    real_rate = drag * jnp.concatenate(speed, axis=1) + LINEAR_DRAG

    for k in range(coefs // 2):
        angular = scalars_ref[2 + k]
        residual = []
        planes = []
        for part in range(2):
            c = 2 * k + part
            planes.append([direction_ref[p, c] * wet for p in range(3)])
        for part in range(2):
            c = 2 * k + part
            height, east, north = planes[part]
            other = planes[1 - part]
            signed = angular if part == 0 else -angular
            east_flux = depth * east
            north_flux = depth * north
            north_up = above(north, edge_ref[0, 0, c : c + 1])
            flux_up = above(north_flux, edge_ref[0, 1, c : c + 1])
            height_down = below(height, edge_ref[0, 2, c : c + 1])
            east_down = below(east, edge_ref[0, 3, c : c + 1])
            res_height = (
                signed * other[0]
                + east_flux
                - west(east_flux, slab_ref[2, c])
                + north_flux
                - flux_up
            )
            north_mean = 0.25 * (
                north
                + east_of(north, slab_ref[4, c])
                + north_up
                + east_of(north_up, slab_ref[5, c])
            )
            east_mean = 0.25 * (
                east
                + west(east, slab_ref[0, c])
                + east_down
                + west(east_down, slab_ref[1, c])
            )
            res_east = (
                signed * other[1]
                + LINEAR_DRAG * east
                - rotation * north_mean
                + GRAVITY * (east_of(height, slab_ref[3, c]) - height)
            )
            res_north = (
                signed * other[2]
                + LINEAR_DRAG * north
                + rotation * east_mean
                + GRAVITY * (height_down - height)
            )
            residual.append(
                (
                    res_height * wet,
                    (res_east + friction[c]) * wet,
                    (res_north + friction[coefs + c]) * wet,
                )
            )
        cos_part, sin_part = residual
        inverse_angular = 1.0 / (angular + jnp.zeros((SUB, columns), jnp.float32))
        out_ref[0, 2 * k] = -sin_part[0] * inverse_angular
        out_ref[0, 2 * k + 1] = cos_part[0] * inverse_angular
        det_real = real_rate * real_rate - angular * angular + rotation * rotation
        det_imag = 2.0 * real_rate * angular
        inverse_norm = 1.0 / (det_real * det_real + det_imag * det_imag)
        inv_real = det_real * inverse_norm
        inv_imag = -det_imag * inverse_norm
        east_re, north_re = cos_part[1], cos_part[2]
        east_im, north_im = -sin_part[1], -sin_part[2]
        num_east_re = real_rate * east_re - angular * east_im + rotation * north_re
        num_east_im = real_rate * east_im + angular * east_re + rotation * north_im
        num_north_re = -rotation * east_re + real_rate * north_re - angular * north_im
        num_north_im = -rotation * east_im + real_rate * north_im + angular * north_re
        out_ref[1, 2 * k] = num_east_re * inv_real - num_east_im * inv_imag
        out_ref[1, 2 * k + 1] = -(num_east_re * inv_imag + num_east_im * inv_real)
        out_ref[2, 2 * k] = num_north_re * inv_real - num_north_im * inv_imag
        out_ref[2, 2 * k + 1] = -(num_north_re * inv_imag + num_north_im * inv_real)


def finish_call(blocks, scalars, direction, wet_mask, depth, drag, edges, slabs, back, result):
    coefs = direction.shape[1]
    columns = direction.shape[3]
    lane_tiles = columns // LANES

    def kernel(blocks_ref, scalars_ref, *refs):
        if result is not None:
            refs = refs[:7] + refs[8:]
        finish_kernel(coefs, lane_tiles, blocks_ref, scalars_ref, refs)

    flat = pl.BlockSpec((SUB, columns), lambda i, at: (at[i], 0))
    planes = pl.BlockSpec((3, coefs, SUB, columns), lambda i, at: (0, 0, at[i], 0))
    in_specs = [
        pl.BlockSpec(memory_space=pltpu.SMEM),
        planes,
        flat,
        flat,
        flat,
        pl.BlockSpec((1, 4, coefs, columns), lambda i, at: (at[i], 0, 0, 0)),
        pl.BlockSpec((6, coefs, SUB, LANES), lambda i, at: (0, 0, at[i], 0)),
        pl.BlockSpec((lane_tiles,) + back.shape[1:], lambda i, at: (i, 0, 0)),
    ]
    operands = [blocks, scalars, direction, wet_mask, depth, drag, edges, slabs, back]
    aliases = {}
    if result is not None:
        in_specs.append(pl.BlockSpec(memory_space=pl.ANY))
        operands.append(result)
        aliases = {9: 0}
    count = blocks.shape[0]
    return pl.pallas_call(
        kernel,
        out_shape=jax.ShapeDtypeStruct(direction.shape, jnp.float32),
        grid_spec=pltpu.PrefetchScalarGridSpec(
            num_scalar_prefetch=1, grid=(count,), in_specs=in_specs, out_specs=planes
        ),
        input_output_aliases=aliases,
        compiler_params=pltpu.CompilerParams(vmem_limit_bytes=VMEM_BYTES),
        cost_estimate=pl.CostEstimate(
            flops=0, bytes_accessed=count * SUB * columns * coefs * 36, transcendentals=0
        ),
        name="finish",
    )(*operands)


def shifted(block, axis, step, wrap):
    count = lax.axis_size(axis)
    pairs = [
        (i, (i + step) % count) for i in range(count) if wrap or 0 <= i + step < count
    ]
    return lax.ppermute(block, axis, pairs)


def halo(direction, wet, depth):
    height, east, north = direction[0], direction[1], direction[2]
    rows = direction.shape[2]
    last = north[:, SUB - 1 :: SUB] * wet[SUB - 1 :: SUB]
    up = jnp.stack([last, last * depth[SUB - 1 :: SUB]])
    first = wet[::SUB]
    down = jnp.stack([height[:, ::SUB] * first, east[:, ::SUB] * first])
    from_above = shifted(up[:, :, -1:], "lat", 1, False)
    from_below = shifted(down[:, :, :1], "lat", -1, False)
    up = jnp.concatenate([from_above, up[:, :, :-1]], axis=2)
    down = jnp.concatenate([down[:, :, 1:], from_below], axis=2)
    edges = jnp.moveaxis(jnp.concatenate([up, down], axis=0), 2, 0)
    wet_last = wet[:, -1]
    east_col = east[:, :, -1] * wet_last
    east_below = jnp.concatenate([east_col[:, 1:], from_below[1, :, :, -1]], axis=1)
    north_col = north[:, :, 0] * wet[:, 0]
    north_above = jnp.concatenate([from_above[0, :, :, 0], north_col[:, :-1]], axis=1)
    to_right = jnp.stack([east_col, east_below, east_col * depth[:, -1]])
    to_left = jnp.stack([height[:, :, 0] * wet[:, 0], north_col, north_above])
    cols = jnp.concatenate(
        [shifted(to_right, "lon", 1, True), shifted(to_left, "lon", -1, True)], axis=0
    )
    slabs = jnp.broadcast_to(cols[:, :, :, None], cols.shape + (LANES,))
    return edges, slabs


def local(direction, base_flow, water_depth, drag_factor, wet_mask):
    coefs, tile_rows, tile_cols = direction.shape[1:]
    groups = lax.axis_size("freq")
    member = lax.axis_index("freq")
    lat_place = lax.axis_index("lat")
    total_rows = tile_rows * lax.axis_size("lat")
    lane_tiles = tile_cols // LANES
    wet = wet_mask.astype(jnp.float32)
    angular = OMEGA_STEP * (
        member * (coefs // 2) + jnp.arange(coefs // 2, dtype=jnp.int32) + 1
    ).astype(jnp.float32)
    row_start = (lat_place * tile_rows).astype(jnp.float32)
    scalars = jnp.concatenate(
        [jnp.stack([row_start, jnp.float32(1.0 / total_rows)]), angular]
    )
    edges, slabs = halo(direction, wet, water_depth)
    place = jnp.reshape(member, (1,)).astype(jnp.int32)
    chunks = tile_rows // (groups * SUB)
    steps = jnp.arange(groups, dtype=jnp.int32)
    sources = (member - steps) % groups
    result = None
    for chunk in range(chunks):
        flows = []
        for step in range(groups):
            target = (member + step) % groups
            start = (chunk * groups + target) * SUB
            base = lax.dynamic_slice_in_dim(base_flow, start, SUB, 2)
            moving = lax.dynamic_slice_in_dim(direction[1:], start, SUB, 2)
            block = jnp.concatenate([base, moving], axis=0)
            block = block.reshape(4, coefs, SUB, lane_tiles, LANES).transpose(2, 3, 0, 1, 4)
            block = block.reshape(SUB * lane_tiles, 4 * coefs, LANES)
            flows.append(block if step == 0 else shifted(block, "freq", step, True))
        back = friction_call(place, flows, coefs)
        back = [
            block if step == 0 else shifted(block, "freq", step, True)
            for step, block in enumerate(back)
        ]
        result = finish_call(
            chunk * groups + sources, scalars, direction, wet_mask, water_depth, drag_factor,
            edges, slabs, jnp.concatenate(back, axis=0), result,
        )
    return result


def solution(mesh):
    placed = (
        P(None, "freq", "lat", "lon"),
        P(None, "freq", "lat", "lon"),
        P("lat", "lon"),
        P("lat", "lon"),
        P("lat", "lon"),
    )
    return jax.shard_map(
        local, mesh=mesh, in_specs=placed, out_specs=P(None, "freq", "lat", "lon"), check_vma=False
    )
```

```python
import math

import jax
import jax.numpy as jnp
import ml_dtypes
import numpy as np
from jax import lax
from jax.experimental import pallas as pl
from jax.experimental.pallas import tpu as pltpu
from jax.sharding import PartitionSpec as P

NCON = 16
NTIME = 256
LANES = 128
SUB = 8

LINEAR_DRAG = 0.5
GRAVITY = 1.0
OMEGA_STEP = 0.25
SPEED_SOFT = 0.01
VMEM_BYTES = 48 * 1024 * 1024
CHUNK_SHARES = (24, 25, 26, 22)
SHARE_UNITS = 128
LOOP_TILES = 8


def split_table():
    sample = np.arange(NTIME)[:, None]
    harmonic = np.arange(1, NCON + 1)[None, :]
    phase = (sample * harmonic % NTIME) * (2.0 * math.pi / NTIME)
    table = np.stack([np.cos(phase), np.sin(phase)], axis=2).reshape(NTIME, 2 * NCON)
    table = table.astype(np.float32)
    high = table.astype(ml_dtypes.bfloat16)
    low = (table - high.astype(np.float32)).astype(ml_dtypes.bfloat16)
    return high, low


def split_value(value):
    high = value.astype(jnp.bfloat16)
    low = (value - high.astype(jnp.float32)).astype(jnp.bfloat16)
    return high, low


def friction_kernel(groups, coefs, tiles, place_ref, synth_ref, analyse_ref, *refs):
    flow_refs, out_refs = refs[:groups], refs[groups:]
    columns = 2 * NCON

    def block(tile, count):
        loaded = []
        for source in range(groups):
            parts = [flow_refs[source][tile + i] for i in range(count)]
            loaded.append(jnp.concatenate(parts, axis=1))
        series = []
        for field in range(4):
            rows = slice(field * coefs, (field + 1) * coefs)
            values = jnp.concatenate([part[rows] for part in loaded], axis=0)
            high, low = split_value(values)
            operand = jnp.concatenate([high, low, high], axis=0)
            series.append(
                jnp.dot(synth_ref[0], operand, preferred_element_type=jnp.float32)
            )
        base_east, base_north, step_east, step_north = series
        square = base_east * base_east + base_north * base_north + SPEED_SOFT
        inverse = lax.rsqrt(square)
        speed = square * inverse
        projected = (base_east * step_east + base_north * step_north) * inverse
        forces = (
            speed * step_east + base_east * projected,
            speed * step_north + base_north * projected,
        )
        mean = jnp.sum(speed, axis=0, keepdims=True) * (1.0 / NTIME)
        analysed = []
        for force in forces:
            high, low = split_value(force)
            both = jnp.dot(analyse_ref[0], high, preferred_element_type=jnp.float32)
            rest = jnp.dot(
                analyse_ref[0, :columns, :], low, preferred_element_type=jnp.float32
            )
            analysed.append(both[:columns] + both[columns:] + rest)
        for part in range(count):
            lanes = slice(part * LANES, (part + 1) * LANES)
            for target in range(groups):
                rows = slice(target * coefs, (target + 1) * coefs)
                values = jnp.concatenate(
                    [analysed[0][rows, lanes], analysed[1][rows, lanes]], axis=0
                )
                start = pl.multiple_of((tile + part) * 2 * coefs, SUB)
                out_refs[target][pl.ds(start, 2 * coefs), :] = values
                at = tiles * 2 * coefs + tile + part
                out_refs[target][pl.ds(at, 1), :] = mean[:, lanes]

    def body(step, carry):
        block(step * 2, 2)
        return carry

    lax.fori_loop(0, tiles // 2, body, 0)
    if tiles % 2:
        block(tiles - 1, 1)


def placed_tables(groups, coefs):
    high, low = split_table()
    synth, analyse = [], []
    for member in range(groups):
        sources = [(member - step) % groups for step in range(groups)]
        targets = [(member + step) % groups for step in range(groups)]
        source = np.concatenate([np.arange(coefs) + m * coefs for m in sources])
        target = np.concatenate([np.arange(coefs) + m * coefs for m in targets])
        synth.append(np.concatenate([high[:, source], high[:, source], low[:, source]], axis=1))
        both = np.concatenate([high[:, target].T, low[:, target].T], axis=0)
        analyse.append((both.astype(np.float32) * (2.0 / NTIME)).astype(ml_dtypes.bfloat16))
    return np.stack(synth), np.stack(analyse)


def piece_rows(tiles, coefs):
    return tiles * 2 * coefs + -(-tiles // SUB) * SUB


def friction_call(place, flows, coefs):
    groups = len(flows)
    tiles = flows[0].shape[0]
    synth, analyse = placed_tables(groups, coefs)
    cells = groups * tiles * LANES
    out_shape = (piece_rows(tiles, coefs), LANES)
    grid_spec = pltpu.PrefetchScalarGridSpec(
        num_scalar_prefetch=1,
        grid=(1,),
        in_specs=[
            pl.BlockSpec((1,) + synth.shape[1:], lambda i, place: (place[0], 0, 0)),
            pl.BlockSpec((1,) + analyse.shape[1:], lambda i, place: (place[0], 0, 0)),
        ]
        + [pl.BlockSpec(flows[0].shape, lambda i, place: (0, 0, 0))] * groups,
        out_specs=[pl.BlockSpec(out_shape, lambda i, place: (0, 0))] * groups,
    )
    return pl.pallas_call(
        lambda *refs: friction_kernel(groups, coefs, tiles, *refs),
        out_shape=[jax.ShapeDtypeStruct(out_shape, jnp.float32)] * groups,
        grid_spec=grid_spec,
        compiler_params=pltpu.CompilerParams(vmem_limit_bytes=VMEM_BYTES),
        cost_estimate=pl.CostEstimate(
            flops=cells * NTIME * 512, bytes_accessed=cells * 128, transcendentals=0
        ),
        name="friction",
    )(place, jnp.asarray(synth), jnp.asarray(analyse), *flows)


def index_kernel(wet_ref, index_ref, place_ref, offset_ref, scratch):
    blocks = scratch.shape[0]
    rows, cols = wet_ref.shape
    at = 0
    for row in range(0, rows, SUB):
        for col in range(0, cols, LANES):
            part = wet_ref[row : row + SUB, col : col + LANES]
            scratch[at : at + SUB, :] = jnp.where(part != 0, 1.0, 0.0)
            at += SUB
    wet = scratch[...].astype(jnp.bfloat16)
    earlier = lax.broadcasted_iota(jnp.int32, (LANES, LANES), 0)
    later = lax.broadcasted_iota(jnp.int32, (LANES, LANES), 1)
    before = jnp.where(earlier < later, 1.0, 0.0).astype(jnp.bfloat16)
    ones = jnp.ones((LANES, LANES), jnp.bfloat16)
    rank = jnp.dot(wet, before, preferred_element_type=jnp.float32)
    count = jnp.dot(wet, ones, preferred_element_type=jnp.float32)
    low = lax.broadcasted_iota(jnp.int32, (blocks, blocks), 0)
    high = lax.broadcasted_iota(jnp.int32, (blocks, blocks), 1)
    summing = jnp.where(high < low, 1.0, 0.0).astype(jnp.bfloat16)
    offset = jnp.dot(summing, count.astype(jnp.bfloat16), preferred_element_type=jnp.float32)
    lane = lax.broadcasted_iota(jnp.int32, (blocks, LANES), 1)
    rank = rank.astype(jnp.int32)
    held = jnp.where(scratch[...] > 0.5, lane + LANES * (lane - rank), 0)
    for bit in range(7):
        step = 1 << bit
        coming = pltpu.roll(held, LANES - step, 1)
        moves = (coming >> (7 + bit)) & 1
        stays = 1 - ((held >> (7 + bit)) & 1)
        held = jnp.where(moves == 1, coming, held * stays)
    source = held & (LANES - 1)
    shift = offset.astype(jnp.int32) & (LANES - 1)
    index_ref[...] = jnp.take_along_axis(
        source, (lane - shift) & (LANES - 1), axis=1, mode="promise_in_bounds"
    )
    place_ref[...] = shift + rank
    eye = jnp.where(earlier == later, 1.0, 0.0)
    cubes = offset.reshape(blocks // LANES, LANES, LANES)
    table = jnp.sum(cubes * eye[None], axis=1)
    total = offset[blocks - 1 : blocks] + count[blocks - 1 : blocks]
    offset_ref[: blocks // LANES, :] = table.astype(jnp.int32)
    offset_ref[blocks // LANES : blocks // LANES + 1, :] = total.astype(jnp.int32)


def index_call(wet_mask):
    rows, cols = wet_mask.shape
    blocks = rows * cols // LANES
    table = -(-(blocks // LANES + 1) // SUB) * SUB
    return pl.pallas_call(
        index_kernel,
        out_shape=[
            jax.ShapeDtypeStruct((blocks, LANES), jnp.int32),
            jax.ShapeDtypeStruct((blocks, LANES), jnp.int32),
            jax.ShapeDtypeStruct((table, LANES), jnp.int32),
        ],
        scratch_shapes=[pltpu.VMEM((blocks, LANES), jnp.float32)],
        compiler_params=pltpu.CompilerParams(vmem_limit_bytes=VMEM_BYTES),
        name="index",
    )(wet_mask)


def pack_kernel(groups, coefs, tiles, params_ref, offset_ref, index_ref, base_ref, step_ref, *refs):
    out_refs = refs[:groups]
    held, stage, in_sem, out_sem = refs[groups:]
    columns = held.shape[-1]
    lane_tiles = columns // LANES
    per_block = SUB * lane_tiles
    row_blocks = index_ref.shape[0] // per_block
    count = groups * tiles
    first_tile = params_ref[1]
    low = first_tile * LANES
    high = low + count * LANES

    def offset_of(block):
        return offset_ref[block // LANES, block % LANES]

    begin = jnp.int32(0)
    end = jnp.int32(0)
    for block in range(row_blocks):
        begin += (offset_of((block + 1) * per_block) <= low).astype(jnp.int32)
        end += (offset_of(block * per_block) < high).astype(jnp.int32)
    end = jnp.maximum(end, begin)

    def copies(block):
        slot = block % 2
        rows = pl.ds(pl.multiple_of(block * SUB, SUB), SUB)
        return (
            pltpu.make_async_copy(
                base_ref.at[:, :, rows, :], held.at[slot, pl.ds(0, 2)], in_sem.at[slot, 0]
            ),
            pltpu.make_async_copy(
                step_ref.at[pl.ds(1, 2), :, rows, :], held.at[slot, pl.ds(2, 2)], in_sem.at[slot, 1]
            ),
        )

    @pl.when(begin < end)
    def _():
        for copy in copies(begin):
            copy.start()

    lane = lax.broadcasted_iota(jnp.int32, (coefs, LANES), 1)

    def place_of(offset):
        return jnp.clip((offset >> 7) - first_tile + 1, 0, count + 1)

    def body(block, current):
        @pl.when(block + 1 < end)
        def _():
            for copy in copies(block + 1):
                copy.start()

        for copy in copies(block):
            copy.wait()
        slot = block % 2
        for lane_tile in range(lane_tiles):
            lanes = slice(lane_tile * LANES, (lane_tile + 1) * LANES)
            turned = [
                jnp.swapaxes(held[slot, field, :, :, lanes], 0, 1) for field in range(4)
            ]
            start = block * per_block + lane_tile * SUB
            index = index_ref[pl.ds(pl.multiple_of(start, SUB), SUB), :]
            for r in range(SUB):
                offset = offset_of(start + r)
                following = offset_of(start + r + 1)
                shift = offset & (LANES - 1)
                crossing = (following >> 7) > (offset >> 7)
                source = jnp.broadcast_to(index[r : r + 1], (coefs, LANES))
                to = place_of(offset)
                renewed = []
                for field in range(4):
                    got = jnp.take_along_axis(
                        turned[field][r], source, axis=1, mode="promise_in_bounds"
                    )
                    full = jnp.where(lane >= shift, got, current[field])
                    stage[to, field * coefs : (field + 1) * coefs, :] = full
                    renewed.append(jnp.where(crossing, got, full))
                current = tuple(renewed)
        return current

    zero = jnp.zeros((coefs, LANES), jnp.float32)
    current = lax.fori_loop(begin, end, body, (zero,) * 4)
    last = place_of(offset_of(end * per_block))
    for field in range(4):
        stage[last, field * coefs : (field + 1) * coefs, :] = current[field]
    outs = []
    for step in range(groups):
        member = lax.rem(params_ref[0] + step, groups)
        outs.append(
            pltpu.make_async_copy(
                stage.at[pl.ds(1 + member * tiles, tiles)], out_refs[step], out_sem.at[step]
            )
        )
    for copy in outs:
        copy.start()
    for copy in outs:
        copy.wait()


def pack_call(params, offset, index, base_flow, direction, groups, tiles):
    coefs, _, columns = direction.shape[1:]
    shape = (tiles, 4 * coefs, LANES)
    anywhere = pl.BlockSpec(memory_space=pl.ANY)
    grid_spec = pltpu.PrefetchScalarGridSpec(
        num_scalar_prefetch=2,
        grid=(1,),
        in_specs=[pl.BlockSpec(index.shape, lambda i, p, o: (0, 0)), anywhere, anywhere],
        out_specs=[anywhere] * groups,
        scratch_shapes=[
            pltpu.VMEM((2, 4, coefs, SUB, columns), jnp.float32),
            pltpu.VMEM((groups * tiles + 2, 4 * coefs, LANES), jnp.float32),
            pltpu.SemaphoreType.DMA((2, 2)),
            pltpu.SemaphoreType.DMA((groups,)),
        ],
    )
    return pl.pallas_call(
        lambda *refs: pack_kernel(groups, coefs, tiles, *refs),
        out_shape=[jax.ShapeDtypeStruct(shape, jnp.float32)] * groups,
        grid_spec=grid_spec,
        compiler_params=pltpu.CompilerParams(vmem_limit_bytes=VMEM_BYTES),
        cost_estimate=pl.CostEstimate(
            flops=0, bytes_accessed=groups * tiles * coefs * 4096, transcendentals=0
        ),
        name="pack",
    )(params, offset, index, base_flow, direction)


def finish_kernel(coefs, lane_tiles, row_block, first_ref, offset_ref, table_ref, scalars_ref, back, refs):
    (direction_ref, wet_ref, depth_ref, drag_ref, edge_ref, slab_ref, cell_ref, out_ref) = refs
    columns = lane_tiles * LANES
    wet = wet_ref[...].astype(jnp.float32)
    depth = depth_ref[...]
    drag = drag_ref[...]
    lane = lax.broadcasted_iota(jnp.int32, (SUB, columns), 1)
    sub = lax.broadcasted_iota(jnp.int32, (SUB, columns), 0)
    block = row_block * SUB
    row = (block + sub).astype(jnp.float32)
    rotation = 0.5 + (row + scalars_ref[0] + 0.5) * scalars_ref[1]

    def wide(slab):
        return jnp.concatenate([slab] * lane_tiles, axis=1)

    def west(value, slab):
        return jnp.where(lane == 0, wide(slab), pltpu.roll(value, 1, 1))

    def east_of(value, slab):
        return jnp.where(lane == columns - 1, wide(slab), pltpu.roll(value, columns - 1, 1))

    def above(value, edge):
        return jnp.where(sub == 0, edge, pltpu.roll(value, 1, 0))

    def below(value, edge):
        return jnp.where(sub == SUB - 1, edge, pltpu.roll(value, SUB - 1, 0))

    def gathered(here, after, index, over):
        first = jnp.take_along_axis(here, index, axis=1, mode="promise_in_bounds")
        second = jnp.take_along_axis(after, index, axis=1, mode="promise_in_bounds")
        return jnp.where(over, second, first)

    spread = []
    speed = []
    for lane_tile in range(lane_tiles):
        places = cell_ref[lane_tile * SUB : (lane_tile + 1) * SUB, :]
        rows = []
        speeds = [[], []]
        for r in range(SUB):
            at = (row_block * lane_tiles + lane_tile) * SUB + r
            tile = offset_ref[at // LANES, at % LANES] >> 7
            found = []
            for which in range(2):
                start = pl.multiple_of(table_ref[first_ref[1] * 2, tile + which], SUB)
                found.append(back[pl.ds(start, 2 * coefs), :])
                start = table_ref[first_ref[1] * 2 + 1, tile + which]
                speeds[which].append(back[pl.ds(start, 1), :])
            place = jnp.broadcast_to(places[r : r + 1], (2 * coefs, LANES))
            rows.append(gathered(found[0], found[1], place & (LANES - 1), place >= LANES))
        spread.append(jnp.swapaxes(jnp.stack(rows, axis=0), 0, 1))
        speed.append(
            gathered(
                jnp.concatenate(speeds[0], axis=0),
                jnp.concatenate(speeds[1], axis=0),
                places & (LANES - 1),
                places >= LANES,
            )
        )
    is_wet = wet > 0.5
    friction = [
        jnp.where(
            is_wet, jnp.concatenate([part[index] for part in spread], axis=1) * drag, 0.0
        )
        for index in range(2 * coefs)
    ]
    speed = jnp.where(is_wet, jnp.concatenate(speed, axis=1), 0.0)
    real_rate = drag * speed + LINEAR_DRAG

    for k in range(coefs // 2):
        angular = scalars_ref[2 + k]
        residual = []
        planes = []
        for part in range(2):
            c = 2 * k + part
            planes.append([direction_ref[p, c] * wet for p in range(3)])
        for part in range(2):
            c = 2 * k + part
            height, east, north = planes[part]
            other = planes[1 - part]
            signed = angular if part == 0 else -angular
            east_flux = depth * east
            north_flux = depth * north
            north_up = above(north, edge_ref[0, 0, c : c + 1])
            flux_up = above(north_flux, edge_ref[0, 1, c : c + 1])
            height_down = below(height, edge_ref[0, 2, c : c + 1])
            east_down = below(east, edge_ref[0, 3, c : c + 1])
            res_height = (
                signed * other[0]
                + east_flux
                - west(east_flux, slab_ref[2, c])
                + north_flux
                - flux_up
            )
            north_mean = 0.25 * (
                north
                + east_of(north, slab_ref[4, c])
                + north_up
                + east_of(north_up, slab_ref[5, c])
            )
            east_mean = 0.25 * (
                east
                + west(east, slab_ref[0, c])
                + east_down
                + west(east_down, slab_ref[1, c])
            )
            res_east = (
                signed * other[1]
                + LINEAR_DRAG * east
                - rotation * north_mean
                + GRAVITY * (east_of(height, slab_ref[3, c]) - height)
            )
            res_north = (
                signed * other[2]
                + LINEAR_DRAG * north
                + rotation * east_mean
                + GRAVITY * (height_down - height)
            )
            residual.append(
                (
                    res_height * wet,
                    (res_east + friction[c]) * wet,
                    (res_north + friction[coefs + c]) * wet,
                )
            )
        cos_part, sin_part = residual
        inverse_angular = 1.0 / (angular + jnp.zeros((SUB, columns), jnp.float32))
        out_ref[0, 2 * k] = -sin_part[0] * inverse_angular
        out_ref[0, 2 * k + 1] = cos_part[0] * inverse_angular
        det_real = real_rate * real_rate - angular * angular + rotation * rotation
        det_imag = 2.0 * real_rate * angular
        inverse_norm = 1.0 / (det_real * det_real + det_imag * det_imag)
        inv_real = det_real * inverse_norm
        inv_imag = -det_imag * inverse_norm
        east_re, north_re = cos_part[1], cos_part[2]
        east_im, north_im = -sin_part[1], -sin_part[2]
        num_east_re = real_rate * east_re - angular * east_im + rotation * north_re
        num_east_im = real_rate * east_im + angular * east_re + rotation * north_im
        num_north_re = -rotation * east_re + real_rate * north_re - angular * north_im
        num_north_im = -rotation * east_im + real_rate * north_im + angular * north_re
        out_ref[1, 2 * k] = num_east_re * inv_real - num_east_im * inv_imag
        out_ref[1, 2 * k + 1] = -(num_east_re * inv_imag + num_east_im * inv_real)
        out_ref[2, 2 * k] = num_north_re * inv_real - num_north_im * inv_imag
        out_ref[2, 2 * k + 1] = -(num_north_re * inv_imag + num_north_im * inv_real)


def finish_call(first, offset, table, scalars, arrays, pieces, rows, result):
    direction, columns = arrays[0], arrays[0].shape[3]
    coefs = direction.shape[1]
    lane_tiles = columns // LANES
    shares = 1 if result is not None else 0

    def kernel(first_ref, offset_ref, table_ref, scalars_ref, *refs):
        array_refs = refs[:7]
        piece_refs = refs[7 + shares : -3]
        out_ref, back, sem = refs[-3:]
        first = first_ref[0]
        copies = []
        at = 0
        for n, piece in enumerate(piece_refs):
            rows = piece.shape[0]
            copies.append(pltpu.make_async_copy(piece, back.at[pl.ds(at, rows)], sem.at[n]))
            at += rows
        for copy in copies:
            copy.start()
        for copy in copies:
            copy.wait()

        def body(*block_refs):
            finish_kernel(
                coefs, lane_tiles, first + pl.program_id(0), first_ref, offset_ref, table_ref,
                scalars_ref, back, block_refs,
            )

        flat = pl.BlockSpec((SUB, columns), lambda i: (first + i, 0))
        planes = pl.BlockSpec((3, coefs, SUB, columns), lambda i: (0, 0, first + i, 0))
        pltpu.emit_pipeline(
            body,
            grid=(first_ref[2],),
            in_specs=[
                planes,
                flat,
                flat,
                flat,
                pl.BlockSpec((1, 4, coefs, columns), lambda i: (first + i, 0, 0, 0)),
                pl.BlockSpec((6, coefs, SUB, LANES), lambda i: (0, 0, first + i, 0)),
                pl.BlockSpec((SUB * lane_tiles, LANES), lambda i: (first + i, 0)),
            ],
            out_specs=[planes],
        )(*array_refs, out_ref)

    anywhere = pl.BlockSpec(memory_space=pl.ANY)
    scalar = pl.BlockSpec(memory_space=pltpu.SMEM)
    operands = [first, offset, table, scalars] + list(arrays)
    if shares:
        operands.append(result)
    operands += pieces
    return pl.pallas_call(
        kernel,
        out_shape=jax.ShapeDtypeStruct(direction.shape, jnp.float32),
        in_specs=[scalar] * 4 + [anywhere] * (7 + shares + len(pieces)),
        out_specs=anywhere,
        scratch_shapes=[
            pltpu.VMEM((rows, LANES), jnp.float32),
            pltpu.SemaphoreType.DMA((len(pieces),)),
        ],
        input_output_aliases={11: 0} if shares else {},
        compiler_params=pltpu.CompilerParams(vmem_limit_bytes=VMEM_BYTES),
        cost_estimate=pl.CostEstimate(
            flops=0, bytes_accessed=8 * SUB * columns * coefs * 36, transcendentals=0
        ),
        name="finish",
    )(*operands)


def shifted(block, axis, step, wrap):
    count = lax.axis_size(axis)
    pairs = [
        (i, (i + step) % count) for i in range(count) if wrap or 0 <= i + step < count
    ]
    return lax.ppermute(block, axis, pairs)


def halo(direction, wet, depth):
    height, east, north = direction[0], direction[1], direction[2]
    rows = direction.shape[2]
    last = north[:, SUB - 1 :: SUB] * wet[SUB - 1 :: SUB]
    up = jnp.stack([last, last * depth[SUB - 1 :: SUB]])
    first = wet[::SUB]
    down = jnp.stack([height[:, ::SUB] * first, east[:, ::SUB] * first])
    from_above = shifted(up[:, :, -1:], "lat", 1, False)
    from_below = shifted(down[:, :, :1], "lat", -1, False)
    up = jnp.concatenate([from_above, up[:, :, :-1]], axis=2)
    down = jnp.concatenate([down[:, :, 1:], from_below], axis=2)
    edges = jnp.moveaxis(jnp.concatenate([up, down], axis=0), 2, 0)
    wet_last = wet[:, -1]
    east_col = east[:, :, -1] * wet_last
    east_below = jnp.concatenate([east_col[:, 1:], from_below[1, :, :, -1]], axis=1)
    north_col = north[:, :, 0] * wet[:, 0]
    north_above = jnp.concatenate([from_above[0, :, :, 0], north_col[:, :-1]], axis=1)
    to_right = jnp.stack([east_col, east_below, east_col * depth[:, -1]])
    to_left = jnp.stack([height[:, :, 0] * wet[:, 0], north_col, north_above])
    cols = jnp.concatenate(
        [shifted(to_right, "lon", 1, True), shifted(to_left, "lon", -1, True)], axis=0
    )
    slabs = jnp.broadcast_to(cols[:, :, :, None], cols.shape + (LANES,))
    return edges, slabs


def spread_out(blocks):
    return [
        block if step == 0 else shifted(block, "freq", step, True)
        for step, block in enumerate(blocks)
    ]


def tile_table(groups, coefs, chunk_tiles, steps, blocks):
    places = list(chunk_tiles) + [LOOP_TILES] * steps
    table = np.zeros((2 * groups, blocks + LANES), np.int32)
    for member in range(groups):
        tile = 0
        row = 0
        for tiles in places:
            for band in range(groups):
                start = row + (member - band) % groups * piece_rows(tiles, coefs)
                for i in range(tiles):
                    if tile < blocks:
                        table[2 * member, tile] = start + i * 2 * coefs
                        table[2 * member + 1, tile] = start + tiles * 2 * coefs + i
                    tile += 1
            row += groups * piece_rows(tiles, coefs)
    return table


def local(direction, base_flow, water_depth, drag_factor, wet_mask):
    coefs, tile_rows, tile_cols = direction.shape[1:]
    groups = lax.axis_size("freq")
    member = lax.axis_index("freq")
    lat_place = lax.axis_index("lat")
    total_rows = tile_rows * lax.axis_size("lat")
    lane_tiles = tile_cols // LANES
    wet = wet_mask.astype(jnp.float32)
    angular = OMEGA_STEP * (
        member * (coefs // 2) + jnp.arange(coefs // 2, dtype=jnp.int32) + 1
    ).astype(jnp.float32)
    row_start = (lat_place * tile_rows).astype(jnp.float32)
    scalars = jnp.concatenate(
        [jnp.stack([row_start, jnp.float32(1.0 / total_rows)]), angular]
    )
    edges, slabs = halo(direction, wet, water_depth)
    place = jnp.reshape(member, (1,)).astype(jnp.int32)
    blocks = tile_rows * lane_tiles
    row_blocks = tile_rows // SUB
    chunk_tiles = [share * blocks // (groups * SHARE_UNITS) for share in CHUNK_SHARES]
    fixed = groups * sum(chunk_tiles)
    steps = -(-(blocks - fixed) // (groups * LOOP_TILES))
    table = jnp.asarray(tile_table(groups, coefs, chunk_tiles, steps, blocks))
    index, cells, offset = index_call(wet_mask)
    offsets = offset.reshape(-1)
    ends = offsets[SUB * lane_tiles : blocks + 1 : SUB * lane_tiles]

    def through(first_tile, tiles):
        params = jnp.stack([place[0], jnp.asarray(first_tile, jnp.int32)])
        flows = pack_call(params, offset, index, base_flow, direction, groups, tiles)
        back = friction_call(place, spread_out(flows), coefs)
        return spread_out(back)

    largest = lax.pmax(offsets[blocks], ("lat", "lon"))
    loop_cells = groups * LOOP_TILES * LANES
    loops = jnp.maximum(largest - fixed * LANES + loop_cells - 1, 0) // loop_cells

    def more(state):
        done, held = state
        back = through(fixed + done * groups * LOOP_TILES, LOOP_TILES)
        held = lax.dynamic_update_slice_in_dim(
            held, jnp.concatenate(back, axis=0)[None], done, 0
        )
        return done + 1, held

    rows = groups * piece_rows(LOOP_TILES, coefs)
    extra = jnp.zeros((steps, rows, LANES), jnp.float32)
    _, extra = lax.while_loop(lambda state: state[0] < loops, more, (jnp.int32(0), extra))

    arrays = (direction, wet_mask, water_depth, drag_factor, edges, slabs, cells)
    pieces = []
    back_rows = rows * steps + groups * sum(piece_rows(tiles, coefs) for tiles in chunk_tiles)
    result = None
    begin = jnp.int32(0)
    tile = 0
    for chunk, tiles in enumerate(chunk_tiles):
        pieces += through(tile, tiles)
        tile += groups * tiles
        if chunk == len(chunk_tiles) - 1:
            end = jnp.int32(row_blocks)
            pieces.append(extra.reshape(-1, LANES))
        elif chunk == len(chunk_tiles) - 2:
            end = jnp.sum((ends <= tile * LANES).astype(jnp.int32))
        else:
            continue
        start = jnp.minimum(begin, row_blocks - 1)
        count = jnp.maximum(end - start, 1)
        first = jnp.stack([start, place[0], count])
        result = finish_call(
            first, offset, table, scalars, arrays, list(pieces), back_rows, result
        )
        begin = end
    return result


def solution(mesh):
    placed = (
        P(None, "freq", "lat", "lon"),
        P(None, "freq", "lat", "lon"),
        P("lat", "lon"),
        P("lat", "lon"),
        P("lat", "lon"),
    )
    return jax.shard_map(
        local, mesh=mesh, in_specs=placed, out_specs=P(None, "freq", "lat", "lon"), check_vma=False
    )
```

```python
import math

import jax
import jax.numpy as jnp
import ml_dtypes
import numpy as np
from jax import lax
from jax.experimental import pallas as pl
from jax.experimental.pallas import tpu as pltpu
from jax.sharding import PartitionSpec as P

NCON = 16
NTIME = 256
LANES = 128
SUB = 8

LINEAR_DRAG = 0.5
GRAVITY = 1.0
OMEGA_STEP = 0.25
SPEED_SOFT = 0.01
VMEM_BYTES = 48 * 1024 * 1024
CHUNK_SHARES = (14, 50, 33)
SHARE_UNITS = 128
LOOP_TILES = 8


def split_table():
    sample = np.arange(NTIME)[:, None]
    harmonic = np.arange(1, NCON + 1)[None, :]
    phase = (sample * harmonic % NTIME) * (2.0 * math.pi / NTIME)
    table = np.stack([np.cos(phase), np.sin(phase)], axis=2).reshape(NTIME, 2 * NCON)
    table = table.astype(np.float32)
    high = table.astype(ml_dtypes.bfloat16)
    low = (table - high.astype(np.float32)).astype(ml_dtypes.bfloat16)
    return high, low


def split_value(value):
    high = value.astype(jnp.bfloat16)
    low = (value - high.astype(jnp.float32)).astype(jnp.bfloat16)
    return high, low


def friction_kernel(groups, coefs, tiles, place_ref, synth_ref, analyse_ref, *refs):
    flow_refs, out_refs, token_ref = refs[:groups], refs[groups:-1], refs[-1]
    token_ref[...] = jnp.zeros_like(token_ref)
    columns = 2 * NCON

    def block(tile, count):
        loaded = []
        for source in range(groups):
            parts = [flow_refs[source][tile + i] for i in range(count)]
            loaded.append(jnp.concatenate(parts, axis=1))
        series = []
        for field in range(4):
            rows = slice(field * coefs, (field + 1) * coefs)
            values = jnp.concatenate([part[rows] for part in loaded], axis=0)
            high, low = split_value(values)
            operand = jnp.concatenate([high, low, high], axis=0)
            series.append(
                jnp.dot(synth_ref[0], operand, preferred_element_type=jnp.float32)
            )
        base_east, base_north, step_east, step_north = series
        square = base_east * base_east + base_north * base_north + SPEED_SOFT
        inverse = lax.rsqrt(square)
        speed = square * inverse
        projected = (base_east * step_east + base_north * step_north) * inverse
        forces = (
            speed * step_east + base_east * projected,
            speed * step_north + base_north * projected,
        )
        mean = jnp.sum(speed, axis=0, keepdims=True) * (1.0 / NTIME)
        analysed = []
        for force in forces:
            high, low = split_value(force)
            both = jnp.dot(analyse_ref[0], high, preferred_element_type=jnp.float32)
            rest = jnp.dot(
                analyse_ref[0, :columns, :], low, preferred_element_type=jnp.float32
            )
            analysed.append(both[:columns] + both[columns:] + rest)
        for part in range(count):
            lanes = slice(part * LANES, (part + 1) * LANES)
            for target in range(groups):
                rows = slice(target * coefs, (target + 1) * coefs)
                values = jnp.concatenate(
                    [analysed[0][rows, lanes], analysed[1][rows, lanes]], axis=0
                )
                start = pl.multiple_of((tile + part) * 2 * coefs, SUB)
                out_refs[target][pl.ds(start, 2 * coefs), :] = values
                at = tiles * 2 * coefs + tile + part
                out_refs[target][pl.ds(at, 1), :] = mean[:, lanes]

    def body(step, carry):
        block(step * 2, 2)
        return carry

    lax.fori_loop(0, tiles // 2, body, 0)
    if tiles % 2:
        block(tiles - 1, 1)


def placed_tables(groups, coefs):
    high, low = split_table()
    synth, analyse = [], []
    for member in range(groups):
        sources = [(member - step) % groups for step in range(groups)]
        targets = [(member + step) % groups for step in range(groups)]
        source = np.concatenate([np.arange(coefs) + m * coefs for m in sources])
        target = np.concatenate([np.arange(coefs) + m * coefs for m in targets])
        synth.append(np.concatenate([high[:, source], high[:, source], low[:, source]], axis=1))
        both = np.concatenate([high[:, target].T, low[:, target].T], axis=0)
        analyse.append((both.astype(np.float32) * (2.0 / NTIME)).astype(ml_dtypes.bfloat16))
    return np.stack(synth), np.stack(analyse)


def piece_rows(tiles, coefs):
    return tiles * 2 * coefs + -(-tiles // SUB) * SUB


def friction_call(place, flows, coefs):
    groups = len(flows)
    tiles = flows[0].shape[0]
    synth, analyse = placed_tables(groups, coefs)
    cells = groups * tiles * LANES
    out_shape = (piece_rows(tiles, coefs), LANES)
    grid_spec = pltpu.PrefetchScalarGridSpec(
        num_scalar_prefetch=1,
        grid=(1,),
        in_specs=[
            pl.BlockSpec((1,) + synth.shape[1:], lambda i, place: (place[0], 0, 0)),
            pl.BlockSpec((1,) + analyse.shape[1:], lambda i, place: (place[0], 0, 0)),
        ]
        + [pl.BlockSpec(flows[0].shape, lambda i, place: (0, 0, 0))] * groups,
        out_specs=[pl.BlockSpec(out_shape, lambda i, place: (0, 0))] * groups
        + [pl.BlockSpec((SUB, LANES), lambda i, place: (0, 0))],
    )
    return pl.pallas_call(
        lambda *refs: friction_kernel(groups, coefs, tiles, *refs),
        out_shape=[jax.ShapeDtypeStruct(out_shape, jnp.float32)] * groups
        + [jax.ShapeDtypeStruct((SUB, LANES), jnp.int32)],
        grid_spec=grid_spec,
        compiler_params=pltpu.CompilerParams(vmem_limit_bytes=VMEM_BYTES),
        cost_estimate=pl.CostEstimate(
            flops=cells * NTIME * 512, bytes_accessed=cells * 128, transcendentals=0
        ),
        name="friction",
    )(place, jnp.asarray(synth), jnp.asarray(analyse), *flows)


def index_kernel(wet_ref, index_ref, place_ref, offset_ref, scratch):
    blocks = scratch.shape[0]
    rows, cols = wet_ref.shape
    at = 0
    for row in range(0, rows, SUB):
        for col in range(0, cols, LANES):
            part = wet_ref[row : row + SUB, col : col + LANES]
            scratch[at : at + SUB, :] = jnp.where(part != 0, 1.0, 0.0)
            at += SUB
    wet = scratch[...].astype(jnp.bfloat16)
    earlier = lax.broadcasted_iota(jnp.int32, (LANES, LANES), 0)
    later = lax.broadcasted_iota(jnp.int32, (LANES, LANES), 1)
    before = jnp.where(earlier < later, 1.0, 0.0).astype(jnp.bfloat16)
    ones = jnp.ones((LANES, LANES), jnp.bfloat16)
    rank = jnp.dot(wet, before, preferred_element_type=jnp.float32)
    count = jnp.dot(wet, ones, preferred_element_type=jnp.float32)
    low = lax.broadcasted_iota(jnp.int32, (blocks, blocks), 0)
    high = lax.broadcasted_iota(jnp.int32, (blocks, blocks), 1)
    summing = jnp.where(high < low, 1.0, 0.0).astype(jnp.bfloat16)
    offset = jnp.dot(summing, count.astype(jnp.bfloat16), preferred_element_type=jnp.float32)
    lane = lax.broadcasted_iota(jnp.int32, (blocks, LANES), 1)
    rank = rank.astype(jnp.int32)
    held = jnp.where(scratch[...] > 0.5, lane + LANES * (lane - rank), 0)
    for bit in range(7):
        step = 1 << bit
        coming = pltpu.roll(held, LANES - step, 1)
        moves = (coming >> (7 + bit)) & 1
        stays = 1 - ((held >> (7 + bit)) & 1)
        held = jnp.where(moves == 1, coming, held * stays)
    source = held & (LANES - 1)
    shift = offset.astype(jnp.int32) & (LANES - 1)
    index_ref[...] = jnp.take_along_axis(
        source, (lane - shift) & (LANES - 1), axis=1, mode="promise_in_bounds"
    )
    place_ref[...] = shift + rank
    eye = jnp.where(earlier == later, 1.0, 0.0)
    cubes = offset.reshape(blocks // LANES, LANES, LANES)
    table = jnp.sum(cubes * eye[None], axis=1)
    total = offset[blocks - 1 : blocks] + count[blocks - 1 : blocks]
    offset_ref[: blocks // LANES, :] = table.astype(jnp.int32)
    offset_ref[blocks // LANES : blocks // LANES + 1, :] = total.astype(jnp.int32)


def index_call(wet_mask):
    rows, cols = wet_mask.shape
    blocks = rows * cols // LANES
    table = -(-(blocks // LANES + 1) // SUB) * SUB
    return pl.pallas_call(
        index_kernel,
        out_shape=[
            jax.ShapeDtypeStruct((blocks, LANES), jnp.int32),
            jax.ShapeDtypeStruct((blocks, LANES), jnp.int32),
            jax.ShapeDtypeStruct((table, LANES), jnp.int32),
        ],
        scratch_shapes=[pltpu.VMEM((blocks, LANES), jnp.float32)],
        compiler_params=pltpu.CompilerParams(vmem_limit_bytes=VMEM_BYTES),
        name="index",
    )(wet_mask)


def pack_kernel(groups, coefs, tiles, params_ref, offset_ref, index_ref, base_ref, step_ref, *refs):
    out_refs = refs[:groups]
    token_ref, held, stage, in_sem, out_sem = refs[groups:]
    token_ref[...] = jnp.zeros_like(token_ref)
    columns = held.shape[-1]
    lane_tiles = columns // LANES
    per_block = SUB * lane_tiles
    row_blocks = index_ref.shape[0] // per_block
    count = groups * tiles
    first_tile = params_ref[1]
    low = first_tile * LANES
    high = low + count * LANES

    def offset_of(block):
        return offset_ref[block // LANES, block % LANES]

    begin = jnp.int32(0)
    end = jnp.int32(0)
    for block in range(row_blocks):
        begin += (offset_of((block + 1) * per_block) <= low).astype(jnp.int32)
        end += (offset_of(block * per_block) < high).astype(jnp.int32)
    end = jnp.maximum(end, begin)

    def copies(block):
        slot = block % 2
        rows = pl.ds(pl.multiple_of(block * SUB, SUB), SUB)
        return (
            pltpu.make_async_copy(
                base_ref.at[:, :, rows, :], held.at[slot, pl.ds(0, 2)], in_sem.at[slot, 0]
            ),
            pltpu.make_async_copy(
                step_ref.at[pl.ds(1, 2), :, rows, :], held.at[slot, pl.ds(2, 2)], in_sem.at[slot, 1]
            ),
        )

    @pl.when(begin < end)
    def _():
        for copy in copies(begin):
            copy.start()

    lane = lax.broadcasted_iota(jnp.int32, (coefs, LANES), 1)

    def place_of(offset):
        return jnp.clip((offset >> 7) - first_tile + 1, 0, count + 1)

    def body(block, current):
        @pl.when(block + 1 < end)
        def _():
            for copy in copies(block + 1):
                copy.start()

        for copy in copies(block):
            copy.wait()
        slot = block % 2
        for lane_tile in range(lane_tiles):
            lanes = slice(lane_tile * LANES, (lane_tile + 1) * LANES)
            turned = [
                jnp.swapaxes(held[slot, field, :, :, lanes], 0, 1) for field in range(4)
            ]
            start = block * per_block + lane_tile * SUB
            index = index_ref[pl.ds(pl.multiple_of(start, SUB), SUB), :]
            for r in range(SUB):
                offset = offset_of(start + r)
                following = offset_of(start + r + 1)
                shift = offset & (LANES - 1)
                crossing = (following >> 7) > (offset >> 7)
                source = jnp.broadcast_to(index[r : r + 1], (coefs, LANES))
                to = place_of(offset)
                renewed = []
                for field in range(4):
                    got = jnp.take_along_axis(
                        turned[field][r], source, axis=1, mode="promise_in_bounds"
                    )
                    full = jnp.where(lane >= shift, got, current[field])
                    stage[to, field * coefs : (field + 1) * coefs, :] = full
                    renewed.append(jnp.where(crossing, got, full))
                current = tuple(renewed)
        return current

    zero = jnp.zeros((coefs, LANES), jnp.float32)
    current = lax.fori_loop(begin, end, body, (zero,) * 4)
    last = place_of(offset_of(end * per_block))
    for field in range(4):
        stage[last, field * coefs : (field + 1) * coefs, :] = current[field]
    outs = []
    for step in range(groups):
        member = lax.rem(params_ref[0] + step, groups)
        outs.append(
            pltpu.make_async_copy(
                stage.at[pl.ds(1 + member * tiles, tiles)], out_refs[step], out_sem.at[step]
            )
        )
    for copy in outs:
        copy.start()
    for copy in outs:
        copy.wait()


def pack_call(params, offset, index, base_flow, direction, groups, tiles):
    coefs, _, columns = direction.shape[1:]
    shape = (tiles, 4 * coefs, LANES)
    anywhere = pl.BlockSpec(memory_space=pl.ANY)
    grid_spec = pltpu.PrefetchScalarGridSpec(
        num_scalar_prefetch=2,
        grid=(1,),
        in_specs=[pl.BlockSpec(index.shape, lambda i, p, o: (0, 0)), anywhere, anywhere],
        out_specs=[anywhere] * groups + [pl.BlockSpec((SUB, LANES), lambda i, p, o: (0, 0))],
        scratch_shapes=[
            pltpu.VMEM((2, 4, coefs, SUB, columns), jnp.float32),
            pltpu.VMEM((groups * tiles + 2, 4 * coefs, LANES), jnp.float32),
            pltpu.SemaphoreType.DMA((2, 2)),
            pltpu.SemaphoreType.DMA((groups,)),
        ],
    )
    return pl.pallas_call(
        lambda *refs: pack_kernel(groups, coefs, tiles, *refs),
        out_shape=[jax.ShapeDtypeStruct(shape, jnp.float32)] * groups
        + [jax.ShapeDtypeStruct((SUB, LANES), jnp.int32)],
        grid_spec=grid_spec,
        compiler_params=pltpu.CompilerParams(vmem_limit_bytes=VMEM_BYTES),
        cost_estimate=pl.CostEstimate(
            flops=0, bytes_accessed=groups * tiles * coefs * 4096, transcendentals=0
        ),
        name="pack",
    )(params, offset, index, base_flow, direction)


def prepare_kernel(coefs, scalars_ref, *refs):
    (here_ref, prev_ref, next_ref, wet_ref, wet_prev_ref, wet_next_ref, depth_ref, depth_prev_ref,
     above_ref, below_ref, slab_ref, out_ref) = refs
    columns = here_ref.shape[-1]
    row_block = pl.program_id(0)
    at_top = row_block == 0
    at_bottom = row_block == pl.num_programs(0) - 1
    wet = wet_ref[...].astype(jnp.float32)
    wet_prev = wet_prev_ref[SUB - 1 :, :].astype(jnp.float32)
    wet_next = wet_next_ref[:1, :].astype(jnp.float32)
    depth = depth_ref[...]
    depth_prev = depth_prev_ref[SUB - 1 :, :]
    lane = lax.broadcasted_iota(jnp.int32, (SUB, columns), 1)
    sub = lax.broadcasted_iota(jnp.int32, (SUB, columns), 0)
    row = (row_block * SUB + sub).astype(jnp.float32)
    rotation = 0.5 + (row + scalars_ref[0] + 0.5) * scalars_ref[1]

    def wide(slab):
        return jnp.concatenate([slab] * (columns // LANES), axis=1)

    def west(value, slab):
        return jnp.where(lane == 0, wide(slab), pltpu.roll(value, 1, 1))

    def east_of(value, slab):
        return jnp.where(lane == columns - 1, wide(slab), pltpu.roll(value, columns - 1, 1))

    def above(value, edge):
        return jnp.where(sub == 0, edge, pltpu.roll(value, 1, 0))

    def below(value, edge):
        return jnp.where(sub == SUB - 1, edge, pltpu.roll(value, SUB - 1, 0))

    for k in range(coefs // 2):
        angular = scalars_ref[2 + k]
        inverse_angular = 1.0 / (angular + jnp.zeros((SUB, columns), jnp.float32))
        planes = [
            [here_ref[p, 2 * k + part] * wet for p in range(3)] for part in range(2)
        ]
        for part in range(2):
            c = 2 * k + part
            height, east, north = planes[part]
            other = planes[1 - part]
            signed = angular if part == 0 else -angular
            east_flux = depth * east
            north_flux = depth * north
            north_edge = prev_ref[0, c, SUB - 1 :, :] * wet_prev
            flux_edge = jnp.where(at_top, above_ref[1, c : c + 1], north_edge * depth_prev)
            north_edge = jnp.where(at_top, above_ref[0, c : c + 1], north_edge)
            height_edge = jnp.where(
                at_bottom, below_ref[0, c : c + 1], next_ref[0, c, :1, :] * wet_next
            )
            east_edge = jnp.where(
                at_bottom, below_ref[1, c : c + 1], next_ref[1, c, :1, :] * wet_next
            )
            north_up = above(north, north_edge)
            east_down = below(east, east_edge)
            res_height = (
                signed * other[0]
                + east_flux
                - west(east_flux, slab_ref[2, c])
                + north_flux
                - above(north_flux, flux_edge)
            )
            north_mean = 0.25 * (
                north
                + east_of(north, slab_ref[4, c])
                + north_up
                + east_of(north_up, slab_ref[5, c])
            )
            east_mean = 0.25 * (
                east
                + west(east, slab_ref[0, c])
                + east_down
                + west(east_down, slab_ref[1, c])
            )
            res_east = (
                signed * other[1]
                + LINEAR_DRAG * east
                - rotation * north_mean
                + GRAVITY * (east_of(height, slab_ref[3, c]) - height)
            )
            res_north = (
                signed * other[2]
                + LINEAR_DRAG * north
                + rotation * east_mean
                + GRAVITY * (below(height, height_edge) - height)
            )
            if part == 0:
                out_ref[0, c + 1] = res_height * wet * inverse_angular
            else:
                out_ref[0, c - 1] = -res_height * wet * inverse_angular
            out_ref[1, c] = res_east * wet
            out_ref[2, c] = res_north * wet


def prepare_call(scalars, direction, wet_mask, depth, above, below, slabs):
    _, coefs, rows, columns = direction.shape
    last = rows // SUB - 1

    def before(i):
        return jnp.maximum(i - 1, 0)

    def after(i):
        return jnp.minimum(i + 1, last)

    planes = pl.BlockSpec((3, coefs, SUB, columns), lambda i: (0, 0, i, 0))
    flat = (SUB, columns)
    edge = pl.BlockSpec((2, coefs, columns), lambda i: (0, 0, 0))
    return pl.pallas_call(
        lambda *refs: prepare_kernel(coefs, *refs),
        out_shape=jax.ShapeDtypeStruct(direction.shape, jnp.float32),
        grid=(rows // SUB,),
        in_specs=[
            pl.BlockSpec(memory_space=pltpu.SMEM),
            planes,
            pl.BlockSpec((1, coefs, SUB, columns), lambda i: (2, 0, before(i), 0)),
            pl.BlockSpec((2, coefs, SUB, columns), lambda i: (0, 0, after(i), 0)),
            pl.BlockSpec(flat, lambda i: (i, 0)),
            pl.BlockSpec(flat, lambda i: (before(i), 0)),
            pl.BlockSpec(flat, lambda i: (after(i), 0)),
            pl.BlockSpec(flat, lambda i: (i, 0)),
            pl.BlockSpec(flat, lambda i: (before(i), 0)),
            edge,
            edge,
            pl.BlockSpec((6, coefs, SUB, LANES), lambda i: (0, 0, i, 0)),
        ],
        out_specs=planes,
        compiler_params=pltpu.CompilerParams(vmem_limit_bytes=VMEM_BYTES),
        cost_estimate=pl.CostEstimate(
            flops=0, bytes_accessed=rows * columns * coefs * 48, transcendentals=0
        ),
        name="prepare",
    )(
        scalars, direction, direction, direction, wet_mask, wet_mask, wet_mask, depth, depth,
        above, below, slabs,
    )


def finish_kernel(coefs, lane_tiles, row_block, first_ref, offset_ref, table_ref, scalars_ref, back, refs):
    wet_ref, drag_ref, cell_ref, east_ref, north_ref, east_out, north_out = refs
    columns = lane_tiles * LANES
    wet = wet_ref[...].astype(jnp.float32)
    drag = drag_ref[...]
    sub = lax.broadcasted_iota(jnp.int32, (SUB, columns), 0)
    row = (row_block * SUB + sub).astype(jnp.float32)
    rotation = 0.5 + (row + scalars_ref[0] + 0.5) * scalars_ref[1]

    def gathered(here, after, index, over):
        first = jnp.take_along_axis(here, index, axis=1, mode="promise_in_bounds")
        second = jnp.take_along_axis(after, index, axis=1, mode="promise_in_bounds")
        return jnp.where(over, second, first)

    spread = []
    speed = []
    for lane_tile in range(lane_tiles):
        places = cell_ref[lane_tile * SUB : (lane_tile + 1) * SUB, :]
        rows = []
        speeds = [[], []]
        for r in range(SUB):
            at = (row_block * lane_tiles + lane_tile) * SUB + r
            tile = offset_ref[at // LANES, at % LANES] >> 7
            found = []
            for which in range(2):
                start = pl.multiple_of(table_ref[first_ref[1] * 2, tile + which], SUB)
                found.append(back[pl.ds(start, 2 * coefs), :])
                start = table_ref[first_ref[1] * 2 + 1, tile + which]
                speeds[which].append(back[pl.ds(start, 1), :])
            place = jnp.broadcast_to(places[r : r + 1], (2 * coefs, LANES))
            rows.append(gathered(found[0], found[1], place & (LANES - 1), place >= LANES))
        spread.append(jnp.swapaxes(jnp.stack(rows, axis=0), 0, 1))
        speed.append(
            gathered(
                jnp.concatenate(speeds[0], axis=0),
                jnp.concatenate(speeds[1], axis=0),
                places & (LANES - 1),
                places >= LANES,
            )
        )
    is_wet = wet > 0.5
    friction = [
        jnp.where(
            is_wet, jnp.concatenate([part[index] for part in spread], axis=1) * drag, 0.0
        )
        for index in range(2 * coefs)
    ]
    speed = jnp.where(is_wet, jnp.concatenate(speed, axis=1), 0.0)
    real_rate = drag * speed + LINEAR_DRAG
    for k in range(coefs // 2):
        angular = scalars_ref[2 + k]
        cos_at, sin_at = 2 * k, 2 * k + 1
        det_real = real_rate * real_rate - angular * angular + rotation * rotation
        det_imag = 2.0 * real_rate * angular
        inverse_norm = 1.0 / (det_real * det_real + det_imag * det_imag)
        inv_real = det_real * inverse_norm
        inv_imag = -det_imag * inverse_norm
        east_re = east_ref[0, cos_at] + friction[cos_at]
        east_im = -(east_ref[0, sin_at] + friction[sin_at])
        north_re = north_ref[0, cos_at] + friction[coefs + cos_at]
        north_im = -(north_ref[0, sin_at] + friction[coefs + sin_at])
        num_east_re = real_rate * east_re - angular * east_im + rotation * north_re
        num_east_im = real_rate * east_im + angular * east_re + rotation * north_im
        num_north_re = -rotation * east_re + real_rate * north_re - angular * north_im
        num_north_im = -rotation * east_im + real_rate * north_im + angular * north_re
        east_out[0, cos_at] = num_east_re * inv_real - num_east_im * inv_imag
        east_out[0, sin_at] = -(num_east_re * inv_imag + num_east_im * inv_real)
        north_out[0, cos_at] = num_north_re * inv_real - num_north_im * inv_imag
        north_out[0, sin_at] = -(num_north_re * inv_imag + num_north_im * inv_real)


def finish_call(first, offset, table, scalars, arrays, pieces, rows, result):
    _, coefs, _, columns = result.shape
    lane_tiles = columns // LANES

    def kernel(first_ref, offset_ref, table_ref, scalars_ref, *refs):
        array_refs = refs[:3]
        piece_refs = refs[4:-3]
        out_ref, back, sem = refs[-3:]
        first = first_ref[0]
        count = first_ref[2]

        def body(*block_refs):
            finish_kernel(
                coefs, lane_tiles, first + pl.program_id(0), first_ref, offset_ref, table_ref,
                scalars_ref, back, block_refs,
            )

        @pl.when(count > 0)
        def _():
            copies = []
            at = 0
            for n, piece in enumerate(piece_refs):
                rows = piece.shape[0]
                copies.append(
                    pltpu.make_async_copy(piece, back.at[pl.ds(at, rows)], sem.at[n])
                )
                at += rows
            for copy in copies:
                copy.start()
            for copy in copies:
                copy.wait()
            flat = pl.BlockSpec((SUB, columns), lambda i: (first + i, 0))
            east = pl.BlockSpec((1, coefs, SUB, columns), lambda i: (1, 0, first + i, 0))
            north = pl.BlockSpec((1, coefs, SUB, columns), lambda i: (2, 0, first + i, 0))
            cells = pl.BlockSpec((SUB * lane_tiles, LANES), lambda i: (first + i, 0))
            pltpu.emit_pipeline(
                body,
                grid=(count,),
                in_specs=[flat, flat, cells, east, north],
                out_specs=[east, north],
            )(*array_refs, out_ref, out_ref, out_ref, out_ref)

    anywhere = pl.BlockSpec(memory_space=pl.ANY)
    scalar = pl.BlockSpec(memory_space=pltpu.SMEM)
    operands = [first, offset, table, scalars] + list(arrays) + [result] + pieces
    return pl.pallas_call(
        kernel,
        out_shape=jax.ShapeDtypeStruct(result.shape, jnp.float32),
        in_specs=[scalar] * 4 + [anywhere] * (4 + len(pieces)),
        out_specs=anywhere,
        scratch_shapes=[
            pltpu.VMEM((rows, LANES), jnp.float32),
            pltpu.SemaphoreType.DMA((len(pieces),)),
        ],
        input_output_aliases={7: 0},
        compiler_params=pltpu.CompilerParams(vmem_limit_bytes=VMEM_BYTES),
        cost_estimate=pl.CostEstimate(
            flops=0, bytes_accessed=8 * SUB * columns * coefs * 36, transcendentals=0
        ),
        name="finish",
    )(*operands)


def shifted(block, axis, step, wrap):
    count = lax.axis_size(axis)
    pairs = [
        (i, (i + step) % count) for i in range(count) if wrap or 0 <= i + step < count
    ]
    return lax.ppermute(block, axis, pairs)


def halo(direction, wet, depth):
    height, east, north = direction[0], direction[1], direction[2]
    last = north[:, -1] * wet[-1]
    above = shifted(jnp.stack([last, last * depth[-1]]), "lat", 1, False)
    below = shifted(direction[:2, :, 0] * wet[0], "lat", -1, False)
    east_col = east[:, :, -1] * wet[:, -1]
    east_below = jnp.concatenate([east_col[:, 1:], below[1, :, -1:]], axis=1)
    north_col = north[:, :, 0] * wet[:, 0]
    north_above = jnp.concatenate([above[0, :, :1], north_col[:, :-1]], axis=1)
    to_right = jnp.stack([east_col, east_below, east_col * depth[:, -1]])
    to_left = jnp.stack([height[:, :, 0] * wet[:, 0], north_col, north_above])
    cols = jnp.concatenate(
        [shifted(to_right, "lon", 1, True), shifted(to_left, "lon", -1, True)], axis=0
    )
    slabs = jnp.broadcast_to(cols[:, :, :, None], cols.shape + (LANES,))
    return above, below, slabs


def spread_out(blocks):
    return [
        block if step == 0 else shifted(block, "freq", step, True)
        for step, block in enumerate(blocks)
    ]


def tile_table(groups, coefs, chunk_tiles, steps, blocks):
    places = list(chunk_tiles) + [LOOP_TILES] * steps
    table = np.zeros((2 * groups, blocks + LANES), np.int32)
    for member in range(groups):
        tile = 0
        row = 0
        for tiles in places:
            for band in range(groups):
                start = row + (member - band) % groups * piece_rows(tiles, coefs)
                for i in range(tiles):
                    if tile < blocks:
                        table[2 * member, tile] = start + i * 2 * coefs
                        table[2 * member + 1, tile] = start + tiles * 2 * coefs + i
                    tile += 1
            row += groups * piece_rows(tiles, coefs)
    return table


def local(direction, base_flow, water_depth, drag_factor, wet_mask):
    coefs, tile_rows, tile_cols = direction.shape[1:]
    groups = lax.axis_size("freq")
    member = lax.axis_index("freq")
    lat_place = lax.axis_index("lat")
    total_rows = tile_rows * lax.axis_size("lat")
    lane_tiles = tile_cols // LANES
    angular = OMEGA_STEP * (
        member * (coefs // 2) + jnp.arange(coefs // 2, dtype=jnp.int32) + 1
    ).astype(jnp.float32)
    row_start = (lat_place * tile_rows).astype(jnp.float32)
    scalars = jnp.concatenate(
        [jnp.stack([row_start, jnp.float32(1.0 / total_rows)]), angular]
    )
    place = jnp.reshape(member, (1,)).astype(jnp.int32)
    blocks = tile_rows * lane_tiles
    row_blocks = tile_rows // SUB
    chunk_tiles = [share * blocks // (groups * SHARE_UNITS) for share in CHUNK_SHARES]
    fixed = groups * sum(chunk_tiles)
    steps = -(-(blocks - fixed) // (groups * LOOP_TILES))
    table = jnp.asarray(tile_table(groups, coefs, chunk_tiles, steps, blocks))
    index, cells, offset = index_call(wet_mask)
    offsets = offset.reshape(-1)
    ends = offsets[SUB * lane_tiles : blocks + 1 : SUB * lane_tiles]

    def packed(first_tile, tiles, token):
        params = jnp.stack([place[0], first_tile + token])
        *flows, token = pack_call(
            params, offset, index, base_flow, direction, groups, tiles
        )
        return spread_out(flows), token[0, 0]

    def through(flows):
        *back, token = friction_call(place, flows, coefs)
        return spread_out(back), token[0, 0]

    flows = []
    backs = []
    tile = 0
    token = jnp.int32(0)
    for chunk, tiles in enumerate(chunk_tiles):
        flow, token = packed(tile, tiles, token)
        flows.append(flow)
        if chunk >= 1:
            back, token_back = through(flows[chunk - 1])
            backs.append(back)
            if chunk == 1:
                token = token + token_back
        tile += groups * tiles
    backs.append(through(flows[-1])[0])
    later_mask = wet_mask + token
    wet = later_mask.astype(jnp.float32)
    above, below, slabs = halo(direction, wet, water_depth)
    result = prepare_call(scalars, direction, later_mask, water_depth, above, below, slabs)

    largest = lax.pmax(offsets[blocks] + token, ("lat", "lon"))
    loop_cells = groups * LOOP_TILES * LANES
    loops = jnp.maximum(largest - fixed * LANES + loop_cells - 1, 0) // loop_cells

    def more(state):
        done, held = state
        back = through(packed(fixed + done * groups * LOOP_TILES, LOOP_TILES, 0)[0])[0]
        held = lax.dynamic_update_slice_in_dim(
            held, jnp.concatenate(back, axis=0)[None], done, 0
        )
        return done + 1, held

    rows = groups * piece_rows(LOOP_TILES, coefs)
    extra = jnp.zeros((steps, rows, LANES), jnp.float32)
    _, extra = lax.while_loop(lambda state: state[0] < loops, more, (jnp.int32(0), extra))

    arrays = (wet_mask, drag_factor, cells)
    pieces = []
    back_rows = rows * steps + groups * sum(piece_rows(tiles, coefs) for tiles in chunk_tiles)
    begin = jnp.int32(0)
    tile = 0
    for chunk, tiles in enumerate(chunk_tiles):
        pieces += backs[chunk]
        tile += groups * tiles
        if chunk == len(chunk_tiles) - 1:
            end = jnp.int32(row_blocks)
            pieces.append(extra.reshape(-1, LANES))
        elif chunk == len(chunk_tiles) - 2:
            end = jnp.sum((ends <= tile * LANES).astype(jnp.int32))
        else:
            continue
        first = jnp.stack([begin, place[0], end - begin])
        result = finish_call(
            first, offset, table, scalars, arrays, list(pieces), back_rows, result
        )
        begin = end
    return result


def solution(mesh):
    placed = (
        P(None, "freq", "lat", "lon"),
        P(None, "freq", "lat", "lon"),
        P("lat", "lon"),
        P("lat", "lon"),
        P("lat", "lon"),
    )
    return jax.shard_map(
        local, mesh=mesh, in_specs=placed, out_specs=P(None, "freq", "lat", "lon"), check_vma=False
    )
```

```python
import math

import jax
import jax.numpy as jnp
import ml_dtypes
import numpy as np
from jax import lax
from jax.experimental import pallas as pl
from jax.experimental.pallas import tpu as pltpu
from jax.sharding import PartitionSpec as P

NCON = 16
NTIME = 256
LANES = 128
SUB = 8

LINEAR_DRAG = 0.5
GRAVITY = 1.0
OMEGA_STEP = 0.25
SPEED_SOFT = 0.01
VMEM_BYTES = 48 * 1024 * 1024
CHUNK_SHARES = (16, 48, 33)
SHARE_UNITS = 128
LOOP_TILES = 8
PACK_COST = 16384


def split_table():
    sample = np.arange(NTIME)[:, None]
    harmonic = np.arange(1, NCON + 1)[None, :]
    phase = (sample * harmonic % NTIME) * (2.0 * math.pi / NTIME)
    table = np.stack([np.cos(phase), np.sin(phase)], axis=2).reshape(NTIME, 2 * NCON)
    table = table.astype(np.float32)
    high = table.astype(ml_dtypes.bfloat16)
    low = (table - high.astype(np.float32)).astype(ml_dtypes.bfloat16)
    return high, low


def split_value(value):
    high = value.astype(jnp.bfloat16)
    low = (value - high.astype(jnp.float32)).astype(jnp.bfloat16)
    return high, low


def friction_kernel(groups, coefs, chunk_tiles, place_ref, synth_ref, analyse_ref, *refs):
    parts = len(chunk_tiles)
    tiles = sum(chunk_tiles)
    out_refs, token_ref = refs[groups * parts : -1], refs[-1]
    token_ref[...] = jnp.zeros_like(token_ref)
    columns = 2 * NCON

    def block(flow_refs, first, at, count):
        tile = first + at
        loaded = []
        for source in range(groups):
            several = [flow_refs[source][at + i] for i in range(count)]
            loaded.append(jnp.concatenate(several, axis=1))
        series = []
        for field in range(4):
            rows = slice(field * coefs, (field + 1) * coefs)
            values = jnp.concatenate([part[rows] for part in loaded], axis=0)
            high, low = split_value(values)
            operand = jnp.concatenate([high, low, high], axis=0)
            series.append(
                jnp.dot(synth_ref[0], operand, preferred_element_type=jnp.float32)
            )
        base_east, base_north, step_east, step_north = series
        square = base_east * base_east + base_north * base_north + SPEED_SOFT
        inverse = lax.rsqrt(square)
        speed = square * inverse
        projected = (base_east * step_east + base_north * step_north) * inverse
        forces = (
            speed * step_east + base_east * projected,
            speed * step_north + base_north * projected,
        )
        mean = jnp.sum(speed, axis=0, keepdims=True) * (1.0 / NTIME)
        analysed = []
        for force in forces:
            high, low = split_value(force)
            both = jnp.dot(analyse_ref[0], high, preferred_element_type=jnp.float32)
            rest = jnp.dot(
                analyse_ref[0, :columns, :], low, preferred_element_type=jnp.float32
            )
            analysed.append(both[:columns] + both[columns:] + rest)
        for part in range(count):
            lanes = slice(part * LANES, (part + 1) * LANES)
            for target in range(groups):
                rows = slice(target * coefs, (target + 1) * coefs)
                values = jnp.concatenate(
                    [analysed[0][rows, lanes], analysed[1][rows, lanes]], axis=0
                )
                start = pl.multiple_of((tile + part) * 2 * coefs, SUB)
                out_refs[target][pl.ds(start, 2 * coefs), :] = values
                at = tiles * 2 * coefs + tile + part
                out_refs[target][pl.ds(at, 1), :] = mean[:, lanes]

    first = 0
    for part, here in enumerate(chunk_tiles):
        flow_refs = refs[part * groups : (part + 1) * groups]

        def body(step, carry, flow_refs=flow_refs, first=first):
            block(flow_refs, first, step * 2, 2)
            return carry

        lax.fori_loop(0, here // 2, body, 0)
        if here % 2:
            block(flow_refs, first, here - 1, 1)
        first += here


def placed_tables(groups, coefs):
    high, low = split_table()
    synth, analyse = [], []
    for member in range(groups):
        sources = [(member - step) % groups for step in range(groups)]
        targets = [(member + step) % groups for step in range(groups)]
        source = np.concatenate([np.arange(coefs) + m * coefs for m in sources])
        target = np.concatenate([np.arange(coefs) + m * coefs for m in targets])
        synth.append(np.concatenate([high[:, source], high[:, source], low[:, source]], axis=1))
        both = np.concatenate([high[:, target].T, low[:, target].T], axis=0)
        analyse.append((both.astype(np.float32) * (2.0 / NTIME)).astype(ml_dtypes.bfloat16))
    return np.stack(synth), np.stack(analyse)


def piece_rows(tiles, coefs):
    return tiles * 2 * coefs + -(-tiles // SUB) * SUB


def friction_call(place, flows, coefs):
    groups = len(flows[0])
    chunk_tiles = [chunk[0].shape[0] for chunk in flows]
    tiles = sum(chunk_tiles)
    synth, analyse = placed_tables(groups, coefs)
    cells = groups * tiles * LANES
    out_shape = (piece_rows(tiles, coefs), LANES)
    grid_spec = pltpu.PrefetchScalarGridSpec(
        num_scalar_prefetch=1,
        grid=(1,),
        in_specs=[
            pl.BlockSpec((1,) + synth.shape[1:], lambda i, place: (place[0], 0, 0)),
            pl.BlockSpec((1,) + analyse.shape[1:], lambda i, place: (place[0], 0, 0)),
        ]
        + [
            pl.BlockSpec(block.shape, lambda i, place: (0, 0, 0))
            for chunk in flows
            for block in chunk
        ],
        out_specs=[pl.BlockSpec(out_shape, lambda i, place: (0, 0))] * groups
        + [pl.BlockSpec((SUB, LANES), lambda i, place: (0, 0))],
    )
    return pl.pallas_call(
        lambda *refs: friction_kernel(groups, coefs, chunk_tiles, *refs),
        out_shape=[jax.ShapeDtypeStruct(out_shape, jnp.float32)] * groups
        + [jax.ShapeDtypeStruct((SUB, LANES), jnp.int32)],
        grid_spec=grid_spec,
        compiler_params=pltpu.CompilerParams(vmem_limit_bytes=VMEM_BYTES),
        cost_estimate=pl.CostEstimate(
            flops=cells * NTIME, bytes_accessed=0, transcendentals=0
        ),
        name="friction",
    )(place, jnp.asarray(synth), jnp.asarray(analyse), *[b for chunk in flows for b in chunk])


def index_kernel(wet_ref, index_ref, place_ref, offset_ref, scratch):
    blocks = scratch.shape[0]
    rows, cols = wet_ref.shape
    at = 0
    for row in range(0, rows, SUB):
        for col in range(0, cols, LANES):
            part = wet_ref[row : row + SUB, col : col + LANES]
            scratch[at : at + SUB, :] = jnp.where(part != 0, 1.0, 0.0)
            at += SUB
    wet = scratch[...].astype(jnp.bfloat16)
    earlier = lax.broadcasted_iota(jnp.int32, (LANES, LANES), 0)
    later = lax.broadcasted_iota(jnp.int32, (LANES, LANES), 1)
    before = jnp.where(earlier < later, 1.0, 0.0).astype(jnp.bfloat16)
    ones = jnp.ones((LANES, LANES), jnp.bfloat16)
    rank = jnp.dot(wet, before, preferred_element_type=jnp.float32)
    count = jnp.dot(wet, ones, preferred_element_type=jnp.float32)
    low = lax.broadcasted_iota(jnp.int32, (blocks, blocks), 0)
    high = lax.broadcasted_iota(jnp.int32, (blocks, blocks), 1)
    summing = jnp.where(high < low, 1.0, 0.0).astype(jnp.bfloat16)
    offset = jnp.dot(summing, count.astype(jnp.bfloat16), preferred_element_type=jnp.float32)
    lane = lax.broadcasted_iota(jnp.int32, (blocks, LANES), 1)
    rank = rank.astype(jnp.int32)
    held = jnp.where(scratch[...] > 0.5, lane + LANES * (lane - rank), 0)
    for bit in range(7):
        step = 1 << bit
        coming = pltpu.roll(held, LANES - step, 1)
        moves = (coming >> (7 + bit)) & 1
        stays = 1 - ((held >> (7 + bit)) & 1)
        held = jnp.where(moves == 1, coming, held * stays)
    source = held & (LANES - 1)
    shift = offset.astype(jnp.int32) & (LANES - 1)
    index_ref[...] = jnp.take_along_axis(
        source, (lane - shift) & (LANES - 1), axis=1, mode="promise_in_bounds"
    )
    place_ref[...] = shift + rank
    eye = jnp.where(earlier == later, 1.0, 0.0)
    cubes = offset.reshape(blocks // LANES, LANES, LANES)
    table = jnp.sum(cubes * eye[None], axis=1)
    total = offset[blocks - 1 : blocks] + count[blocks - 1 : blocks]
    offset_ref[: blocks // LANES, :] = table.astype(jnp.int32)
    offset_ref[blocks // LANES : blocks // LANES + 1, :] = total.astype(jnp.int32)


def index_call(wet_mask):
    rows, cols = wet_mask.shape
    blocks = rows * cols // LANES
    table = -(-(blocks // LANES + 1) // SUB) * SUB
    return pl.pallas_call(
        index_kernel,
        out_shape=[
            jax.ShapeDtypeStruct((blocks, LANES), jnp.int32),
            jax.ShapeDtypeStruct((blocks, LANES), jnp.int32),
            jax.ShapeDtypeStruct((table, LANES), jnp.int32),
        ],
        scratch_shapes=[pltpu.VMEM((blocks, LANES), jnp.float32)],
        compiler_params=pltpu.CompilerParams(vmem_limit_bytes=VMEM_BYTES),
        name="index",
    )(wet_mask)


def pack_kernel(groups, coefs, tiles, waited, params_ref, offset_ref, index_ref, base_ref, step_ref, *refs):
    refs = refs[waited:]
    out_refs = refs[:groups]
    token_ref, held, stage, in_sem, out_sem = refs[groups:]
    token_ref[...] = jnp.zeros_like(token_ref)
    columns = held.shape[-1]
    lane_tiles = columns // LANES
    per_block = SUB * lane_tiles
    row_blocks = index_ref.shape[0] // per_block
    count = groups * tiles
    first_tile = params_ref[1]
    low = first_tile * LANES
    high = low + count * LANES

    def offset_of(block):
        return offset_ref[block // LANES, block % LANES]

    begin = jnp.int32(0)
    end = jnp.int32(0)
    for block in range(row_blocks):
        begin += (offset_of((block + 1) * per_block) <= low).astype(jnp.int32)
        end += (offset_of(block * per_block) < high).astype(jnp.int32)
    end = jnp.maximum(end, begin)

    def copies(block):
        slot = block % 2
        rows = pl.ds(pl.multiple_of(block * SUB, SUB), SUB)
        return (
            pltpu.make_async_copy(
                base_ref.at[:, :, rows, :], held.at[slot, pl.ds(0, 2)], in_sem.at[slot, 0]
            ),
            pltpu.make_async_copy(
                step_ref.at[pl.ds(1, 2), :, rows, :], held.at[slot, pl.ds(2, 2)], in_sem.at[slot, 1]
            ),
        )

    @pl.when(begin < end)
    def _():
        for copy in copies(begin):
            copy.start()

    lane = lax.broadcasted_iota(jnp.int32, (coefs, LANES), 1)

    def place_of(offset):
        return jnp.clip((offset >> 7) - first_tile + 1, 0, count + 1)

    def body(block, current):
        @pl.when(block + 1 < end)
        def _():
            for copy in copies(block + 1):
                copy.start()

        for copy in copies(block):
            copy.wait()
        slot = block % 2
        for lane_tile in range(lane_tiles):
            lanes = slice(lane_tile * LANES, (lane_tile + 1) * LANES)
            turned = [
                jnp.swapaxes(held[slot, field, :, :, lanes], 0, 1) for field in range(4)
            ]
            start = block * per_block + lane_tile * SUB
            index = index_ref[pl.ds(pl.multiple_of(start, SUB), SUB), :]
            for r in range(SUB):
                offset = offset_of(start + r)
                following = offset_of(start + r + 1)
                shift = offset & (LANES - 1)
                crossing = (following >> 7) > (offset >> 7)
                source = jnp.broadcast_to(index[r : r + 1], (coefs, LANES))
                to = place_of(offset)
                renewed = []
                for field in range(4):
                    got = jnp.take_along_axis(
                        turned[field][r], source, axis=1, mode="promise_in_bounds"
                    )
                    full = jnp.where(lane >= shift, got, current[field])
                    stage[to, field * coefs : (field + 1) * coefs, :] = full
                    renewed.append(jnp.where(crossing, got, full))
                current = tuple(renewed)
        return current

    zero = jnp.zeros((coefs, LANES), jnp.float32)
    current = lax.fori_loop(begin, end, body, (zero,) * 4)
    last = place_of(offset_of(end * per_block))
    for field in range(4):
        stage[last, field * coefs : (field + 1) * coefs, :] = current[field]
    outs = []
    for step in range(groups):
        member = lax.rem(params_ref[0] + step, groups)
        outs.append(
            pltpu.make_async_copy(
                stage.at[pl.ds(1 + member * tiles, tiles)], out_refs[step], out_sem.at[step]
            )
        )
    for copy in outs:
        copy.start()
    for copy in outs:
        copy.wait()


def pack_call(params, offset, index, base_flow, direction, groups, tiles, waited):
    coefs, _, columns = direction.shape[1:]
    shape = (tiles, 4 * coefs, LANES)
    anywhere = pl.BlockSpec(memory_space=pl.ANY)
    grid_spec = pltpu.PrefetchScalarGridSpec(
        num_scalar_prefetch=2,
        grid=(1,),
        in_specs=[pl.BlockSpec(index.shape, lambda i, p, o: (0, 0))]
        + [anywhere] * (2 + len(waited)),
        out_specs=[anywhere] * groups + [pl.BlockSpec((SUB, LANES), lambda i, p, o: (0, 0))],
        scratch_shapes=[
            pltpu.VMEM((2, 4, coefs, SUB, columns), jnp.float32),
            pltpu.VMEM((groups * tiles + 2, 4 * coefs, LANES), jnp.float32),
            pltpu.SemaphoreType.DMA((2, 2)),
            pltpu.SemaphoreType.DMA((groups,)),
        ],
    )
    return pl.pallas_call(
        lambda *refs: pack_kernel(groups, coefs, tiles, len(waited), *refs),
        out_shape=[jax.ShapeDtypeStruct(shape, jnp.float32)] * groups
        + [jax.ShapeDtypeStruct((SUB, LANES), jnp.int32)],
        grid_spec=grid_spec,
        compiler_params=pltpu.CompilerParams(vmem_limit_bytes=VMEM_BYTES),
        cost_estimate=pl.CostEstimate(
            flops=0, bytes_accessed=groups * tiles * coefs * PACK_COST, transcendentals=0
        ),
        name="pack",
    )(params, offset, index, base_flow, direction, *waited)


def prepare_kernel(coefs, scalars_ref, *refs):
    (here_ref, prev_ref, next_ref, wet_ref, wet_prev_ref, wet_next_ref, depth_ref, depth_prev_ref,
     above_ref, below_ref, slab_ref, out_ref, token_ref) = refs
    token_ref[...] = jnp.zeros_like(token_ref)
    columns = here_ref.shape[-1]
    row_block = pl.program_id(0)
    at_top = row_block == 0
    at_bottom = row_block == pl.num_programs(0) - 1
    wet = wet_ref[...].astype(jnp.float32)
    wet_prev = wet_prev_ref[SUB - 1 :, :].astype(jnp.float32)
    wet_next = wet_next_ref[:1, :].astype(jnp.float32)
    depth = depth_ref[...]
    depth_prev = depth_prev_ref[SUB - 1 :, :]
    lane = lax.broadcasted_iota(jnp.int32, (SUB, columns), 1)
    sub = lax.broadcasted_iota(jnp.int32, (SUB, columns), 0)
    row = (row_block * SUB + sub).astype(jnp.float32)
    rotation = 0.5 + (row + scalars_ref[0] + 0.5) * scalars_ref[1]

    def wide(slab):
        return jnp.concatenate([slab] * (columns // LANES), axis=1)

    def west(value, slab):
        return jnp.where(lane == 0, wide(slab), pltpu.roll(value, 1, 1))

    def east_of(value, slab):
        return jnp.where(lane == columns - 1, wide(slab), pltpu.roll(value, columns - 1, 1))

    def above(value, edge):
        return jnp.where(sub == 0, edge, pltpu.roll(value, 1, 0))

    def below(value, edge):
        return jnp.where(sub == SUB - 1, edge, pltpu.roll(value, SUB - 1, 0))

    for k in range(coefs // 2):
        angular = scalars_ref[2 + k]
        inverse_angular = 1.0 / (angular + jnp.zeros((SUB, columns), jnp.float32))
        planes = [
            [here_ref[p, 2 * k + part] * wet for p in range(3)] for part in range(2)
        ]
        for part in range(2):
            c = 2 * k + part
            height, east, north = planes[part]
            other = planes[1 - part]
            signed = angular if part == 0 else -angular
            east_flux = depth * east
            north_flux = depth * north
            north_edge = prev_ref[0, c, SUB - 1 :, :] * wet_prev
            flux_edge = jnp.where(at_top, above_ref[1, c : c + 1], north_edge * depth_prev)
            north_edge = jnp.where(at_top, above_ref[0, c : c + 1], north_edge)
            height_edge = jnp.where(
                at_bottom, below_ref[0, c : c + 1], next_ref[0, c, :1, :] * wet_next
            )
            east_edge = jnp.where(
                at_bottom, below_ref[1, c : c + 1], next_ref[1, c, :1, :] * wet_next
            )
            north_up = above(north, north_edge)
            east_down = below(east, east_edge)
            res_height = (
                signed * other[0]
                + east_flux
                - west(east_flux, slab_ref[2, c])
                + north_flux
                - above(north_flux, flux_edge)
            )
            north_mean = 0.25 * (
                north
                + east_of(north, slab_ref[4, c])
                + north_up
                + east_of(north_up, slab_ref[5, c])
            )
            east_mean = 0.25 * (
                east
                + west(east, slab_ref[0, c])
                + east_down
                + west(east_down, slab_ref[1, c])
            )
            res_east = (
                signed * other[1]
                + LINEAR_DRAG * east
                - rotation * north_mean
                + GRAVITY * (east_of(height, slab_ref[3, c]) - height)
            )
            res_north = (
                signed * other[2]
                + LINEAR_DRAG * north
                + rotation * east_mean
                + GRAVITY * (below(height, height_edge) - height)
            )
            if part == 0:
                out_ref[0, c + 1] = res_height * wet * inverse_angular
            else:
                out_ref[0, c - 1] = -res_height * wet * inverse_angular
            out_ref[1, c] = res_east * wet
            out_ref[2, c] = res_north * wet


def prepare_call(scalars, direction, wet_mask, depth, above, below, slabs):
    _, coefs, rows, columns = direction.shape
    last = rows // SUB - 1

    def before(i):
        return jnp.maximum(i - 1, 0)

    def after(i):
        return jnp.minimum(i + 1, last)

    planes = pl.BlockSpec((3, coefs, SUB, columns), lambda i: (0, 0, i, 0))
    flat = (SUB, columns)
    edge = pl.BlockSpec((2, coefs, columns), lambda i: (0, 0, 0))
    return pl.pallas_call(
        lambda *refs: prepare_kernel(coefs, *refs),
        out_shape=[
            jax.ShapeDtypeStruct(direction.shape, jnp.float32),
            jax.ShapeDtypeStruct((SUB, LANES), jnp.int32),
        ],
        grid=(rows // SUB,),
        in_specs=[
            pl.BlockSpec(memory_space=pltpu.SMEM),
            planes,
            pl.BlockSpec((1, coefs, SUB, columns), lambda i: (2, 0, before(i), 0)),
            pl.BlockSpec((2, coefs, SUB, columns), lambda i: (0, 0, after(i), 0)),
            pl.BlockSpec(flat, lambda i: (i, 0)),
            pl.BlockSpec(flat, lambda i: (before(i), 0)),
            pl.BlockSpec(flat, lambda i: (after(i), 0)),
            pl.BlockSpec(flat, lambda i: (i, 0)),
            pl.BlockSpec(flat, lambda i: (before(i), 0)),
            edge,
            edge,
            pl.BlockSpec((6, coefs, SUB, LANES), lambda i: (0, 0, i, 0)),
        ],
        out_specs=[planes, pl.BlockSpec((SUB, LANES), lambda i: (0, 0))],
        compiler_params=pltpu.CompilerParams(vmem_limit_bytes=VMEM_BYTES),
        cost_estimate=pl.CostEstimate(
            flops=rows * columns * coefs, bytes_accessed=0, transcendentals=0
        ),
        name="prepare",
    )(
        scalars, direction, direction, direction, wet_mask, wet_mask, wet_mask, depth, depth,
        above, below, slabs,
    )


def finish_kernel(coefs, lane_tiles, row_block, first_ref, offset_ref, table_ref, scalars_ref, back, refs):
    wet_ref, drag_ref, cell_ref, east_ref, north_ref, east_out, north_out = refs
    columns = lane_tiles * LANES
    wet = wet_ref[...].astype(jnp.float32)
    drag = drag_ref[...]
    sub = lax.broadcasted_iota(jnp.int32, (SUB, columns), 0)
    row = (row_block * SUB + sub).astype(jnp.float32)
    rotation = 0.5 + (row + scalars_ref[0] + 0.5) * scalars_ref[1]

    def gathered(here, after, index, over):
        first = jnp.take_along_axis(here, index, axis=1, mode="promise_in_bounds")
        second = jnp.take_along_axis(after, index, axis=1, mode="promise_in_bounds")
        return jnp.where(over, second, first)

    spread = []
    speed = []
    for lane_tile in range(lane_tiles):
        places = cell_ref[lane_tile * SUB : (lane_tile + 1) * SUB, :]
        rows = []
        speeds = [[], []]
        for r in range(SUB):
            at = (row_block * lane_tiles + lane_tile) * SUB + r
            tile = offset_ref[at // LANES, at % LANES] >> 7
            found = []
            for which in range(2):
                start = pl.multiple_of(table_ref[first_ref[1] * 2, tile + which], SUB)
                found.append(back[pl.ds(start, 2 * coefs), :])
                start = table_ref[first_ref[1] * 2 + 1, tile + which]
                speeds[which].append(back[pl.ds(start, 1), :])
            place = jnp.broadcast_to(places[r : r + 1], (2 * coefs, LANES))
            rows.append(gathered(found[0], found[1], place & (LANES - 1), place >= LANES))
        spread.append(jnp.swapaxes(jnp.stack(rows, axis=0), 0, 1))
        speed.append(
            gathered(
                jnp.concatenate(speeds[0], axis=0),
                jnp.concatenate(speeds[1], axis=0),
                places & (LANES - 1),
                places >= LANES,
            )
        )
    is_wet = wet > 0.5
    friction = [
        jnp.where(
            is_wet, jnp.concatenate([part[index] for part in spread], axis=1) * drag, 0.0
        )
        for index in range(2 * coefs)
    ]
    speed = jnp.where(is_wet, jnp.concatenate(speed, axis=1), 0.0)
    real_rate = drag * speed + LINEAR_DRAG
    for k in range(coefs // 2):
        angular = scalars_ref[2 + k]
        cos_at, sin_at = 2 * k, 2 * k + 1
        det_real = real_rate * real_rate - angular * angular + rotation * rotation
        det_imag = 2.0 * real_rate * angular
        inverse_norm = 1.0 / (det_real * det_real + det_imag * det_imag)
        inv_real = det_real * inverse_norm
        inv_imag = -det_imag * inverse_norm
        east_re = east_ref[0, cos_at] + friction[cos_at]
        east_im = -(east_ref[0, sin_at] + friction[sin_at])
        north_re = north_ref[0, cos_at] + friction[coefs + cos_at]
        north_im = -(north_ref[0, sin_at] + friction[coefs + sin_at])
        num_east_re = real_rate * east_re - angular * east_im + rotation * north_re
        num_east_im = real_rate * east_im + angular * east_re + rotation * north_im
        num_north_re = -rotation * east_re + real_rate * north_re - angular * north_im
        num_north_im = -rotation * east_im + real_rate * north_im + angular * north_re
        east_out[0, cos_at] = num_east_re * inv_real - num_east_im * inv_imag
        east_out[0, sin_at] = -(num_east_re * inv_imag + num_east_im * inv_real)
        north_out[0, cos_at] = num_north_re * inv_real - num_north_im * inv_imag
        north_out[0, sin_at] = -(num_north_re * inv_imag + num_north_im * inv_real)


def finish_call(first, offset, table, scalars, arrays, pieces, rows, result):
    _, coefs, _, columns = result.shape
    lane_tiles = columns // LANES

    def kernel(first_ref, offset_ref, table_ref, scalars_ref, *refs):
        array_refs = refs[:3]
        piece_refs = refs[4:-3]
        out_ref, back, sem = refs[-3:]
        first = first_ref[0]
        count = first_ref[2]

        def body(*block_refs):
            finish_kernel(
                coefs, lane_tiles, first + pl.program_id(0), first_ref, offset_ref, table_ref,
                scalars_ref, back, block_refs,
            )

        @pl.when(count > 0)
        def _():
            copies = []
            at = 0
            for n, piece in enumerate(piece_refs):
                rows = piece.shape[0]
                copies.append(
                    pltpu.make_async_copy(piece, back.at[pl.ds(at, rows)], sem.at[n])
                )
                at += rows
            for copy in copies:
                copy.start()
            for copy in copies:
                copy.wait()
            flat = pl.BlockSpec((SUB, columns), lambda i: (first + i, 0))
            east = pl.BlockSpec((1, coefs, SUB, columns), lambda i: (1, 0, first + i, 0))
            north = pl.BlockSpec((1, coefs, SUB, columns), lambda i: (2, 0, first + i, 0))
            cells = pl.BlockSpec((SUB * lane_tiles, LANES), lambda i: (first + i, 0))
            pltpu.emit_pipeline(
                body,
                grid=(count,),
                in_specs=[flat, flat, cells, east, north],
                out_specs=[east, north],
            )(*array_refs, out_ref, out_ref, out_ref, out_ref)

    anywhere = pl.BlockSpec(memory_space=pl.ANY)
    scalar = pl.BlockSpec(memory_space=pltpu.SMEM)
    operands = [first, offset, table, scalars] + list(arrays) + [result] + pieces
    return pl.pallas_call(
        kernel,
        out_shape=jax.ShapeDtypeStruct(result.shape, jnp.float32),
        in_specs=[scalar] * 4 + [anywhere] * (4 + len(pieces)),
        out_specs=anywhere,
        scratch_shapes=[
            pltpu.VMEM((rows, LANES), jnp.float32),
            pltpu.SemaphoreType.DMA((len(pieces),)),
        ],
        input_output_aliases={7: 0},
        compiler_params=pltpu.CompilerParams(vmem_limit_bytes=VMEM_BYTES),
        cost_estimate=pl.CostEstimate(
            flops=0, bytes_accessed=8 * SUB * columns * coefs * 36, transcendentals=0
        ),
        name="finish",
    )(*operands)


def shifted(block, axis, step, wrap):
    count = lax.axis_size(axis)
    pairs = [
        (i, (i + step) % count) for i in range(count) if wrap or 0 <= i + step < count
    ]
    return lax.ppermute(block, axis, pairs)


def edge_kernel(coefs, east_ref, height_ref, north_ref, last_ref, first_ref, wet_ref, depth_ref, *refs):
    up_ref, down_ref, right_ref, left_ref = refs[-4:]
    rows, columns = wet_ref.shape
    wet = wet_ref[...].astype(jnp.float32)
    end = slice(columns - LANES, columns)
    wet_end = wet[:, end]
    wet_start = wet[:, :LANES]
    depth_end = depth_ref[:, end]
    wet_last = wet[rows - 1 :, :]
    depth_last = depth_ref[rows - 1 :, :]
    for c in range(coefs):
        at = slice(c, c + 1)
        north_row = last_ref[0, c, SUB - 1 :, :] * wet_last
        up_ref[0, at, :] = north_row
        up_ref[1, at, :] = north_row * depth_last
        down_ref[0, at, :] = first_ref[0, c, :1, :] * wet[:1, :]
        down_ref[1, at, :] = first_ref[1, c, :1, :] * wet[:1, :]
        east = east_ref[0, c] * wet_end
        right_ref[0, at, :] = jnp.transpose(east)[LANES - 1 :, :]
        right_ref[1, at, :] = jnp.transpose(east * depth_end)[LANES - 1 :, :]
        left_ref[0, at, :] = jnp.transpose(height_ref[0, c] * wet_start)[:1, :]
        left_ref[1, at, :] = jnp.transpose(north_ref[0, c] * wet_start)[:1, :]


def edge_call(direction, wet_mask, depth, waited):
    _, coefs, rows, columns = direction.shape
    last_tile = columns // LANES - 1
    last_block = rows // SUB - 1
    tall = (1, coefs, rows, LANES)
    whole = pl.BlockSpec((rows, columns), lambda i: (0, 0))
    row_out = (2, coefs, columns)
    col_out = (2, coefs, rows)
    shapes = [row_out, row_out, col_out, col_out]
    return pl.pallas_call(
        lambda *refs: edge_kernel(coefs, *refs),
        out_shape=[jax.ShapeDtypeStruct(shape, jnp.float32) for shape in shapes],
        grid=(1,),
        in_specs=[
            pl.BlockSpec(tall, lambda i: (1, 0, 0, last_tile)),
            pl.BlockSpec(tall, lambda i: (0, 0, 0, 0)),
            pl.BlockSpec(tall, lambda i: (2, 0, 0, 0)),
            pl.BlockSpec((1, coefs, SUB, columns), lambda i: (2, 0, last_block, 0)),
            pl.BlockSpec((2, coefs, SUB, columns), lambda i: (0, 0, 0, 0)),
            whole,
            whole,
        ]
        + [pl.BlockSpec(memory_space=pl.ANY)] * len(waited),
        out_specs=[pl.BlockSpec(shape, lambda i: (0, 0, 0)) for shape in shapes],
        compiler_params=pltpu.CompilerParams(vmem_limit_bytes=VMEM_BYTES),
        cost_estimate=pl.CostEstimate(
            flops=rows * columns, bytes_accessed=0, transcendentals=0
        ),
        name="edges",
    )(direction, direction, direction, direction, direction, wet_mask, depth, *waited)


def halo(direction, wet_mask, depth, waited):
    up, down, right, left = edge_call(direction, wet_mask, depth, waited)
    above = shifted(up, "lat", 1, False)
    below = shifted(down, "lat", -1, False)
    east_below = jnp.concatenate([right[0, :, 1:], below[1, :, -1:]], axis=1)
    north_above = jnp.concatenate([above[0, :, :1], left[1, :, :-1]], axis=1)
    to_right = jnp.stack([right[0], east_below, right[1]])
    to_left = jnp.stack([left[0], left[1], north_above])
    cols = jnp.concatenate(
        [shifted(to_right, "lon", 1, True), shifted(to_left, "lon", -1, True)], axis=0
    )
    slabs = jnp.broadcast_to(cols[:, :, :, None], cols.shape + (LANES,))
    return above, below, slabs


def spread_out(blocks):
    return [
        block if step == 0 else shifted(block, "freq", step, True)
        for step, block in enumerate(blocks)
    ]


def tile_table(groups, coefs, back_chunks, blocks):
    table = np.zeros((2 * groups, blocks + LANES), np.int32)
    for member in range(groups):
        tile = 0
        row = 0
        for chunk_tiles in back_chunks:
            together = sum(chunk_tiles)
            before = 0
            for tiles in chunk_tiles:
                for band in range(groups):
                    start = row + (member - band) % groups * piece_rows(together, coefs)
                    for i in range(before, before + tiles):
                        if tile < blocks:
                            table[2 * member, tile] = start + i * 2 * coefs
                            table[2 * member + 1, tile] = start + together * 2 * coefs + i
                        tile += 1
                before += tiles
            row += groups * piece_rows(together, coefs)
    return table


def local(direction, base_flow, water_depth, drag_factor, wet_mask):
    coefs, tile_rows, tile_cols = direction.shape[1:]
    groups = lax.axis_size("freq")
    member = lax.axis_index("freq")
    lat_place = lax.axis_index("lat")
    total_rows = tile_rows * lax.axis_size("lat")
    lane_tiles = tile_cols // LANES
    angular = OMEGA_STEP * (
        member * (coefs // 2) + jnp.arange(coefs // 2, dtype=jnp.int32) + 1
    ).astype(jnp.float32)
    row_start = (lat_place * tile_rows).astype(jnp.float32)
    scalars = jnp.concatenate(
        [jnp.stack([row_start, jnp.float32(1.0 / total_rows)]), angular]
    )
    place = jnp.reshape(member, (1,)).astype(jnp.int32)
    blocks = tile_rows * lane_tiles
    row_blocks = tile_rows // SUB
    chunk_tiles = [share * blocks // (groups * SHARE_UNITS) for share in CHUNK_SHARES]
    fixed = groups * sum(chunk_tiles)
    steps = -(-(blocks - fixed) // (groups * LOOP_TILES))
    back_chunks = [chunk_tiles[:-1], chunk_tiles[-1:]]
    table = jnp.asarray(
        tile_table(groups, coefs, back_chunks + [[LOOP_TILES]] * steps, blocks)
    )
    index, cells, offset = index_call(wet_mask)
    offsets = offset.reshape(-1)
    ends = offsets[SUB * lane_tiles : blocks + 1 : SUB * lane_tiles]

    def packed(first_tile, tiles, token, waited=()):
        params = jnp.stack([place[0], first_tile + token])
        *flows, token = pack_call(
            params, offset, index, base_flow, direction, groups, tiles, waited
        )
        return spread_out(flows), token[0, 0]

    def through(flows, token):
        *back, token = friction_call(place + token, flows, coefs)
        return spread_out(back), token[0, 0]

    flows = []
    tile = 0
    token = jnp.int32(0)
    for chunk, tiles in enumerate(chunk_tiles):
        waited = flows[0][1:] if chunk == 2 else ()
        flow, token = packed(tile, tiles, token, waited)
        flows.append(flow)
        tile += groups * tiles
    above, below, slabs = halo(direction, wet_mask, water_depth, flows[-1][:1])
    result, prepared = prepare_call(
        scalars, direction, wet_mask, water_depth, above, below, slabs
    )
    back, token = through(flows[:-1], prepared[0, 0])
    backs = [back]
    back, token = through(flows[-1:], token)
    backs.append(back)
    loop_cells = groups * LOOP_TILES * LANES
    beyond = offsets[blocks] + token - fixed * LANES
    loops = jnp.maximum(beyond + loop_cells - 1, 0) // loop_cells

    def more(state):
        done, held = state
        flow, _ = packed(fixed + done * groups * LOOP_TILES, LOOP_TILES, 0)
        back, _ = through([flow], 0)
        held = lax.dynamic_update_slice_in_dim(
            held, jnp.concatenate(back, axis=0)[None], done, 0
        )
        return done + 1, held

    rows = groups * piece_rows(LOOP_TILES, coefs)
    extra = jnp.zeros((steps, rows, LANES), jnp.float32)
    _, extra = lax.while_loop(lambda state: state[0] < loops, more, (jnp.int32(0), extra))

    arrays = (wet_mask, drag_factor, cells)
    pieces = []
    back_rows = rows * steps
    back_rows += groups * sum(piece_rows(sum(several), coefs) for several in back_chunks)
    begin = jnp.int32(0)
    tile = 0
    for last, several in enumerate(back_chunks):
        pieces += backs[last]
        tile += groups * sum(several)
        if last:
            end = jnp.int32(row_blocks)
            pieces.append(extra.reshape(-1, LANES))
        else:
            end = jnp.sum((ends <= tile * LANES).astype(jnp.int32))
        first = jnp.stack([begin, place[0], end - begin])
        result = finish_call(
            first, offset, table, scalars, arrays, list(pieces), back_rows, result
        )
        begin = end
    return result


def solution(mesh):
    placed = (
        P(None, "freq", "lat", "lon"),
        P(None, "freq", "lat", "lon"),
        P("lat", "lon"),
        P("lat", "lon"),
        P("lat", "lon"),
    )
    return jax.shard_map(
        local, mesh=mesh, in_specs=placed, out_specs=P(None, "freq", "lat", "lon"), check_vma=False
    )
```

```python
import math

import jax
import jax.numpy as jnp
import ml_dtypes
import numpy as np
from jax import lax
from jax.experimental import pallas as pl
from jax.experimental.pallas import tpu as pltpu
from jax.sharding import PartitionSpec as P

NCON = 16
NTIME = 256
LANES = 128
SUB = 8

LINEAR_DRAG = 0.5
GRAVITY = 1.0
OMEGA_STEP = 0.25
SPEED_SOFT = 0.01
VMEM_BYTES = 48 * 1024 * 1024
CHUNK_SHARES = (12, 60, 25)
SHARE_UNITS = 128
LOOP_TILES = 8
PACK_COST = 16384
LATE_WEIGHT = 2048


def split_table():
    sample = np.arange(NTIME)[:, None]
    harmonic = np.arange(1, NCON + 1)[None, :]
    phase = (sample * harmonic % NTIME) * (2.0 * math.pi / NTIME)
    table = np.stack([np.cos(phase), np.sin(phase)], axis=2).reshape(NTIME, 2 * NCON)
    table = table.astype(np.float32)
    high = table.astype(ml_dtypes.bfloat16)
    low = (table - high.astype(np.float32)).astype(ml_dtypes.bfloat16)
    return high, low


def split_value(value):
    high = value.astype(jnp.bfloat16)
    low = (value - high.astype(jnp.float32)).astype(jnp.bfloat16)
    return high, low


def friction_kernel(groups, coefs, chunk_tiles, place_ref, synth_ref, analyse_ref, *refs):
    parts = len(chunk_tiles)
    tiles = sum(chunk_tiles)
    out_refs, token_ref = refs[groups * parts : -1], refs[-1]
    token_ref[...] = jnp.zeros_like(token_ref)
    columns = 2 * NCON

    def block(flow_refs, first, at, count):
        tile = first + at
        loaded = []
        for source in range(groups):
            several = [flow_refs[source][at + i] for i in range(count)]
            loaded.append(jnp.concatenate(several, axis=1))
        series = []
        for field in range(4):
            rows = slice(field * coefs, (field + 1) * coefs)
            values = jnp.concatenate([part[rows] for part in loaded], axis=0)
            high, low = split_value(values)
            operand = jnp.concatenate([high, low, high], axis=0)
            series.append(
                jnp.dot(synth_ref[0], operand, preferred_element_type=jnp.float32)
            )
        base_east, base_north, step_east, step_north = series
        square = base_east * base_east + base_north * base_north + SPEED_SOFT
        inverse = lax.rsqrt(square)
        speed = square * inverse
        projected = (base_east * step_east + base_north * step_north) * inverse
        forces = (
            speed * step_east + base_east * projected,
            speed * step_north + base_north * projected,
        )
        mean = jnp.sum(speed, axis=0, keepdims=True) * (1.0 / NTIME)
        analysed = []
        for force in forces:
            high, low = split_value(force)
            both = jnp.dot(analyse_ref[0], high, preferred_element_type=jnp.float32)
            rest = jnp.dot(
                analyse_ref[0, :columns, :], low, preferred_element_type=jnp.float32
            )
            analysed.append(both[:columns] + both[columns:] + rest)
        for part in range(count):
            lanes = slice(part * LANES, (part + 1) * LANES)
            for target in range(groups):
                rows = slice(target * coefs, (target + 1) * coefs)
                values = jnp.concatenate(
                    [analysed[0][rows, lanes], analysed[1][rows, lanes]], axis=0
                )
                start = pl.multiple_of((tile + part) * 2 * coefs, SUB)
                out_refs[target][pl.ds(start, 2 * coefs), :] = values
                at = tiles * 2 * coefs + tile + part
                out_refs[target][pl.ds(at, 1), :] = mean[:, lanes]

    first = 0
    for part, here in enumerate(chunk_tiles):
        flow_refs = refs[part * groups : (part + 1) * groups]

        def body(step, carry, flow_refs=flow_refs, first=first):
            block(flow_refs, first, step * 2, 2)
            return carry

        lax.fori_loop(0, here // 2, body, 0)
        if here % 2:
            block(flow_refs, first, here - 1, 1)
        first += here


def placed_tables(groups, coefs):
    high, low = split_table()
    synth, analyse = [], []
    for member in range(groups):
        sources = [(member - step) % groups for step in range(groups)]
        targets = [(member + step) % groups for step in range(groups)]
        source = np.concatenate([np.arange(coefs) + m * coefs for m in sources])
        target = np.concatenate([np.arange(coefs) + m * coefs for m in targets])
        synth.append(np.concatenate([high[:, source], high[:, source], low[:, source]], axis=1))
        both = np.concatenate([high[:, target].T, low[:, target].T], axis=0)
        analyse.append((both.astype(np.float32) * (2.0 / NTIME)).astype(ml_dtypes.bfloat16))
    return np.stack(synth), np.stack(analyse)


def piece_rows(tiles, coefs):
    return tiles * 2 * coefs + -(-tiles // SUB) * SUB


def friction_call(place, flows, coefs, weight):
    groups = len(flows[0])
    chunk_tiles = [chunk[0].shape[0] for chunk in flows]
    tiles = sum(chunk_tiles)
    synth, analyse = placed_tables(groups, coefs)
    cells = groups * tiles * LANES
    out_shape = (piece_rows(tiles, coefs), LANES)
    grid_spec = pltpu.PrefetchScalarGridSpec(
        num_scalar_prefetch=1,
        grid=(1,),
        in_specs=[
            pl.BlockSpec((1,) + synth.shape[1:], lambda i, place: (place[0], 0, 0)),
            pl.BlockSpec((1,) + analyse.shape[1:], lambda i, place: (place[0], 0, 0)),
        ]
        + [
            pl.BlockSpec(block.shape, lambda i, place: (0, 0, 0))
            for chunk in flows
            for block in chunk
        ],
        out_specs=[pl.BlockSpec(out_shape, lambda i, place: (0, 0))] * groups
        + [pl.BlockSpec((SUB, LANES), lambda i, place: (0, 0))],
    )
    return pl.pallas_call(
        lambda *refs: friction_kernel(groups, coefs, chunk_tiles, *refs),
        out_shape=[jax.ShapeDtypeStruct(out_shape, jnp.float32)] * groups
        + [jax.ShapeDtypeStruct((SUB, LANES), jnp.int32)],
        grid_spec=grid_spec,
        compiler_params=pltpu.CompilerParams(vmem_limit_bytes=VMEM_BYTES),
        cost_estimate=pl.CostEstimate(
            flops=cells * NTIME * weight, bytes_accessed=0, transcendentals=0
        ),
        name="friction",
    )(place, jnp.asarray(synth), jnp.asarray(analyse), *[b for chunk in flows for b in chunk])


def index_kernel(wet_ref, index_ref, place_ref, offset_ref, scratch):
    blocks = scratch.shape[0]
    rows, cols = wet_ref.shape
    at = 0
    for row in range(0, rows, SUB):
        for col in range(0, cols, LANES):
            part = wet_ref[row : row + SUB, col : col + LANES]
            scratch[at : at + SUB, :] = jnp.where(part != 0, 1.0, 0.0)
            at += SUB
    wet = scratch[...].astype(jnp.bfloat16)
    earlier = lax.broadcasted_iota(jnp.int32, (LANES, LANES), 0)
    later = lax.broadcasted_iota(jnp.int32, (LANES, LANES), 1)
    before = jnp.where(earlier < later, 1.0, 0.0).astype(jnp.bfloat16)
    ones = jnp.ones((LANES, LANES), jnp.bfloat16)
    rank = jnp.dot(wet, before, preferred_element_type=jnp.float32)
    count = jnp.dot(wet, ones, preferred_element_type=jnp.float32)
    low = lax.broadcasted_iota(jnp.int32, (blocks, blocks), 0)
    high = lax.broadcasted_iota(jnp.int32, (blocks, blocks), 1)
    summing = jnp.where(high < low, 1.0, 0.0).astype(jnp.bfloat16)
    offset = jnp.dot(summing, count.astype(jnp.bfloat16), preferred_element_type=jnp.float32)
    lane = lax.broadcasted_iota(jnp.int32, (blocks, LANES), 1)
    rank = rank.astype(jnp.int32)
    held = jnp.where(scratch[...] > 0.5, lane + LANES * (lane - rank), 0)
    for bit in range(7):
        step = 1 << bit
        coming = pltpu.roll(held, LANES - step, 1)
        moves = (coming >> (7 + bit)) & 1
        stays = 1 - ((held >> (7 + bit)) & 1)
        held = jnp.where(moves == 1, coming, held * stays)
    source = held & (LANES - 1)
    shift = offset.astype(jnp.int32) & (LANES - 1)
    index_ref[...] = jnp.take_along_axis(
        source, (lane - shift) & (LANES - 1), axis=1, mode="promise_in_bounds"
    )
    place_ref[...] = shift + rank
    eye = jnp.where(earlier == later, 1.0, 0.0)
    cubes = offset.reshape(blocks // LANES, LANES, LANES)
    table = jnp.sum(cubes * eye[None], axis=1)
    total = offset[blocks - 1 : blocks] + count[blocks - 1 : blocks]
    offset_ref[: blocks // LANES, :] = table.astype(jnp.int32)
    offset_ref[blocks // LANES : blocks // LANES + 1, :] = total.astype(jnp.int32)


def index_call(wet_mask):
    rows, cols = wet_mask.shape
    blocks = rows * cols // LANES
    table = -(-(blocks // LANES + 1) // SUB) * SUB
    return pl.pallas_call(
        index_kernel,
        out_shape=[
            jax.ShapeDtypeStruct((blocks, LANES), jnp.int32),
            jax.ShapeDtypeStruct((blocks, LANES), jnp.int32),
            jax.ShapeDtypeStruct((table, LANES), jnp.int32),
        ],
        scratch_shapes=[pltpu.VMEM((blocks, LANES), jnp.float32)],
        compiler_params=pltpu.CompilerParams(vmem_limit_bytes=VMEM_BYTES),
        name="index",
    )(wet_mask)


def pack_kernel(groups, coefs, tiles, waited, params_ref, offset_ref, index_ref, base_ref, step_ref, *refs):
    refs = refs[waited:]
    out_refs = refs[:groups]
    token_ref, held, stage, in_sem, out_sem = refs[groups:]
    token_ref[...] = jnp.zeros_like(token_ref)
    columns = held.shape[-1]
    lane_tiles = columns // LANES
    per_block = SUB * lane_tiles
    row_blocks = index_ref.shape[0] // per_block
    count = groups * tiles
    first_tile = params_ref[1]
    low = first_tile * LANES
    high = low + count * LANES

    def offset_of(block):
        return offset_ref[block >> 7, block & (LANES - 1)]

    begin = jnp.int32(0)
    end = jnp.int32(0)
    for block in range(row_blocks):
        begin += (offset_of((block + 1) * per_block) <= low).astype(jnp.int32)
        end += (offset_of(block * per_block) < high).astype(jnp.int32)
    end = jnp.maximum(end, begin)

    def copies(block):
        slot = block & 1
        rows = pl.ds(pl.multiple_of(block * SUB, SUB), SUB)
        return (
            pltpu.make_async_copy(
                base_ref.at[:, :, rows, :], held.at[slot, pl.ds(0, 2)], in_sem.at[slot, 0]
            ),
            pltpu.make_async_copy(
                step_ref.at[pl.ds(1, 2), :, rows, :], held.at[slot, pl.ds(2, 2)], in_sem.at[slot, 1]
            ),
        )

    @pl.when(begin < end)
    def _():
        for copy in copies(begin):
            copy.start()

    lane = lax.broadcasted_iota(jnp.int32, (coefs, LANES), 1)

    def place_of(offset):
        return jnp.clip((offset >> 7) - first_tile + 1, 0, count + 1)

    def body(block, current):
        @pl.when(block + 1 < end)
        def _():
            for copy in copies(block + 1):
                copy.start()

        for copy in copies(block):
            copy.wait()
        slot = block & 1
        for lane_tile in range(lane_tiles):
            lanes = slice(lane_tile * LANES, (lane_tile + 1) * LANES)
            turned = [
                jnp.swapaxes(held[slot, field, :, :, lanes], 0, 1) for field in range(4)
            ]
            start = block * per_block + lane_tile * SUB
            index = index_ref[pl.ds(pl.multiple_of(start, SUB), SUB), :]
            following = offset_of(start)
            for r in range(SUB):
                offset = following
                following = offset_of(start + r + 1)
                shift = offset & (LANES - 1)
                crossing = (following >> 7) > (offset >> 7)
                source = jnp.broadcast_to(index[r : r + 1], (coefs, LANES))
                to = place_of(offset)
                renewed = []
                for field in range(4):
                    got = jnp.take_along_axis(
                        turned[field][r], source, axis=1, mode="promise_in_bounds"
                    )
                    full = jnp.where(lane >= shift, got, current[field])
                    stage[to, field * coefs : (field + 1) * coefs, :] = full
                    renewed.append(jnp.where(crossing, got, full))
                current = tuple(renewed)
        return current

    zero = jnp.zeros((coefs, LANES), jnp.float32)
    current = lax.fori_loop(begin, end, body, (zero,) * 4)
    last = place_of(offset_of(end * per_block))
    for field in range(4):
        stage[last, field * coefs : (field + 1) * coefs, :] = current[field]
    outs = []
    for step in range(groups):
        member = lax.rem(params_ref[0] + step, groups)
        outs.append(
            pltpu.make_async_copy(
                stage.at[pl.ds(1 + member * tiles, tiles)], out_refs[step], out_sem.at[step]
            )
        )
    for copy in outs:
        copy.start()
    for copy in outs:
        copy.wait()


def pack_call(params, offset, index, base_flow, direction, groups, tiles, waited):
    coefs, _, columns = direction.shape[1:]
    shape = (tiles, 4 * coefs, LANES)
    anywhere = pl.BlockSpec(memory_space=pl.ANY)
    grid_spec = pltpu.PrefetchScalarGridSpec(
        num_scalar_prefetch=2,
        grid=(1,),
        in_specs=[pl.BlockSpec(index.shape, lambda i, p, o: (0, 0))]
        + [anywhere] * (2 + len(waited)),
        out_specs=[anywhere] * groups + [pl.BlockSpec((SUB, LANES), lambda i, p, o: (0, 0))],
        scratch_shapes=[
            pltpu.VMEM((2, 4, coefs, SUB, columns), jnp.float32),
            pltpu.VMEM((groups * tiles + 2, 4 * coefs, LANES), jnp.float32),
            pltpu.SemaphoreType.DMA((2, 2)),
            pltpu.SemaphoreType.DMA((groups,)),
        ],
    )
    return pl.pallas_call(
        lambda *refs: pack_kernel(groups, coefs, tiles, len(waited), *refs),
        out_shape=[jax.ShapeDtypeStruct(shape, jnp.float32)] * groups
        + [jax.ShapeDtypeStruct((SUB, LANES), jnp.int32)],
        grid_spec=grid_spec,
        compiler_params=pltpu.CompilerParams(vmem_limit_bytes=VMEM_BYTES),
        cost_estimate=pl.CostEstimate(
            flops=0, bytes_accessed=groups * tiles * coefs * PACK_COST, transcendentals=0
        ),
        name="pack",
    )(params, offset, index, base_flow, direction, *waited)


def prepare_kernel(coefs, scalars_ref, *refs):
    (here_ref, prev_ref, next_ref, wet_ref, wet_prev_ref, wet_next_ref, depth_ref, depth_prev_ref,
     above_ref, below_ref, slab_ref, out_ref, token_ref) = refs
    token_ref[...] = jnp.zeros_like(token_ref)
    columns = here_ref.shape[-1]
    row_block = pl.program_id(0)
    at_top = row_block == 0
    at_bottom = row_block == pl.num_programs(0) - 1
    wet = wet_ref[...].astype(jnp.float32)
    wet_prev = wet_prev_ref[SUB - 1 :, :].astype(jnp.float32)
    wet_next = wet_next_ref[:1, :].astype(jnp.float32)
    depth = depth_ref[...]
    depth_prev = depth_prev_ref[SUB - 1 :, :]
    lane = lax.broadcasted_iota(jnp.int32, (SUB, columns), 1)
    sub = lax.broadcasted_iota(jnp.int32, (SUB, columns), 0)
    row = (row_block * SUB + sub).astype(jnp.float32)
    rotation = 0.5 + (row + scalars_ref[0] + 0.5) * scalars_ref[1]

    def wide(slab):
        return jnp.concatenate([slab] * (columns // LANES), axis=1)

    def west(value, slab):
        return jnp.where(lane == 0, wide(slab), pltpu.roll(value, 1, 1))

    def east_of(value, slab):
        return jnp.where(lane == columns - 1, wide(slab), pltpu.roll(value, columns - 1, 1))

    def above(value, edge):
        return jnp.where(sub == 0, edge, pltpu.roll(value, 1, 0))

    def below(value, edge):
        return jnp.where(sub == SUB - 1, edge, pltpu.roll(value, SUB - 1, 0))

    for k in range(coefs // 2):
        angular = scalars_ref[2 + k]
        inverse_angular = 1.0 / (angular + jnp.zeros((SUB, columns), jnp.float32))
        planes = [
            [here_ref[p, 2 * k + part] * wet for p in range(3)] for part in range(2)
        ]
        for part in range(2):
            c = 2 * k + part
            height, east, north = planes[part]
            other = planes[1 - part]
            signed = angular if part == 0 else -angular
            east_flux = depth * east
            north_flux = depth * north
            north_edge = prev_ref[0, c, SUB - 1 :, :] * wet_prev
            flux_edge = jnp.where(at_top, above_ref[1, c : c + 1], north_edge * depth_prev)
            north_edge = jnp.where(at_top, above_ref[0, c : c + 1], north_edge)
            height_edge = jnp.where(
                at_bottom, below_ref[0, c : c + 1], next_ref[0, c, :1, :] * wet_next
            )
            east_edge = jnp.where(
                at_bottom, below_ref[1, c : c + 1], next_ref[1, c, :1, :] * wet_next
            )
            north_up = above(north, north_edge)
            east_down = below(east, east_edge)
            res_height = (
                signed * other[0]
                + east_flux
                - west(east_flux, slab_ref[2, c])
                + north_flux
                - above(north_flux, flux_edge)
            )
            north_mean = 0.25 * (
                north
                + east_of(north, slab_ref[4, c])
                + north_up
                + east_of(north_up, slab_ref[5, c])
            )
            east_mean = 0.25 * (
                east
                + west(east, slab_ref[0, c])
                + east_down
                + west(east_down, slab_ref[1, c])
            )
            res_east = (
                signed * other[1]
                + LINEAR_DRAG * east
                - rotation * north_mean
                + GRAVITY * (east_of(height, slab_ref[3, c]) - height)
            )
            res_north = (
                signed * other[2]
                + LINEAR_DRAG * north
                + rotation * east_mean
                + GRAVITY * (below(height, height_edge) - height)
            )
            if part == 0:
                out_ref[0, c + 1] = res_height * wet * inverse_angular
            else:
                out_ref[0, c - 1] = -res_height * wet * inverse_angular
            out_ref[1, c] = res_east * wet
            out_ref[2, c] = res_north * wet


def prepare_call(scalars, direction, wet_mask, depth, above, below, slabs):
    _, coefs, rows, columns = direction.shape
    last = rows // SUB - 1

    def before(i):
        return jnp.maximum(i - 1, 0)

    def after(i):
        return jnp.minimum(i + 1, last)

    planes = pl.BlockSpec((3, coefs, SUB, columns), lambda i: (0, 0, i, 0))
    flat = (SUB, columns)
    edge = pl.BlockSpec((2, coefs, columns), lambda i: (0, 0, 0))
    return pl.pallas_call(
        lambda *refs: prepare_kernel(coefs, *refs),
        out_shape=[
            jax.ShapeDtypeStruct(direction.shape, jnp.float32),
            jax.ShapeDtypeStruct((SUB, LANES), jnp.int32),
        ],
        grid=(rows // SUB,),
        in_specs=[
            pl.BlockSpec(memory_space=pltpu.SMEM),
            planes,
            pl.BlockSpec((1, coefs, SUB, columns), lambda i: (2, 0, before(i), 0)),
            pl.BlockSpec((2, coefs, SUB, columns), lambda i: (0, 0, after(i), 0)),
            pl.BlockSpec(flat, lambda i: (i, 0)),
            pl.BlockSpec(flat, lambda i: (before(i), 0)),
            pl.BlockSpec(flat, lambda i: (after(i), 0)),
            pl.BlockSpec(flat, lambda i: (i, 0)),
            pl.BlockSpec(flat, lambda i: (before(i), 0)),
            edge,
            edge,
            pl.BlockSpec((6, coefs, SUB, LANES), lambda i: (0, 0, i, 0)),
        ],
        out_specs=[planes, pl.BlockSpec((SUB, LANES), lambda i: (0, 0))],
        compiler_params=pltpu.CompilerParams(vmem_limit_bytes=VMEM_BYTES),
        cost_estimate=pl.CostEstimate(
            flops=rows * columns * coefs, bytes_accessed=0, transcendentals=0
        ),
        name="prepare",
    )(
        scalars, direction, direction, direction, wet_mask, wet_mask, wet_mask, depth, depth,
        above, below, slabs,
    )


def finish_kernel(coefs, lane_tiles, row_block, first_ref, offset_ref, table_ref, scalars_ref, back, refs):
    wet_ref, drag_ref, cell_ref, east_ref, north_ref, east_out, north_out = refs
    columns = lane_tiles * LANES
    wet = wet_ref[...].astype(jnp.float32)
    drag = drag_ref[...]
    sub = lax.broadcasted_iota(jnp.int32, (SUB, columns), 0)
    row = (row_block * SUB + sub).astype(jnp.float32)
    rotation = 0.5 + (row + scalars_ref[0] + 0.5) * scalars_ref[1]

    def gathered(here, after, index, over):
        first = jnp.take_along_axis(here, index, axis=1, mode="promise_in_bounds")
        second = jnp.take_along_axis(after, index, axis=1, mode="promise_in_bounds")
        return jnp.where(over, second, first)

    spread = []
    speed = []
    for lane_tile in range(lane_tiles):
        places = cell_ref[lane_tile * SUB : (lane_tile + 1) * SUB, :]
        rows = []
        speeds = [[], []]
        for r in range(SUB):
            at = (row_block * lane_tiles + lane_tile) * SUB + r
            tile = offset_ref[at >> 7, at & (LANES - 1)] >> 7
            found = []
            for which in range(2):
                start = pl.multiple_of(table_ref[first_ref[1] * 2, tile + which], SUB)
                found.append(back[pl.ds(start, 2 * coefs), :])
                start = table_ref[first_ref[1] * 2 + 1, tile + which]
                speeds[which].append(back[pl.ds(start, 1), :])
            place = jnp.broadcast_to(places[r : r + 1], (2 * coefs, LANES))
            rows.append(gathered(found[0], found[1], place & (LANES - 1), place >= LANES))
        spread.append(jnp.swapaxes(jnp.stack(rows, axis=0), 0, 1))
        speed.append(
            gathered(
                jnp.concatenate(speeds[0], axis=0),
                jnp.concatenate(speeds[1], axis=0),
                places & (LANES - 1),
                places >= LANES,
            )
        )
    is_wet = wet > 0.5
    friction = [
        jnp.where(
            is_wet, jnp.concatenate([part[index] for part in spread], axis=1) * drag, 0.0
        )
        for index in range(2 * coefs)
    ]
    speed = jnp.where(is_wet, jnp.concatenate(speed, axis=1), 0.0)
    real_rate = drag * speed + LINEAR_DRAG
    for k in range(coefs // 2):
        angular = scalars_ref[2 + k]
        cos_at, sin_at = 2 * k, 2 * k + 1
        det_real = real_rate * real_rate - angular * angular + rotation * rotation
        det_imag = 2.0 * real_rate * angular
        inverse_norm = 1.0 / (det_real * det_real + det_imag * det_imag)
        inv_real = det_real * inverse_norm
        inv_imag = -det_imag * inverse_norm
        east_re = east_ref[0, cos_at] + friction[cos_at]
        east_im = -(east_ref[0, sin_at] + friction[sin_at])
        north_re = north_ref[0, cos_at] + friction[coefs + cos_at]
        north_im = -(north_ref[0, sin_at] + friction[coefs + sin_at])
        num_east_re = real_rate * east_re - angular * east_im + rotation * north_re
        num_east_im = real_rate * east_im + angular * east_re + rotation * north_im
        num_north_re = -rotation * east_re + real_rate * north_re - angular * north_im
        num_north_im = -rotation * east_im + real_rate * north_im + angular * north_re
        east_out[0, cos_at] = num_east_re * inv_real - num_east_im * inv_imag
        east_out[0, sin_at] = -(num_east_re * inv_imag + num_east_im * inv_real)
        north_out[0, cos_at] = num_north_re * inv_real - num_north_im * inv_imag
        north_out[0, sin_at] = -(num_north_re * inv_imag + num_north_im * inv_real)


def finish_call(first, offset, table, scalars, arrays, pieces, rows, result):
    _, coefs, _, columns = result.shape
    lane_tiles = columns // LANES

    def kernel(first_ref, offset_ref, table_ref, scalars_ref, *refs):
        array_refs = refs[:3]
        piece_refs = refs[4:-3]
        out_ref, back, sem = refs[-3:]
        first = first_ref[0]
        count = first_ref[2]

        def body(*block_refs):
            finish_kernel(
                coefs, lane_tiles, first + pl.program_id(0), first_ref, offset_ref, table_ref,
                scalars_ref, back, block_refs,
            )

        @pl.when(count > 0)
        def _():
            copies = []
            at = 0
            for n, piece in enumerate(piece_refs):
                rows = piece.shape[0]
                copies.append(
                    pltpu.make_async_copy(piece, back.at[pl.ds(at, rows)], sem.at[n])
                )
                at += rows
            for copy in copies:
                copy.start()
            for copy in copies:
                copy.wait()
            flat = pl.BlockSpec((SUB, columns), lambda i: (first + i, 0))
            east = pl.BlockSpec((1, coefs, SUB, columns), lambda i: (1, 0, first + i, 0))
            north = pl.BlockSpec((1, coefs, SUB, columns), lambda i: (2, 0, first + i, 0))
            cells = pl.BlockSpec((SUB * lane_tiles, LANES), lambda i: (first + i, 0))
            pltpu.emit_pipeline(
                body,
                grid=(count,),
                in_specs=[flat, flat, cells, east, north],
                out_specs=[east, north],
            )(*array_refs, out_ref, out_ref, out_ref, out_ref)

    anywhere = pl.BlockSpec(memory_space=pl.ANY)
    scalar = pl.BlockSpec(memory_space=pltpu.SMEM)
    operands = [first, offset, table, scalars] + list(arrays) + [result] + pieces
    return pl.pallas_call(
        kernel,
        out_shape=jax.ShapeDtypeStruct(result.shape, jnp.float32),
        in_specs=[scalar] * 4 + [anywhere] * (4 + len(pieces)),
        out_specs=anywhere,
        scratch_shapes=[
            pltpu.VMEM((rows, LANES), jnp.float32),
            pltpu.SemaphoreType.DMA((len(pieces),)),
        ],
        input_output_aliases={7: 0},
        compiler_params=pltpu.CompilerParams(vmem_limit_bytes=VMEM_BYTES),
        cost_estimate=pl.CostEstimate(
            flops=0, bytes_accessed=8 * SUB * columns * coefs * 36, transcendentals=0
        ),
        name="finish",
    )(*operands)


def shifted(block, axis, step, wrap):
    count = lax.axis_size(axis)
    pairs = [
        (i, (i + step) % count) for i in range(count) if wrap or 0 <= i + step < count
    ]
    return lax.ppermute(block, axis, pairs)


def edge_kernel(coefs, east_ref, height_ref, north_ref, last_ref, first_ref, wet_ref, depth_ref, *refs):
    up_ref, down_ref, right_ref, left_ref = refs[-4:]
    rows, columns = wet_ref.shape
    wet = wet_ref[...].astype(jnp.float32)
    end = slice(columns - LANES, columns)
    wet_end = wet[:, end]
    wet_start = wet[:, :LANES]
    depth_end = depth_ref[:, end]
    wet_last = wet[rows - 1 :, :]
    depth_last = depth_ref[rows - 1 :, :]
    for c in range(coefs):
        at = slice(c, c + 1)
        north_row = last_ref[0, c, SUB - 1 :, :] * wet_last
        up_ref[0, at, :] = north_row
        up_ref[1, at, :] = north_row * depth_last
        down_ref[0, at, :] = first_ref[0, c, :1, :] * wet[:1, :]
        down_ref[1, at, :] = first_ref[1, c, :1, :] * wet[:1, :]
        east = east_ref[0, c] * wet_end
        right_ref[0, at, :] = jnp.transpose(east)[LANES - 1 :, :]
        right_ref[1, at, :] = jnp.transpose(east * depth_end)[LANES - 1 :, :]
        left_ref[0, at, :] = jnp.transpose(height_ref[0, c] * wet_start)[:1, :]
        left_ref[1, at, :] = jnp.transpose(north_ref[0, c] * wet_start)[:1, :]


def edge_call(direction, wet_mask, depth, waited):
    _, coefs, rows, columns = direction.shape
    last_tile = columns // LANES - 1
    last_block = rows // SUB - 1
    tall = (1, coefs, rows, LANES)
    whole = pl.BlockSpec((rows, columns), lambda i: (0, 0))
    row_out = (2, coefs, columns)
    col_out = (2, coefs, rows)
    shapes = [row_out, row_out, col_out, col_out]
    return pl.pallas_call(
        lambda *refs: edge_kernel(coefs, *refs),
        out_shape=[jax.ShapeDtypeStruct(shape, jnp.float32) for shape in shapes],
        grid=(1,),
        in_specs=[
            pl.BlockSpec(tall, lambda i: (1, 0, 0, last_tile)),
            pl.BlockSpec(tall, lambda i: (0, 0, 0, 0)),
            pl.BlockSpec(tall, lambda i: (2, 0, 0, 0)),
            pl.BlockSpec((1, coefs, SUB, columns), lambda i: (2, 0, last_block, 0)),
            pl.BlockSpec((2, coefs, SUB, columns), lambda i: (0, 0, 0, 0)),
            whole,
            whole,
        ]
        + [pl.BlockSpec(memory_space=pl.ANY)] * len(waited),
        out_specs=[pl.BlockSpec(shape, lambda i: (0, 0, 0)) for shape in shapes],
        compiler_params=pltpu.CompilerParams(vmem_limit_bytes=VMEM_BYTES),
        cost_estimate=pl.CostEstimate(
            flops=rows * columns, bytes_accessed=0, transcendentals=0
        ),
        name="edges",
    )(direction, direction, direction, direction, direction, wet_mask, depth, *waited)


def halo(direction, wet_mask, depth, waited):
    up, down, right, left = edge_call(direction, wet_mask, depth, waited)
    above = shifted(up, "lat", 1, False)
    below = shifted(down, "lat", -1, False)
    east_below = jnp.concatenate([right[0, :, 1:], below[1, :, -1:]], axis=1)
    north_above = jnp.concatenate([above[0, :, :1], left[1, :, :-1]], axis=1)
    to_right = jnp.stack([right[0], east_below, right[1]])
    to_left = jnp.stack([left[0], left[1], north_above])
    cols = jnp.concatenate(
        [shifted(to_right, "lon", 1, True), shifted(to_left, "lon", -1, True)], axis=0
    )
    slabs = jnp.broadcast_to(cols[:, :, :, None], cols.shape + (LANES,))
    return above, below, slabs


def spread_out(blocks):
    return [
        block if step == 0 else shifted(block, "freq", step, True)
        for step, block in enumerate(blocks)
    ]


def tile_table(groups, coefs, back_chunks, blocks):
    table = np.zeros((2 * groups, blocks + LANES), np.int32)
    for member in range(groups):
        tile = 0
        row = 0
        for chunk_tiles in back_chunks:
            together = sum(chunk_tiles)
            before = 0
            for tiles in chunk_tiles:
                for band in range(groups):
                    start = row + (member - band) % groups * piece_rows(together, coefs)
                    for i in range(before, before + tiles):
                        if tile < blocks:
                            table[2 * member, tile] = start + i * 2 * coefs
                            table[2 * member + 1, tile] = start + together * 2 * coefs + i
                        tile += 1
                before += tiles
            row += groups * piece_rows(together, coefs)
    return table


def local(direction, base_flow, water_depth, drag_factor, wet_mask):
    coefs, tile_rows, tile_cols = direction.shape[1:]
    groups = lax.axis_size("freq")
    member = lax.axis_index("freq")
    lat_place = lax.axis_index("lat")
    total_rows = tile_rows * lax.axis_size("lat")
    lane_tiles = tile_cols // LANES
    angular = OMEGA_STEP * (
        member * (coefs // 2) + jnp.arange(coefs // 2, dtype=jnp.int32) + 1
    ).astype(jnp.float32)
    row_start = (lat_place * tile_rows).astype(jnp.float32)
    scalars = jnp.concatenate(
        [jnp.stack([row_start, jnp.float32(1.0 / total_rows)]), angular]
    )
    place = jnp.reshape(member, (1,)).astype(jnp.int32)
    blocks = tile_rows * lane_tiles
    row_blocks = tile_rows // SUB
    chunk_tiles = [share * blocks // (groups * SHARE_UNITS) for share in CHUNK_SHARES]
    fixed = groups * sum(chunk_tiles)
    steps = -(-(blocks - fixed) // (groups * LOOP_TILES))
    back_chunks = [chunk_tiles[:-1], chunk_tiles[-1:]]
    table = jnp.asarray(
        tile_table(groups, coefs, back_chunks + [[LOOP_TILES]] * steps, blocks)
    )
    index, cells, offset = index_call(wet_mask)
    offsets = offset.reshape(-1)
    ends = offsets[SUB * lane_tiles : blocks + 1 : SUB * lane_tiles]

    def packed(first_tile, tiles, token, waited=()):
        params = jnp.stack([place[0], first_tile + token])
        *flows, token = pack_call(
            params, offset, index, base_flow, direction, groups, tiles, waited
        )
        return spread_out(flows), token[0, 0]

    def through(flows, token, weight):
        *back, token = friction_call(place + token, flows, coefs, weight)
        return spread_out(back), token[0, 0]

    flows = []
    tile = 0
    token = jnp.int32(0)
    for tiles in chunk_tiles[:-1]:
        flow, token = packed(tile, tiles, token)
        flows.append(flow)
        tile += groups * tiles

    loop_cells = groups * LOOP_TILES * LANES
    beyond = offsets[blocks] + token - fixed * LANES
    loops = jnp.maximum(beyond + loop_cells - 1, 0) // loop_cells

    def more(state):
        done, held = state
        flow, _ = packed(fixed + done * groups * LOOP_TILES, LOOP_TILES, 0)
        back, _ = through([flow], 0, 1)
        held = lax.dynamic_update_slice_in_dim(
            held, jnp.concatenate(back, axis=0)[None], done, 0
        )
        return done + 1, held

    rows = groups * piece_rows(LOOP_TILES, coefs)
    extra = jnp.zeros((steps, rows, LANES), jnp.float32)
    done, extra = lax.while_loop(lambda state: state[0] < loops, more, (jnp.int32(0), extra))

    token = token + jnp.minimum(done, 0)
    flows.append(packed(tile, chunk_tiles[-1], token, flows[0][1:])[0])
    above, below, slabs = halo(direction, wet_mask, water_depth, flows[-1][:1])
    result, prepared = prepare_call(
        scalars, direction, wet_mask, water_depth, above, below, slabs
    )
    back, token = through(flows[:-1], prepared[0, 0], 1)
    backs = [back]
    back, token = through(flows[-1:], token, LATE_WEIGHT)
    backs.append(back)

    arrays = (wet_mask, drag_factor, cells)
    pieces = []
    back_rows = rows * steps
    back_rows += groups * sum(piece_rows(sum(several), coefs) for several in back_chunks)
    begin = jnp.int32(0)
    tile = 0
    for last, several in enumerate(back_chunks):
        pieces += backs[last]
        tile += groups * sum(several)
        if last:
            end = jnp.int32(row_blocks)
            pieces.append(extra.reshape(-1, LANES))
        else:
            end = jnp.sum((ends <= tile * LANES).astype(jnp.int32))
        first = jnp.stack([begin, place[0], end - begin])
        result = finish_call(
            first, offset, table, scalars, arrays, list(pieces), back_rows, result
        )
        begin = end
    return result


def solution(mesh):
    placed = (
        P(None, "freq", "lat", "lon"),
        P(None, "freq", "lat", "lon"),
        P("lat", "lon"),
        P("lat", "lon"),
        P("lat", "lon"),
    )
    return jax.shard_map(
        local, mesh=mesh, in_specs=placed, out_specs=P(None, "freq", "lat", "lon"), check_vma=False
    )
```

```python
import math

import jax
import jax.numpy as jnp
import ml_dtypes
import numpy as np
from jax import lax
from jax.experimental import pallas as pl
from jax.experimental.pallas import tpu as pltpu
from jax.sharding import PartitionSpec as P

NCON = 16
NTIME = 256
LANES = 128
SUB = 8

LINEAR_DRAG = 0.5
GRAVITY = 1.0
OMEGA_STEP = 0.25
SPEED_SOFT = 0.01
VMEM_BYTES = 48 * 1024 * 1024
CHUNK_SHARES = (16, 50, 31)
SHARE_UNITS = 128
LOOP_TILES = 8
PACK_COST = 16384
LATE_WEIGHT = 2048


def split_table():
    sample = np.arange(NTIME)[:, None]
    harmonic = np.arange(1, NCON + 1)[None, :]
    phase = (sample * harmonic % NTIME) * (2.0 * math.pi / NTIME)
    table = np.stack([np.cos(phase), np.sin(phase)], axis=2).reshape(NTIME, 2 * NCON)
    table = table.astype(np.float32)
    high = table.astype(ml_dtypes.bfloat16)
    low = (table - high.astype(np.float32)).astype(ml_dtypes.bfloat16)
    return high, low


def split_value(value):
    high = value.astype(jnp.bfloat16)
    low = (value - high.astype(jnp.float32)).astype(jnp.bfloat16)
    return high, low


def friction_kernel(groups, coefs, chunk_tiles, place_ref, synth_ref, analyse_ref, *refs):
    parts = len(chunk_tiles)
    tiles = sum(chunk_tiles)
    out_refs, token_ref = refs[groups * parts : -1], refs[-1]
    token_ref[...] = jnp.zeros_like(token_ref)
    columns = 2 * NCON

    def block(flow_refs, first, at, count):
        tile = first + at
        loaded = []
        for source in range(groups):
            several = [flow_refs[source][at + i] for i in range(count)]
            loaded.append(jnp.concatenate(several, axis=1))
        series = []
        for field in range(4):
            rows = slice(field * coefs, (field + 1) * coefs)
            values = jnp.concatenate([part[rows] for part in loaded], axis=0)
            high, low = split_value(values)
            operand = jnp.concatenate([high, low, high], axis=0)
            series.append(
                jnp.dot(synth_ref[0], operand, preferred_element_type=jnp.float32)
            )
        base_east, base_north, step_east, step_north = series
        square = base_east * base_east + base_north * base_north + SPEED_SOFT
        inverse = lax.rsqrt(square)
        speed = square * inverse
        projected = (base_east * step_east + base_north * step_north) * inverse
        forces = (
            speed * step_east + base_east * projected,
            speed * step_north + base_north * projected,
        )
        mean = jnp.sum(speed, axis=0, keepdims=True) * (1.0 / NTIME)
        analysed = []
        for force in forces:
            high, low = split_value(force)
            both = jnp.dot(analyse_ref[0], high, preferred_element_type=jnp.float32)
            rest = jnp.dot(
                analyse_ref[0, :columns, :], low, preferred_element_type=jnp.float32
            )
            analysed.append(both[:columns] + both[columns:] + rest)
        for part in range(count):
            lanes = slice(part * LANES, (part + 1) * LANES)
            for target in range(groups):
                rows = slice(target * coefs, (target + 1) * coefs)
                values = jnp.concatenate(
                    [analysed[0][rows, lanes], analysed[1][rows, lanes]], axis=0
                )
                start = pl.multiple_of((tile + part) * 2 * coefs, SUB)
                out_refs[target][pl.ds(start, 2 * coefs), :] = values
                at = tiles * 2 * coefs + tile + part
                out_refs[target][pl.ds(at, 1), :] = mean[:, lanes]

    first = 0
    for part, here in enumerate(chunk_tiles):
        flow_refs = refs[part * groups : (part + 1) * groups]

        def body(step, carry, flow_refs=flow_refs, first=first):
            block(flow_refs, first, step * 2, 2)
            return carry

        lax.fori_loop(0, here // 2, body, 0)
        if here % 2:
            block(flow_refs, first, here - 1, 1)
        first += here


def placed_tables(groups, coefs):
    high, low = split_table()
    synth, analyse = [], []
    for member in range(groups):
        sources = [(member - step) % groups for step in range(groups)]
        targets = [(member + step) % groups for step in range(groups)]
        source = np.concatenate([np.arange(coefs) + m * coefs for m in sources])
        target = np.concatenate([np.arange(coefs) + m * coefs for m in targets])
        synth.append(np.concatenate([high[:, source], high[:, source], low[:, source]], axis=1))
        both = np.concatenate([high[:, target].T, low[:, target].T], axis=0)
        analyse.append((both.astype(np.float32) * (2.0 / NTIME)).astype(ml_dtypes.bfloat16))
    return np.stack(synth), np.stack(analyse)


def piece_rows(tiles, coefs):
    return tiles * 2 * coefs + -(-tiles // SUB) * SUB


def friction_call(place, flows, coefs, weight):
    groups = len(flows[0])
    chunk_tiles = [chunk[0].shape[0] for chunk in flows]
    tiles = sum(chunk_tiles)
    synth, analyse = placed_tables(groups, coefs)
    cells = groups * tiles * LANES
    out_shape = (piece_rows(tiles, coefs), LANES)
    grid_spec = pltpu.PrefetchScalarGridSpec(
        num_scalar_prefetch=1,
        grid=(1,),
        in_specs=[
            pl.BlockSpec((1,) + synth.shape[1:], lambda i, place: (place[0], 0, 0)),
            pl.BlockSpec((1,) + analyse.shape[1:], lambda i, place: (place[0], 0, 0)),
        ]
        + [
            pl.BlockSpec(block.shape, lambda i, place: (0, 0, 0))
            for chunk in flows
            for block in chunk
        ],
        out_specs=[pl.BlockSpec(out_shape, lambda i, place: (0, 0))] * groups
        + [pl.BlockSpec((SUB, LANES), lambda i, place: (0, 0))],
    )
    return pl.pallas_call(
        lambda *refs: friction_kernel(groups, coefs, chunk_tiles, *refs),
        out_shape=[jax.ShapeDtypeStruct(out_shape, jnp.float32)] * groups
        + [jax.ShapeDtypeStruct((SUB, LANES), jnp.int32)],
        grid_spec=grid_spec,
        compiler_params=pltpu.CompilerParams(vmem_limit_bytes=VMEM_BYTES),
        cost_estimate=pl.CostEstimate(
            flops=cells * NTIME * weight, bytes_accessed=0, transcendentals=0
        ),
        name="friction",
    )(place, jnp.asarray(synth), jnp.asarray(analyse), *[b for chunk in flows for b in chunk])


def index_kernel(wet_ref, index_ref, place_ref, offset_ref, scratch):
    blocks = scratch.shape[0]
    rows, cols = wet_ref.shape
    at = 0
    for row in range(0, rows, SUB):
        for col in range(0, cols, LANES):
            part = wet_ref[row : row + SUB, col : col + LANES]
            scratch[at : at + SUB, :] = jnp.where(part != 0, 1.0, 0.0)
            at += SUB
    wet = scratch[...].astype(jnp.bfloat16)
    earlier = lax.broadcasted_iota(jnp.int32, (LANES, LANES), 0)
    later = lax.broadcasted_iota(jnp.int32, (LANES, LANES), 1)
    before = jnp.where(earlier < later, 1.0, 0.0).astype(jnp.bfloat16)
    ones = jnp.ones((LANES, LANES), jnp.bfloat16)
    rank = jnp.dot(wet, before, preferred_element_type=jnp.float32)
    count = jnp.dot(wet, ones, preferred_element_type=jnp.float32)
    low = lax.broadcasted_iota(jnp.int32, (blocks, blocks), 0)
    high = lax.broadcasted_iota(jnp.int32, (blocks, blocks), 1)
    summing = jnp.where(high < low, 1.0, 0.0).astype(jnp.bfloat16)
    offset = jnp.dot(summing, count.astype(jnp.bfloat16), preferred_element_type=jnp.float32)
    lane = lax.broadcasted_iota(jnp.int32, (blocks, LANES), 1)
    rank = rank.astype(jnp.int32)
    held = jnp.where(scratch[...] > 0.5, lane + LANES * (lane - rank), 0)
    for bit in range(7):
        step = 1 << bit
        coming = pltpu.roll(held, LANES - step, 1)
        moves = (coming >> (7 + bit)) & 1
        stays = 1 - ((held >> (7 + bit)) & 1)
        held = jnp.where(moves == 1, coming, held * stays)
    source = held & (LANES - 1)
    shift = offset.astype(jnp.int32) & (LANES - 1)
    index_ref[...] = jnp.take_along_axis(
        source, (lane - shift) & (LANES - 1), axis=1, mode="promise_in_bounds"
    )
    place_ref[...] = shift + rank
    eye = jnp.where(earlier == later, 1.0, 0.0)
    cubes = offset.reshape(blocks // LANES, LANES, LANES)
    table = jnp.sum(cubes * eye[None], axis=1)
    total = offset[blocks - 1 : blocks] + count[blocks - 1 : blocks]
    offset_ref[: blocks // LANES, :] = table.astype(jnp.int32)
    offset_ref[blocks // LANES : blocks // LANES + 1, :] = total.astype(jnp.int32)


def index_call(wet_mask):
    rows, cols = wet_mask.shape
    blocks = rows * cols // LANES
    table = -(-(blocks // LANES + 1) // SUB) * SUB
    return pl.pallas_call(
        index_kernel,
        out_shape=[
            jax.ShapeDtypeStruct((blocks, LANES), jnp.int32),
            jax.ShapeDtypeStruct((blocks, LANES), jnp.int32),
            jax.ShapeDtypeStruct((table, LANES), jnp.int32),
        ],
        scratch_shapes=[pltpu.VMEM((blocks, LANES), jnp.float32)],
        compiler_params=pltpu.CompilerParams(vmem_limit_bytes=VMEM_BYTES),
        name="index",
    )(wet_mask)


def pack_kernel(groups, coefs, tiles, waited, params_ref, offset_ref, index_ref, base_ref, step_ref, *refs):
    refs = refs[waited:]
    out_refs = refs[:groups]
    token_ref, held, stage, in_sem, out_sem = refs[groups:]
    token_ref[...] = jnp.zeros_like(token_ref)
    columns = held.shape[-1]
    lane_tiles = columns // LANES
    per_block = SUB * lane_tiles
    row_blocks = index_ref.shape[0] // per_block
    count = groups * tiles
    first_tile = params_ref[1]
    low = first_tile * LANES
    high = low + count * LANES

    def offset_of(block):
        return offset_ref[block >> 7, block & (LANES - 1)]

    begin = jnp.int32(0)
    end = jnp.int32(0)
    for block in range(row_blocks):
        begin += (offset_of((block + 1) * per_block) <= low).astype(jnp.int32)
        end += (offset_of(block * per_block) < high).astype(jnp.int32)
    end = jnp.maximum(end, begin)

    def copies(block):
        slot = block & 1
        rows = pl.ds(pl.multiple_of(block * SUB, SUB), SUB)
        return (
            pltpu.make_async_copy(
                base_ref.at[:, :, rows, :], held.at[slot, pl.ds(0, 2)], in_sem.at[slot, 0]
            ),
            pltpu.make_async_copy(
                step_ref.at[pl.ds(1, 2), :, rows, :], held.at[slot, pl.ds(2, 2)], in_sem.at[slot, 1]
            ),
        )

    @pl.when(begin < end)
    def _():
        for copy in copies(begin):
            copy.start()

    lane = lax.broadcasted_iota(jnp.int32, (coefs, LANES), 1)

    def place_of(offset):
        return jnp.clip((offset >> 7) - first_tile + 1, 0, count + 1)

    def body(block, current):
        @pl.when(block + 1 < end)
        def _():
            for copy in copies(block + 1):
                copy.start()

        for copy in copies(block):
            copy.wait()
        slot = block & 1
        for lane_tile in range(lane_tiles):
            lanes = slice(lane_tile * LANES, (lane_tile + 1) * LANES)
            turned = [
                jnp.swapaxes(held[slot, field, :, :, lanes], 0, 1) for field in range(4)
            ]
            start = block * per_block + lane_tile * SUB
            index = index_ref[pl.ds(pl.multiple_of(start, SUB), SUB), :]
            following = offset_of(start)
            for r in range(SUB):
                offset = following
                following = offset_of(start + r + 1)
                shift = offset & (LANES - 1)
                crossing = (following >> 7) > (offset >> 7)
                source = jnp.broadcast_to(index[r : r + 1], (coefs, LANES))
                to = place_of(offset)
                renewed = []
                for field in range(4):
                    got = jnp.take_along_axis(
                        turned[field][r], source, axis=1, mode="promise_in_bounds"
                    )
                    full = jnp.where(lane >= shift, got, current[field])
                    stage[to, field * coefs : (field + 1) * coefs, :] = full
                    renewed.append(jnp.where(crossing, got, full))
                current = tuple(renewed)
        return current

    zero = jnp.zeros((coefs, LANES), jnp.float32)
    current = lax.fori_loop(begin, end, body, (zero,) * 4)
    last = place_of(offset_of(end * per_block))
    for field in range(4):
        stage[last, field * coefs : (field + 1) * coefs, :] = current[field]
    outs = []
    for step in range(groups):
        member = lax.rem(params_ref[0] + step, groups)
        outs.append(
            pltpu.make_async_copy(
                stage.at[pl.ds(1 + member * tiles, tiles)], out_refs[step], out_sem.at[step]
            )
        )
    for copy in outs:
        copy.start()
    for copy in outs:
        copy.wait()


def pack_call(params, offset, index, base_flow, direction, groups, tiles, waited):
    coefs, _, columns = direction.shape[1:]
    shape = (tiles, 4 * coefs, LANES)
    anywhere = pl.BlockSpec(memory_space=pl.ANY)
    grid_spec = pltpu.PrefetchScalarGridSpec(
        num_scalar_prefetch=2,
        grid=(1,),
        in_specs=[pl.BlockSpec(index.shape, lambda i, p, o: (0, 0))]
        + [anywhere] * (2 + len(waited)),
        out_specs=[anywhere] * groups + [pl.BlockSpec((SUB, LANES), lambda i, p, o: (0, 0))],
        scratch_shapes=[
            pltpu.VMEM((2, 4, coefs, SUB, columns), jnp.float32),
            pltpu.VMEM((groups * tiles + 2, 4 * coefs, LANES), jnp.float32),
            pltpu.SemaphoreType.DMA((2, 2)),
            pltpu.SemaphoreType.DMA((groups,)),
        ],
    )
    return pl.pallas_call(
        lambda *refs: pack_kernel(groups, coefs, tiles, len(waited), *refs),
        out_shape=[jax.ShapeDtypeStruct(shape, jnp.float32)] * groups
        + [jax.ShapeDtypeStruct((SUB, LANES), jnp.int32)],
        grid_spec=grid_spec,
        compiler_params=pltpu.CompilerParams(vmem_limit_bytes=VMEM_BYTES),
        cost_estimate=pl.CostEstimate(
            flops=0, bytes_accessed=groups * tiles * coefs * PACK_COST, transcendentals=0
        ),
        name="pack",
    )(params, offset, index, base_flow, direction, *waited)


def prepare_kernel(coefs, scalars_ref, *refs):
    (here_ref, prev_ref, next_ref, wet_ref, wet_prev_ref, wet_next_ref, depth_ref, depth_prev_ref,
     above_ref, below_ref, slab_ref, out_ref, token_ref) = refs
    token_ref[...] = jnp.zeros_like(token_ref)
    columns = here_ref.shape[-1]
    row_block = pl.program_id(0)
    at_top = row_block == 0
    at_bottom = row_block == pl.num_programs(0) - 1
    wet = wet_ref[...].astype(jnp.float32)
    wet_prev = wet_prev_ref[SUB - 1 :, :].astype(jnp.float32)
    wet_next = wet_next_ref[:1, :].astype(jnp.float32)
    depth = depth_ref[...]
    depth_prev = depth_prev_ref[SUB - 1 :, :]
    lane = lax.broadcasted_iota(jnp.int32, (SUB, columns), 1)
    sub = lax.broadcasted_iota(jnp.int32, (SUB, columns), 0)
    row = (row_block * SUB + sub).astype(jnp.float32)
    rotation = 0.5 + (row + scalars_ref[0] + 0.5) * scalars_ref[1]

    def wide(slab):
        return jnp.concatenate([slab] * (columns // LANES), axis=1)

    def west(value, slab):
        return jnp.where(lane == 0, wide(slab), pltpu.roll(value, 1, 1))

    def east_of(value, slab):
        return jnp.where(lane == columns - 1, wide(slab), pltpu.roll(value, columns - 1, 1))

    def above(value, edge):
        return jnp.where(sub == 0, edge, pltpu.roll(value, 1, 0))

    def below(value, edge):
        return jnp.where(sub == SUB - 1, edge, pltpu.roll(value, SUB - 1, 0))

    for k in range(coefs // 2):
        angular = scalars_ref[2 + k]
        inverse_angular = 1.0 / (angular + jnp.zeros((SUB, columns), jnp.float32))
        planes = [
            [here_ref[p, 2 * k + part] * wet for p in range(3)] for part in range(2)
        ]
        for part in range(2):
            c = 2 * k + part
            height, east, north = planes[part]
            other = planes[1 - part]
            signed = angular if part == 0 else -angular
            east_flux = depth * east
            north_flux = depth * north
            north_edge = prev_ref[0, c, SUB - 1 :, :] * wet_prev
            flux_edge = jnp.where(at_top, above_ref[1, c : c + 1], north_edge * depth_prev)
            north_edge = jnp.where(at_top, above_ref[0, c : c + 1], north_edge)
            height_edge = jnp.where(
                at_bottom, below_ref[0, c : c + 1], next_ref[0, c, :1, :] * wet_next
            )
            east_edge = jnp.where(
                at_bottom, below_ref[1, c : c + 1], next_ref[1, c, :1, :] * wet_next
            )
            north_up = above(north, north_edge)
            east_down = below(east, east_edge)
            res_height = (
                signed * other[0]
                + east_flux
                - west(east_flux, slab_ref[2, c])
                + north_flux
                - above(north_flux, flux_edge)
            )
            north_mean = 0.25 * (
                north
                + east_of(north, slab_ref[4, c])
                + north_up
                + east_of(north_up, slab_ref[5, c])
            )
            east_mean = 0.25 * (
                east
                + west(east, slab_ref[0, c])
                + east_down
                + west(east_down, slab_ref[1, c])
            )
            res_east = (
                signed * other[1]
                + LINEAR_DRAG * east
                - rotation * north_mean
                + GRAVITY * (east_of(height, slab_ref[3, c]) - height)
            )
            res_north = (
                signed * other[2]
                + LINEAR_DRAG * north
                + rotation * east_mean
                + GRAVITY * (below(height, height_edge) - height)
            )
            if part == 0:
                out_ref[0, c + 1] = res_height * wet * inverse_angular
            else:
                out_ref[0, c - 1] = -res_height * wet * inverse_angular
            out_ref[1, c] = res_east * wet
            out_ref[2, c] = res_north * wet


def prepare_call(scalars, direction, wet_mask, depth, above, below, slabs):
    _, coefs, rows, columns = direction.shape
    last = rows // SUB - 1

    def before(i):
        return jnp.maximum(i - 1, 0)

    def after(i):
        return jnp.minimum(i + 1, last)

    planes = pl.BlockSpec((3, coefs, SUB, columns), lambda i: (0, 0, i, 0))
    flat = (SUB, columns)
    edge = pl.BlockSpec((2, coefs, columns), lambda i: (0, 0, 0))
    return pl.pallas_call(
        lambda *refs: prepare_kernel(coefs, *refs),
        out_shape=[
            jax.ShapeDtypeStruct(direction.shape, jnp.float32),
            jax.ShapeDtypeStruct((SUB, LANES), jnp.int32),
        ],
        grid=(rows // SUB,),
        in_specs=[
            pl.BlockSpec(memory_space=pltpu.SMEM),
            planes,
            pl.BlockSpec((1, coefs, SUB, columns), lambda i: (2, 0, before(i), 0)),
            pl.BlockSpec((2, coefs, SUB, columns), lambda i: (0, 0, after(i), 0)),
            pl.BlockSpec(flat, lambda i: (i, 0)),
            pl.BlockSpec(flat, lambda i: (before(i), 0)),
            pl.BlockSpec(flat, lambda i: (after(i), 0)),
            pl.BlockSpec(flat, lambda i: (i, 0)),
            pl.BlockSpec(flat, lambda i: (before(i), 0)),
            edge,
            edge,
            pl.BlockSpec((6, coefs, SUB, LANES), lambda i: (0, 0, i, 0)),
        ],
        out_specs=[planes, pl.BlockSpec((SUB, LANES), lambda i: (0, 0))],
        compiler_params=pltpu.CompilerParams(vmem_limit_bytes=VMEM_BYTES),
        cost_estimate=pl.CostEstimate(
            flops=rows * columns * coefs, bytes_accessed=0, transcendentals=0
        ),
        name="prepare",
    )(
        scalars, direction, direction, direction, wet_mask, wet_mask, wet_mask, depth, depth,
        above, below, slabs,
    )


def finish_kernel(coefs, lane_tiles, row_block, first_ref, offset_ref, table_ref, scalars_ref, back, refs):
    wet_ref, drag_ref, cell_ref, east_ref, north_ref, east_out, north_out = refs
    columns = lane_tiles * LANES
    wet = wet_ref[...].astype(jnp.float32)
    drag = drag_ref[...]
    sub = lax.broadcasted_iota(jnp.int32, (SUB, columns), 0)
    row = (row_block * SUB + sub).astype(jnp.float32)
    rotation = 0.5 + (row + scalars_ref[0] + 0.5) * scalars_ref[1]

    def gathered(here, after, index, over):
        first = jnp.take_along_axis(here, index, axis=1, mode="promise_in_bounds")
        second = jnp.take_along_axis(after, index, axis=1, mode="promise_in_bounds")
        return jnp.where(over, second, first)

    spread = []
    speed = []
    for lane_tile in range(lane_tiles):
        places = cell_ref[lane_tile * SUB : (lane_tile + 1) * SUB, :]
        rows = []
        speeds = [[], []]
        for r in range(SUB):
            at = (row_block * lane_tiles + lane_tile) * SUB + r
            tile = offset_ref[at >> 7, at & (LANES - 1)] >> 7
            found = []
            for which in range(2):
                start = pl.multiple_of(table_ref[first_ref[1] * 2, tile + which], SUB)
                found.append(back[pl.ds(start, 2 * coefs), :])
                start = table_ref[first_ref[1] * 2 + 1, tile + which]
                speeds[which].append(back[pl.ds(start, 1), :])
            place = jnp.broadcast_to(places[r : r + 1], (2 * coefs, LANES))
            rows.append(gathered(found[0], found[1], place & (LANES - 1), place >= LANES))
        spread.append(jnp.swapaxes(jnp.stack(rows, axis=0), 0, 1))
        speed.append(
            gathered(
                jnp.concatenate(speeds[0], axis=0),
                jnp.concatenate(speeds[1], axis=0),
                places & (LANES - 1),
                places >= LANES,
            )
        )
    is_wet = wet > 0.5
    friction = [
        jnp.where(
            is_wet, jnp.concatenate([part[index] for part in spread], axis=1) * drag, 0.0
        )
        for index in range(2 * coefs)
    ]
    speed = jnp.where(is_wet, jnp.concatenate(speed, axis=1), 0.0)
    real_rate = drag * speed + LINEAR_DRAG
    for k in range(coefs // 2):
        angular = scalars_ref[2 + k]
        cos_at, sin_at = 2 * k, 2 * k + 1
        det_real = real_rate * real_rate - angular * angular + rotation * rotation
        det_imag = 2.0 * real_rate * angular
        inverse_norm = 1.0 / (det_real * det_real + det_imag * det_imag)
        inv_real = det_real * inverse_norm
        inv_imag = -det_imag * inverse_norm
        east_re = east_ref[0, cos_at] + friction[cos_at]
        east_im = -(east_ref[0, sin_at] + friction[sin_at])
        north_re = north_ref[0, cos_at] + friction[coefs + cos_at]
        north_im = -(north_ref[0, sin_at] + friction[coefs + sin_at])
        num_east_re = real_rate * east_re - angular * east_im + rotation * north_re
        num_east_im = real_rate * east_im + angular * east_re + rotation * north_im
        num_north_re = -rotation * east_re + real_rate * north_re - angular * north_im
        num_north_im = -rotation * east_im + real_rate * north_im + angular * north_re
        east_out[0, cos_at] = num_east_re * inv_real - num_east_im * inv_imag
        east_out[0, sin_at] = -(num_east_re * inv_imag + num_east_im * inv_real)
        north_out[0, cos_at] = num_north_re * inv_real - num_north_im * inv_imag
        north_out[0, sin_at] = -(num_north_re * inv_imag + num_north_im * inv_real)


def finish_call(first, offset, table, scalars, arrays, pieces, rows, result):
    _, coefs, _, columns = result.shape
    lane_tiles = columns // LANES

    def kernel(first_ref, offset_ref, table_ref, scalars_ref, *refs):
        array_refs = refs[:3]
        piece_refs = refs[4:-3]
        out_ref, back, sem = refs[-3:]
        first = first_ref[0]
        count = first_ref[2]

        def body(*block_refs):
            finish_kernel(
                coefs, lane_tiles, first + pl.program_id(0), first_ref, offset_ref, table_ref,
                scalars_ref, back, block_refs,
            )

        @pl.when(count > 0)
        def _():
            copies = []
            at = 0
            for n, piece in enumerate(piece_refs):
                rows = piece.shape[0]
                copies.append(
                    pltpu.make_async_copy(piece, back.at[pl.ds(at, rows)], sem.at[n])
                )
                at += rows
            for copy in copies:
                copy.start()
            for copy in copies:
                copy.wait()
            flat = pl.BlockSpec((SUB, columns), lambda i: (first + i, 0))
            east = pl.BlockSpec((1, coefs, SUB, columns), lambda i: (1, 0, first + i, 0))
            north = pl.BlockSpec((1, coefs, SUB, columns), lambda i: (2, 0, first + i, 0))
            cells = pl.BlockSpec((SUB * lane_tiles, LANES), lambda i: (first + i, 0))
            pltpu.emit_pipeline(
                body,
                grid=(count,),
                in_specs=[flat, flat, cells, east, north],
                out_specs=[east, north],
            )(*array_refs, out_ref, out_ref, out_ref, out_ref)

    anywhere = pl.BlockSpec(memory_space=pl.ANY)
    scalar = pl.BlockSpec(memory_space=pltpu.SMEM)
    operands = [first, offset, table, scalars] + list(arrays) + [result] + pieces
    return pl.pallas_call(
        kernel,
        out_shape=jax.ShapeDtypeStruct(result.shape, jnp.float32),
        in_specs=[scalar] * 4 + [anywhere] * (4 + len(pieces)),
        out_specs=anywhere,
        scratch_shapes=[
            pltpu.VMEM((rows, LANES), jnp.float32),
            pltpu.SemaphoreType.DMA((len(pieces),)),
        ],
        input_output_aliases={7: 0},
        compiler_params=pltpu.CompilerParams(vmem_limit_bytes=VMEM_BYTES),
        cost_estimate=pl.CostEstimate(
            flops=0, bytes_accessed=8 * SUB * columns * coefs * 36, transcendentals=0
        ),
        name="finish",
    )(*operands)


def shifted(block, axis, step, wrap):
    count = lax.axis_size(axis)
    pairs = [
        (i, (i + step) % count) for i in range(count) if wrap or 0 <= i + step < count
    ]
    return lax.ppermute(block, axis, pairs)


def edge_kernel(coefs, east_ref, height_ref, north_ref, last_ref, first_ref, wet_ref, depth_ref, *refs):
    up_ref, down_ref, right_ref, left_ref = refs[-4:]
    rows, columns = wet_ref.shape
    wet = wet_ref[...].astype(jnp.float32)
    end = slice(columns - LANES, columns)
    wet_end = wet[:, end]
    wet_start = wet[:, :LANES]
    depth_end = depth_ref[:, end]
    wet_last = wet[rows - 1 :, :]
    depth_last = depth_ref[rows - 1 :, :]
    for c in range(coefs):
        at = slice(c, c + 1)
        north_row = last_ref[0, c, SUB - 1 :, :] * wet_last
        up_ref[0, at, :] = north_row
        up_ref[1, at, :] = north_row * depth_last
        down_ref[0, at, :] = first_ref[0, c, :1, :] * wet[:1, :]
        down_ref[1, at, :] = first_ref[1, c, :1, :] * wet[:1, :]
        east = east_ref[0, c] * wet_end
        right_ref[0, at, :] = jnp.transpose(east)[LANES - 1 :, :]
        right_ref[1, at, :] = jnp.transpose(east * depth_end)[LANES - 1 :, :]
        left_ref[0, at, :] = jnp.transpose(height_ref[0, c] * wet_start)[:1, :]
        left_ref[1, at, :] = jnp.transpose(north_ref[0, c] * wet_start)[:1, :]


def edge_call(direction, wet_mask, depth, waited):
    _, coefs, rows, columns = direction.shape
    last_tile = columns // LANES - 1
    last_block = rows // SUB - 1
    tall = (1, coefs, rows, LANES)
    whole = pl.BlockSpec((rows, columns), lambda i: (0, 0))
    row_out = (2, coefs, columns)
    col_out = (2, coefs, rows)
    shapes = [row_out, row_out, col_out, col_out]
    return pl.pallas_call(
        lambda *refs: edge_kernel(coefs, *refs),
        out_shape=[jax.ShapeDtypeStruct(shape, jnp.float32) for shape in shapes],
        grid=(1,),
        in_specs=[
            pl.BlockSpec(tall, lambda i: (1, 0, 0, last_tile)),
            pl.BlockSpec(tall, lambda i: (0, 0, 0, 0)),
            pl.BlockSpec(tall, lambda i: (2, 0, 0, 0)),
            pl.BlockSpec((1, coefs, SUB, columns), lambda i: (2, 0, last_block, 0)),
            pl.BlockSpec((2, coefs, SUB, columns), lambda i: (0, 0, 0, 0)),
            whole,
            whole,
        ]
        + [pl.BlockSpec(memory_space=pl.ANY)] * len(waited),
        out_specs=[pl.BlockSpec(shape, lambda i: (0, 0, 0)) for shape in shapes],
        compiler_params=pltpu.CompilerParams(vmem_limit_bytes=VMEM_BYTES),
        cost_estimate=pl.CostEstimate(
            flops=rows * columns, bytes_accessed=0, transcendentals=0
        ),
        name="edges",
    )(direction, direction, direction, direction, direction, wet_mask, depth, *waited)


def halo(direction, wet_mask, depth, waited):
    up, down, right, left = edge_call(direction, wet_mask, depth, waited)
    above = shifted(up, "lat", 1, False)
    below = shifted(down, "lat", -1, False)
    east_below = jnp.concatenate([right[0, :, 1:], below[1, :, -1:]], axis=1)
    north_above = jnp.concatenate([above[0, :, :1], left[1, :, :-1]], axis=1)
    to_right = jnp.stack([right[0], east_below, right[1]])
    to_left = jnp.stack([left[0], left[1], north_above])
    cols = jnp.concatenate(
        [shifted(to_right, "lon", 1, True), shifted(to_left, "lon", -1, True)], axis=0
    )
    slabs = jnp.broadcast_to(cols[:, :, :, None], cols.shape + (LANES,))
    return above, below, slabs


def spread_out(blocks):
    return [
        block if step == 0 else shifted(block, "freq", step, True)
        for step, block in enumerate(blocks)
    ]


def tile_table(groups, coefs, back_chunks, blocks):
    table = np.zeros((2 * groups, blocks + LANES), np.int32)
    for member in range(groups):
        tile = 0
        row = 0
        for chunk_tiles in back_chunks:
            together = sum(chunk_tiles)
            before = 0
            for tiles in chunk_tiles:
                for band in range(groups):
                    start = row + (member - band) % groups * piece_rows(together, coefs)
                    for i in range(before, before + tiles):
                        if tile < blocks:
                            table[2 * member, tile] = start + i * 2 * coefs
                            table[2 * member + 1, tile] = start + together * 2 * coefs + i
                        tile += 1
                before += tiles
            row += groups * piece_rows(together, coefs)
    return table


def local(direction, base_flow, water_depth, drag_factor, wet_mask):
    coefs, tile_rows, tile_cols = direction.shape[1:]
    groups = lax.axis_size("freq")
    member = lax.axis_index("freq")
    lat_place = lax.axis_index("lat")
    total_rows = tile_rows * lax.axis_size("lat")
    lane_tiles = tile_cols // LANES
    angular = OMEGA_STEP * (
        member * (coefs // 2) + jnp.arange(coefs // 2, dtype=jnp.int32) + 1
    ).astype(jnp.float32)
    row_start = (lat_place * tile_rows).astype(jnp.float32)
    scalars = jnp.concatenate(
        [jnp.stack([row_start, jnp.float32(1.0 / total_rows)]), angular]
    )
    place = jnp.reshape(member, (1,)).astype(jnp.int32)
    blocks = tile_rows * lane_tiles
    row_blocks = tile_rows // SUB
    chunk_tiles = [share * blocks // (groups * SHARE_UNITS) for share in CHUNK_SHARES]
    fixed = groups * sum(chunk_tiles)
    steps = -(-(blocks - fixed) // (groups * LOOP_TILES))
    back_chunks = [chunk_tiles[:-1], chunk_tiles[-1:]]
    table = jnp.asarray(
        tile_table(groups, coefs, back_chunks + [[LOOP_TILES]] * steps, blocks)
    )
    index, cells, offset = index_call(wet_mask)
    offsets = offset.reshape(-1)
    ends = offsets[SUB * lane_tiles : blocks + 1 : SUB * lane_tiles]

    def packed(first_tile, tiles, token, waited=()):
        params = jnp.stack([place[0], first_tile + token])
        *flows, token = pack_call(
            params, offset, index, base_flow, direction, groups, tiles, waited
        )
        return spread_out(flows), token[0, 0]

    def through(flows, token, weight):
        *back, token = friction_call(place + token, flows, coefs, weight)
        return spread_out(back), token[0, 0]

    flows = []
    tile = 0
    token = jnp.int32(0)
    for tiles in chunk_tiles[:-1]:
        flow, token = packed(tile, tiles, token)
        flows.append(flow)
        tile += groups * tiles

    loop_cells = groups * LOOP_TILES * LANES
    beyond = offsets[blocks] + token - fixed * LANES
    loops = jnp.maximum(beyond + loop_cells - 1, 0) // loop_cells

    def more(state):
        done, held = state
        flow, _ = packed(fixed + done * groups * LOOP_TILES, LOOP_TILES, 0)
        back, _ = through([flow], 0, 1)
        held = lax.dynamic_update_slice_in_dim(
            held, jnp.concatenate(back, axis=0)[None], done, 0
        )
        return done + 1, held

    rows = groups * piece_rows(LOOP_TILES, coefs)
    extra = jnp.zeros((steps, rows, LANES), jnp.float32)
    done, extra = lax.while_loop(lambda state: state[0] < loops, more, (jnp.int32(0), extra))

    token = token + jnp.minimum(done, 0)
    flows.append(packed(tile, chunk_tiles[-1], token)[0])
    above, below, slabs = halo(direction, wet_mask, water_depth, flows[0][1:] + flows[-1][:1])
    result, prepared = prepare_call(
        scalars, direction, wet_mask, water_depth, above, below, slabs
    )
    back, token = through(flows[:-1], prepared[0, 0], 1)
    backs = [back]
    back, token = through(flows[-1:], token, LATE_WEIGHT)
    backs.append(back)

    arrays = (wet_mask, drag_factor, cells)
    pieces = []
    back_rows = rows * steps
    back_rows += groups * sum(piece_rows(sum(several), coefs) for several in back_chunks)
    begin = jnp.int32(0)
    tile = 0
    for last, several in enumerate(back_chunks):
        pieces += backs[last]
        tile += groups * sum(several)
        if last:
            end = jnp.int32(row_blocks)
            pieces.append(extra.reshape(-1, LANES))
        else:
            end = jnp.sum((ends <= tile * LANES).astype(jnp.int32))
        first = jnp.stack([begin, place[0], end - begin])
        result = finish_call(
            first, offset, table, scalars, arrays, list(pieces), back_rows, result
        )
        begin = end
    return result


def solution(mesh):
    placed = (
        P(None, "freq", "lat", "lon"),
        P(None, "freq", "lat", "lon"),
        P("lat", "lon"),
        P("lat", "lon"),
        P("lat", "lon"),
    )
    return jax.shard_map(
        local, mesh=mesh, in_specs=placed, out_specs=P(None, "freq", "lat", "lon"), check_vma=False
    )
```

```python
import math

import jax
import jax.numpy as jnp
import ml_dtypes
import numpy as np
from jax import lax
from jax.experimental import pallas as pl
from jax.experimental.pallas import tpu as pltpu
from jax.sharding import PartitionSpec as P

NCON = 16
NTIME = 256
LANES = 128
SUB = 8

LINEAR_DRAG = 0.5
GRAVITY = 1.0
OMEGA_STEP = 0.25
SPEED_SOFT = 0.01
VMEM_BYTES = 48 * 1024 * 1024
CHUNK_SHARES = (16, 50, 31)
SHARE_UNITS = 128
LOOP_TILES = 8
PACK_COST = 16384
LATE_WEIGHT = 2048


def split_table():
    sample = np.arange(NTIME)[:, None]
    harmonic = np.arange(1, NCON + 1)[None, :]
    phase = (sample * harmonic % NTIME) * (2.0 * math.pi / NTIME)
    table = np.stack([np.cos(phase), np.sin(phase)], axis=2).reshape(NTIME, 2 * NCON)
    table = table.astype(np.float32)
    high = table.astype(ml_dtypes.bfloat16)
    low = (table - high.astype(np.float32)).astype(ml_dtypes.bfloat16)
    return high, low


def split_value(value):
    high = value.astype(jnp.bfloat16)
    low = (value - high.astype(jnp.float32)).astype(jnp.bfloat16)
    return high, low


def friction_kernel(groups, coefs, chunk_tiles, place_ref, synth_ref, analyse_ref, *refs):
    parts = len(chunk_tiles)
    tiles = sum(chunk_tiles)
    out_refs, token_ref = refs[groups * parts : -1], refs[-1]
    token_ref[...] = jnp.zeros_like(token_ref)
    columns = 2 * NCON

    def block(flow_refs, first, at, count):
        tile = first + at
        loaded = []
        for source in range(groups):
            several = [flow_refs[source][at + i] for i in range(count)]
            loaded.append(jnp.concatenate(several, axis=1))
        series = []
        for field in range(4):
            rows = slice(field * coefs, (field + 1) * coefs)
            values = jnp.concatenate([part[rows] for part in loaded], axis=0)
            high, low = split_value(values)
            operand = jnp.concatenate([high, low, high], axis=0)
            series.append(
                jnp.dot(synth_ref[0], operand, preferred_element_type=jnp.float32)
            )
        base_east, base_north, step_east, step_north = series
        square = base_east * base_east + base_north * base_north + SPEED_SOFT
        inverse = lax.rsqrt(square)
        speed = square * inverse
        projected = (base_east * step_east + base_north * step_north) * inverse
        forces = (
            speed * step_east + base_east * projected,
            speed * step_north + base_north * projected,
        )
        mean = jnp.sum(speed, axis=0, keepdims=True) * (1.0 / NTIME)
        analysed = []
        for force in forces:
            high, low = split_value(force)
            both = jnp.dot(analyse_ref[0], high, preferred_element_type=jnp.float32)
            rest = jnp.dot(
                analyse_ref[0, :columns, :], low, preferred_element_type=jnp.float32
            )
            analysed.append(both[:columns] + both[columns:] + rest)
        for part in range(count):
            lanes = slice(part * LANES, (part + 1) * LANES)
            for target in range(groups):
                rows = slice(target * coefs, (target + 1) * coefs)
                values = jnp.concatenate(
                    [analysed[0][rows, lanes], analysed[1][rows, lanes]], axis=0
                )
                start = pl.multiple_of((tile + part) * 2 * coefs, SUB)
                out_refs[target][pl.ds(start, 2 * coefs), :] = values
                at = tiles * 2 * coefs + tile + part
                out_refs[target][pl.ds(at, 1), :] = mean[:, lanes]

    first = 0
    for part, here in enumerate(chunk_tiles):
        flow_refs = refs[part * groups : (part + 1) * groups]

        def body(step, carry, flow_refs=flow_refs, first=first):
            block(flow_refs, first, step * 2, 2)
            return carry

        lax.fori_loop(0, here // 2, body, 0)
        if here % 2:
            block(flow_refs, first, here - 1, 1)
        first += here


def placed_tables(groups, coefs):
    high, low = split_table()
    synth, analyse = [], []
    for member in range(groups):
        sources = [(member - step) % groups for step in range(groups)]
        targets = [(member + step) % groups for step in range(groups)]
        source = np.concatenate([np.arange(coefs) + m * coefs for m in sources])
        target = np.concatenate([np.arange(coefs) + m * coefs for m in targets])
        synth.append(np.concatenate([high[:, source], high[:, source], low[:, source]], axis=1))
        both = np.concatenate([high[:, target].T, low[:, target].T], axis=0)
        analyse.append((both.astype(np.float32) * (2.0 / NTIME)).astype(ml_dtypes.bfloat16))
    return np.stack(synth), np.stack(analyse)


def piece_rows(tiles, coefs):
    return tiles * 2 * coefs + -(-tiles // SUB) * SUB


def friction_call(place, flows, coefs, weight):
    groups = len(flows[0])
    chunk_tiles = [chunk[0].shape[0] for chunk in flows]
    tiles = sum(chunk_tiles)
    synth, analyse = placed_tables(groups, coefs)
    cells = groups * tiles * LANES
    out_shape = (piece_rows(tiles, coefs), LANES)
    grid_spec = pltpu.PrefetchScalarGridSpec(
        num_scalar_prefetch=1,
        grid=(1,),
        in_specs=[
            pl.BlockSpec((1,) + synth.shape[1:], lambda i, place: (place[0], 0, 0)),
            pl.BlockSpec((1,) + analyse.shape[1:], lambda i, place: (place[0], 0, 0)),
        ]
        + [
            pl.BlockSpec(block.shape, lambda i, place: (0, 0, 0))
            for chunk in flows
            for block in chunk
        ],
        out_specs=[pl.BlockSpec(out_shape, lambda i, place: (0, 0))] * groups
        + [pl.BlockSpec((SUB, LANES), lambda i, place: (0, 0))],
    )
    return pl.pallas_call(
        lambda *refs: friction_kernel(groups, coefs, chunk_tiles, *refs),
        out_shape=[jax.ShapeDtypeStruct(out_shape, jnp.float32)] * groups
        + [jax.ShapeDtypeStruct((SUB, LANES), jnp.int32)],
        grid_spec=grid_spec,
        compiler_params=pltpu.CompilerParams(vmem_limit_bytes=VMEM_BYTES),
        cost_estimate=pl.CostEstimate(
            flops=cells * NTIME * weight, bytes_accessed=0, transcendentals=0
        ),
        name="friction",
    )(place, jnp.asarray(synth), jnp.asarray(analyse), *[b for chunk in flows for b in chunk])


def index_kernel(wet_ref, index_ref, place_ref, offset_ref, scratch):
    blocks = scratch.shape[0]
    rows, cols = wet_ref.shape
    at = 0
    for row in range(0, rows, SUB):
        for col in range(0, cols, LANES):
            part = wet_ref[row : row + SUB, col : col + LANES]
            scratch[at : at + SUB, :] = jnp.where(part != 0, 1.0, 0.0)
            at += SUB
    wet = scratch[...].astype(jnp.bfloat16)
    earlier = lax.broadcasted_iota(jnp.int32, (LANES, LANES), 0)
    later = lax.broadcasted_iota(jnp.int32, (LANES, LANES), 1)
    before = jnp.where(earlier < later, 1.0, 0.0).astype(jnp.bfloat16)
    ones = jnp.ones((LANES, LANES), jnp.bfloat16)
    rank = jnp.dot(wet, before, preferred_element_type=jnp.float32)
    count = jnp.dot(wet, ones, preferred_element_type=jnp.float32)
    low = lax.broadcasted_iota(jnp.int32, (blocks, blocks), 0)
    high = lax.broadcasted_iota(jnp.int32, (blocks, blocks), 1)
    summing = jnp.where(high < low, 1.0, 0.0).astype(jnp.bfloat16)
    offset = jnp.dot(summing, count.astype(jnp.bfloat16), preferred_element_type=jnp.float32)
    lane = lax.broadcasted_iota(jnp.int32, (blocks, LANES), 1)
    rank = rank.astype(jnp.int32)
    held = jnp.where(scratch[...] > 0.5, lane + LANES * (lane - rank), 0)
    for bit in range(7):
        step = 1 << bit
        coming = pltpu.roll(held, LANES - step, 1)
        moves = (coming >> (7 + bit)) & 1
        stays = 1 - ((held >> (7 + bit)) & 1)
        held = jnp.where(moves == 1, coming, held * stays)
    source = held & (LANES - 1)
    shift = offset.astype(jnp.int32) & (LANES - 1)
    index_ref[...] = jnp.take_along_axis(
        source, (lane - shift) & (LANES - 1), axis=1, mode="promise_in_bounds"
    )
    place_ref[...] = shift + rank
    eye = jnp.where(earlier == later, 1.0, 0.0)
    cubes = offset.reshape(blocks // LANES, LANES, LANES)
    table = jnp.sum(cubes * eye[None], axis=1)
    total = offset[blocks - 1 : blocks] + count[blocks - 1 : blocks]
    offset_ref[: blocks // LANES, :] = table.astype(jnp.int32)
    offset_ref[blocks // LANES : blocks // LANES + 1, :] = total.astype(jnp.int32)


def index_call(wet_mask):
    rows, cols = wet_mask.shape
    blocks = rows * cols // LANES
    table = -(-(blocks // LANES + 1) // SUB) * SUB
    return pl.pallas_call(
        index_kernel,
        out_shape=[
            jax.ShapeDtypeStruct((blocks, LANES), jnp.int32),
            jax.ShapeDtypeStruct((blocks, LANES), jnp.int32),
            jax.ShapeDtypeStruct((table, LANES), jnp.int32),
        ],
        scratch_shapes=[pltpu.VMEM((blocks, LANES), jnp.float32)],
        compiler_params=pltpu.CompilerParams(vmem_limit_bytes=VMEM_BYTES),
        name="index",
    )(wet_mask)


def pack_kernel(groups, coefs, tiles, waited, params_ref, offset_ref, index_ref, base_ref, step_ref, *refs):
    refs = refs[waited:]
    out_refs = refs[:groups]
    token_ref, held, stage, in_sem, out_sem = refs[groups:]
    token_ref[...] = jnp.zeros_like(token_ref)
    lane_tiles = held.shape[1]
    per_block = SUB * lane_tiles
    row_blocks = index_ref.shape[0] // per_block
    count = groups * tiles
    first_tile = params_ref[1]
    low = first_tile * LANES
    high = low + count * LANES

    def offset_of(block):
        return offset_ref[block >> 7, block & (LANES - 1)]

    begin = jnp.int32(0)
    end = jnp.int32(0)
    for block in range(row_blocks):
        begin += (offset_of((block + 1) * per_block) <= low).astype(jnp.int32)
        end += (offset_of(block * per_block) < high).astype(jnp.int32)
    end = jnp.maximum(end, begin)

    def copies(block):
        slot = block & 1
        rows = pl.ds(pl.multiple_of(block * SUB, SUB), SUB)
        started = []
        for lane_tile in range(lane_tiles):
            lanes = pl.ds(lane_tile * LANES, LANES)
            landing = held.at[slot, lane_tile]
            started.append(
                pltpu.make_async_copy(
                    base_ref.at[:, :, rows, lanes],
                    landing.at[pl.ds(0, 2)],
                    in_sem.at[slot, 2 * lane_tile],
                )
            )
            started.append(
                pltpu.make_async_copy(
                    step_ref.at[pl.ds(1, 2), :, rows, lanes],
                    landing.at[pl.ds(2, 2)],
                    in_sem.at[slot, 2 * lane_tile + 1],
                )
            )
        return started

    @pl.when(begin < end)
    def _():
        for copy in copies(begin):
            copy.start()

    lane = lax.broadcasted_iota(jnp.int32, (coefs, LANES), 1)

    def place_of(offset):
        return jnp.clip((offset >> 7) - first_tile + 1, 0, count + 1)

    def body(block, current):
        @pl.when(block + 1 < end)
        def _():
            for copy in copies(block + 1):
                copy.start()

        for copy in copies(block):
            copy.wait()
        slot = block & 1
        for lane_tile in range(lane_tiles):
            fields = [
                held.at[slot, lane_tile, field].reshape(coefs * SUB, LANES) for field in range(4)
            ]
            start = block * per_block + lane_tile * SUB
            index = index_ref[pl.ds(pl.multiple_of(start, SUB), SUB), :]
            following = offset_of(start)
            for r in range(SUB):
                offset = following
                following = offset_of(start + r + 1)
                shift = offset & (LANES - 1)
                crossing = (following >> 7) > (offset >> 7)
                source = jnp.broadcast_to(index[r : r + 1], (coefs, LANES))
                to = place_of(offset)
                renewed = []
                for field in range(4):
                    got = jnp.take_along_axis(
                        fields[field][pl.ds(r, coefs, stride=SUB), :],
                        source,
                        axis=1,
                        mode="promise_in_bounds",
                    )
                    full = jnp.where(lane >= shift, got, current[field])
                    stage[to, field * coefs : (field + 1) * coefs, :] = full
                    renewed.append(jnp.where(crossing, got, full))
                current = tuple(renewed)
        return current

    zero = jnp.zeros((coefs, LANES), jnp.float32)
    current = lax.fori_loop(begin, end, body, (zero,) * 4)
    last = place_of(offset_of(end * per_block))
    for field in range(4):
        stage[last, field * coefs : (field + 1) * coefs, :] = current[field]
    outs = []
    for step in range(groups):
        member = lax.rem(params_ref[0] + step, groups)
        outs.append(
            pltpu.make_async_copy(
                stage.at[pl.ds(1 + member * tiles, tiles)], out_refs[step], out_sem.at[step]
            )
        )
    for copy in outs:
        copy.start()
    for copy in outs:
        copy.wait()


def pack_call(params, offset, index, base_flow, direction, groups, tiles, waited):
    coefs, _, columns = direction.shape[1:]
    shape = (tiles, 4 * coefs, LANES)
    anywhere = pl.BlockSpec(memory_space=pl.ANY)
    grid_spec = pltpu.PrefetchScalarGridSpec(
        num_scalar_prefetch=2,
        grid=(1,),
        in_specs=[pl.BlockSpec(index.shape, lambda i, p, o: (0, 0))]
        + [anywhere] * (2 + len(waited)),
        out_specs=[anywhere] * groups + [pl.BlockSpec((SUB, LANES), lambda i, p, o: (0, 0))],
        scratch_shapes=[
            pltpu.VMEM((2, columns // LANES, 4, coefs, SUB, LANES), jnp.float32),
            pltpu.VMEM((groups * tiles + 2, 4 * coefs, LANES), jnp.float32),
            pltpu.SemaphoreType.DMA((2, 2 * (columns // LANES))),
            pltpu.SemaphoreType.DMA((groups,)),
        ],
    )
    return pl.pallas_call(
        lambda *refs: pack_kernel(groups, coefs, tiles, len(waited), *refs),
        out_shape=[jax.ShapeDtypeStruct(shape, jnp.float32)] * groups
        + [jax.ShapeDtypeStruct((SUB, LANES), jnp.int32)],
        grid_spec=grid_spec,
        compiler_params=pltpu.CompilerParams(vmem_limit_bytes=VMEM_BYTES),
        cost_estimate=pl.CostEstimate(
            flops=0, bytes_accessed=groups * tiles * coefs * PACK_COST, transcendentals=0
        ),
        name="pack",
    )(params, offset, index, base_flow, direction, *waited)


def prepare_kernel(coefs, scalars_ref, *refs):
    (here_ref, prev_ref, next_ref, wet_ref, wet_prev_ref, wet_next_ref, depth_ref, depth_prev_ref,
     above_ref, below_ref, slab_ref, out_ref, token_ref) = refs
    token_ref[...] = jnp.zeros_like(token_ref)
    columns = here_ref.shape[-1]
    row_block = pl.program_id(0)
    at_top = row_block == 0
    at_bottom = row_block == pl.num_programs(0) - 1
    wet = wet_ref[...].astype(jnp.float32)
    wet_prev = wet_prev_ref[SUB - 1 :, :].astype(jnp.float32)
    wet_next = wet_next_ref[:1, :].astype(jnp.float32)
    depth = depth_ref[...]
    depth_prev = depth_prev_ref[SUB - 1 :, :]
    lane = lax.broadcasted_iota(jnp.int32, (SUB, columns), 1)
    sub = lax.broadcasted_iota(jnp.int32, (SUB, columns), 0)
    row = (row_block * SUB + sub).astype(jnp.float32)
    rotation = 0.5 + (row + scalars_ref[0] + 0.5) * scalars_ref[1]

    def wide(slab):
        return jnp.concatenate([slab] * (columns // LANES), axis=1)

    def west(value, slab):
        return jnp.where(lane == 0, wide(slab), pltpu.roll(value, 1, 1))

    def east_of(value, slab):
        return jnp.where(lane == columns - 1, wide(slab), pltpu.roll(value, columns - 1, 1))

    def above(value, edge):
        return jnp.where(sub == 0, edge, pltpu.roll(value, 1, 0))

    def below(value, edge):
        return jnp.where(sub == SUB - 1, edge, pltpu.roll(value, SUB - 1, 0))

    for k in range(coefs // 2):
        angular = scalars_ref[2 + k]
        inverse_angular = 1.0 / (angular + jnp.zeros((SUB, columns), jnp.float32))
        planes = [
            [here_ref[p, 2 * k + part] * wet for p in range(3)] for part in range(2)
        ]
        for part in range(2):
            c = 2 * k + part
            height, east, north = planes[part]
            other = planes[1 - part]
            signed = angular if part == 0 else -angular
            east_flux = depth * east
            north_flux = depth * north
            north_edge = prev_ref[0, c, SUB - 1 :, :] * wet_prev
            flux_edge = jnp.where(at_top, above_ref[1, c : c + 1], north_edge * depth_prev)
            north_edge = jnp.where(at_top, above_ref[0, c : c + 1], north_edge)
            height_edge = jnp.where(
                at_bottom, below_ref[0, c : c + 1], next_ref[0, c, :1, :] * wet_next
            )
            east_edge = jnp.where(
                at_bottom, below_ref[1, c : c + 1], next_ref[1, c, :1, :] * wet_next
            )
            north_up = above(north, north_edge)
            east_down = below(east, east_edge)
            res_height = (
                signed * other[0]
                + east_flux
                - west(east_flux, slab_ref[2, c])
                + north_flux
                - above(north_flux, flux_edge)
            )
            north_mean = 0.25 * (
                north
                + east_of(north, slab_ref[4, c])
                + north_up
                + east_of(north_up, slab_ref[5, c])
            )
            east_mean = 0.25 * (
                east
                + west(east, slab_ref[0, c])
                + east_down
                + west(east_down, slab_ref[1, c])
            )
            res_east = (
                signed * other[1]
                + LINEAR_DRAG * east
                - rotation * north_mean
                + GRAVITY * (east_of(height, slab_ref[3, c]) - height)
            )
            res_north = (
                signed * other[2]
                + LINEAR_DRAG * north
                + rotation * east_mean
                + GRAVITY * (below(height, height_edge) - height)
            )
            if part == 0:
                out_ref[0, c + 1] = res_height * wet * inverse_angular
            else:
                out_ref[0, c - 1] = -res_height * wet * inverse_angular
            out_ref[1, c] = res_east * wet
            out_ref[2, c] = res_north * wet


def prepare_call(scalars, direction, wet_mask, depth, above, below, slabs):
    _, coefs, rows, columns = direction.shape
    last = rows // SUB - 1

    def before(i):
        return jnp.maximum(i - 1, 0)

    def after(i):
        return jnp.minimum(i + 1, last)

    planes = pl.BlockSpec((3, coefs, SUB, columns), lambda i: (0, 0, i, 0))
    flat = (SUB, columns)
    edge = pl.BlockSpec((2, coefs, columns), lambda i: (0, 0, 0))
    return pl.pallas_call(
        lambda *refs: prepare_kernel(coefs, *refs),
        out_shape=[
            jax.ShapeDtypeStruct(direction.shape, jnp.float32),
            jax.ShapeDtypeStruct((SUB, LANES), jnp.int32),
        ],
        grid=(rows // SUB,),
        in_specs=[
            pl.BlockSpec(memory_space=pltpu.SMEM),
            planes,
            pl.BlockSpec((1, coefs, SUB, columns), lambda i: (2, 0, before(i), 0)),
            pl.BlockSpec((2, coefs, SUB, columns), lambda i: (0, 0, after(i), 0)),
            pl.BlockSpec(flat, lambda i: (i, 0)),
            pl.BlockSpec(flat, lambda i: (before(i), 0)),
            pl.BlockSpec(flat, lambda i: (after(i), 0)),
            pl.BlockSpec(flat, lambda i: (i, 0)),
            pl.BlockSpec(flat, lambda i: (before(i), 0)),
            edge,
            edge,
            pl.BlockSpec((6, coefs, SUB, LANES), lambda i: (0, 0, i, 0)),
        ],
        out_specs=[planes, pl.BlockSpec((SUB, LANES), lambda i: (0, 0))],
        compiler_params=pltpu.CompilerParams(vmem_limit_bytes=VMEM_BYTES),
        cost_estimate=pl.CostEstimate(
            flops=rows * columns * coefs, bytes_accessed=0, transcendentals=0
        ),
        name="prepare",
    )(
        scalars, direction, direction, direction, wet_mask, wet_mask, wet_mask, depth, depth,
        above, below, slabs,
    )


def finish_kernel(coefs, lane_tiles, row_block, first_ref, offset_ref, table_ref, scalars_ref, back, spread_ref, refs):
    wet_ref, drag_ref, cell_ref, east_ref, north_ref, east_out, north_out = refs
    columns = lane_tiles * LANES
    wet = wet_ref[...].astype(jnp.float32)
    drag = drag_ref[...]
    sub = lax.broadcasted_iota(jnp.int32, (SUB, columns), 0)
    row = (row_block * SUB + sub).astype(jnp.float32)
    rotation = 0.5 + (row + scalars_ref[0] + 0.5) * scalars_ref[1]

    def gathered(here, after, index, over):
        first = jnp.take_along_axis(here, index, axis=1, mode="promise_in_bounds")
        second = jnp.take_along_axis(after, index, axis=1, mode="promise_in_bounds")
        return jnp.where(over, second, first)

    speed = []
    for lane_tile in range(lane_tiles):
        places = cell_ref[lane_tile * SUB : (lane_tile + 1) * SUB, :]
        turned = spread_ref.at[lane_tile].reshape(2 * coefs * SUB, LANES)
        speeds = [[], []]
        for r in range(SUB):
            at = (row_block * lane_tiles + lane_tile) * SUB + r
            tile = offset_ref[at >> 7, at & (LANES - 1)] >> 7
            found = []
            for which in range(2):
                start = pl.multiple_of(table_ref[first_ref[1] * 2, tile + which], SUB)
                found.append(back[pl.ds(start, 2 * coefs), :])
                start = table_ref[first_ref[1] * 2 + 1, tile + which]
                speeds[which].append(back[pl.ds(start, 1), :])
            place = jnp.broadcast_to(places[r : r + 1], (2 * coefs, LANES))
            turned[pl.ds(r, 2 * coefs, stride=SUB), :] = gathered(
                found[0], found[1], place & (LANES - 1), place >= LANES
            )
        speed.append(
            gathered(
                jnp.concatenate(speeds[0], axis=0),
                jnp.concatenate(speeds[1], axis=0),
                places & (LANES - 1),
                places >= LANES,
            )
        )
    is_wet = wet > 0.5
    friction = [
        jnp.where(
            is_wet,
            jnp.concatenate([spread_ref[n, index] for n in range(lane_tiles)], axis=1) * drag,
            0.0,
        )
        for index in range(2 * coefs)
    ]
    speed = jnp.where(is_wet, jnp.concatenate(speed, axis=1), 0.0)
    real_rate = drag * speed + LINEAR_DRAG
    for k in range(coefs // 2):
        angular = scalars_ref[2 + k]
        cos_at, sin_at = 2 * k, 2 * k + 1
        det_real = real_rate * real_rate - angular * angular + rotation * rotation
        det_imag = 2.0 * real_rate * angular
        inverse_norm = 1.0 / (det_real * det_real + det_imag * det_imag)
        inv_real = det_real * inverse_norm
        inv_imag = -det_imag * inverse_norm
        east_re = east_ref[0, cos_at] + friction[cos_at]
        east_im = -(east_ref[0, sin_at] + friction[sin_at])
        north_re = north_ref[0, cos_at] + friction[coefs + cos_at]
        north_im = -(north_ref[0, sin_at] + friction[coefs + sin_at])
        num_east_re = real_rate * east_re - angular * east_im + rotation * north_re
        num_east_im = real_rate * east_im + angular * east_re + rotation * north_im
        num_north_re = -rotation * east_re + real_rate * north_re - angular * north_im
        num_north_im = -rotation * east_im + real_rate * north_im + angular * north_re
        east_out[0, cos_at] = num_east_re * inv_real - num_east_im * inv_imag
        east_out[0, sin_at] = -(num_east_re * inv_imag + num_east_im * inv_real)
        north_out[0, cos_at] = num_north_re * inv_real - num_north_im * inv_imag
        north_out[0, sin_at] = -(num_north_re * inv_imag + num_north_im * inv_real)


def finish_call(first, offset, table, scalars, arrays, pieces, rows, result):
    _, coefs, _, columns = result.shape
    lane_tiles = columns // LANES

    def kernel(first_ref, offset_ref, table_ref, scalars_ref, *refs):
        array_refs = refs[:3]
        piece_refs = refs[4:-4]
        out_ref, back, spread_ref, sem = refs[-4:]
        first = first_ref[0]
        count = first_ref[2]

        def body(*block_refs):
            finish_kernel(
                coefs, lane_tiles, first + pl.program_id(0), first_ref, offset_ref, table_ref,
                scalars_ref, back, spread_ref, block_refs,
            )

        @pl.when(count > 0)
        def _():
            copies = []
            at = 0
            for n, piece in enumerate(piece_refs):
                rows = piece.shape[0]
                copies.append(
                    pltpu.make_async_copy(piece, back.at[pl.ds(at, rows)], sem.at[n])
                )
                at += rows
            for copy in copies:
                copy.start()
            for copy in copies:
                copy.wait()
            flat = pl.BlockSpec((SUB, columns), lambda i: (first + i, 0))
            east = pl.BlockSpec((1, coefs, SUB, columns), lambda i: (1, 0, first + i, 0))
            north = pl.BlockSpec((1, coefs, SUB, columns), lambda i: (2, 0, first + i, 0))
            cells = pl.BlockSpec((SUB * lane_tiles, LANES), lambda i: (first + i, 0))
            pltpu.emit_pipeline(
                body,
                grid=(count,),
                in_specs=[flat, flat, cells, east, north],
                out_specs=[east, north],
            )(*array_refs, out_ref, out_ref, out_ref, out_ref)

    anywhere = pl.BlockSpec(memory_space=pl.ANY)
    scalar = pl.BlockSpec(memory_space=pltpu.SMEM)
    operands = [first, offset, table, scalars] + list(arrays) + [result] + pieces
    return pl.pallas_call(
        kernel,
        out_shape=jax.ShapeDtypeStruct(result.shape, jnp.float32),
        in_specs=[scalar] * 4 + [anywhere] * (4 + len(pieces)),
        out_specs=anywhere,
        scratch_shapes=[
            pltpu.VMEM((rows, LANES), jnp.float32),
            pltpu.VMEM((lane_tiles, 2 * coefs, SUB, LANES), jnp.float32),
            pltpu.SemaphoreType.DMA((len(pieces),)),
        ],
        input_output_aliases={7: 0},
        compiler_params=pltpu.CompilerParams(vmem_limit_bytes=VMEM_BYTES),
        cost_estimate=pl.CostEstimate(
            flops=0, bytes_accessed=8 * SUB * columns * coefs * 36, transcendentals=0
        ),
        name="finish",
    )(*operands)


def shifted(block, axis, step, wrap):
    count = lax.axis_size(axis)
    pairs = [
        (i, (i + step) % count) for i in range(count) if wrap or 0 <= i + step < count
    ]
    return lax.ppermute(block, axis, pairs)


def edge_kernel(coefs, east_ref, height_ref, north_ref, last_ref, first_ref, wet_ref, depth_ref, *refs):
    up_ref, down_ref, right_ref, left_ref = refs[-4:]
    rows, columns = wet_ref.shape
    wet = wet_ref[...].astype(jnp.float32)
    end = slice(columns - LANES, columns)
    wet_end = wet[:, end]
    wet_start = wet[:, :LANES]
    depth_end = depth_ref[:, end]
    wet_last = wet[rows - 1 :, :]
    depth_last = depth_ref[rows - 1 :, :]
    for c in range(coefs):
        at = slice(c, c + 1)
        north_row = last_ref[0, c, SUB - 1 :, :] * wet_last
        up_ref[0, at, :] = north_row
        up_ref[1, at, :] = north_row * depth_last
        down_ref[0, at, :] = first_ref[0, c, :1, :] * wet[:1, :]
        down_ref[1, at, :] = first_ref[1, c, :1, :] * wet[:1, :]
        east = east_ref[0, c] * wet_end
        right_ref[0, at, :] = jnp.transpose(east)[LANES - 1 :, :]
        right_ref[1, at, :] = jnp.transpose(east * depth_end)[LANES - 1 :, :]
        left_ref[0, at, :] = jnp.transpose(height_ref[0, c] * wet_start)[:1, :]
        left_ref[1, at, :] = jnp.transpose(north_ref[0, c] * wet_start)[:1, :]


def edge_call(direction, wet_mask, depth, waited):
    _, coefs, rows, columns = direction.shape
    last_tile = columns // LANES - 1
    last_block = rows // SUB - 1
    tall = (1, coefs, rows, LANES)
    whole = pl.BlockSpec((rows, columns), lambda i: (0, 0))
    row_out = (2, coefs, columns)
    col_out = (2, coefs, rows)
    shapes = [row_out, row_out, col_out, col_out]
    return pl.pallas_call(
        lambda *refs: edge_kernel(coefs, *refs),
        out_shape=[jax.ShapeDtypeStruct(shape, jnp.float32) for shape in shapes],
        grid=(1,),
        in_specs=[
            pl.BlockSpec(tall, lambda i: (1, 0, 0, last_tile)),
            pl.BlockSpec(tall, lambda i: (0, 0, 0, 0)),
            pl.BlockSpec(tall, lambda i: (2, 0, 0, 0)),
            pl.BlockSpec((1, coefs, SUB, columns), lambda i: (2, 0, last_block, 0)),
            pl.BlockSpec((2, coefs, SUB, columns), lambda i: (0, 0, 0, 0)),
            whole,
            whole,
        ]
        + [pl.BlockSpec(memory_space=pl.ANY)] * len(waited),
        out_specs=[pl.BlockSpec(shape, lambda i: (0, 0, 0)) for shape in shapes],
        compiler_params=pltpu.CompilerParams(vmem_limit_bytes=VMEM_BYTES),
        cost_estimate=pl.CostEstimate(
            flops=rows * columns, bytes_accessed=0, transcendentals=0
        ),
        name="edges",
    )(direction, direction, direction, direction, direction, wet_mask, depth, *waited)


def halo(direction, wet_mask, depth, waited):
    up, down, right, left = edge_call(direction, wet_mask, depth, waited)
    above = shifted(up, "lat", 1, False)
    below = shifted(down, "lat", -1, False)
    east_below = jnp.concatenate([right[0, :, 1:], below[1, :, -1:]], axis=1)
    north_above = jnp.concatenate([above[0, :, :1], left[1, :, :-1]], axis=1)
    to_right = jnp.stack([right[0], east_below, right[1]])
    to_left = jnp.stack([left[0], left[1], north_above])
    cols = jnp.concatenate(
        [shifted(to_right, "lon", 1, True), shifted(to_left, "lon", -1, True)], axis=0
    )
    slabs = jnp.broadcast_to(cols[:, :, :, None], cols.shape + (LANES,))
    return above, below, slabs


def spread_out(blocks):
    return [
        block if step == 0 else shifted(block, "freq", step, True)
        for step, block in enumerate(blocks)
    ]


def tile_table(groups, coefs, back_chunks, blocks):
    table = np.zeros((2 * groups, blocks + LANES), np.int32)
    for member in range(groups):
        tile = 0
        row = 0
        for chunk_tiles in back_chunks:
            together = sum(chunk_tiles)
            before = 0
            for tiles in chunk_tiles:
                for band in range(groups):
                    start = row + (member - band) % groups * piece_rows(together, coefs)
                    for i in range(before, before + tiles):
                        if tile < blocks:
                            table[2 * member, tile] = start + i * 2 * coefs
                            table[2 * member + 1, tile] = start + together * 2 * coefs + i
                        tile += 1
                before += tiles
            row += groups * piece_rows(together, coefs)
    return table


def local(direction, base_flow, water_depth, drag_factor, wet_mask):
    coefs, tile_rows, tile_cols = direction.shape[1:]
    groups = lax.axis_size("freq")
    member = lax.axis_index("freq")
    lat_place = lax.axis_index("lat")
    total_rows = tile_rows * lax.axis_size("lat")
    lane_tiles = tile_cols // LANES
    angular = OMEGA_STEP * (
        member * (coefs // 2) + jnp.arange(coefs // 2, dtype=jnp.int32) + 1
    ).astype(jnp.float32)
    row_start = (lat_place * tile_rows).astype(jnp.float32)
    scalars = jnp.concatenate(
        [jnp.stack([row_start, jnp.float32(1.0 / total_rows)]), angular]
    )
    place = jnp.reshape(member, (1,)).astype(jnp.int32)
    blocks = tile_rows * lane_tiles
    row_blocks = tile_rows // SUB
    chunk_tiles = [share * blocks // (groups * SHARE_UNITS) for share in CHUNK_SHARES]
    fixed = groups * sum(chunk_tiles)
    steps = -(-(blocks - fixed) // (groups * LOOP_TILES))
    back_chunks = [chunk_tiles[:-1], chunk_tiles[-1:]]
    table = jnp.asarray(
        tile_table(groups, coefs, back_chunks + [[LOOP_TILES]] * steps, blocks)
    )
    index, cells, offset = index_call(wet_mask)
    offsets = offset.reshape(-1)
    ends = offsets[SUB * lane_tiles : blocks + 1 : SUB * lane_tiles]

    def packed(first_tile, tiles, token, waited=()):
        params = jnp.stack([place[0], first_tile + token])
        *flows, token = pack_call(
            params, offset, index, base_flow, direction, groups, tiles, waited
        )
        return spread_out(flows), token[0, 0]

    def through(flows, token, weight):
        *back, token = friction_call(place + token, flows, coefs, weight)
        return spread_out(back), token[0, 0]

    flows = []
    tile = 0
    token = jnp.int32(0)
    for tiles in chunk_tiles[:-1]:
        flow, token = packed(tile, tiles, token)
        flows.append(flow)
        tile += groups * tiles

    loop_cells = groups * LOOP_TILES * LANES
    beyond = offsets[blocks] + token - fixed * LANES
    loops = jnp.maximum(beyond + loop_cells - 1, 0) // loop_cells

    def more(state):
        done, held = state
        flow, _ = packed(fixed + done * groups * LOOP_TILES, LOOP_TILES, 0)
        back, _ = through([flow], 0, 1)
        held = lax.dynamic_update_slice_in_dim(
            held, jnp.concatenate(back, axis=0)[None], done, 0
        )
        return done + 1, held

    rows = groups * piece_rows(LOOP_TILES, coefs)
    extra = jnp.zeros((steps, rows, LANES), jnp.float32)
    done, extra = lax.while_loop(lambda state: state[0] < loops, more, (jnp.int32(0), extra))

    token = token + jnp.minimum(done, 0)
    flows.append(packed(tile, chunk_tiles[-1], token)[0])
    above, below, slabs = halo(direction, wet_mask, water_depth, flows[0][1:] + flows[-1][:1])
    result, prepared = prepare_call(
        scalars, direction, wet_mask, water_depth, above, below, slabs
    )
    back, token = through(flows[:-1], prepared[0, 0], 1)
    backs = [back]
    back, token = through(flows[-1:], token, LATE_WEIGHT)
    backs.append(back)

    arrays = (wet_mask, drag_factor, cells)
    pieces = []
    back_rows = rows * steps
    back_rows += groups * sum(piece_rows(sum(several), coefs) for several in back_chunks)
    begin = jnp.int32(0)
    tile = 0
    for last, several in enumerate(back_chunks):
        pieces += backs[last]
        tile += groups * sum(several)
        if last:
            end = jnp.int32(row_blocks)
            pieces.append(extra.reshape(-1, LANES))
        else:
            end = jnp.sum((ends <= tile * LANES).astype(jnp.int32))
        first = jnp.stack([begin, place[0], end - begin])
        result = finish_call(
            first, offset, table, scalars, arrays, list(pieces), back_rows, result
        )
        begin = end
    return result


def solution(mesh):
    placed = (
        P(None, "freq", "lat", "lon"),
        P(None, "freq", "lat", "lon"),
        P("lat", "lon"),
        P("lat", "lon"),
        P("lat", "lon"),
    )
    return jax.shard_map(
        local, mesh=mesh, in_specs=placed, out_specs=P(None, "freq", "lat", "lon"), check_vma=False
    )
```

```python
import math

import jax
import jax.numpy as jnp
import ml_dtypes
import numpy as np
from jax import lax
from jax.experimental import pallas as pl
from jax.experimental.pallas import tpu as pltpu
from jax.sharding import PartitionSpec as P

NCON = 16
NTIME = 256
LANES = 128
SUB = 8

LINEAR_DRAG = 0.5
GRAVITY = 1.0
OMEGA_STEP = 0.25
SPEED_SOFT = 0.01
VMEM_BYTES = 48 * 1024 * 1024
CHUNK_SHARES = (16, 50, 31)
SHARE_UNITS = 128
LOOP_TILES = 8
PACK_COST = 16384
AHEAD = 4
LATE_WEIGHT = 2048


def split_table():
    sample = np.arange(NTIME)[:, None]
    harmonic = np.arange(1, NCON + 1)[None, :]
    phase = (sample * harmonic % NTIME) * (2.0 * math.pi / NTIME)
    table = np.stack([np.cos(phase), np.sin(phase)], axis=2).reshape(NTIME, 2 * NCON)
    table = table.astype(np.float32)
    high = table.astype(ml_dtypes.bfloat16)
    low = (table - high.astype(np.float32)).astype(ml_dtypes.bfloat16)
    return high, low


def split_value(value):
    high = value.astype(jnp.bfloat16)
    low = (value - high.astype(jnp.float32)).astype(jnp.bfloat16)
    return high, low


def friction_kernel(groups, coefs, chunk_tiles, place_ref, synth_ref, analyse_ref, *refs):
    parts = len(chunk_tiles)
    tiles = sum(chunk_tiles)
    out_refs, token_ref = refs[groups * parts : -1], refs[-1]
    token_ref[...] = jnp.zeros_like(token_ref)
    columns = 2 * NCON

    def block(flow_refs, first, at, count):
        tile = first + at
        loaded = []
        for source in range(groups):
            several = [flow_refs[source][at + i] for i in range(count)]
            loaded.append(jnp.concatenate(several, axis=1))
        series = []
        for field in range(4):
            rows = slice(field * coefs, (field + 1) * coefs)
            values = jnp.concatenate([part[rows] for part in loaded], axis=0)
            high, low = split_value(values)
            operand = jnp.concatenate([high, low, high], axis=0)
            series.append(
                jnp.dot(synth_ref[0], operand, preferred_element_type=jnp.float32)
            )
        base_east, base_north, step_east, step_north = series
        square = base_east * base_east + base_north * base_north + SPEED_SOFT
        inverse = lax.rsqrt(square)
        speed = square * inverse
        projected = (base_east * step_east + base_north * step_north) * inverse
        forces = (
            speed * step_east + base_east * projected,
            speed * step_north + base_north * projected,
        )
        mean = jnp.sum(speed, axis=0, keepdims=True) * (1.0 / NTIME)
        analysed = []
        for force in forces:
            high, low = split_value(force)
            both = jnp.dot(analyse_ref[0], high, preferred_element_type=jnp.float32)
            rest = jnp.dot(
                analyse_ref[0, :columns, :], low, preferred_element_type=jnp.float32
            )
            analysed.append(both[:columns] + both[columns:] + rest)
        for part in range(count):
            lanes = slice(part * LANES, (part + 1) * LANES)
            for target in range(groups):
                rows = slice(target * coefs, (target + 1) * coefs)
                values = jnp.concatenate(
                    [analysed[0][rows, lanes], analysed[1][rows, lanes]], axis=0
                )
                start = pl.multiple_of((tile + part) * 2 * coefs, SUB)
                out_refs[target][pl.ds(start, 2 * coefs), :] = values
                at = tiles * 2 * coefs + tile + part
                out_refs[target][pl.ds(at, 1), :] = mean[:, lanes]

    first = 0
    for part, here in enumerate(chunk_tiles):
        flow_refs = refs[part * groups : (part + 1) * groups]

        def body(step, carry, flow_refs=flow_refs, first=first):
            block(flow_refs, first, step * 2, 2)
            return carry

        lax.fori_loop(0, here // 2, body, 0)
        if here % 2:
            block(flow_refs, first, here - 1, 1)
        first += here


def placed_tables(groups, coefs):
    high, low = split_table()
    synth, analyse = [], []
    for member in range(groups):
        sources = [(member - step) % groups for step in range(groups)]
        targets = [(member + step) % groups for step in range(groups)]
        source = np.concatenate([np.arange(coefs) + m * coefs for m in sources])
        target = np.concatenate([np.arange(coefs) + m * coefs for m in targets])
        synth.append(np.concatenate([high[:, source], high[:, source], low[:, source]], axis=1))
        both = np.concatenate([high[:, target].T, low[:, target].T], axis=0)
        analyse.append((both.astype(np.float32) * (2.0 / NTIME)).astype(ml_dtypes.bfloat16))
    return np.stack(synth), np.stack(analyse)


def piece_rows(tiles, coefs):
    return tiles * 2 * coefs + -(-tiles // SUB) * SUB


def friction_call(place, flows, coefs, weight):
    groups = len(flows[0])
    chunk_tiles = [chunk[0].shape[0] for chunk in flows]
    tiles = sum(chunk_tiles)
    synth, analyse = placed_tables(groups, coefs)
    cells = groups * tiles * LANES
    out_shape = (piece_rows(tiles, coefs), LANES)
    grid_spec = pltpu.PrefetchScalarGridSpec(
        num_scalar_prefetch=1,
        grid=(1,),
        in_specs=[
            pl.BlockSpec((1,) + synth.shape[1:], lambda i, place: (place[0], 0, 0)),
            pl.BlockSpec((1,) + analyse.shape[1:], lambda i, place: (place[0], 0, 0)),
        ]
        + [
            pl.BlockSpec(block.shape, lambda i, place: (0, 0, 0))
            for chunk in flows
            for block in chunk
        ],
        out_specs=[pl.BlockSpec(out_shape, lambda i, place: (0, 0))] * groups
        + [pl.BlockSpec((SUB, LANES), lambda i, place: (0, 0))],
    )
    return pl.pallas_call(
        lambda *refs: friction_kernel(groups, coefs, chunk_tiles, *refs),
        out_shape=[jax.ShapeDtypeStruct(out_shape, jnp.float32)] * groups
        + [jax.ShapeDtypeStruct((SUB, LANES), jnp.int32)],
        grid_spec=grid_spec,
        compiler_params=pltpu.CompilerParams(vmem_limit_bytes=VMEM_BYTES),
        cost_estimate=pl.CostEstimate(
            flops=cells * NTIME * weight, bytes_accessed=0, transcendentals=0
        ),
        name="friction",
    )(place, jnp.asarray(synth), jnp.asarray(analyse), *[b for chunk in flows for b in chunk])


def index_kernel(wet_ref, index_ref, place_ref, offset_ref, scratch):
    blocks = scratch.shape[0]
    rows, cols = wet_ref.shape
    at = 0
    for row in range(0, rows, SUB):
        for col in range(0, cols, LANES):
            part = wet_ref[row : row + SUB, col : col + LANES]
            scratch[at : at + SUB, :] = jnp.where(part != 0, 1.0, 0.0)
            at += SUB
    wet = scratch[...].astype(jnp.bfloat16)
    earlier = lax.broadcasted_iota(jnp.int32, (LANES, LANES), 0)
    later = lax.broadcasted_iota(jnp.int32, (LANES, LANES), 1)
    before = jnp.where(earlier < later, 1.0, 0.0).astype(jnp.bfloat16)
    ones = jnp.ones((LANES, LANES), jnp.bfloat16)
    rank = jnp.dot(wet, before, preferred_element_type=jnp.float32)
    count = jnp.dot(wet, ones, preferred_element_type=jnp.float32)
    low = lax.broadcasted_iota(jnp.int32, (blocks, blocks), 0)
    high = lax.broadcasted_iota(jnp.int32, (blocks, blocks), 1)
    summing = jnp.where(high < low, 1.0, 0.0).astype(jnp.bfloat16)
    offset = jnp.dot(summing, count.astype(jnp.bfloat16), preferred_element_type=jnp.float32)
    lane = lax.broadcasted_iota(jnp.int32, (blocks, LANES), 1)
    rank = rank.astype(jnp.int32)
    held = jnp.where(scratch[...] > 0.5, lane + LANES * (lane - rank), 0)
    for bit in range(7):
        step = 1 << bit
        coming = pltpu.roll(held, LANES - step, 1)
        moves = (coming >> (7 + bit)) & 1
        stays = 1 - ((held >> (7 + bit)) & 1)
        held = jnp.where(moves == 1, coming, held * stays)
    source = held & (LANES - 1)
    shift = offset.astype(jnp.int32) & (LANES - 1)
    index_ref[...] = jnp.take_along_axis(
        source, (lane - shift) & (LANES - 1), axis=1, mode="promise_in_bounds"
    )
    place_ref[...] = shift + rank
    eye = jnp.where(earlier == later, 1.0, 0.0)
    cubes = offset.reshape(blocks // LANES, LANES, LANES)
    table = jnp.sum(cubes * eye[None], axis=1)
    total = offset[blocks - 1 : blocks] + count[blocks - 1 : blocks]
    offset_ref[: blocks // LANES, :] = table.astype(jnp.int32)
    offset_ref[blocks // LANES : blocks // LANES + 1, :] = total.astype(jnp.int32)


def index_call(wet_mask):
    rows, cols = wet_mask.shape
    blocks = rows * cols // LANES
    table = -(-(blocks // LANES + 1) // SUB) * SUB
    return pl.pallas_call(
        index_kernel,
        out_shape=[
            jax.ShapeDtypeStruct((blocks, LANES), jnp.int32),
            jax.ShapeDtypeStruct((blocks, LANES), jnp.int32),
            jax.ShapeDtypeStruct((table, LANES), jnp.int32),
        ],
        scratch_shapes=[pltpu.VMEM((blocks, LANES), jnp.float32)],
        compiler_params=pltpu.CompilerParams(vmem_limit_bytes=VMEM_BYTES),
        name="index",
    )(wet_mask)


def pack_kernel(groups, coefs, tiles, waited, params_ref, offset_ref, index_ref, base_ref, step_ref, *refs):
    refs = refs[waited:]
    out_refs = refs[:groups]
    token_ref, held, stage, in_sem, out_sem = refs[groups:]
    token_ref[...] = jnp.zeros_like(token_ref)
    lane_tiles = held.shape[1]
    per_block = SUB * lane_tiles
    row_blocks = index_ref.shape[0] // per_block
    count = groups * tiles
    first_tile = params_ref[1]
    low = first_tile * LANES
    high = low + count * LANES

    def offset_of(block):
        return offset_ref[block >> 7, block & (LANES - 1)]

    begin = jnp.int32(0)
    end = jnp.int32(0)
    for block in range(row_blocks):
        begin += (offset_of((block + 1) * per_block) <= low).astype(jnp.int32)
        end += (offset_of(block * per_block) < high).astype(jnp.int32)
    end = jnp.maximum(end, begin)

    def copies(block):
        slot = lax.rem(block, AHEAD)
        rows = pl.ds(pl.multiple_of(block * SUB, SUB), SUB)
        started = []
        for lane_tile in range(lane_tiles):
            lanes = pl.ds(lane_tile * LANES, LANES)
            landing = held.at[slot, lane_tile]
            started.append(
                pltpu.make_async_copy(
                    base_ref.at[:, :, rows, lanes],
                    landing.at[pl.ds(0, 2)],
                    in_sem.at[slot, 2 * lane_tile],
                )
            )
            started.append(
                pltpu.make_async_copy(
                    step_ref.at[pl.ds(1, 2), :, rows, lanes],
                    landing.at[pl.ds(2, 2)],
                    in_sem.at[slot, 2 * lane_tile + 1],
                )
            )
        return started

    for step in range(AHEAD - 1):

        @pl.when(begin + step < end)
        def _():
            for copy in copies(begin + step):
                copy.start()

    lane = lax.broadcasted_iota(jnp.int32, (coefs, LANES), 1)

    def place_of(offset):
        return jnp.clip((offset >> 7) - first_tile + 1, 0, count + 1)

    def body(block, current):
        @pl.when(block + AHEAD - 1 < end)
        def _():
            for copy in copies(block + AHEAD - 1):
                copy.start()

        for copy in copies(block):
            copy.wait()
        slot = lax.rem(block, AHEAD)
        for lane_tile in range(lane_tiles):
            fields = [
                held.at[slot, lane_tile, field].reshape(coefs * SUB, LANES) for field in range(4)
            ]
            start = block * per_block + lane_tile * SUB
            index = index_ref[pl.ds(pl.multiple_of(start, SUB), SUB), :]
            following = offset_of(start)
            for r in range(SUB):
                offset = following
                following = offset_of(start + r + 1)
                shift = offset & (LANES - 1)
                crossing = (following >> 7) > (offset >> 7)
                source = jnp.broadcast_to(index[r : r + 1], (coefs, LANES))
                to = place_of(offset)
                renewed = []
                for field in range(4):
                    got = jnp.take_along_axis(
                        fields[field][pl.ds(r, coefs, stride=SUB), :],
                        source,
                        axis=1,
                        mode="promise_in_bounds",
                    )
                    full = jnp.where(lane >= shift, got, current[field])
                    stage[to, field * coefs : (field + 1) * coefs, :] = full
                    renewed.append(jnp.where(crossing, got, full))
                current = tuple(renewed)
        return current

    zero = jnp.zeros((coefs, LANES), jnp.float32)
    current = lax.fori_loop(begin, end, body, (zero,) * 4)
    last = place_of(offset_of(end * per_block))
    for field in range(4):
        stage[last, field * coefs : (field + 1) * coefs, :] = current[field]
    outs = []
    for step in range(groups):
        member = lax.rem(params_ref[0] + step, groups)
        outs.append(
            pltpu.make_async_copy(
                stage.at[pl.ds(1 + member * tiles, tiles)], out_refs[step], out_sem.at[step]
            )
        )
    for copy in outs:
        copy.start()
    for copy in outs:
        copy.wait()


def pack_call(params, offset, index, base_flow, direction, groups, tiles, waited):
    coefs, _, columns = direction.shape[1:]
    shape = (tiles, 4 * coefs, LANES)
    anywhere = pl.BlockSpec(memory_space=pl.ANY)
    grid_spec = pltpu.PrefetchScalarGridSpec(
        num_scalar_prefetch=2,
        grid=(1,),
        in_specs=[pl.BlockSpec(index.shape, lambda i, p, o: (0, 0))]
        + [anywhere] * (2 + len(waited)),
        out_specs=[anywhere] * groups + [pl.BlockSpec((SUB, LANES), lambda i, p, o: (0, 0))],
        scratch_shapes=[
            pltpu.VMEM((AHEAD, columns // LANES, 4, coefs, SUB, LANES), jnp.float32),
            pltpu.VMEM((groups * tiles + 2, 4 * coefs, LANES), jnp.float32),
            pltpu.SemaphoreType.DMA((AHEAD, 2 * (columns // LANES))),
            pltpu.SemaphoreType.DMA((groups,)),
        ],
    )
    return pl.pallas_call(
        lambda *refs: pack_kernel(groups, coefs, tiles, len(waited), *refs),
        out_shape=[jax.ShapeDtypeStruct(shape, jnp.float32)] * groups
        + [jax.ShapeDtypeStruct((SUB, LANES), jnp.int32)],
        grid_spec=grid_spec,
        compiler_params=pltpu.CompilerParams(vmem_limit_bytes=VMEM_BYTES),
        cost_estimate=pl.CostEstimate(
            flops=0, bytes_accessed=groups * tiles * coefs * PACK_COST, transcendentals=0
        ),
        name="pack",
    )(params, offset, index, base_flow, direction, *waited)


def prepare_kernel(coefs, scalars_ref, *refs):
    (here_ref, prev_ref, next_ref, wet_ref, wet_prev_ref, wet_next_ref, depth_ref, depth_prev_ref,
     above_ref, below_ref, slab_ref, out_ref, token_ref) = refs
    token_ref[...] = jnp.zeros_like(token_ref)
    columns = here_ref.shape[-1]
    row_block = pl.program_id(0)
    at_top = row_block == 0
    at_bottom = row_block == pl.num_programs(0) - 1
    wet = wet_ref[...].astype(jnp.float32)
    wet_prev = wet_prev_ref[SUB - 1 :, :].astype(jnp.float32)
    wet_next = wet_next_ref[:1, :].astype(jnp.float32)
    depth = depth_ref[...]
    depth_prev = depth_prev_ref[SUB - 1 :, :]
    lane = lax.broadcasted_iota(jnp.int32, (SUB, columns), 1)
    sub = lax.broadcasted_iota(jnp.int32, (SUB, columns), 0)
    row = (row_block * SUB + sub).astype(jnp.float32)
    rotation = 0.5 + (row + scalars_ref[0] + 0.5) * scalars_ref[1]

    def wide(slab):
        return jnp.concatenate([slab] * (columns // LANES), axis=1)

    def west(value, slab):
        return jnp.where(lane == 0, wide(slab), pltpu.roll(value, 1, 1))

    def east_of(value, slab):
        return jnp.where(lane == columns - 1, wide(slab), pltpu.roll(value, columns - 1, 1))

    def above(value, edge):
        return jnp.where(sub == 0, edge, pltpu.roll(value, 1, 0))

    def below(value, edge):
        return jnp.where(sub == SUB - 1, edge, pltpu.roll(value, SUB - 1, 0))

    for k in range(coefs // 2):
        angular = scalars_ref[2 + k]
        inverse_angular = 1.0 / (angular + jnp.zeros((SUB, columns), jnp.float32))
        planes = [
            [here_ref[p, 2 * k + part] * wet for p in range(3)] for part in range(2)
        ]
        for part in range(2):
            c = 2 * k + part
            height, east, north = planes[part]
            other = planes[1 - part]
            signed = angular if part == 0 else -angular
            east_flux = depth * east
            north_flux = depth * north
            north_edge = prev_ref[0, c, SUB - 1 :, :] * wet_prev
            flux_edge = jnp.where(at_top, above_ref[1, c : c + 1], north_edge * depth_prev)
            north_edge = jnp.where(at_top, above_ref[0, c : c + 1], north_edge)
            height_edge = jnp.where(
                at_bottom, below_ref[0, c : c + 1], next_ref[0, c, :1, :] * wet_next
            )
            east_edge = jnp.where(
                at_bottom, below_ref[1, c : c + 1], next_ref[1, c, :1, :] * wet_next
            )
            north_up = above(north, north_edge)
            east_down = below(east, east_edge)
            res_height = (
                signed * other[0]
                + east_flux
                - west(east_flux, slab_ref[2, c])
                + north_flux
                - above(north_flux, flux_edge)
            )
            north_mean = 0.25 * (
                north
                + east_of(north, slab_ref[4, c])
                + north_up
                + east_of(north_up, slab_ref[5, c])
            )
            east_mean = 0.25 * (
                east
                + west(east, slab_ref[0, c])
                + east_down
                + west(east_down, slab_ref[1, c])
            )
            res_east = (
                signed * other[1]
                + LINEAR_DRAG * east
                - rotation * north_mean
                + GRAVITY * (east_of(height, slab_ref[3, c]) - height)
            )
            res_north = (
                signed * other[2]
                + LINEAR_DRAG * north
                + rotation * east_mean
                + GRAVITY * (below(height, height_edge) - height)
            )
            if part == 0:
                out_ref[0, c + 1] = res_height * wet * inverse_angular
            else:
                out_ref[0, c - 1] = -res_height * wet * inverse_angular
            out_ref[1, c] = res_east * wet
            out_ref[2, c] = res_north * wet


def prepare_call(scalars, direction, wet_mask, depth, above, below, slabs):
    _, coefs, rows, columns = direction.shape
    last = rows // SUB - 1

    def before(i):
        return jnp.maximum(i - 1, 0)

    def after(i):
        return jnp.minimum(i + 1, last)

    planes = pl.BlockSpec((3, coefs, SUB, columns), lambda i: (0, 0, i, 0))
    flat = (SUB, columns)
    edge = pl.BlockSpec((2, coefs, columns), lambda i: (0, 0, 0))
    return pl.pallas_call(
        lambda *refs: prepare_kernel(coefs, *refs),
        out_shape=[
            jax.ShapeDtypeStruct(direction.shape, jnp.float32),
            jax.ShapeDtypeStruct((SUB, LANES), jnp.int32),
        ],
        grid=(rows // SUB,),
        in_specs=[
            pl.BlockSpec(memory_space=pltpu.SMEM),
            planes,
            pl.BlockSpec((1, coefs, SUB, columns), lambda i: (2, 0, before(i), 0)),
            pl.BlockSpec((2, coefs, SUB, columns), lambda i: (0, 0, after(i), 0)),
            pl.BlockSpec(flat, lambda i: (i, 0)),
            pl.BlockSpec(flat, lambda i: (before(i), 0)),
            pl.BlockSpec(flat, lambda i: (after(i), 0)),
            pl.BlockSpec(flat, lambda i: (i, 0)),
            pl.BlockSpec(flat, lambda i: (before(i), 0)),
            edge,
            edge,
            pl.BlockSpec((6, coefs, SUB, LANES), lambda i: (0, 0, i, 0)),
        ],
        out_specs=[planes, pl.BlockSpec((SUB, LANES), lambda i: (0, 0))],
        compiler_params=pltpu.CompilerParams(vmem_limit_bytes=VMEM_BYTES),
        cost_estimate=pl.CostEstimate(
            flops=rows * columns * coefs, bytes_accessed=0, transcendentals=0
        ),
        name="prepare",
    )(
        scalars, direction, direction, direction, wet_mask, wet_mask, wet_mask, depth, depth,
        above, below, slabs,
    )


def finish_kernel(coefs, lane_tiles, row_block, first_ref, offset_ref, table_ref, scalars_ref, back, spread_ref, refs):
    wet_ref, drag_ref, cell_ref, east_ref, north_ref, east_out, north_out = refs
    columns = lane_tiles * LANES
    wet = wet_ref[...].astype(jnp.float32)
    drag = drag_ref[...]
    sub = lax.broadcasted_iota(jnp.int32, (SUB, columns), 0)
    row = (row_block * SUB + sub).astype(jnp.float32)
    rotation = 0.5 + (row + scalars_ref[0] + 0.5) * scalars_ref[1]

    def gathered(here, after, index, over):
        first = jnp.take_along_axis(here, index, axis=1, mode="promise_in_bounds")
        second = jnp.take_along_axis(after, index, axis=1, mode="promise_in_bounds")
        return jnp.where(over, second, first)

    speed = []
    for lane_tile in range(lane_tiles):
        places = cell_ref[lane_tile * SUB : (lane_tile + 1) * SUB, :]
        turned = spread_ref.at[lane_tile].reshape(2 * coefs * SUB, LANES)
        speeds = [[], []]
        for r in range(SUB):
            at = (row_block * lane_tiles + lane_tile) * SUB + r
            tile = offset_ref[at >> 7, at & (LANES - 1)] >> 7
            found = []
            for which in range(2):
                start = pl.multiple_of(table_ref[first_ref[1] * 2, tile + which], SUB)
                found.append(back[pl.ds(start, 2 * coefs), :])
                start = table_ref[first_ref[1] * 2 + 1, tile + which]
                speeds[which].append(back[pl.ds(start, 1), :])
            place = jnp.broadcast_to(places[r : r + 1], (2 * coefs, LANES))
            turned[pl.ds(r, 2 * coefs, stride=SUB), :] = gathered(
                found[0], found[1], place & (LANES - 1), place >= LANES
            )
        speed.append(
            gathered(
                jnp.concatenate(speeds[0], axis=0),
                jnp.concatenate(speeds[1], axis=0),
                places & (LANES - 1),
                places >= LANES,
            )
        )
    is_wet = wet > 0.5
    friction = [
        jnp.where(
            is_wet,
            jnp.concatenate([spread_ref[n, index] for n in range(lane_tiles)], axis=1) * drag,
            0.0,
        )
        for index in range(2 * coefs)
    ]
    speed = jnp.where(is_wet, jnp.concatenate(speed, axis=1), 0.0)
    real_rate = drag * speed + LINEAR_DRAG
    for k in range(coefs // 2):
        angular = scalars_ref[2 + k]
        cos_at, sin_at = 2 * k, 2 * k + 1
        det_real = real_rate * real_rate - angular * angular + rotation * rotation
        det_imag = 2.0 * real_rate * angular
        inverse_norm = 1.0 / (det_real * det_real + det_imag * det_imag)
        inv_real = det_real * inverse_norm
        inv_imag = -det_imag * inverse_norm
        east_re = east_ref[0, cos_at] + friction[cos_at]
        east_im = -(east_ref[0, sin_at] + friction[sin_at])
        north_re = north_ref[0, cos_at] + friction[coefs + cos_at]
        north_im = -(north_ref[0, sin_at] + friction[coefs + sin_at])
        num_east_re = real_rate * east_re - angular * east_im + rotation * north_re
        num_east_im = real_rate * east_im + angular * east_re + rotation * north_im
        num_north_re = -rotation * east_re + real_rate * north_re - angular * north_im
        num_north_im = -rotation * east_im + real_rate * north_im + angular * north_re
        east_out[0, cos_at] = num_east_re * inv_real - num_east_im * inv_imag
        east_out[0, sin_at] = -(num_east_re * inv_imag + num_east_im * inv_real)
        north_out[0, cos_at] = num_north_re * inv_real - num_north_im * inv_imag
        north_out[0, sin_at] = -(num_north_re * inv_imag + num_north_im * inv_real)


def finish_call(first, offset, table, scalars, arrays, pieces, rows, result):
    _, coefs, _, columns = result.shape
    lane_tiles = columns // LANES

    def kernel(first_ref, offset_ref, table_ref, scalars_ref, *refs):
        array_refs = refs[:3]
        piece_refs = refs[4:-4]
        out_ref, back, spread_ref, sem = refs[-4:]
        first = first_ref[0]
        count = first_ref[2]

        def body(*block_refs):
            finish_kernel(
                coefs, lane_tiles, first + pl.program_id(0), first_ref, offset_ref, table_ref,
                scalars_ref, back, spread_ref, block_refs,
            )

        @pl.when(count > 0)
        def _():
            copies = []
            at = 0
            for n, piece in enumerate(piece_refs):
                rows = piece.shape[0]
                copies.append(
                    pltpu.make_async_copy(piece, back.at[pl.ds(at, rows)], sem.at[n])
                )
                at += rows
            for copy in copies:
                copy.start()
            for copy in copies:
                copy.wait()
            deep = pl.Buffered(3)

            def flat(rows, width):
                return pl.BlockSpec(
                    (rows, width), lambda i: (first + i, 0), pipeline_mode=deep
                )

            def plane(p, mode):
                return pl.BlockSpec(
                    (1, coefs, SUB, columns), lambda i: (p, 0, first + i, 0), pipeline_mode=mode
                )

            pltpu.emit_pipeline(
                body,
                grid=(count,),
                in_specs=[
                    flat(SUB, columns),
                    flat(SUB, columns),
                    flat(SUB * lane_tiles, LANES),
                    plane(1, deep),
                    plane(2, deep),
                ],
                out_specs=[plane(1, None), plane(2, None)],
            )(*array_refs, out_ref, out_ref, out_ref, out_ref)

    anywhere = pl.BlockSpec(memory_space=pl.ANY)
    scalar = pl.BlockSpec(memory_space=pltpu.SMEM)
    operands = [first, offset, table, scalars] + list(arrays) + [result] + pieces
    return pl.pallas_call(
        kernel,
        out_shape=jax.ShapeDtypeStruct(result.shape, jnp.float32),
        in_specs=[scalar] * 4 + [anywhere] * (4 + len(pieces)),
        out_specs=anywhere,
        scratch_shapes=[
            pltpu.VMEM((rows, LANES), jnp.float32),
            pltpu.VMEM((lane_tiles, 2 * coefs, SUB, LANES), jnp.float32),
            pltpu.SemaphoreType.DMA((len(pieces),)),
        ],
        input_output_aliases={7: 0},
        compiler_params=pltpu.CompilerParams(vmem_limit_bytes=VMEM_BYTES),
        cost_estimate=pl.CostEstimate(
            flops=0, bytes_accessed=8 * SUB * columns * coefs * 36, transcendentals=0
        ),
        name="finish",
    )(*operands)


def shifted(block, axis, step, wrap):
    count = lax.axis_size(axis)
    pairs = [
        (i, (i + step) % count) for i in range(count) if wrap or 0 <= i + step < count
    ]
    return lax.ppermute(block, axis, pairs)


def edge_kernel(coefs, east_ref, height_ref, north_ref, last_ref, first_ref, wet_ref, depth_ref, *refs):
    up_ref, down_ref, right_ref, left_ref = refs[-4:]
    rows, columns = wet_ref.shape
    wet = wet_ref[...].astype(jnp.float32)
    end = slice(columns - LANES, columns)
    wet_end = wet[:, end]
    wet_start = wet[:, :LANES]
    depth_end = depth_ref[:, end]
    wet_last = wet[rows - 1 :, :]
    depth_last = depth_ref[rows - 1 :, :]
    for c in range(coefs):
        at = slice(c, c + 1)
        north_row = last_ref[0, c, SUB - 1 :, :] * wet_last
        up_ref[0, at, :] = north_row
        up_ref[1, at, :] = north_row * depth_last
        down_ref[0, at, :] = first_ref[0, c, :1, :] * wet[:1, :]
        down_ref[1, at, :] = first_ref[1, c, :1, :] * wet[:1, :]
        east = east_ref[0, c] * wet_end
        right_ref[0, at, :] = jnp.transpose(east)[LANES - 1 :, :]
        right_ref[1, at, :] = jnp.transpose(east * depth_end)[LANES - 1 :, :]
        left_ref[0, at, :] = jnp.transpose(height_ref[0, c] * wet_start)[:1, :]
        left_ref[1, at, :] = jnp.transpose(north_ref[0, c] * wet_start)[:1, :]


def edge_call(direction, wet_mask, depth, waited):
    _, coefs, rows, columns = direction.shape
    last_tile = columns // LANES - 1
    last_block = rows // SUB - 1
    tall = (1, coefs, rows, LANES)
    whole = pl.BlockSpec((rows, columns), lambda i: (0, 0))
    row_out = (2, coefs, columns)
    col_out = (2, coefs, rows)
    shapes = [row_out, row_out, col_out, col_out]
    return pl.pallas_call(
        lambda *refs: edge_kernel(coefs, *refs),
        out_shape=[jax.ShapeDtypeStruct(shape, jnp.float32) for shape in shapes],
        grid=(1,),
        in_specs=[
            pl.BlockSpec(tall, lambda i: (1, 0, 0, last_tile)),
            pl.BlockSpec(tall, lambda i: (0, 0, 0, 0)),
            pl.BlockSpec(tall, lambda i: (2, 0, 0, 0)),
            pl.BlockSpec((1, coefs, SUB, columns), lambda i: (2, 0, last_block, 0)),
            pl.BlockSpec((2, coefs, SUB, columns), lambda i: (0, 0, 0, 0)),
            whole,
            whole,
        ]
        + [pl.BlockSpec(memory_space=pl.ANY)] * len(waited),
        out_specs=[pl.BlockSpec(shape, lambda i: (0, 0, 0)) for shape in shapes],
        compiler_params=pltpu.CompilerParams(vmem_limit_bytes=VMEM_BYTES),
        cost_estimate=pl.CostEstimate(
            flops=rows * columns, bytes_accessed=0, transcendentals=0
        ),
        name="edges",
    )(direction, direction, direction, direction, direction, wet_mask, depth, *waited)


def halo(direction, wet_mask, depth, waited):
    up, down, right, left = edge_call(direction, wet_mask, depth, waited)
    above = shifted(up, "lat", 1, False)
    below = shifted(down, "lat", -1, False)
    east_below = jnp.concatenate([right[0, :, 1:], below[1, :, -1:]], axis=1)
    north_above = jnp.concatenate([above[0, :, :1], left[1, :, :-1]], axis=1)
    to_right = jnp.stack([right[0], east_below, right[1]])
    to_left = jnp.stack([left[0], left[1], north_above])
    cols = jnp.concatenate(
        [shifted(to_right, "lon", 1, True), shifted(to_left, "lon", -1, True)], axis=0
    )
    slabs = jnp.broadcast_to(cols[:, :, :, None], cols.shape + (LANES,))
    return above, below, slabs


def spread_out(blocks):
    return [
        block if step == 0 else shifted(block, "freq", step, True)
        for step, block in enumerate(blocks)
    ]


def tile_table(groups, coefs, back_chunks, blocks):
    table = np.zeros((2 * groups, blocks + LANES), np.int32)
    for member in range(groups):
        tile = 0
        row = 0
        for chunk_tiles in back_chunks:
            together = sum(chunk_tiles)
            before = 0
            for tiles in chunk_tiles:
                for band in range(groups):
                    start = row + (member - band) % groups * piece_rows(together, coefs)
                    for i in range(before, before + tiles):
                        if tile < blocks:
                            table[2 * member, tile] = start + i * 2 * coefs
                            table[2 * member + 1, tile] = start + together * 2 * coefs + i
                        tile += 1
                before += tiles
            row += groups * piece_rows(together, coefs)
    return table


def local(direction, base_flow, water_depth, drag_factor, wet_mask):
    coefs, tile_rows, tile_cols = direction.shape[1:]
    groups = lax.axis_size("freq")
    member = lax.axis_index("freq")
    lat_place = lax.axis_index("lat")
    total_rows = tile_rows * lax.axis_size("lat")
    lane_tiles = tile_cols // LANES
    angular = OMEGA_STEP * (
        member * (coefs // 2) + jnp.arange(coefs // 2, dtype=jnp.int32) + 1
    ).astype(jnp.float32)
    row_start = (lat_place * tile_rows).astype(jnp.float32)
    scalars = jnp.concatenate(
        [jnp.stack([row_start, jnp.float32(1.0 / total_rows)]), angular]
    )
    place = jnp.reshape(member, (1,)).astype(jnp.int32)
    blocks = tile_rows * lane_tiles
    row_blocks = tile_rows // SUB
    chunk_tiles = [share * blocks // (groups * SHARE_UNITS) for share in CHUNK_SHARES]
    fixed = groups * sum(chunk_tiles)
    steps = -(-(blocks - fixed) // (groups * LOOP_TILES))
    back_chunks = [chunk_tiles[:-1], chunk_tiles[-1:]]
    table = jnp.asarray(
        tile_table(groups, coefs, back_chunks + [[LOOP_TILES]] * steps, blocks)
    )
    index, cells, offset = index_call(wet_mask)
    offsets = offset.reshape(-1)
    ends = offsets[SUB * lane_tiles : blocks + 1 : SUB * lane_tiles]

    def packed(first_tile, tiles, token, waited=()):
        params = jnp.stack([place[0], first_tile + token])
        *flows, token = pack_call(
            params, offset, index, base_flow, direction, groups, tiles, waited
        )
        return spread_out(flows), token[0, 0]

    def through(flows, token, weight):
        *back, token = friction_call(place + token, flows, coefs, weight)
        return spread_out(back), token[0, 0]

    flows = []
    tile = 0
    token = jnp.int32(0)
    for tiles in chunk_tiles[:-1]:
        flow, token = packed(tile, tiles, token)
        flows.append(flow)
        tile += groups * tiles

    loop_cells = groups * LOOP_TILES * LANES
    beyond = offsets[blocks] + token - fixed * LANES
    loops = jnp.maximum(beyond + loop_cells - 1, 0) // loop_cells

    def more(state):
        done, held = state
        flow, _ = packed(fixed + done * groups * LOOP_TILES, LOOP_TILES, 0)
        back, _ = through([flow], 0, 1)
        held = lax.dynamic_update_slice_in_dim(
            held, jnp.concatenate(back, axis=0)[None], done, 0
        )
        return done + 1, held

    rows = groups * piece_rows(LOOP_TILES, coefs)
    extra = jnp.zeros((steps, rows, LANES), jnp.float32)
    done, extra = lax.while_loop(lambda state: state[0] < loops, more, (jnp.int32(0), extra))

    token = token + jnp.minimum(done, 0)
    flows.append(packed(tile, chunk_tiles[-1], token)[0])
    above, below, slabs = halo(direction, wet_mask, water_depth, flows[0][1:] + flows[-1][:1])
    result, prepared = prepare_call(
        scalars, direction, wet_mask, water_depth, above, below, slabs
    )
    back, token = through(flows[:-1], prepared[0, 0], 1)
    backs = [back]
    back, token = through(flows[-1:], token, LATE_WEIGHT)
    backs.append(back)

    arrays = (wet_mask, drag_factor, cells)
    pieces = []
    back_rows = rows * steps
    back_rows += groups * sum(piece_rows(sum(several), coefs) for several in back_chunks)
    begin = jnp.int32(0)
    tile = 0
    for last, several in enumerate(back_chunks):
        pieces += backs[last]
        tile += groups * sum(several)
        if last:
            end = jnp.int32(row_blocks)
            pieces.append(extra.reshape(-1, LANES))
        else:
            end = jnp.sum((ends <= tile * LANES).astype(jnp.int32))
        first = jnp.stack([begin, place[0], end - begin])
        result = finish_call(
            first, offset, table, scalars, arrays, list(pieces), back_rows, result
        )
        begin = end
    return result


def solution(mesh):
    placed = (
        P(None, "freq", "lat", "lon"),
        P(None, "freq", "lat", "lon"),
        P("lat", "lon"),
        P("lat", "lon"),
        P("lat", "lon"),
    )
    return jax.shard_map(
        local, mesh=mesh, in_specs=placed, out_specs=P(None, "freq", "lat", "lon"), check_vma=False
    )
```

```python
import math

import jax
import jax.numpy as jnp
import ml_dtypes
import numpy as np
from jax import lax
from jax.experimental import pallas as pl
from jax.experimental.pallas import tpu as pltpu
from jax.sharding import PartitionSpec as P

NCON = 16
NTIME = 256
LANES = 128
SUB = 8

LINEAR_DRAG = 0.5
GRAVITY = 1.0
OMEGA_STEP = 0.25
SPEED_SOFT = 0.01
VMEM_BYTES = 48 * 1024 * 1024
CHUNK_SHARES = (12, 55, 30)
SHARE_UNITS = 128
LOOP_TILES = 8
PACK_COST = 16384
AHEAD = 4
LATE_WEIGHT = 2048


def split_table():
    sample = np.arange(NTIME)[:, None]
    harmonic = np.arange(1, NCON + 1)[None, :]
    phase = (sample * harmonic % NTIME) * (2.0 * math.pi / NTIME)
    table = np.stack([np.cos(phase), np.sin(phase)], axis=2).reshape(NTIME, 2 * NCON)
    table = table.astype(np.float32)
    high = table.astype(ml_dtypes.bfloat16)
    low = (table - high.astype(np.float32)).astype(ml_dtypes.bfloat16)
    return high, low


def split_value(value):
    high = value.astype(jnp.bfloat16)
    low = (value - high.astype(jnp.float32)).astype(jnp.bfloat16)
    return high, low


def friction_kernel(groups, coefs, chunk_tiles, place_ref, synth_ref, analyse_ref, *refs):
    parts = len(chunk_tiles)
    tiles = sum(chunk_tiles)
    out_refs, token_ref = refs[groups * parts : -1], refs[-1]
    token_ref[...] = jnp.zeros_like(token_ref)
    columns = 2 * NCON

    def block(flow_refs, first, at, count):
        tile = first + at
        loaded = []
        for source in range(groups):
            several = [flow_refs[source][at + i] for i in range(count)]
            loaded.append(jnp.concatenate(several, axis=1))
        series = []
        for field in range(4):
            rows = slice(field * coefs, (field + 1) * coefs)
            values = jnp.concatenate([part[rows] for part in loaded], axis=0)
            high, low = split_value(values)
            operand = jnp.concatenate([high, low, high], axis=0)
            series.append(
                jnp.dot(synth_ref[0], operand, preferred_element_type=jnp.float32)
            )
        base_east, base_north, step_east, step_north = series
        square = base_east * base_east + base_north * base_north + SPEED_SOFT
        inverse = lax.rsqrt(square)
        speed = square * inverse
        projected = (base_east * step_east + base_north * step_north) * inverse
        forces = (
            speed * step_east + base_east * projected,
            speed * step_north + base_north * projected,
        )
        mean = jnp.sum(speed, axis=0, keepdims=True) * (1.0 / NTIME)
        analysed = []
        for force in forces:
            high, low = split_value(force)
            both = jnp.dot(analyse_ref[0], high, preferred_element_type=jnp.float32)
            rest = jnp.dot(
                analyse_ref[0, :columns, :], low, preferred_element_type=jnp.float32
            )
            analysed.append(both[:columns] + both[columns:] + rest)
        for part in range(count):
            lanes = slice(part * LANES, (part + 1) * LANES)
            for target in range(groups):
                rows = slice(target * coefs, (target + 1) * coefs)
                values = jnp.concatenate(
                    [analysed[0][rows, lanes], analysed[1][rows, lanes]], axis=0
                )
                start = pl.multiple_of((tile + part) * 2 * coefs, SUB)
                out_refs[target][pl.ds(start, 2 * coefs), :] = values
                at = tiles * 2 * coefs + tile + part
                out_refs[target][pl.ds(at, 1), :] = mean[:, lanes]

    first = 0
    for part, here in enumerate(chunk_tiles):
        flow_refs = refs[part * groups : (part + 1) * groups]

        def body(step, carry, flow_refs=flow_refs, first=first):
            block(flow_refs, first, step * 2, 2)
            return carry

        lax.fori_loop(0, here // 2, body, 0)
        if here % 2:
            block(flow_refs, first, here - 1, 1)
        first += here


def placed_tables(groups, coefs):
    high, low = split_table()
    synth, analyse = [], []
    for member in range(groups):
        sources = [(member - step) % groups for step in range(groups)]
        targets = [(member + step) % groups for step in range(groups)]
        source = np.concatenate([np.arange(coefs) + m * coefs for m in sources])
        target = np.concatenate([np.arange(coefs) + m * coefs for m in targets])
        synth.append(np.concatenate([high[:, source], high[:, source], low[:, source]], axis=1))
        both = np.concatenate([high[:, target].T, low[:, target].T], axis=0)
        analyse.append((both.astype(np.float32) * (2.0 / NTIME)).astype(ml_dtypes.bfloat16))
    return np.stack(synth), np.stack(analyse)


def piece_rows(tiles, coefs):
    return tiles * 2 * coefs + -(-tiles // SUB) * SUB


def friction_call(place, flows, coefs, weight):
    groups = len(flows[0])
    chunk_tiles = [chunk[0].shape[0] for chunk in flows]
    tiles = sum(chunk_tiles)
    synth, analyse = placed_tables(groups, coefs)
    cells = groups * tiles * LANES
    out_shape = (piece_rows(tiles, coefs), LANES)
    grid_spec = pltpu.PrefetchScalarGridSpec(
        num_scalar_prefetch=1,
        grid=(1,),
        in_specs=[
            pl.BlockSpec((1,) + synth.shape[1:], lambda i, place: (place[0], 0, 0)),
            pl.BlockSpec((1,) + analyse.shape[1:], lambda i, place: (place[0], 0, 0)),
        ]
        + [
            pl.BlockSpec(block.shape, lambda i, place: (0, 0, 0))
            for chunk in flows
            for block in chunk
        ],
        out_specs=[pl.BlockSpec(out_shape, lambda i, place: (0, 0))] * groups
        + [pl.BlockSpec((SUB, LANES), lambda i, place: (0, 0))],
    )
    return pl.pallas_call(
        lambda *refs: friction_kernel(groups, coefs, chunk_tiles, *refs),
        out_shape=[jax.ShapeDtypeStruct(out_shape, jnp.float32)] * groups
        + [jax.ShapeDtypeStruct((SUB, LANES), jnp.int32)],
        grid_spec=grid_spec,
        compiler_params=pltpu.CompilerParams(vmem_limit_bytes=VMEM_BYTES),
        cost_estimate=pl.CostEstimate(
            flops=cells * NTIME * weight, bytes_accessed=0, transcendentals=0
        ),
        name="friction",
    )(place, jnp.asarray(synth), jnp.asarray(analyse), *[b for chunk in flows for b in chunk])


def index_kernel(wet_ref, index_ref, place_ref, offset_ref, scratch):
    blocks = scratch.shape[0]
    rows, cols = wet_ref.shape
    at = 0
    for row in range(0, rows, SUB):
        for col in range(0, cols, LANES):
            part = wet_ref[row : row + SUB, col : col + LANES]
            scratch[at : at + SUB, :] = jnp.where(part != 0, 1.0, 0.0)
            at += SUB
    wet = scratch[...].astype(jnp.bfloat16)
    earlier = lax.broadcasted_iota(jnp.int32, (LANES, LANES), 0)
    later = lax.broadcasted_iota(jnp.int32, (LANES, LANES), 1)
    before = jnp.where(earlier < later, 1.0, 0.0).astype(jnp.bfloat16)
    ones = jnp.ones((LANES, LANES), jnp.bfloat16)
    rank = jnp.dot(wet, before, preferred_element_type=jnp.float32)
    count = jnp.dot(wet, ones, preferred_element_type=jnp.float32)
    low = lax.broadcasted_iota(jnp.int32, (blocks, blocks), 0)
    high = lax.broadcasted_iota(jnp.int32, (blocks, blocks), 1)
    summing = jnp.where(high < low, 1.0, 0.0).astype(jnp.bfloat16)
    offset = jnp.dot(summing, count.astype(jnp.bfloat16), preferred_element_type=jnp.float32)
    lane = lax.broadcasted_iota(jnp.int32, (blocks, LANES), 1)
    rank = rank.astype(jnp.int32)
    held = jnp.where(scratch[...] > 0.5, lane + LANES * (lane - rank), 0)
    for bit in range(7):
        step = 1 << bit
        coming = pltpu.roll(held, LANES - step, 1)
        moves = (coming >> (7 + bit)) & 1
        stays = 1 - ((held >> (7 + bit)) & 1)
        held = jnp.where(moves == 1, coming, held * stays)
    source = held & (LANES - 1)
    shift = offset.astype(jnp.int32) & (LANES - 1)
    index_ref[...] = jnp.take_along_axis(
        source, (lane - shift) & (LANES - 1), axis=1, mode="promise_in_bounds"
    )
    place_ref[...] = shift + rank
    eye = jnp.where(earlier == later, 1.0, 0.0)
    cubes = offset.reshape(blocks // LANES, LANES, LANES)
    table = jnp.sum(cubes * eye[None], axis=1)
    total = offset[blocks - 1 : blocks] + count[blocks - 1 : blocks]
    offset_ref[: blocks // LANES, :] = table.astype(jnp.int32)
    offset_ref[blocks // LANES : blocks // LANES + 1, :] = total.astype(jnp.int32)


def index_call(wet_mask):
    rows, cols = wet_mask.shape
    blocks = rows * cols // LANES
    table = -(-(blocks // LANES + 1) // SUB) * SUB
    return pl.pallas_call(
        index_kernel,
        out_shape=[
            jax.ShapeDtypeStruct((blocks, LANES), jnp.int32),
            jax.ShapeDtypeStruct((blocks, LANES), jnp.int32),
            jax.ShapeDtypeStruct((table, LANES), jnp.int32),
        ],
        scratch_shapes=[pltpu.VMEM((blocks, LANES), jnp.float32)],
        compiler_params=pltpu.CompilerParams(vmem_limit_bytes=VMEM_BYTES),
        name="index",
    )(wet_mask)


def pack_kernel(groups, coefs, tiles, waited, params_ref, offset_ref, index_ref, base_ref, step_ref, *refs):
    refs = refs[waited:]
    out_refs = refs[:groups]
    token_ref, held, stage, in_sem, out_sem = refs[groups:]
    token_ref[...] = jnp.zeros_like(token_ref)
    lane_tiles = held.shape[1]
    per_block = SUB * lane_tiles
    row_blocks = index_ref.shape[0] // per_block
    count = groups * tiles
    first_tile = params_ref[1]
    low = first_tile * LANES
    high = low + count * LANES

    def offset_of(block):
        return offset_ref[block >> 7, block & (LANES - 1)]

    begin = jnp.int32(0)
    end = jnp.int32(0)
    for block in range(row_blocks):
        begin += (offset_of((block + 1) * per_block) <= low).astype(jnp.int32)
        end += (offset_of(block * per_block) < high).astype(jnp.int32)
    end = jnp.maximum(end, begin)

    def copies(block):
        slot = lax.rem(block, AHEAD)
        rows = pl.ds(pl.multiple_of(block * SUB, SUB), SUB)
        started = []
        for lane_tile in range(lane_tiles):
            lanes = pl.ds(lane_tile * LANES, LANES)
            landing = held.at[slot, lane_tile]
            started.append(
                pltpu.make_async_copy(
                    base_ref.at[:, :, rows, lanes],
                    landing.at[pl.ds(0, 2)],
                    in_sem.at[slot, 2 * lane_tile],
                )
            )
            started.append(
                pltpu.make_async_copy(
                    step_ref.at[pl.ds(1, 2), :, rows, lanes],
                    landing.at[pl.ds(2, 2)],
                    in_sem.at[slot, 2 * lane_tile + 1],
                )
            )
        return started

    for step in range(AHEAD - 1):

        @pl.when(begin + step < end)
        def _():
            for copy in copies(begin + step):
                copy.start()

    lane = lax.broadcasted_iota(jnp.int32, (coefs, LANES), 1)

    def place_of(offset):
        return jnp.clip((offset >> 7) - first_tile + 1, 0, count + 1)

    def body(block, current):
        @pl.when(block + AHEAD - 1 < end)
        def _():
            for copy in copies(block + AHEAD - 1):
                copy.start()

        for copy in copies(block):
            copy.wait()
        slot = lax.rem(block, AHEAD)
        for lane_tile in range(lane_tiles):
            fields = [
                held.at[slot, lane_tile, field].reshape(coefs * SUB, LANES) for field in range(4)
            ]
            start = block * per_block + lane_tile * SUB
            index = index_ref[pl.ds(pl.multiple_of(start, SUB), SUB), :]
            following = offset_of(start)
            for r in range(SUB):
                offset = following
                following = offset_of(start + r + 1)
                shift = offset & (LANES - 1)
                crossing = (following >> 7) > (offset >> 7)
                source = jnp.broadcast_to(index[r : r + 1], (coefs, LANES))
                to = place_of(offset)
                renewed = []
                for field in range(4):
                    got = jnp.take_along_axis(
                        fields[field][pl.ds(r, coefs, stride=SUB), :],
                        source,
                        axis=1,
                        mode="promise_in_bounds",
                    )
                    full = jnp.where(lane >= shift, got, current[field])
                    stage[to, field * coefs : (field + 1) * coefs, :] = full
                    renewed.append(jnp.where(crossing, got, full))
                current = tuple(renewed)
        return current

    zero = jnp.zeros((coefs, LANES), jnp.float32)
    current = lax.fori_loop(begin, end, body, (zero,) * 4)
    last = place_of(offset_of(end * per_block))
    for field in range(4):
        stage[last, field * coefs : (field + 1) * coefs, :] = current[field]
    outs = []
    for step in range(groups):
        member = lax.rem(params_ref[0] + step, groups)
        outs.append(
            pltpu.make_async_copy(
                stage.at[pl.ds(1 + member * tiles, tiles)], out_refs[step], out_sem.at[step]
            )
        )
    for copy in outs:
        copy.start()
    for copy in outs:
        copy.wait()


def pack_call(params, offset, index, base_flow, direction, groups, tiles, waited):
    coefs, _, columns = direction.shape[1:]
    shape = (tiles, 4 * coefs, LANES)
    anywhere = pl.BlockSpec(memory_space=pl.ANY)
    grid_spec = pltpu.PrefetchScalarGridSpec(
        num_scalar_prefetch=2,
        grid=(1,),
        in_specs=[pl.BlockSpec(index.shape, lambda i, p, o: (0, 0))]
        + [anywhere] * (2 + len(waited)),
        out_specs=[anywhere] * groups + [pl.BlockSpec((SUB, LANES), lambda i, p, o: (0, 0))],
        scratch_shapes=[
            pltpu.VMEM((AHEAD, columns // LANES, 4, coefs, SUB, LANES), jnp.float32),
            pltpu.VMEM((groups * tiles + 2, 4 * coefs, LANES), jnp.float32),
            pltpu.SemaphoreType.DMA((AHEAD, 2 * (columns // LANES))),
            pltpu.SemaphoreType.DMA((groups,)),
        ],
    )
    return pl.pallas_call(
        lambda *refs: pack_kernel(groups, coefs, tiles, len(waited), *refs),
        out_shape=[jax.ShapeDtypeStruct(shape, jnp.float32)] * groups
        + [jax.ShapeDtypeStruct((SUB, LANES), jnp.int32)],
        grid_spec=grid_spec,
        compiler_params=pltpu.CompilerParams(vmem_limit_bytes=VMEM_BYTES),
        cost_estimate=pl.CostEstimate(
            flops=0, bytes_accessed=groups * tiles * coefs * PACK_COST, transcendentals=0
        ),
        name="pack",
    )(params, offset, index, base_flow, direction, *waited)


def prepare_kernel(coefs, scalars_ref, *refs):
    (here_ref, prev_ref, next_ref, wet_ref, wet_prev_ref, wet_next_ref, depth_ref, depth_prev_ref,
     above_ref, below_ref, slab_ref, out_ref, token_ref) = refs
    token_ref[...] = jnp.zeros_like(token_ref)
    columns = here_ref.shape[-1]
    row_block = pl.program_id(0)
    at_top = row_block == 0
    at_bottom = row_block == pl.num_programs(0) - 1
    wet = wet_ref[...].astype(jnp.float32)
    wet_prev = wet_prev_ref[SUB - 1 :, :].astype(jnp.float32)
    wet_next = wet_next_ref[:1, :].astype(jnp.float32)
    depth = depth_ref[...]
    depth_prev = depth_prev_ref[SUB - 1 :, :]
    lane = lax.broadcasted_iota(jnp.int32, (SUB, columns), 1)
    sub = lax.broadcasted_iota(jnp.int32, (SUB, columns), 0)
    row = (row_block * SUB + sub).astype(jnp.float32)
    rotation = 0.5 + (row + scalars_ref[0] + 0.5) * scalars_ref[1]

    def wide(slab):
        return jnp.concatenate([slab] * (columns // LANES), axis=1)

    def west(value, slab):
        return jnp.where(lane == 0, wide(slab), pltpu.roll(value, 1, 1))

    def east_of(value, slab):
        return jnp.where(lane == columns - 1, wide(slab), pltpu.roll(value, columns - 1, 1))

    def above(value, edge):
        return jnp.where(sub == 0, edge, pltpu.roll(value, 1, 0))

    def below(value, edge):
        return jnp.where(sub == SUB - 1, edge, pltpu.roll(value, SUB - 1, 0))

    for k in range(coefs // 2):
        angular = scalars_ref[2 + k]
        inverse_angular = 1.0 / (angular + jnp.zeros((SUB, columns), jnp.float32))
        planes = [
            [here_ref[p, 2 * k + part] * wet for p in range(3)] for part in range(2)
        ]
        for part in range(2):
            c = 2 * k + part
            height, east, north = planes[part]
            other = planes[1 - part]
            signed = angular if part == 0 else -angular
            east_flux = depth * east
            north_flux = depth * north
            north_edge = prev_ref[0, c, SUB - 1 :, :] * wet_prev
            flux_edge = jnp.where(at_top, above_ref[1, c : c + 1], north_edge * depth_prev)
            north_edge = jnp.where(at_top, above_ref[0, c : c + 1], north_edge)
            height_edge = jnp.where(
                at_bottom, below_ref[0, c : c + 1], next_ref[0, c, :1, :] * wet_next
            )
            east_edge = jnp.where(
                at_bottom, below_ref[1, c : c + 1], next_ref[1, c, :1, :] * wet_next
            )
            north_up = above(north, north_edge)
            east_down = below(east, east_edge)
            res_height = (
                signed * other[0]
                + east_flux
                - west(east_flux, slab_ref[2, c])
                + north_flux
                - above(north_flux, flux_edge)
            )
            north_mean = 0.25 * (
                north
                + east_of(north, slab_ref[4, c])
                + north_up
                + east_of(north_up, slab_ref[5, c])
            )
            east_mean = 0.25 * (
                east
                + west(east, slab_ref[0, c])
                + east_down
                + west(east_down, slab_ref[1, c])
            )
            res_east = (
                signed * other[1]
                + LINEAR_DRAG * east
                - rotation * north_mean
                + GRAVITY * (east_of(height, slab_ref[3, c]) - height)
            )
            res_north = (
                signed * other[2]
                + LINEAR_DRAG * north
                + rotation * east_mean
                + GRAVITY * (below(height, height_edge) - height)
            )
            if part == 0:
                out_ref[0, c + 1] = res_height * wet * inverse_angular
            else:
                out_ref[0, c - 1] = -res_height * wet * inverse_angular
            out_ref[1, c] = res_east * wet
            out_ref[2, c] = res_north * wet


def prepare_call(scalars, direction, wet_mask, depth, above, below, slabs):
    _, coefs, rows, columns = direction.shape
    last = rows // SUB - 1

    def before(i):
        return jnp.maximum(i - 1, 0)

    def after(i):
        return jnp.minimum(i + 1, last)

    planes = pl.BlockSpec((3, coefs, SUB, columns), lambda i: (0, 0, i, 0))
    flat = (SUB, columns)
    edge = pl.BlockSpec((2, coefs, columns), lambda i: (0, 0, 0))
    return pl.pallas_call(
        lambda *refs: prepare_kernel(coefs, *refs),
        out_shape=[
            jax.ShapeDtypeStruct(direction.shape, jnp.float32),
            jax.ShapeDtypeStruct((SUB, LANES), jnp.int32),
        ],
        grid=(rows // SUB,),
        in_specs=[
            pl.BlockSpec(memory_space=pltpu.SMEM),
            planes,
            pl.BlockSpec((1, coefs, SUB, columns), lambda i: (2, 0, before(i), 0)),
            pl.BlockSpec((2, coefs, SUB, columns), lambda i: (0, 0, after(i), 0)),
            pl.BlockSpec(flat, lambda i: (i, 0)),
            pl.BlockSpec(flat, lambda i: (before(i), 0)),
            pl.BlockSpec(flat, lambda i: (after(i), 0)),
            pl.BlockSpec(flat, lambda i: (i, 0)),
            pl.BlockSpec(flat, lambda i: (before(i), 0)),
            edge,
            edge,
            pl.BlockSpec((6, coefs, SUB, LANES), lambda i: (0, 0, i, 0)),
        ],
        out_specs=[planes, pl.BlockSpec((SUB, LANES), lambda i: (0, 0))],
        compiler_params=pltpu.CompilerParams(vmem_limit_bytes=VMEM_BYTES),
        cost_estimate=pl.CostEstimate(
            flops=rows * columns * coefs, bytes_accessed=0, transcendentals=0
        ),
        name="prepare",
    )(
        scalars, direction, direction, direction, wet_mask, wet_mask, wet_mask, depth, depth,
        above, below, slabs,
    )


def finish_kernel(coefs, lane_tiles, row_block, first_ref, offset_ref, table_ref, scalars_ref, back, spread_ref, refs):
    wet_ref, drag_ref, cell_ref, east_ref, north_ref, east_out, north_out = refs
    columns = lane_tiles * LANES
    wet = wet_ref[...].astype(jnp.float32)
    drag = drag_ref[...]
    sub = lax.broadcasted_iota(jnp.int32, (SUB, columns), 0)
    row = (row_block * SUB + sub).astype(jnp.float32)
    rotation = 0.5 + (row + scalars_ref[0] + 0.5) * scalars_ref[1]

    def gathered(here, after, index, over):
        first = jnp.take_along_axis(here, index, axis=1, mode="promise_in_bounds")
        second = jnp.take_along_axis(after, index, axis=1, mode="promise_in_bounds")
        return jnp.where(over, second, first)

    speed = []
    for lane_tile in range(lane_tiles):
        places = cell_ref[lane_tile * SUB : (lane_tile + 1) * SUB, :]
        turned = spread_ref.at[lane_tile].reshape(2 * coefs * SUB, LANES)
        speeds = [[], []]
        for r in range(SUB):
            at = (row_block * lane_tiles + lane_tile) * SUB + r
            tile = offset_ref[at >> 7, at & (LANES - 1)] >> 7
            found = []
            for which in range(2):
                start = pl.multiple_of(table_ref[first_ref[1] * 2, tile + which], SUB)
                found.append(back[pl.ds(start, 2 * coefs), :])
                start = table_ref[first_ref[1] * 2 + 1, tile + which]
                speeds[which].append(back[pl.ds(start, 1), :])
            place = jnp.broadcast_to(places[r : r + 1], (2 * coefs, LANES))
            turned[pl.ds(r, 2 * coefs, stride=SUB), :] = gathered(
                found[0], found[1], place & (LANES - 1), place >= LANES
            )
        speed.append(
            gathered(
                jnp.concatenate(speeds[0], axis=0),
                jnp.concatenate(speeds[1], axis=0),
                places & (LANES - 1),
                places >= LANES,
            )
        )
    is_wet = wet > 0.5
    friction = [
        jnp.where(
            is_wet,
            jnp.concatenate([spread_ref[n, index] for n in range(lane_tiles)], axis=1) * drag,
            0.0,
        )
        for index in range(2 * coefs)
    ]
    speed = jnp.where(is_wet, jnp.concatenate(speed, axis=1), 0.0)
    real_rate = drag * speed + LINEAR_DRAG
    for k in range(coefs // 2):
        angular = scalars_ref[2 + k]
        cos_at, sin_at = 2 * k, 2 * k + 1
        det_real = real_rate * real_rate - angular * angular + rotation * rotation
        det_imag = 2.0 * real_rate * angular
        inverse_norm = 1.0 / (det_real * det_real + det_imag * det_imag)
        inv_real = det_real * inverse_norm
        inv_imag = -det_imag * inverse_norm
        east_re = east_ref[0, cos_at] + friction[cos_at]
        east_im = -(east_ref[0, sin_at] + friction[sin_at])
        north_re = north_ref[0, cos_at] + friction[coefs + cos_at]
        north_im = -(north_ref[0, sin_at] + friction[coefs + sin_at])
        num_east_re = real_rate * east_re - angular * east_im + rotation * north_re
        num_east_im = real_rate * east_im + angular * east_re + rotation * north_im
        num_north_re = -rotation * east_re + real_rate * north_re - angular * north_im
        num_north_im = -rotation * east_im + real_rate * north_im + angular * north_re
        east_out[0, cos_at] = num_east_re * inv_real - num_east_im * inv_imag
        east_out[0, sin_at] = -(num_east_re * inv_imag + num_east_im * inv_real)
        north_out[0, cos_at] = num_north_re * inv_real - num_north_im * inv_imag
        north_out[0, sin_at] = -(num_north_re * inv_imag + num_north_im * inv_real)


def finish_call(first, offset, table, scalars, arrays, pieces, rows, result, groups, early):
    _, coefs, _, columns = result.shape
    lane_tiles = columns // LANES

    def kernel(first_ref, offset_ref, table_ref, scalars_ref, *refs):
        array_refs = refs[:3]
        piece_refs = refs[4:-4]
        out_ref, back, spread_ref, sem = refs[-4:]
        first = first_ref[0]
        count = first_ref[2]

        @pl.when(count > 0)
        def _():
            at = 0
            copies = []
            for n, piece in enumerate(piece_refs):
                rows = piece.shape[0]
                copy = pltpu.make_async_copy(piece, back.at[pl.ds(at, rows)], sem.at[n])
                needed = True
                if n < early[0]:
                    source = lax.rem(first_ref[1] + groups - n % groups, groups)
                    needed = source >= groups - early[1]
                elif n >= early[0] + groups:
                    needed = first_ref[3] > 0
                copies.append((copy, needed))
                at += rows

            def each(act):
                for copy, needed in copies:
                    if needed is True:
                        act(copy)
                    else:
                        pl.when(needed)(lambda copy=copy: act(copy))

            each(lambda copy: copy.start())

            def body(*block_refs):
                @pl.when(pl.program_id(0) == 0)
                def _():
                    each(lambda copy: copy.wait())

                finish_kernel(
                    coefs, lane_tiles, first + pl.program_id(0), first_ref, offset_ref,
                    table_ref, scalars_ref, back, spread_ref, block_refs,
                )

            deep = pl.Buffered(3)

            def flat(rows, width):
                return pl.BlockSpec(
                    (rows, width), lambda i: (first + i, 0), pipeline_mode=deep
                )

            def plane(p, mode):
                return pl.BlockSpec(
                    (1, coefs, SUB, columns), lambda i: (p, 0, first + i, 0), pipeline_mode=mode
                )

            pltpu.emit_pipeline(
                body,
                grid=(count,),
                in_specs=[
                    flat(SUB, columns),
                    flat(SUB, columns),
                    flat(SUB * lane_tiles, LANES),
                    plane(1, deep),
                    plane(2, deep),
                ],
                out_specs=[plane(1, None), plane(2, None)],
            )(*array_refs, out_ref, out_ref, out_ref, out_ref)

    anywhere = pl.BlockSpec(memory_space=pl.ANY)
    scalar = pl.BlockSpec(memory_space=pltpu.SMEM)
    operands = [first, offset, table, scalars] + list(arrays) + [result] + pieces
    return pl.pallas_call(
        kernel,
        out_shape=jax.ShapeDtypeStruct(result.shape, jnp.float32),
        in_specs=[scalar] * 4 + [anywhere] * (4 + len(pieces)),
        out_specs=anywhere,
        scratch_shapes=[
            pltpu.VMEM((rows, LANES), jnp.float32),
            pltpu.VMEM((lane_tiles, 2 * coefs, SUB, LANES), jnp.float32),
            pltpu.SemaphoreType.DMA((len(pieces),)),
        ],
        input_output_aliases={7: 0},
        compiler_params=pltpu.CompilerParams(vmem_limit_bytes=VMEM_BYTES),
        cost_estimate=pl.CostEstimate(
            flops=0, bytes_accessed=8 * SUB * columns * coefs * 36, transcendentals=0
        ),
        name="finish",
    )(*operands)


def shifted(block, axis, step, wrap):
    count = lax.axis_size(axis)
    pairs = [
        (i, (i + step) % count) for i in range(count) if wrap or 0 <= i + step < count
    ]
    return lax.ppermute(block, axis, pairs)


def edge_kernel(coefs, east_ref, height_ref, north_ref, last_ref, first_ref, wet_ref, depth_ref, *refs):
    up_ref, down_ref, right_ref, left_ref = refs[-4:]
    rows, columns = wet_ref.shape
    wet = wet_ref[...].astype(jnp.float32)
    end = slice(columns - LANES, columns)
    wet_end = wet[:, end]
    wet_start = wet[:, :LANES]
    depth_end = depth_ref[:, end]
    wet_last = wet[rows - 1 :, :]
    depth_last = depth_ref[rows - 1 :, :]
    for c in range(coefs):
        at = slice(c, c + 1)
        north_row = last_ref[0, c, SUB - 1 :, :] * wet_last
        up_ref[0, at, :] = north_row
        up_ref[1, at, :] = north_row * depth_last
        down_ref[0, at, :] = first_ref[0, c, :1, :] * wet[:1, :]
        down_ref[1, at, :] = first_ref[1, c, :1, :] * wet[:1, :]
        east = east_ref[0, c] * wet_end
        right_ref[0, at, :] = jnp.transpose(east)[LANES - 1 :, :]
        right_ref[1, at, :] = jnp.transpose(east * depth_end)[LANES - 1 :, :]
        left_ref[0, at, :] = jnp.transpose(height_ref[0, c] * wet_start)[:1, :]
        left_ref[1, at, :] = jnp.transpose(north_ref[0, c] * wet_start)[:1, :]


def edge_call(direction, wet_mask, depth, waited):
    _, coefs, rows, columns = direction.shape
    last_tile = columns // LANES - 1
    last_block = rows // SUB - 1
    tall = (1, coefs, rows, LANES)
    whole = pl.BlockSpec((rows, columns), lambda i: (0, 0))
    row_out = (2, coefs, columns)
    col_out = (2, coefs, rows)
    shapes = [row_out, row_out, col_out, col_out]
    return pl.pallas_call(
        lambda *refs: edge_kernel(coefs, *refs),
        out_shape=[jax.ShapeDtypeStruct(shape, jnp.float32) for shape in shapes],
        grid=(1,),
        in_specs=[
            pl.BlockSpec(tall, lambda i: (1, 0, 0, last_tile)),
            pl.BlockSpec(tall, lambda i: (0, 0, 0, 0)),
            pl.BlockSpec(tall, lambda i: (2, 0, 0, 0)),
            pl.BlockSpec((1, coefs, SUB, columns), lambda i: (2, 0, last_block, 0)),
            pl.BlockSpec((2, coefs, SUB, columns), lambda i: (0, 0, 0, 0)),
            whole,
            whole,
        ]
        + [pl.BlockSpec(memory_space=pl.ANY)] * len(waited),
        out_specs=[pl.BlockSpec(shape, lambda i: (0, 0, 0)) for shape in shapes],
        compiler_params=pltpu.CompilerParams(vmem_limit_bytes=VMEM_BYTES),
        cost_estimate=pl.CostEstimate(
            flops=rows * columns, bytes_accessed=0, transcendentals=0
        ),
        name="edges",
    )(direction, direction, direction, direction, direction, wet_mask, depth, *waited)


def halo(direction, wet_mask, depth, waited):
    up, down, right, left = edge_call(direction, wet_mask, depth, waited)
    above = shifted(up, "lat", 1, False)
    below = shifted(down, "lat", -1, False)
    east_below = jnp.concatenate([right[0, :, 1:], below[1, :, -1:]], axis=1)
    north_above = jnp.concatenate([above[0, :, :1], left[1, :, :-1]], axis=1)
    to_right = jnp.stack([right[0], east_below, right[1]])
    to_left = jnp.stack([left[0], left[1], north_above])
    cols = jnp.concatenate(
        [shifted(to_right, "lon", 1, True), shifted(to_left, "lon", -1, True)], axis=0
    )
    slabs = jnp.broadcast_to(cols[:, :, :, None], cols.shape + (LANES,))
    return above, below, slabs


def spread_out(blocks):
    return [
        block if step == 0 else shifted(block, "freq", step, True)
        for step, block in enumerate(blocks)
    ]


def tile_table(groups, coefs, back_chunks, blocks):
    table = np.zeros((2 * groups, blocks + LANES), np.int32)
    for member in range(groups):
        tile = 0
        row = 0
        for chunk_tiles in back_chunks:
            together = sum(chunk_tiles)
            before = 0
            for tiles in chunk_tiles:
                for band in range(groups):
                    start = row + (member - band) % groups * piece_rows(together, coefs)
                    for i in range(before, before + tiles):
                        if tile < blocks:
                            table[2 * member, tile] = start + i * 2 * coefs
                            table[2 * member + 1, tile] = start + together * 2 * coefs + i
                        tile += 1
                before += tiles
            row += groups * piece_rows(together, coefs)
    return table


def local(direction, base_flow, water_depth, drag_factor, wet_mask):
    coefs, tile_rows, tile_cols = direction.shape[1:]
    groups = lax.axis_size("freq")
    member = lax.axis_index("freq")
    lat_place = lax.axis_index("lat")
    total_rows = tile_rows * lax.axis_size("lat")
    lane_tiles = tile_cols // LANES
    angular = OMEGA_STEP * (
        member * (coefs // 2) + jnp.arange(coefs // 2, dtype=jnp.int32) + 1
    ).astype(jnp.float32)
    row_start = (lat_place * tile_rows).astype(jnp.float32)
    scalars = jnp.concatenate(
        [jnp.stack([row_start, jnp.float32(1.0 / total_rows)]), angular]
    )
    place = jnp.reshape(member, (1,)).astype(jnp.int32)
    blocks = tile_rows * lane_tiles
    row_blocks = tile_rows // SUB
    chunk_tiles = [share * blocks // (groups * SHARE_UNITS) for share in CHUNK_SHARES]
    fixed = groups * sum(chunk_tiles)
    steps = -(-(blocks - fixed) // (groups * LOOP_TILES))
    back_chunks = [chunk_tiles[:-1], chunk_tiles[-1:]]
    table = jnp.asarray(
        tile_table(groups, coefs, back_chunks + [[LOOP_TILES]] * steps, blocks)
    )
    index, cells, offset = index_call(wet_mask)
    offsets = offset.reshape(-1)
    ends = offsets[SUB * lane_tiles : blocks + 1 : SUB * lane_tiles]

    def packed(first_tile, tiles, token, waited=()):
        params = jnp.stack([place[0], first_tile + token])
        *flows, token = pack_call(
            params, offset, index, base_flow, direction, groups, tiles, waited
        )
        return spread_out(flows), token[0, 0]

    def through(flows, token, weight):
        *back, token = friction_call(place + token, flows, coefs, weight)
        return spread_out(back), token[0, 0]

    flows = []
    tile = 0
    token = jnp.int32(0)
    for tiles in chunk_tiles[:-1]:
        flow, token = packed(tile, tiles, token)
        flows.append(flow)
        tile += groups * tiles

    loop_cells = groups * LOOP_TILES * LANES
    beyond = offsets[blocks] + token - fixed * LANES
    loops = jnp.maximum(beyond + loop_cells - 1, 0) // loop_cells

    def more(state):
        done, held = state
        flow, _ = packed(fixed + done * groups * LOOP_TILES, LOOP_TILES, 0)
        back, _ = through([flow], 0, 1)
        held = lax.dynamic_update_slice_in_dim(
            held, jnp.concatenate(back, axis=0)[None], done, 0
        )
        return done + 1, held

    rows = groups * piece_rows(LOOP_TILES, coefs)
    extra = jnp.zeros((steps, rows, LANES), jnp.float32)
    done, extra = lax.while_loop(lambda state: state[0] < loops, more, (jnp.int32(0), extra))

    token = token + jnp.minimum(done, 0)
    flows.append(packed(tile, chunk_tiles[-1], token)[0])
    above, below, slabs = halo(direction, wet_mask, water_depth, flows[0][1:] + flows[-1][:1])
    result, prepared = prepare_call(
        scalars, direction, wet_mask, water_depth, above, below, slabs
    )
    back, token = through(flows[:-1], prepared[0, 0], 1)
    backs = [back]
    back, token = through(flows[-1:], token, LATE_WEIGHT)
    backs.append(back)

    arrays = (wet_mask, drag_factor, cells)
    pieces = []
    back_rows = rows * steps
    back_rows += groups * sum(piece_rows(sum(several), coefs) for several in back_chunks)
    begin = jnp.int32(0)
    tile = 0
    for last, several in enumerate(back_chunks):
        pieces += backs[last]
        tile += groups * sum(several)
        if last:
            end = jnp.int32(row_blocks)
            pieces.append(extra.reshape(-1, LANES))
        else:
            end = jnp.sum((ends <= tile * LANES).astype(jnp.int32))
        first = jnp.stack([begin, place[0], end - begin, loops])
        result = finish_call(
            first, offset, table, scalars, arrays, list(pieces), back_rows, result, groups,
            (groups, -(-SUB * lane_tiles // chunk_tiles[-2])) if last else (0, 0),
        )
        begin = end
    return result


def solution(mesh):
    placed = (
        P(None, "freq", "lat", "lon"),
        P(None, "freq", "lat", "lon"),
        P("lat", "lon"),
        P("lat", "lon"),
        P("lat", "lon"),
    )
    return jax.shard_map(
        local, mesh=mesh, in_specs=placed, out_specs=P(None, "freq", "lat", "lon"), check_vma=False
    )
```

```python
import math

import jax
import jax.numpy as jnp
import ml_dtypes
import numpy as np
from jax import lax
from jax.experimental import pallas as pl
from jax.experimental.pallas import tpu as pltpu
from jax.sharding import PartitionSpec as P

NCON = 16
NTIME = 256
LANES = 128
SUB = 8

LINEAR_DRAG = 0.5
GRAVITY = 1.0
OMEGA_STEP = 0.25
SPEED_SOFT = 0.01
VMEM_BYTES = 48 * 1024 * 1024
CHUNK_SHARES = (18, 49, 30)
SHARE_UNITS = 128
LOOP_TILES = 8
PACK_COST = 16384
AHEAD = 4
LATE_WEIGHT = 2048


def split_table():
    sample = np.arange(NTIME)[:, None]
    harmonic = np.arange(1, NCON + 1)[None, :]
    phase = (sample * harmonic % NTIME) * (2.0 * math.pi / NTIME)
    table = np.stack([np.cos(phase), np.sin(phase)], axis=2).reshape(NTIME, 2 * NCON)
    table = table.astype(np.float32)
    high = table.astype(ml_dtypes.bfloat16)
    low = (table - high.astype(np.float32)).astype(ml_dtypes.bfloat16)
    return high, low


def split_value(value):
    high = value.astype(jnp.bfloat16)
    low = (value - high.astype(jnp.float32)).astype(jnp.bfloat16)
    return high, low


def friction_kernel(groups, coefs, chunk_tiles, place_ref, synth_ref, analyse_ref, *refs):
    parts = len(chunk_tiles)
    tiles = sum(chunk_tiles)
    out_refs, token_ref = refs[groups * parts : -1], refs[-1]
    token_ref[...] = jnp.zeros_like(token_ref)
    columns = 2 * NCON

    def block(flow_refs, first, at, count):
        tile = first + at
        loaded = []
        for source in range(groups):
            several = [flow_refs[source][at + i] for i in range(count)]
            loaded.append(jnp.concatenate(several, axis=1))
        series = []
        for field in range(4):
            rows = slice(field * coefs, (field + 1) * coefs)
            values = jnp.concatenate([part[rows] for part in loaded], axis=0)
            high, low = split_value(values)
            operand = jnp.concatenate([high, low, high], axis=0)
            series.append(
                jnp.dot(synth_ref[0], operand, preferred_element_type=jnp.float32)
            )
        base_east, base_north, step_east, step_north = series
        square = base_east * base_east + base_north * base_north + SPEED_SOFT
        inverse = lax.rsqrt(square)
        speed = square * inverse
        projected = (base_east * step_east + base_north * step_north) * inverse
        forces = (
            speed * step_east + base_east * projected,
            speed * step_north + base_north * projected,
        )
        mean = jnp.sum(speed, axis=0, keepdims=True) * (1.0 / NTIME)
        analysed = []
        for force in forces:
            high, low = split_value(force)
            both = jnp.dot(analyse_ref[0], high, preferred_element_type=jnp.float32)
            rest = jnp.dot(
                analyse_ref[0, :columns, :], low, preferred_element_type=jnp.float32
            )
            analysed.append(both[:columns] + both[columns:] + rest)
        for part in range(count):
            lanes = slice(part * LANES, (part + 1) * LANES)
            for target in range(groups):
                rows = slice(target * coefs, (target + 1) * coefs)
                values = jnp.concatenate(
                    [analysed[0][rows, lanes], analysed[1][rows, lanes]], axis=0
                )
                start = pl.multiple_of((tile + part) * 2 * coefs, SUB)
                out_refs[target][pl.ds(start, 2 * coefs), :] = values
                at = tiles * 2 * coefs + tile + part
                out_refs[target][pl.ds(at, 1), :] = mean[:, lanes]

    first = 0
    for part, here in enumerate(chunk_tiles):
        flow_refs = refs[part * groups : (part + 1) * groups]

        def body(step, carry, flow_refs=flow_refs, first=first):
            block(flow_refs, first, step * 2, 2)
            return carry

        lax.fori_loop(0, here // 2, body, 0)
        if here % 2:
            block(flow_refs, first, here - 1, 1)
        first += here


def placed_tables(groups, coefs):
    high, low = split_table()
    synth, analyse = [], []
    for member in range(groups):
        sources = [(member - step) % groups for step in range(groups)]
        targets = [(member + step) % groups for step in range(groups)]
        source = np.concatenate([np.arange(coefs) + m * coefs for m in sources])
        target = np.concatenate([np.arange(coefs) + m * coefs for m in targets])
        synth.append(np.concatenate([high[:, source], high[:, source], low[:, source]], axis=1))
        both = np.concatenate([high[:, target].T, low[:, target].T], axis=0)
        analyse.append((both.astype(np.float32) * (2.0 / NTIME)).astype(ml_dtypes.bfloat16))
    return np.stack(synth), np.stack(analyse)


def piece_rows(tiles, coefs):
    return tiles * 2 * coefs + -(-tiles // SUB) * SUB


def friction_call(place, flows, coefs, weight):
    groups = len(flows[0])
    chunk_tiles = [chunk[0].shape[0] for chunk in flows]
    tiles = sum(chunk_tiles)
    synth, analyse = placed_tables(groups, coefs)
    cells = groups * tiles * LANES
    out_shape = (piece_rows(tiles, coefs), LANES)
    grid_spec = pltpu.PrefetchScalarGridSpec(
        num_scalar_prefetch=1,
        grid=(1,),
        in_specs=[
            pl.BlockSpec((1,) + synth.shape[1:], lambda i, place: (place[0], 0, 0)),
            pl.BlockSpec((1,) + analyse.shape[1:], lambda i, place: (place[0], 0, 0)),
        ]
        + [
            pl.BlockSpec(block.shape, lambda i, place: (0, 0, 0))
            for chunk in flows
            for block in chunk
        ],
        out_specs=[pl.BlockSpec(out_shape, lambda i, place: (0, 0))] * groups
        + [pl.BlockSpec((SUB, LANES), lambda i, place: (0, 0))],
    )
    return pl.pallas_call(
        lambda *refs: friction_kernel(groups, coefs, chunk_tiles, *refs),
        out_shape=[jax.ShapeDtypeStruct(out_shape, jnp.float32)] * groups
        + [jax.ShapeDtypeStruct((SUB, LANES), jnp.int32)],
        grid_spec=grid_spec,
        compiler_params=pltpu.CompilerParams(vmem_limit_bytes=VMEM_BYTES),
        cost_estimate=pl.CostEstimate(
            flops=cells * NTIME * weight, bytes_accessed=0, transcendentals=0
        ),
        name="friction",
    )(place, jnp.asarray(synth), jnp.asarray(analyse), *[b for chunk in flows for b in chunk])


def index_kernel(wet_ref, index_ref, place_ref, offset_ref, scratch):
    blocks = scratch.shape[0]
    rows, cols = wet_ref.shape
    at = 0
    for row in range(0, rows, SUB):
        for col in range(0, cols, LANES):
            part = wet_ref[row : row + SUB, col : col + LANES]
            scratch[at : at + SUB, :] = jnp.where(part != 0, 1.0, 0.0)
            at += SUB
    wet = scratch[...].astype(jnp.bfloat16)
    earlier = lax.broadcasted_iota(jnp.int32, (LANES, LANES), 0)
    later = lax.broadcasted_iota(jnp.int32, (LANES, LANES), 1)
    before = jnp.where(earlier < later, 1.0, 0.0).astype(jnp.bfloat16)
    ones = jnp.ones((LANES, LANES), jnp.bfloat16)
    rank = jnp.dot(wet, before, preferred_element_type=jnp.float32)
    count = jnp.dot(wet, ones, preferred_element_type=jnp.float32)
    low = lax.broadcasted_iota(jnp.int32, (blocks, blocks), 0)
    high = lax.broadcasted_iota(jnp.int32, (blocks, blocks), 1)
    summing = jnp.where(high < low, 1.0, 0.0).astype(jnp.bfloat16)
    offset = jnp.dot(summing, count.astype(jnp.bfloat16), preferred_element_type=jnp.float32)
    lane = lax.broadcasted_iota(jnp.int32, (blocks, LANES), 1)
    rank = rank.astype(jnp.int32)
    held = jnp.where(scratch[...] > 0.5, lane + LANES * (lane - rank), 0)
    for bit in range(7):
        step = 1 << bit
        coming = pltpu.roll(held, LANES - step, 1)
        moves = (coming >> (7 + bit)) & 1
        stays = 1 - ((held >> (7 + bit)) & 1)
        held = jnp.where(moves == 1, coming, held * stays)
    source = held & (LANES - 1)
    shift = offset.astype(jnp.int32) & (LANES - 1)
    index_ref[...] = jnp.take_along_axis(
        source, (lane - shift) & (LANES - 1), axis=1, mode="promise_in_bounds"
    )
    place_ref[...] = shift + rank
    eye = jnp.where(earlier == later, 1.0, 0.0)
    cubes = offset.reshape(blocks // LANES, LANES, LANES)
    table = jnp.sum(cubes * eye[None], axis=1)
    total = offset[blocks - 1 : blocks] + count[blocks - 1 : blocks]
    offset_ref[: blocks // LANES, :] = table.astype(jnp.int32)
    offset_ref[blocks // LANES : blocks // LANES + 1, :] = total.astype(jnp.int32)


def index_call(wet_mask):
    rows, cols = wet_mask.shape
    blocks = rows * cols // LANES
    table = -(-(blocks // LANES + 1) // SUB) * SUB
    return pl.pallas_call(
        index_kernel,
        out_shape=[
            jax.ShapeDtypeStruct((blocks, LANES), jnp.int32),
            jax.ShapeDtypeStruct((blocks, LANES), jnp.int32),
            jax.ShapeDtypeStruct((table, LANES), jnp.int32),
        ],
        scratch_shapes=[pltpu.VMEM((blocks, LANES), jnp.float32)],
        compiler_params=pltpu.CompilerParams(vmem_limit_bytes=VMEM_BYTES),
        name="index",
    )(wet_mask)


def pack_kernel(groups, coefs, tiles, waited, params_ref, offset_ref, index_ref, base_ref, step_ref, *refs):
    refs = refs[waited:]
    out_refs = refs[:groups]
    token_ref, held, stage, in_sem, out_sem = refs[groups:]
    token_ref[...] = jnp.zeros_like(token_ref)
    lane_tiles = held.shape[1]
    per_block = SUB * lane_tiles
    row_blocks = index_ref.shape[0] // per_block
    count = groups * tiles
    first_tile = params_ref[1]
    low = first_tile * LANES
    high = low + count * LANES

    def offset_of(block):
        return offset_ref[block >> 7, block & (LANES - 1)]

    begin = jnp.int32(0)
    end = jnp.int32(0)
    for block in range(row_blocks):
        begin += (offset_of((block + 1) * per_block) <= low).astype(jnp.int32)
        end += (offset_of(block * per_block) < high).astype(jnp.int32)
    end = jnp.maximum(end, begin)

    def copies(block):
        slot = lax.rem(block, AHEAD)
        rows = pl.ds(pl.multiple_of(block * SUB, SUB), SUB)
        started = []
        for lane_tile in range(lane_tiles):
            lanes = pl.ds(lane_tile * LANES, LANES)
            landing = held.at[slot, lane_tile]
            started.append(
                pltpu.make_async_copy(
                    base_ref.at[:, :, rows, lanes],
                    landing.at[pl.ds(0, 2)],
                    in_sem.at[slot, 2 * lane_tile],
                )
            )
            started.append(
                pltpu.make_async_copy(
                    step_ref.at[pl.ds(1, 2), :, rows, lanes],
                    landing.at[pl.ds(2, 2)],
                    in_sem.at[slot, 2 * lane_tile + 1],
                )
            )
        return started

    for step in range(AHEAD - 1):

        @pl.when(begin + step < end)
        def _():
            for copy in copies(begin + step):
                copy.start()

    lane = lax.broadcasted_iota(jnp.int32, (coefs, LANES), 1)

    def place_of(offset):
        return jnp.clip((offset >> 7) - first_tile + 1, 0, count + 1)

    def body(block, current):
        @pl.when(block + AHEAD - 1 < end)
        def _():
            for copy in copies(block + AHEAD - 1):
                copy.start()

        for copy in copies(block):
            copy.wait()
        slot = lax.rem(block, AHEAD)
        for lane_tile in range(lane_tiles):
            fields = [
                held.at[slot, lane_tile, field].reshape(coefs * SUB, LANES) for field in range(4)
            ]
            start = block * per_block + lane_tile * SUB
            index = index_ref[pl.ds(pl.multiple_of(start, SUB), SUB), :]
            following = offset_of(start)
            for r in range(SUB):
                offset = following
                following = offset_of(start + r + 1)
                shift = offset & (LANES - 1)
                crossing = (following >> 7) > (offset >> 7)
                source = jnp.broadcast_to(index[r : r + 1], (coefs, LANES))
                to = place_of(offset)
                renewed = []
                for field in range(4):
                    got = jnp.take_along_axis(
                        fields[field][pl.ds(r, coefs, stride=SUB), :],
                        source,
                        axis=1,
                        mode="promise_in_bounds",
                    )
                    full = jnp.where(lane >= shift, got, current[field])
                    stage[to, field * coefs : (field + 1) * coefs, :] = full
                    renewed.append(jnp.where(crossing, got, full))
                current = tuple(renewed)
        return current

    zero = jnp.zeros((coefs, LANES), jnp.float32)
    current = lax.fori_loop(begin, end, body, (zero,) * 4)
    last = place_of(offset_of(end * per_block))
    for field in range(4):
        stage[last, field * coefs : (field + 1) * coefs, :] = current[field]
    outs = []
    for step in range(groups):
        member = lax.rem(params_ref[0] + step, groups)
        outs.append(
            pltpu.make_async_copy(
                stage.at[pl.ds(1 + member * tiles, tiles)], out_refs[step], out_sem.at[step]
            )
        )
    for copy in outs:
        copy.start()
    for copy in outs:
        copy.wait()


def pack_call(params, offset, index, base_flow, direction, groups, tiles, waited):
    coefs, _, columns = direction.shape[1:]
    shape = (tiles, 4 * coefs, LANES)
    anywhere = pl.BlockSpec(memory_space=pl.ANY)
    grid_spec = pltpu.PrefetchScalarGridSpec(
        num_scalar_prefetch=2,
        grid=(1,),
        in_specs=[pl.BlockSpec(index.shape, lambda i, p, o: (0, 0))]
        + [anywhere] * (2 + len(waited)),
        out_specs=[anywhere] * groups + [pl.BlockSpec((SUB, LANES), lambda i, p, o: (0, 0))],
        scratch_shapes=[
            pltpu.VMEM((AHEAD, columns // LANES, 4, coefs, SUB, LANES), jnp.float32),
            pltpu.VMEM((groups * tiles + 2, 4 * coefs, LANES), jnp.float32),
            pltpu.SemaphoreType.DMA((AHEAD, 2 * (columns // LANES))),
            pltpu.SemaphoreType.DMA((groups,)),
        ],
    )
    return pl.pallas_call(
        lambda *refs: pack_kernel(groups, coefs, tiles, len(waited), *refs),
        out_shape=[jax.ShapeDtypeStruct(shape, jnp.float32)] * groups
        + [jax.ShapeDtypeStruct((SUB, LANES), jnp.int32)],
        grid_spec=grid_spec,
        compiler_params=pltpu.CompilerParams(vmem_limit_bytes=VMEM_BYTES),
        cost_estimate=pl.CostEstimate(
            flops=0, bytes_accessed=groups * tiles * coefs * PACK_COST, transcendentals=0
        ),
        name="pack",
    )(params, offset, index, base_flow, direction, *waited)


def prepare_kernel(coefs, scalars_ref, *refs):
    (here_ref, prev_ref, next_ref, wet_ref, wet_prev_ref, wet_next_ref, depth_ref, depth_prev_ref,
     above_ref, below_ref, slab_ref, out_ref, token_ref) = refs
    token_ref[...] = jnp.zeros_like(token_ref)
    columns = here_ref.shape[-1]
    row_block = pl.program_id(0)
    at_top = row_block == 0
    at_bottom = row_block == pl.num_programs(0) - 1
    wet = wet_ref[...].astype(jnp.float32)
    wet_prev = wet_prev_ref[SUB - 1 :, :].astype(jnp.float32)
    wet_next = wet_next_ref[:1, :].astype(jnp.float32)
    depth = depth_ref[...]
    depth_prev = depth_prev_ref[SUB - 1 :, :]
    lane = lax.broadcasted_iota(jnp.int32, (SUB, columns), 1)
    sub = lax.broadcasted_iota(jnp.int32, (SUB, columns), 0)
    row = (row_block * SUB + sub).astype(jnp.float32)
    rotation = 0.5 + (row + scalars_ref[0] + 0.5) * scalars_ref[1]

    def wide(slab):
        return jnp.concatenate([slab] * (columns // LANES), axis=1)

    def west(value, slab):
        return jnp.where(lane == 0, wide(slab), pltpu.roll(value, 1, 1))

    def east_of(value, slab):
        return jnp.where(lane == columns - 1, wide(slab), pltpu.roll(value, columns - 1, 1))

    def above(value, edge):
        return jnp.where(sub == 0, edge, pltpu.roll(value, 1, 0))

    def below(value, edge):
        return jnp.where(sub == SUB - 1, edge, pltpu.roll(value, SUB - 1, 0))

    for k in range(coefs // 2):
        angular = scalars_ref[2 + k]
        inverse_angular = 1.0 / (angular + jnp.zeros((SUB, columns), jnp.float32))
        planes = [
            [here_ref[p, 2 * k + part] * wet for p in range(3)] for part in range(2)
        ]
        for part in range(2):
            c = 2 * k + part
            height, east, north = planes[part]
            other = planes[1 - part]
            signed = angular if part == 0 else -angular
            east_flux = depth * east
            north_flux = depth * north
            north_edge = prev_ref[0, c, SUB - 1 :, :] * wet_prev
            flux_edge = jnp.where(at_top, above_ref[1, c : c + 1], north_edge * depth_prev)
            north_edge = jnp.where(at_top, above_ref[0, c : c + 1], north_edge)
            height_edge = jnp.where(
                at_bottom, below_ref[0, c : c + 1], next_ref[0, c, :1, :] * wet_next
            )
            east_edge = jnp.where(
                at_bottom, below_ref[1, c : c + 1], next_ref[1, c, :1, :] * wet_next
            )
            north_up = above(north, north_edge)
            east_down = below(east, east_edge)
            res_height = (
                signed * other[0]
                + east_flux
                - west(east_flux, slab_ref[2, c])
                + north_flux
                - above(north_flux, flux_edge)
            )
            north_mean = 0.25 * (
                north
                + east_of(north, slab_ref[4, c])
                + north_up
                + east_of(north_up, slab_ref[5, c])
            )
            east_mean = 0.25 * (
                east
                + west(east, slab_ref[0, c])
                + east_down
                + west(east_down, slab_ref[1, c])
            )
            res_east = (
                signed * other[1]
                + LINEAR_DRAG * east
                - rotation * north_mean
                + GRAVITY * (east_of(height, slab_ref[3, c]) - height)
            )
            res_north = (
                signed * other[2]
                + LINEAR_DRAG * north
                + rotation * east_mean
                + GRAVITY * (below(height, height_edge) - height)
            )
            if part == 0:
                out_ref[0, c + 1] = res_height * wet * inverse_angular
            else:
                out_ref[0, c - 1] = -res_height * wet * inverse_angular
            out_ref[1, c] = res_east * wet
            out_ref[2, c] = res_north * wet


def prepare_call(scalars, direction, wet_mask, depth, above, below, slabs):
    _, coefs, rows, columns = direction.shape
    last = rows // SUB - 1

    def before(i):
        return jnp.maximum(i - 1, 0)

    def after(i):
        return jnp.minimum(i + 1, last)

    planes = pl.BlockSpec((3, coefs, SUB, columns), lambda i: (0, 0, i, 0))
    flat = (SUB, columns)
    edge = pl.BlockSpec((2, coefs, columns), lambda i: (0, 0, 0))
    return pl.pallas_call(
        lambda *refs: prepare_kernel(coefs, *refs),
        out_shape=[
            jax.ShapeDtypeStruct(direction.shape, jnp.float32),
            jax.ShapeDtypeStruct((SUB, LANES), jnp.int32),
        ],
        grid=(rows // SUB,),
        in_specs=[
            pl.BlockSpec(memory_space=pltpu.SMEM),
            planes,
            pl.BlockSpec((1, coefs, SUB, columns), lambda i: (2, 0, before(i), 0)),
            pl.BlockSpec((2, coefs, SUB, columns), lambda i: (0, 0, after(i), 0)),
            pl.BlockSpec(flat, lambda i: (i, 0)),
            pl.BlockSpec(flat, lambda i: (before(i), 0)),
            pl.BlockSpec(flat, lambda i: (after(i), 0)),
            pl.BlockSpec(flat, lambda i: (i, 0)),
            pl.BlockSpec(flat, lambda i: (before(i), 0)),
            edge,
            edge,
            pl.BlockSpec((6, coefs, SUB, LANES), lambda i: (0, 0, i, 0)),
        ],
        out_specs=[planes, pl.BlockSpec((SUB, LANES), lambda i: (0, 0))],
        compiler_params=pltpu.CompilerParams(vmem_limit_bytes=VMEM_BYTES),
        cost_estimate=pl.CostEstimate(
            flops=rows * columns * coefs, bytes_accessed=0, transcendentals=0
        ),
        name="prepare",
    )(
        scalars, direction, direction, direction, wet_mask, wet_mask, wet_mask, depth, depth,
        above, below, slabs,
    )


def finish_kernel(coefs, lane_tiles, row_block, first_ref, offset_ref, table_ref, scalars_ref, back, spread_ref, refs):
    wet_ref, drag_ref, cell_ref, east_ref, north_ref, east_out, north_out = refs
    columns = lane_tiles * LANES
    wet = wet_ref[...].astype(jnp.float32)
    drag = drag_ref[...]
    sub = lax.broadcasted_iota(jnp.int32, (SUB, columns), 0)
    row = (row_block * SUB + sub).astype(jnp.float32)
    rotation = 0.5 + (row + scalars_ref[0] + 0.5) * scalars_ref[1]

    def gathered(here, after, index, over):
        first = jnp.take_along_axis(here, index, axis=1, mode="promise_in_bounds")
        second = jnp.take_along_axis(after, index, axis=1, mode="promise_in_bounds")
        return jnp.where(over, second, first)

    speed = []
    for lane_tile in range(lane_tiles):
        places = cell_ref[lane_tile * SUB : (lane_tile + 1) * SUB, :]
        turned = spread_ref.at[lane_tile].reshape(2 * coefs * SUB, LANES)
        speeds = [[], []]
        for r in range(SUB):
            at = (row_block * lane_tiles + lane_tile) * SUB + r
            tile = offset_ref[at >> 7, at & (LANES - 1)] >> 7
            found = []
            for which in range(2):
                start = pl.multiple_of(table_ref[first_ref[1] * 2, tile + which], SUB)
                found.append(back[pl.ds(start, 2 * coefs), :])
                start = table_ref[first_ref[1] * 2 + 1, tile + which]
                speeds[which].append(back[pl.ds(start, 1), :])
            place = jnp.broadcast_to(places[r : r + 1], (2 * coefs, LANES))
            turned[pl.ds(r, 2 * coefs, stride=SUB), :] = gathered(
                found[0], found[1], place & (LANES - 1), place >= LANES
            )
        speed.append(
            gathered(
                jnp.concatenate(speeds[0], axis=0),
                jnp.concatenate(speeds[1], axis=0),
                places & (LANES - 1),
                places >= LANES,
            )
        )
    is_wet = wet > 0.5
    friction = [
        jnp.where(
            is_wet,
            jnp.concatenate([spread_ref[n, index] for n in range(lane_tiles)], axis=1) * drag,
            0.0,
        )
        for index in range(2 * coefs)
    ]
    speed = jnp.where(is_wet, jnp.concatenate(speed, axis=1), 0.0)
    real_rate = drag * speed + LINEAR_DRAG
    for k in range(coefs // 2):
        angular = scalars_ref[2 + k]
        cos_at, sin_at = 2 * k, 2 * k + 1
        det_real = real_rate * real_rate - angular * angular + rotation * rotation
        det_imag = 2.0 * real_rate * angular
        inverse_norm = 1.0 / (det_real * det_real + det_imag * det_imag)
        inv_real = det_real * inverse_norm
        inv_imag = -det_imag * inverse_norm
        east_re = east_ref[0, cos_at] + friction[cos_at]
        east_im = -(east_ref[0, sin_at] + friction[sin_at])
        north_re = north_ref[0, cos_at] + friction[coefs + cos_at]
        north_im = -(north_ref[0, sin_at] + friction[coefs + sin_at])
        num_east_re = real_rate * east_re - angular * east_im + rotation * north_re
        num_east_im = real_rate * east_im + angular * east_re + rotation * north_im
        num_north_re = -rotation * east_re + real_rate * north_re - angular * north_im
        num_north_im = -rotation * east_im + real_rate * north_im + angular * north_re
        east_out[0, cos_at] = num_east_re * inv_real - num_east_im * inv_imag
        east_out[0, sin_at] = -(num_east_re * inv_imag + num_east_im * inv_real)
        north_out[0, cos_at] = num_north_re * inv_real - num_north_im * inv_imag
        north_out[0, sin_at] = -(num_north_re * inv_imag + num_north_im * inv_real)


def finish_call(first, offset, table, scalars, arrays, pieces, rows, result, groups, early):
    _, coefs, _, columns = result.shape
    lane_tiles = columns // LANES

    def kernel(first_ref, offset_ref, table_ref, scalars_ref, *refs):
        array_refs = refs[:3]
        piece_refs = refs[4:-4]
        out_ref, back, spread_ref, sem = refs[-4:]
        first = first_ref[0]
        count = first_ref[2]

        @pl.when(count > 0)
        def _():
            at = 0
            copies = []
            for n, piece in enumerate(piece_refs):
                rows = piece.shape[0]
                copy = pltpu.make_async_copy(piece, back.at[pl.ds(at, rows)], sem.at[n])
                needed = True
                if n < early[0]:
                    source = lax.rem(first_ref[1] + groups - n % groups, groups)
                    needed = source >= groups - early[1]
                elif n >= early[0] + groups:
                    needed = first_ref[3] > 0
                copies.append((copy, needed))
                at += rows

            def each(act):
                for copy, needed in copies:
                    if needed is True:
                        act(copy)
                    else:
                        pl.when(needed)(lambda copy=copy: act(copy))

            each(lambda copy: copy.start())

            def body(*block_refs):
                @pl.when(pl.program_id(0) == 0)
                def _():
                    each(lambda copy: copy.wait())

                finish_kernel(
                    coefs, lane_tiles, first + pl.program_id(0), first_ref, offset_ref,
                    table_ref, scalars_ref, back, spread_ref, block_refs,
                )

            deep = pl.Buffered(3)

            def flat(rows, width):
                return pl.BlockSpec(
                    (rows, width), lambda i: (first + i, 0), pipeline_mode=deep
                )

            def plane(p, mode):
                return pl.BlockSpec(
                    (1, coefs, SUB, columns), lambda i: (p, 0, first + i, 0), pipeline_mode=mode
                )

            pltpu.emit_pipeline(
                body,
                grid=(count,),
                in_specs=[
                    flat(SUB, columns),
                    flat(SUB, columns),
                    flat(SUB * lane_tiles, LANES),
                    plane(1, deep),
                    plane(2, deep),
                ],
                out_specs=[plane(1, None), plane(2, None)],
            )(*array_refs, out_ref, out_ref, out_ref, out_ref)

    anywhere = pl.BlockSpec(memory_space=pl.ANY)
    scalar = pl.BlockSpec(memory_space=pltpu.SMEM)
    operands = [first, offset, table, scalars] + list(arrays) + [result] + pieces
    return pl.pallas_call(
        kernel,
        out_shape=jax.ShapeDtypeStruct(result.shape, jnp.float32),
        in_specs=[scalar] * 4 + [anywhere] * (4 + len(pieces)),
        out_specs=anywhere,
        scratch_shapes=[
            pltpu.VMEM((rows, LANES), jnp.float32),
            pltpu.VMEM((lane_tiles, 2 * coefs, SUB, LANES), jnp.float32),
            pltpu.SemaphoreType.DMA((len(pieces),)),
        ],
        input_output_aliases={7: 0},
        compiler_params=pltpu.CompilerParams(vmem_limit_bytes=VMEM_BYTES),
        cost_estimate=pl.CostEstimate(
            flops=0, bytes_accessed=8 * SUB * columns * coefs * 36, transcendentals=0
        ),
        name="finish",
    )(*operands)


def shifted(block, axis, step, wrap):
    count = lax.axis_size(axis)
    pairs = [
        (i, (i + step) % count) for i in range(count) if wrap or 0 <= i + step < count
    ]
    return lax.ppermute(block, axis, pairs)


def edge_kernel(coefs, east_ref, height_ref, north_ref, last_ref, first_ref, wet_ref, depth_ref, *refs):
    up_ref, down_ref, right_ref, left_ref = refs[-4:]
    rows, columns = wet_ref.shape
    wet = wet_ref[...].astype(jnp.float32)
    end = slice(columns - LANES, columns)
    wet_end = wet[:, end]
    wet_start = wet[:, :LANES]
    depth_end = depth_ref[:, end]
    wet_last = wet[rows - 1 :, :]
    depth_last = depth_ref[rows - 1 :, :]
    for c in range(coefs):
        at = slice(c, c + 1)
        north_row = last_ref[0, c, SUB - 1 :, :] * wet_last
        up_ref[0, at, :] = north_row
        up_ref[1, at, :] = north_row * depth_last
        down_ref[0, at, :] = first_ref[0, c, :1, :] * wet[:1, :]
        down_ref[1, at, :] = first_ref[1, c, :1, :] * wet[:1, :]
        east = east_ref[0, c] * wet_end
        right_ref[0, at, :] = jnp.transpose(east)[LANES - 1 :, :]
        right_ref[1, at, :] = jnp.transpose(east * depth_end)[LANES - 1 :, :]
        left_ref[0, at, :] = jnp.transpose(height_ref[0, c] * wet_start)[:1, :]
        left_ref[1, at, :] = jnp.transpose(north_ref[0, c] * wet_start)[:1, :]


def edge_call(direction, wet_mask, depth, waited):
    _, coefs, rows, columns = direction.shape
    last_tile = columns // LANES - 1
    last_block = rows // SUB - 1
    tall = (1, coefs, rows, LANES)
    whole = pl.BlockSpec((rows, columns), lambda i: (0, 0))
    row_out = (2, coefs, columns)
    col_out = (2, coefs, rows)
    shapes = [row_out, row_out, col_out, col_out]
    return pl.pallas_call(
        lambda *refs: edge_kernel(coefs, *refs),
        out_shape=[jax.ShapeDtypeStruct(shape, jnp.float32) for shape in shapes],
        grid=(1,),
        in_specs=[
            pl.BlockSpec(tall, lambda i: (1, 0, 0, last_tile)),
            pl.BlockSpec(tall, lambda i: (0, 0, 0, 0)),
            pl.BlockSpec(tall, lambda i: (2, 0, 0, 0)),
            pl.BlockSpec((1, coefs, SUB, columns), lambda i: (2, 0, last_block, 0)),
            pl.BlockSpec((2, coefs, SUB, columns), lambda i: (0, 0, 0, 0)),
            whole,
            whole,
        ]
        + [pl.BlockSpec(memory_space=pl.ANY)] * len(waited),
        out_specs=[pl.BlockSpec(shape, lambda i: (0, 0, 0)) for shape in shapes],
        compiler_params=pltpu.CompilerParams(vmem_limit_bytes=VMEM_BYTES),
        cost_estimate=pl.CostEstimate(
            flops=rows * columns, bytes_accessed=0, transcendentals=0
        ),
        name="edges",
    )(direction, direction, direction, direction, direction, wet_mask, depth, *waited)


def halo(direction, wet_mask, depth, waited):
    up, down, right, left = edge_call(direction, wet_mask, depth, waited)
    above = shifted(up, "lat", 1, False)
    below = shifted(down, "lat", -1, False)
    east_below = jnp.concatenate([right[0, :, 1:], below[1, :, -1:]], axis=1)
    north_above = jnp.concatenate([above[0, :, :1], left[1, :, :-1]], axis=1)
    to_right = jnp.stack([right[0], east_below, right[1]])
    to_left = jnp.stack([left[0], left[1], north_above])
    cols = jnp.concatenate(
        [shifted(to_right, "lon", 1, True), shifted(to_left, "lon", -1, True)], axis=0
    )
    slabs = jnp.broadcast_to(cols[:, :, :, None], cols.shape + (LANES,))
    return above, below, slabs


def spread_out(blocks):
    return [
        block if step == 0 else shifted(block, "freq", step, True)
        for step, block in enumerate(blocks)
    ]


def tile_table(groups, coefs, back_chunks, blocks):
    table = np.zeros((2 * groups, blocks + LANES), np.int32)
    for member in range(groups):
        tile = 0
        row = 0
        for chunk_tiles in back_chunks:
            together = sum(chunk_tiles)
            before = 0
            for tiles in chunk_tiles:
                for band in range(groups):
                    start = row + (member - band) % groups * piece_rows(together, coefs)
                    for i in range(before, before + tiles):
                        if tile < blocks:
                            table[2 * member, tile] = start + i * 2 * coefs
                            table[2 * member + 1, tile] = start + together * 2 * coefs + i
                        tile += 1
                before += tiles
            row += groups * piece_rows(together, coefs)
    return table


def local(direction, base_flow, water_depth, drag_factor, wet_mask):
    coefs, tile_rows, tile_cols = direction.shape[1:]
    groups = lax.axis_size("freq")
    member = lax.axis_index("freq")
    lat_place = lax.axis_index("lat")
    total_rows = tile_rows * lax.axis_size("lat")
    lane_tiles = tile_cols // LANES
    angular = OMEGA_STEP * (
        member * (coefs // 2) + jnp.arange(coefs // 2, dtype=jnp.int32) + 1
    ).astype(jnp.float32)
    row_start = (lat_place * tile_rows).astype(jnp.float32)
    scalars = jnp.concatenate(
        [jnp.stack([row_start, jnp.float32(1.0 / total_rows)]), angular]
    )
    place = jnp.reshape(member, (1,)).astype(jnp.int32)
    blocks = tile_rows * lane_tiles
    row_blocks = tile_rows // SUB
    chunk_tiles = [share * blocks // (groups * SHARE_UNITS) for share in CHUNK_SHARES]
    fixed = groups * sum(chunk_tiles)
    steps = -(-(blocks - fixed) // (groups * LOOP_TILES))
    back_chunks = [chunk_tiles[:-1], chunk_tiles[-1:]]
    table = jnp.asarray(
        tile_table(groups, coefs, back_chunks + [[LOOP_TILES]] * steps, blocks)
    )
    index, cells, offset = index_call(wet_mask)
    offsets = offset.reshape(-1)
    ends = offsets[SUB * lane_tiles : blocks + 1 : SUB * lane_tiles]

    def packed(first_tile, tiles, token, waited=()):
        params = jnp.stack([place[0], first_tile + token])
        *flows, token = pack_call(
            params, offset, index, base_flow, direction, groups, tiles, waited
        )
        return spread_out(flows), token[0, 0]

    def through(flows, token, weight):
        *back, token = friction_call(place + token, flows, coefs, weight)
        return spread_out(back), token[0, 0]

    flows = []
    tile = 0
    token = jnp.int32(0)
    for tiles in chunk_tiles[:-1]:
        flow, token = packed(tile, tiles, token)
        flows.append(flow)
        tile += groups * tiles

    loop_cells = groups * LOOP_TILES * LANES
    beyond = offsets[blocks] + token - fixed * LANES
    loops = jnp.maximum(beyond + loop_cells - 1, 0) // loop_cells

    def more(state):
        done, held = state
        flow, _ = packed(fixed + done * groups * LOOP_TILES, LOOP_TILES, 0)
        back, _ = through([flow], 0, 1)
        held = lax.dynamic_update_slice_in_dim(
            held, jnp.concatenate(back, axis=0)[None], done, 0
        )
        return done + 1, held

    rows = groups * piece_rows(LOOP_TILES, coefs)
    extra = jnp.zeros((steps, rows, LANES), jnp.float32)
    done, extra = lax.while_loop(lambda state: state[0] < loops, more, (jnp.int32(0), extra))

    token = token + jnp.minimum(done, 0)
    flows.append(packed(tile, chunk_tiles[-1], token)[0])
    above, below, slabs = halo(direction, wet_mask, water_depth, flows[0][1:] + flows[-1][:1])
    result, prepared = prepare_call(
        scalars, direction, wet_mask, water_depth, above, below, slabs
    )
    back, token = through(flows[:-1], prepared[0, 0], 1)
    backs = [back]
    back, token = through(flows[-1:], token, LATE_WEIGHT)
    backs.append(back)

    arrays = (wet_mask, drag_factor, cells)
    pieces = []
    back_rows = rows * steps
    back_rows += groups * sum(piece_rows(sum(several), coefs) for several in back_chunks)
    begin = jnp.int32(0)
    tile = 0
    for last, several in enumerate(back_chunks):
        pieces += backs[last]
        tile += groups * sum(several)
        if last:
            end = jnp.int32(row_blocks)
            pieces.append(extra.reshape(-1, LANES))
        else:
            end = jnp.sum((ends <= tile * LANES).astype(jnp.int32))
        first = jnp.stack([begin, place[0], end - begin, loops])
        result = finish_call(
            first, offset, table, scalars, arrays, list(pieces), back_rows, result, groups,
            (groups, -(-SUB * lane_tiles // chunk_tiles[-2])) if last else (0, 0),
        )
        begin = end
    return result


def solution(mesh):
    placed = (
        P(None, "freq", "lat", "lon"),
        P(None, "freq", "lat", "lon"),
        P("lat", "lon"),
        P("lat", "lon"),
        P("lat", "lon"),
    )
    return jax.shard_map(
        local, mesh=mesh, in_specs=placed, out_specs=P(None, "freq", "lat", "lon"), check_vma=False
    )
```

```python
import math

import jax
import jax.numpy as jnp
import ml_dtypes
import numpy as np
from jax import lax
from jax.experimental import pallas as pl
from jax.experimental.pallas import tpu as pltpu
from jax.sharding import PartitionSpec as P

NCON = 16
NTIME = 256
LANES = 128
SUB = 8

LINEAR_DRAG = 0.5
GRAVITY = 1.0
OMEGA_STEP = 0.25
SPEED_SOFT = 0.01
VMEM_BYTES = 48 * 1024 * 1024
CHUNK_SHARES = (16, 50, 31)
SHARE_UNITS = 128
LOOP_TILES = 8
PACK_COST = 16384
AHEAD = 4
LATE_WEIGHT = 2048


def split_table():
    sample = np.arange(NTIME)[:, None]
    harmonic = np.arange(1, NCON + 1)[None, :]
    phase = (sample * harmonic % NTIME) * (2.0 * math.pi / NTIME)
    table = np.stack([np.cos(phase), np.sin(phase)], axis=2).reshape(NTIME, 2 * NCON)
    table = table.astype(np.float32)
    high = table.astype(ml_dtypes.bfloat16)
    low = (table - high.astype(np.float32)).astype(ml_dtypes.bfloat16)
    return high, low


def split_value(value):
    high = value.astype(jnp.bfloat16)
    low = (value - high.astype(jnp.float32)).astype(jnp.bfloat16)
    return high, low


def friction_kernel(groups, coefs, chunk_tiles, place_ref, synth_ref, analyse_ref, *refs):
    parts = len(chunk_tiles)
    tiles = sum(chunk_tiles)
    out_refs, token_ref = refs[groups * parts : -1], refs[-1]
    token_ref[...] = jnp.zeros_like(token_ref)
    columns = 2 * NCON

    def block(flow_refs, first, at, count):
        tile = first + at
        loaded = []
        for source in range(groups):
            several = [flow_refs[source][at + i] for i in range(count)]
            loaded.append(jnp.concatenate(several, axis=1))
        series = []
        for field in range(4):
            rows = slice(field * coefs, (field + 1) * coefs)
            values = jnp.concatenate([part[rows] for part in loaded], axis=0)
            high, low = split_value(values)
            operand = jnp.concatenate([high, low, high], axis=0)
            series.append(
                jnp.dot(synth_ref[0], operand, preferred_element_type=jnp.float32)
            )
        base_east, base_north, step_east, step_north = series
        square = base_east * base_east + base_north * base_north + SPEED_SOFT
        inverse = lax.rsqrt(square)
        speed = square * inverse
        projected = (base_east * step_east + base_north * step_north) * inverse
        forces = (
            speed * step_east + base_east * projected,
            speed * step_north + base_north * projected,
        )
        mean = jnp.sum(speed, axis=0, keepdims=True) * (1.0 / NTIME)
        analysed = []
        for force in forces:
            high, low = split_value(force)
            both = jnp.dot(analyse_ref[0], high, preferred_element_type=jnp.float32)
            rest = jnp.dot(
                analyse_ref[0, :columns, :], low, preferred_element_type=jnp.float32
            )
            analysed.append(both[:columns] + both[columns:] + rest)
        for part in range(count):
            lanes = slice(part * LANES, (part + 1) * LANES)
            for target in range(groups):
                rows = slice(target * coefs, (target + 1) * coefs)
                values = jnp.concatenate(
                    [analysed[0][rows, lanes], analysed[1][rows, lanes]], axis=0
                )
                start = pl.multiple_of((tile + part) * 2 * coefs, SUB)
                out_refs[target][pl.ds(start, 2 * coefs), :] = values
                at = tiles * 2 * coefs + tile + part
                out_refs[target][pl.ds(at, 1), :] = mean[:, lanes]

    first = 0
    for part, here in enumerate(chunk_tiles):
        flow_refs = refs[part * groups : (part + 1) * groups]

        def body(step, carry, flow_refs=flow_refs, first=first):
            block(flow_refs, first, step * 2, 2)
            return carry

        lax.fori_loop(0, here // 2, body, 0)
        if here % 2:
            block(flow_refs, first, here - 1, 1)
        first += here


def placed_tables(groups, coefs):
    high, low = split_table()
    synth, analyse = [], []
    for member in range(groups):
        sources = [(member - step) % groups for step in range(groups)]
        targets = [(member + step) % groups for step in range(groups)]
        source = np.concatenate([np.arange(coefs) + m * coefs for m in sources])
        target = np.concatenate([np.arange(coefs) + m * coefs for m in targets])
        synth.append(np.concatenate([high[:, source], high[:, source], low[:, source]], axis=1))
        both = np.concatenate([high[:, target].T, low[:, target].T], axis=0)
        analyse.append((both.astype(np.float32) * (2.0 / NTIME)).astype(ml_dtypes.bfloat16))
    return np.stack(synth), np.stack(analyse)


def piece_rows(tiles, coefs):
    return tiles * 2 * coefs + -(-tiles // SUB) * SUB


def friction_call(place, flows, coefs, weight):
    groups = len(flows[0])
    chunk_tiles = [chunk[0].shape[0] for chunk in flows]
    tiles = sum(chunk_tiles)
    synth, analyse = placed_tables(groups, coefs)
    cells = groups * tiles * LANES
    out_shape = (piece_rows(tiles, coefs), LANES)
    grid_spec = pltpu.PrefetchScalarGridSpec(
        num_scalar_prefetch=1,
        grid=(1,),
        in_specs=[
            pl.BlockSpec((1,) + synth.shape[1:], lambda i, place: (place[0], 0, 0)),
            pl.BlockSpec((1,) + analyse.shape[1:], lambda i, place: (place[0], 0, 0)),
        ]
        + [
            pl.BlockSpec(block.shape, lambda i, place: (0, 0, 0))
            for chunk in flows
            for block in chunk
        ],
        out_specs=[pl.BlockSpec(out_shape, lambda i, place: (0, 0))] * groups
        + [pl.BlockSpec((SUB, LANES), lambda i, place: (0, 0))],
    )
    return pl.pallas_call(
        lambda *refs: friction_kernel(groups, coefs, chunk_tiles, *refs),
        out_shape=[jax.ShapeDtypeStruct(out_shape, jnp.float32)] * groups
        + [jax.ShapeDtypeStruct((SUB, LANES), jnp.int32)],
        grid_spec=grid_spec,
        compiler_params=pltpu.CompilerParams(vmem_limit_bytes=VMEM_BYTES),
        cost_estimate=pl.CostEstimate(
            flops=cells * NTIME * weight, bytes_accessed=0, transcendentals=0
        ),
        name="friction",
    )(place, jnp.asarray(synth), jnp.asarray(analyse), *[b for chunk in flows for b in chunk])


def index_kernel(wet_ref, index_ref, place_ref, offset_ref, scratch):
    blocks = scratch.shape[0]
    rows, cols = wet_ref.shape
    at = 0
    for row in range(0, rows, SUB):
        for col in range(0, cols, LANES):
            part = wet_ref[row : row + SUB, col : col + LANES]
            scratch[at : at + SUB, :] = jnp.where(part != 0, 1.0, 0.0)
            at += SUB
    wet = scratch[...].astype(jnp.bfloat16)
    earlier = lax.broadcasted_iota(jnp.int32, (LANES, LANES), 0)
    later = lax.broadcasted_iota(jnp.int32, (LANES, LANES), 1)
    before = jnp.where(earlier < later, 1.0, 0.0).astype(jnp.bfloat16)
    ones = jnp.ones((LANES, LANES), jnp.bfloat16)
    rank = jnp.dot(wet, before, preferred_element_type=jnp.float32)
    count = jnp.dot(wet, ones, preferred_element_type=jnp.float32)
    low = lax.broadcasted_iota(jnp.int32, (blocks, blocks), 0)
    high = lax.broadcasted_iota(jnp.int32, (blocks, blocks), 1)
    summing = jnp.where(high < low, 1.0, 0.0).astype(jnp.bfloat16)
    offset = jnp.dot(summing, count.astype(jnp.bfloat16), preferred_element_type=jnp.float32)
    lane = lax.broadcasted_iota(jnp.int32, (blocks, LANES), 1)
    rank = rank.astype(jnp.int32)
    held = jnp.where(scratch[...] > 0.5, lane + LANES * (lane - rank), 0)
    for bit in range(7):
        step = 1 << bit
        coming = pltpu.roll(held, LANES - step, 1)
        moves = (coming >> (7 + bit)) & 1
        stays = 1 - ((held >> (7 + bit)) & 1)
        held = jnp.where(moves == 1, coming, held * stays)
    source = held & (LANES - 1)
    shift = offset.astype(jnp.int32) & (LANES - 1)
    index_ref[...] = jnp.take_along_axis(
        source, (lane - shift) & (LANES - 1), axis=1, mode="promise_in_bounds"
    )
    place_ref[...] = shift + rank
    eye = jnp.where(earlier == later, 1.0, 0.0)
    cubes = offset.reshape(blocks // LANES, LANES, LANES)
    table = jnp.sum(cubes * eye[None], axis=1)
    total = offset[blocks - 1 : blocks] + count[blocks - 1 : blocks]
    offset_ref[: blocks // LANES, :] = table.astype(jnp.int32)
    offset_ref[blocks // LANES : blocks // LANES + 1, :] = total.astype(jnp.int32)


def index_call(wet_mask):
    rows, cols = wet_mask.shape
    blocks = rows * cols // LANES
    table = -(-(blocks // LANES + 1) // SUB) * SUB
    return pl.pallas_call(
        index_kernel,
        out_shape=[
            jax.ShapeDtypeStruct((blocks, LANES), jnp.int32),
            jax.ShapeDtypeStruct((blocks, LANES), jnp.int32),
            jax.ShapeDtypeStruct((table, LANES), jnp.int32),
        ],
        scratch_shapes=[pltpu.VMEM((blocks, LANES), jnp.float32)],
        compiler_params=pltpu.CompilerParams(vmem_limit_bytes=VMEM_BYTES),
        name="index",
    )(wet_mask)


def pack_kernel(groups, coefs, tiles, waited, params_ref, offset_ref, index_ref, base_ref, step_ref, *refs):
    refs = refs[waited:]
    out_refs = refs[:groups]
    token_ref, held, stage, in_sem, out_sem = refs[groups:]
    token_ref[...] = jnp.zeros_like(token_ref)
    lane_tiles = held.shape[1]
    per_block = SUB * lane_tiles
    row_blocks = index_ref.shape[0] // per_block
    count = groups * tiles
    first_tile = params_ref[1]
    low = first_tile * LANES
    high = low + count * LANES

    def offset_of(block):
        return offset_ref[block >> 7, block & (LANES - 1)]

    begin = jnp.int32(0)
    end = jnp.int32(0)
    for block in range(row_blocks):
        begin += (offset_of((block + 1) * per_block) <= low).astype(jnp.int32)
        end += (offset_of(block * per_block) < high).astype(jnp.int32)
    end = jnp.maximum(end, begin)

    def copies(block):
        slot = lax.rem(block, AHEAD)
        rows = pl.ds(pl.multiple_of(block * SUB, SUB), SUB)
        started = []
        for lane_tile in range(lane_tiles):
            lanes = pl.ds(lane_tile * LANES, LANES)
            landing = held.at[slot, lane_tile]
            started.append(
                pltpu.make_async_copy(
                    base_ref.at[:, :, rows, lanes],
                    landing.at[pl.ds(0, 2)],
                    in_sem.at[slot, 2 * lane_tile],
                )
            )
            started.append(
                pltpu.make_async_copy(
                    step_ref.at[pl.ds(1, 2), :, rows, lanes],
                    landing.at[pl.ds(2, 2)],
                    in_sem.at[slot, 2 * lane_tile + 1],
                )
            )
        return started

    for step in range(AHEAD - 1):

        @pl.when(begin + step < end)
        def _():
            for copy in copies(begin + step):
                copy.start()

    lane = lax.broadcasted_iota(jnp.int32, (coefs, LANES), 1)

    def place_of(offset):
        return jnp.clip((offset >> 7) - first_tile + 1, 0, count + 1)

    def body(block, current):
        @pl.when(block + AHEAD - 1 < end)
        def _():
            for copy in copies(block + AHEAD - 1):
                copy.start()

        for copy in copies(block):
            copy.wait()
        slot = lax.rem(block, AHEAD)
        for lane_tile in range(lane_tiles):
            fields = [
                held.at[slot, lane_tile, field].reshape(coefs * SUB, LANES) for field in range(4)
            ]
            start = block * per_block + lane_tile * SUB
            index = index_ref[pl.ds(pl.multiple_of(start, SUB), SUB), :]
            following = offset_of(start)
            for r in range(SUB):
                offset = following
                following = offset_of(start + r + 1)
                shift = offset & (LANES - 1)
                crossing = (following >> 7) > (offset >> 7)
                source = jnp.broadcast_to(index[r : r + 1], (coefs, LANES))
                to = place_of(offset)
                renewed = []
                for field in range(4):
                    got = jnp.take_along_axis(
                        fields[field][pl.ds(r, coefs, stride=SUB), :],
                        source,
                        axis=1,
                        mode="promise_in_bounds",
                    )
                    full = jnp.where(lane >= shift, got, current[field])
                    stage[to, field * coefs : (field + 1) * coefs, :] = full
                    renewed.append(jnp.where(crossing, got, full))
                current = tuple(renewed)
        return current

    zero = jnp.zeros((coefs, LANES), jnp.float32)
    current = lax.fori_loop(begin, end, body, (zero,) * 4)
    last = place_of(offset_of(end * per_block))
    for field in range(4):
        stage[last, field * coefs : (field + 1) * coefs, :] = current[field]
    outs = []
    for step in range(groups):
        member = lax.rem(params_ref[0] + step, groups)
        outs.append(
            pltpu.make_async_copy(
                stage.at[pl.ds(1 + member * tiles, tiles)], out_refs[step], out_sem.at[step]
            )
        )
    for copy in outs:
        copy.start()
    for copy in outs:
        copy.wait()


def pack_call(params, offset, index, base_flow, direction, groups, tiles, waited):
    coefs, _, columns = direction.shape[1:]
    shape = (tiles, 4 * coefs, LANES)
    anywhere = pl.BlockSpec(memory_space=pl.ANY)
    grid_spec = pltpu.PrefetchScalarGridSpec(
        num_scalar_prefetch=2,
        grid=(1,),
        in_specs=[pl.BlockSpec(index.shape, lambda i, p, o: (0, 0))]
        + [anywhere] * (2 + len(waited)),
        out_specs=[anywhere] * groups + [pl.BlockSpec((SUB, LANES), lambda i, p, o: (0, 0))],
        scratch_shapes=[
            pltpu.VMEM((AHEAD, columns // LANES, 4, coefs, SUB, LANES), jnp.float32),
            pltpu.VMEM((groups * tiles + 2, 4 * coefs, LANES), jnp.float32),
            pltpu.SemaphoreType.DMA((AHEAD, 2 * (columns // LANES))),
            pltpu.SemaphoreType.DMA((groups,)),
        ],
    )
    return pl.pallas_call(
        lambda *refs: pack_kernel(groups, coefs, tiles, len(waited), *refs),
        out_shape=[jax.ShapeDtypeStruct(shape, jnp.float32)] * groups
        + [jax.ShapeDtypeStruct((SUB, LANES), jnp.int32)],
        grid_spec=grid_spec,
        compiler_params=pltpu.CompilerParams(vmem_limit_bytes=VMEM_BYTES),
        cost_estimate=pl.CostEstimate(
            flops=0, bytes_accessed=groups * tiles * coefs * PACK_COST, transcendentals=0
        ),
        name="pack",
    )(params, offset, index, base_flow, direction, *waited)


def prepare_kernel(coefs, scalars_ref, *refs):
    (here_ref, prev_ref, next_ref, wet_ref, wet_prev_ref, wet_next_ref, depth_ref, depth_prev_ref,
     above_ref, below_ref, slab_ref, out_ref, token_ref) = refs
    token_ref[...] = jnp.zeros_like(token_ref)
    columns = here_ref.shape[-1]
    row_block = pl.program_id(0)
    at_top = row_block == 0
    at_bottom = row_block == pl.num_programs(0) - 1
    wet = wet_ref[...].astype(jnp.float32)
    wet_prev = wet_prev_ref[SUB - 1 :, :].astype(jnp.float32)
    wet_next = wet_next_ref[:1, :].astype(jnp.float32)
    depth = depth_ref[...]
    depth_prev = depth_prev_ref[SUB - 1 :, :]
    lane = lax.broadcasted_iota(jnp.int32, (SUB, columns), 1)
    sub = lax.broadcasted_iota(jnp.int32, (SUB, columns), 0)
    row = (row_block * SUB + sub).astype(jnp.float32)
    rotation = 0.5 + (row + scalars_ref[0] + 0.5) * scalars_ref[1]

    def wide(slab):
        return jnp.concatenate([slab] * (columns // LANES), axis=1)

    def west(value, slab):
        return jnp.where(lane == 0, wide(slab), pltpu.roll(value, 1, 1))

    def east_of(value, slab):
        return jnp.where(lane == columns - 1, wide(slab), pltpu.roll(value, columns - 1, 1))

    def above(value, edge):
        return jnp.where(sub == 0, edge, pltpu.roll(value, 1, 0))

    def below(value, edge):
        return jnp.where(sub == SUB - 1, edge, pltpu.roll(value, SUB - 1, 0))

    for k in range(coefs // 2):
        angular = scalars_ref[2 + k]
        inverse_angular = 1.0 / (angular + jnp.zeros((SUB, columns), jnp.float32))
        planes = [
            [here_ref[p, 2 * k + part] * wet for p in range(3)] for part in range(2)
        ]
        for part in range(2):
            c = 2 * k + part
            height, east, north = planes[part]
            other = planes[1 - part]
            signed = angular if part == 0 else -angular
            east_flux = depth * east
            north_flux = depth * north
            north_edge = prev_ref[0, c, SUB - 1 :, :] * wet_prev
            flux_edge = jnp.where(at_top, above_ref[1, c : c + 1], north_edge * depth_prev)
            north_edge = jnp.where(at_top, above_ref[0, c : c + 1], north_edge)
            height_edge = jnp.where(
                at_bottom, below_ref[0, c : c + 1], next_ref[0, c, :1, :] * wet_next
            )
            east_edge = jnp.where(
                at_bottom, below_ref[1, c : c + 1], next_ref[1, c, :1, :] * wet_next
            )
            north_up = above(north, north_edge)
            east_down = below(east, east_edge)
            res_height = (
                signed * other[0]
                + east_flux
                - west(east_flux, slab_ref[2, c])
                + north_flux
                - above(north_flux, flux_edge)
            )
            north_mean = 0.25 * (
                north
                + east_of(north, slab_ref[4, c])
                + north_up
                + east_of(north_up, slab_ref[5, c])
            )
            east_mean = 0.25 * (
                east
                + west(east, slab_ref[0, c])
                + east_down
                + west(east_down, slab_ref[1, c])
            )
            res_east = (
                signed * other[1]
                + LINEAR_DRAG * east
                - rotation * north_mean
                + GRAVITY * (east_of(height, slab_ref[3, c]) - height)
            )
            res_north = (
                signed * other[2]
                + LINEAR_DRAG * north
                + rotation * east_mean
                + GRAVITY * (below(height, height_edge) - height)
            )
            if part == 0:
                out_ref[0, c + 1] = res_height * wet * inverse_angular
            else:
                out_ref[0, c - 1] = -res_height * wet * inverse_angular
            out_ref[1, c] = res_east * wet
            out_ref[2, c] = res_north * wet


def prepare_call(scalars, direction, wet_mask, depth, above, below, slabs):
    _, coefs, rows, columns = direction.shape
    last = rows // SUB - 1

    def before(i):
        return jnp.maximum(i - 1, 0)

    def after(i):
        return jnp.minimum(i + 1, last)

    planes = pl.BlockSpec((3, coefs, SUB, columns), lambda i: (0, 0, i, 0))
    flat = (SUB, columns)
    edge = pl.BlockSpec((2, coefs, columns), lambda i: (0, 0, 0))
    return pl.pallas_call(
        lambda *refs: prepare_kernel(coefs, *refs),
        out_shape=[
            jax.ShapeDtypeStruct(direction.shape, jnp.float32),
            jax.ShapeDtypeStruct((SUB, LANES), jnp.int32),
        ],
        grid=(rows // SUB,),
        in_specs=[
            pl.BlockSpec(memory_space=pltpu.SMEM),
            planes,
            pl.BlockSpec((1, coefs, SUB, columns), lambda i: (2, 0, before(i), 0)),
            pl.BlockSpec((2, coefs, SUB, columns), lambda i: (0, 0, after(i), 0)),
            pl.BlockSpec(flat, lambda i: (i, 0)),
            pl.BlockSpec(flat, lambda i: (before(i), 0)),
            pl.BlockSpec(flat, lambda i: (after(i), 0)),
            pl.BlockSpec(flat, lambda i: (i, 0)),
            pl.BlockSpec(flat, lambda i: (before(i), 0)),
            edge,
            edge,
            pl.BlockSpec((6, coefs, SUB, LANES), lambda i: (0, 0, i, 0)),
        ],
        out_specs=[planes, pl.BlockSpec((SUB, LANES), lambda i: (0, 0))],
        compiler_params=pltpu.CompilerParams(vmem_limit_bytes=VMEM_BYTES),
        cost_estimate=pl.CostEstimate(
            flops=rows * columns * coefs, bytes_accessed=0, transcendentals=0
        ),
        name="prepare",
    )(
        scalars, direction, direction, direction, wet_mask, wet_mask, wet_mask, depth, depth,
        above, below, slabs,
    )


def finish_kernel(coefs, lane_tiles, row_block, first_ref, offset_ref, table_ref, scalars_ref, back, spread_ref, refs):
    wet_ref, drag_ref, cell_ref, east_ref, north_ref, east_out, north_out = refs
    columns = lane_tiles * LANES
    wet = wet_ref[...].astype(jnp.float32)
    drag = drag_ref[...]
    sub = lax.broadcasted_iota(jnp.int32, (SUB, columns), 0)
    row = (row_block * SUB + sub).astype(jnp.float32)
    rotation = 0.5 + (row + scalars_ref[0] + 0.5) * scalars_ref[1]

    def gathered(here, after, index, over):
        first = jnp.take_along_axis(here, index, axis=1, mode="promise_in_bounds")
        second = jnp.take_along_axis(after, index, axis=1, mode="promise_in_bounds")
        return jnp.where(over, second, first)

    speed = []
    for lane_tile in range(lane_tiles):
        places = cell_ref[lane_tile * SUB : (lane_tile + 1) * SUB, :]
        turned = spread_ref.at[lane_tile].reshape(2 * coefs * SUB, LANES)
        speeds = [[], []]
        for r in range(SUB):
            at = (row_block * lane_tiles + lane_tile) * SUB + r
            tile = offset_ref[at >> 7, at & (LANES - 1)] >> 7
            found = []
            for which in range(2):
                start = pl.multiple_of(table_ref[first_ref[1] * 2, tile + which], SUB)
                found.append(back[pl.ds(start, 2 * coefs), :])
                start = table_ref[first_ref[1] * 2 + 1, tile + which]
                speeds[which].append(back[pl.ds(start, 1), :])
            place = jnp.broadcast_to(places[r : r + 1], (2 * coefs, LANES))
            turned[pl.ds(r, 2 * coefs, stride=SUB), :] = gathered(
                found[0], found[1], place & (LANES - 1), place >= LANES
            )
        speed.append(
            gathered(
                jnp.concatenate(speeds[0], axis=0),
                jnp.concatenate(speeds[1], axis=0),
                places & (LANES - 1),
                places >= LANES,
            )
        )
    is_wet = wet > 0.5
    friction = [
        jnp.where(
            is_wet,
            jnp.concatenate([spread_ref[n, index] for n in range(lane_tiles)], axis=1) * drag,
            0.0,
        )
        for index in range(2 * coefs)
    ]
    speed = jnp.where(is_wet, jnp.concatenate(speed, axis=1), 0.0)
    real_rate = drag * speed + LINEAR_DRAG
    for k in range(coefs // 2):
        angular = scalars_ref[2 + k]
        cos_at, sin_at = 2 * k, 2 * k + 1
        det_real = real_rate * real_rate - angular * angular + rotation * rotation
        det_imag = 2.0 * real_rate * angular
        inverse_norm = 1.0 / (det_real * det_real + det_imag * det_imag)
        inv_real = det_real * inverse_norm
        inv_imag = -det_imag * inverse_norm
        east_re = east_ref[0, cos_at] + friction[cos_at]
        east_im = -(east_ref[0, sin_at] + friction[sin_at])
        north_re = north_ref[0, cos_at] + friction[coefs + cos_at]
        north_im = -(north_ref[0, sin_at] + friction[coefs + sin_at])
        num_east_re = real_rate * east_re - angular * east_im + rotation * north_re
        num_east_im = real_rate * east_im + angular * east_re + rotation * north_im
        num_north_re = -rotation * east_re + real_rate * north_re - angular * north_im
        num_north_im = -rotation * east_im + real_rate * north_im + angular * north_re
        east_out[0, cos_at] = num_east_re * inv_real - num_east_im * inv_imag
        east_out[0, sin_at] = -(num_east_re * inv_imag + num_east_im * inv_real)
        north_out[0, cos_at] = num_north_re * inv_real - num_north_im * inv_imag
        north_out[0, sin_at] = -(num_north_re * inv_imag + num_north_im * inv_real)


def finish_call(first, offset, table, scalars, arrays, pieces, rows, result, groups, early):
    _, coefs, _, columns = result.shape
    lane_tiles = columns // LANES

    def kernel(first_ref, offset_ref, table_ref, scalars_ref, *refs):
        array_refs = refs[:3]
        piece_refs = refs[4:-4]
        out_ref, back, spread_ref, sem = refs[-4:]
        first = first_ref[0]
        count = first_ref[2]

        @pl.when(count > 0)
        def _():
            at = 0
            copies = []
            for n, piece in enumerate(piece_refs):
                rows = piece.shape[0]
                copy = pltpu.make_async_copy(piece, back.at[pl.ds(at, rows)], sem.at[n])
                needed = True
                if n < early[0]:
                    source = lax.rem(first_ref[1] + groups - n % groups, groups)
                    needed = source >= groups - early[1]
                elif n >= early[0] + groups:
                    needed = first_ref[3] > 0
                copies.append((copy, needed))
                at += rows

            def each(act):
                for copy, needed in copies:
                    if needed is True:
                        act(copy)
                    else:
                        pl.when(needed)(lambda copy=copy: act(copy))

            each(lambda copy: copy.start())

            def body(*block_refs):
                @pl.when(pl.program_id(0) == 0)
                def _():
                    each(lambda copy: copy.wait())

                finish_kernel(
                    coefs, lane_tiles, first + pl.program_id(0), first_ref, offset_ref,
                    table_ref, scalars_ref, back, spread_ref, block_refs,
                )

            deep = pl.Buffered(3)

            def flat(rows, width):
                return pl.BlockSpec(
                    (rows, width), lambda i: (first + i, 0), pipeline_mode=deep
                )

            def plane(p, mode):
                return pl.BlockSpec(
                    (1, coefs, SUB, columns), lambda i: (p, 0, first + i, 0), pipeline_mode=mode
                )

            pltpu.emit_pipeline(
                body,
                grid=(count,),
                in_specs=[
                    flat(SUB, columns),
                    flat(SUB, columns),
                    flat(SUB * lane_tiles, LANES),
                    plane(1, deep),
                    plane(2, deep),
                ],
                out_specs=[plane(1, None), plane(2, None)],
            )(*array_refs, out_ref, out_ref, out_ref, out_ref)

    anywhere = pl.BlockSpec(memory_space=pl.ANY)
    scalar = pl.BlockSpec(memory_space=pltpu.SMEM)
    operands = [first, offset, table, scalars] + list(arrays) + [result] + pieces
    return pl.pallas_call(
        kernel,
        out_shape=jax.ShapeDtypeStruct(result.shape, jnp.float32),
        in_specs=[scalar] * 4 + [anywhere] * (4 + len(pieces)),
        out_specs=anywhere,
        scratch_shapes=[
            pltpu.VMEM((rows, LANES), jnp.float32),
            pltpu.VMEM((lane_tiles, 2 * coefs, SUB, LANES), jnp.float32),
            pltpu.SemaphoreType.DMA((len(pieces),)),
        ],
        input_output_aliases={7: 0},
        compiler_params=pltpu.CompilerParams(vmem_limit_bytes=VMEM_BYTES),
        cost_estimate=pl.CostEstimate(
            flops=0, bytes_accessed=8 * SUB * columns * coefs * 36, transcendentals=0
        ),
        name="finish",
    )(*operands)


def shifted(block, axis, step, wrap):
    count = lax.axis_size(axis)
    pairs = [
        (i, (i + step) % count) for i in range(count) if wrap or 0 <= i + step < count
    ]
    return lax.ppermute(block, axis, pairs)


def edge_kernel(coefs, east_ref, height_ref, north_ref, last_ref, first_ref, wet_ref, depth_ref, *refs):
    up_ref, down_ref, right_ref, left_ref = refs[-4:]
    rows, columns = wet_ref.shape
    wet = wet_ref[...].astype(jnp.float32)
    end = slice(columns - LANES, columns)
    wet_end = wet[:, end]
    wet_start = wet[:, :LANES]
    depth_end = depth_ref[:, end]
    wet_last = wet[rows - 1 :, :]
    depth_last = depth_ref[rows - 1 :, :]
    for c in range(coefs):
        at = slice(c, c + 1)
        north_row = last_ref[0, c, SUB - 1 :, :] * wet_last
        up_ref[0, at, :] = north_row
        up_ref[1, at, :] = north_row * depth_last
        down_ref[0, at, :] = first_ref[0, c, :1, :] * wet[:1, :]
        down_ref[1, at, :] = first_ref[1, c, :1, :] * wet[:1, :]
        east = east_ref[0, c] * wet_end
        right_ref[0, at, :] = jnp.transpose(east)[LANES - 1 :, :]
        right_ref[1, at, :] = jnp.transpose(east * depth_end)[LANES - 1 :, :]
        left_ref[0, at, :] = jnp.transpose(height_ref[0, c] * wet_start)[:1, :]
        left_ref[1, at, :] = jnp.transpose(north_ref[0, c] * wet_start)[:1, :]


def edge_call(direction, wet_mask, depth, waited):
    _, coefs, rows, columns = direction.shape
    last_tile = columns // LANES - 1
    last_block = rows // SUB - 1
    tall = (1, coefs, rows, LANES)
    whole = pl.BlockSpec((rows, columns), lambda i: (0, 0))
    row_out = (2, coefs, columns)
    col_out = (2, coefs, rows)
    shapes = [row_out, row_out, col_out, col_out]
    return pl.pallas_call(
        lambda *refs: edge_kernel(coefs, *refs),
        out_shape=[jax.ShapeDtypeStruct(shape, jnp.float32) for shape in shapes],
        grid=(1,),
        in_specs=[
            pl.BlockSpec(tall, lambda i: (1, 0, 0, last_tile)),
            pl.BlockSpec(tall, lambda i: (0, 0, 0, 0)),
            pl.BlockSpec(tall, lambda i: (2, 0, 0, 0)),
            pl.BlockSpec((1, coefs, SUB, columns), lambda i: (2, 0, last_block, 0)),
            pl.BlockSpec((2, coefs, SUB, columns), lambda i: (0, 0, 0, 0)),
            whole,
            whole,
        ]
        + [pl.BlockSpec(memory_space=pl.ANY)] * len(waited),
        out_specs=[pl.BlockSpec(shape, lambda i: (0, 0, 0)) for shape in shapes],
        compiler_params=pltpu.CompilerParams(vmem_limit_bytes=VMEM_BYTES),
        cost_estimate=pl.CostEstimate(
            flops=rows * columns, bytes_accessed=0, transcendentals=0
        ),
        name="edges",
    )(direction, direction, direction, direction, direction, wet_mask, depth, *waited)


def halo(direction, wet_mask, depth, waited):
    up, down, right, left = edge_call(direction, wet_mask, depth, waited)
    above = shifted(up, "lat", 1, False)
    below = shifted(down, "lat", -1, False)
    east_below = jnp.concatenate([right[0, :, 1:], below[1, :, -1:]], axis=1)
    north_above = jnp.concatenate([above[0, :, :1], left[1, :, :-1]], axis=1)
    to_right = jnp.stack([right[0], east_below, right[1]])
    to_left = jnp.stack([left[0], left[1], north_above])
    cols = jnp.concatenate(
        [shifted(to_right, "lon", 1, True), shifted(to_left, "lon", -1, True)], axis=0
    )
    slabs = jnp.broadcast_to(cols[:, :, :, None], cols.shape + (LANES,))
    return above, below, slabs


def spread_out(blocks):
    return [
        block if step == 0 else shifted(block, "freq", step, True)
        for step, block in enumerate(blocks)
    ]


def tile_table(groups, coefs, back_chunks, blocks):
    table = np.zeros((2 * groups, blocks + LANES), np.int32)
    for member in range(groups):
        tile = 0
        row = 0
        for chunk_tiles in back_chunks:
            together = sum(chunk_tiles)
            before = 0
            for tiles in chunk_tiles:
                for band in range(groups):
                    start = row + (member - band) % groups * piece_rows(together, coefs)
                    for i in range(before, before + tiles):
                        if tile < blocks:
                            table[2 * member, tile] = start + i * 2 * coefs
                            table[2 * member + 1, tile] = start + together * 2 * coefs + i
                        tile += 1
                before += tiles
            row += groups * piece_rows(together, coefs)
    return table


def local(direction, base_flow, water_depth, drag_factor, wet_mask):
    coefs, tile_rows, tile_cols = direction.shape[1:]
    groups = lax.axis_size("freq")
    member = lax.axis_index("freq")
    lat_place = lax.axis_index("lat")
    total_rows = tile_rows * lax.axis_size("lat")
    lane_tiles = tile_cols // LANES
    angular = OMEGA_STEP * (
        member * (coefs // 2) + jnp.arange(coefs // 2, dtype=jnp.int32) + 1
    ).astype(jnp.float32)
    row_start = (lat_place * tile_rows).astype(jnp.float32)
    scalars = jnp.concatenate(
        [jnp.stack([row_start, jnp.float32(1.0 / total_rows)]), angular]
    )
    place = jnp.reshape(member, (1,)).astype(jnp.int32)
    blocks = tile_rows * lane_tiles
    row_blocks = tile_rows // SUB
    chunk_tiles = [share * blocks // (groups * SHARE_UNITS) for share in CHUNK_SHARES]
    fixed = groups * sum(chunk_tiles)
    steps = -(-(blocks - fixed) // (groups * LOOP_TILES))
    back_chunks = [chunk_tiles[:-1], chunk_tiles[-1:]]
    table = jnp.asarray(
        tile_table(groups, coefs, back_chunks + [[LOOP_TILES]] * steps, blocks)
    )
    index, cells, offset = index_call(wet_mask)
    offsets = offset.reshape(-1)
    ends = offsets[SUB * lane_tiles : blocks + 1 : SUB * lane_tiles]

    def packed(first_tile, tiles, token, waited=()):
        params = jnp.stack([place[0], first_tile + token])
        *flows, token = pack_call(
            params, offset, index, base_flow, direction, groups, tiles, waited
        )
        return spread_out(flows), token[0, 0]

    def through(flows, token, weight):
        *back, token = friction_call(place + token, flows, coefs, weight)
        return spread_out(back), token[0, 0]

    flows = []
    tile = 0
    token = jnp.int32(0)
    for tiles in chunk_tiles[:-1]:
        flow, token = packed(tile, tiles, token)
        flows.append(flow)
        tile += groups * tiles

    loop_cells = groups * LOOP_TILES * LANES
    beyond = offsets[blocks] + token - fixed * LANES
    loops = jnp.maximum(beyond + loop_cells - 1, 0) // loop_cells

    def more(state):
        done, held = state
        flow, _ = packed(fixed + done * groups * LOOP_TILES, LOOP_TILES, 0)
        back, _ = through([flow], 0, 1)
        held = lax.dynamic_update_slice_in_dim(
            held, jnp.concatenate(back, axis=0)[None], done, 0
        )
        return done + 1, held

    rows = groups * piece_rows(LOOP_TILES, coefs)
    extra = jnp.zeros((steps, rows, LANES), jnp.float32)
    done, extra = lax.while_loop(lambda state: state[0] < loops, more, (jnp.int32(0), extra))

    token = token + jnp.minimum(done, 0)
    flows.append(packed(tile, chunk_tiles[-1], token)[0])
    above, below, slabs = halo(direction, wet_mask, water_depth, flows[0][1:] + flows[-1][:1])
    result, prepared = prepare_call(
        scalars, direction, wet_mask, water_depth, above, below, slabs
    )
    back, token = through(flows[:-1], prepared[0, 0], 1)
    backs = [back]
    back, token = through(flows[-1:], token, LATE_WEIGHT)
    backs.append(back)

    arrays = (wet_mask, drag_factor, cells)
    pieces = []
    back_rows = rows * steps
    back_rows += groups * sum(piece_rows(sum(several), coefs) for several in back_chunks)
    begin = jnp.int32(0)
    tile = 0
    for last, several in enumerate(back_chunks):
        pieces += backs[last]
        tile += groups * sum(several)
        if last:
            end = jnp.int32(row_blocks)
            pieces.append(extra.reshape(-1, LANES))
        else:
            end = jnp.sum((ends <= tile * LANES).astype(jnp.int32))
        first = jnp.stack([begin, place[0], end - begin, loops])
        result = finish_call(
            first, offset, table, scalars, arrays, list(pieces), back_rows, result, groups,
            (groups, -(-SUB * lane_tiles // chunk_tiles[-2])) if last else (0, 0),
        )
        begin = end
    return result


def solution(mesh):
    placed = (
        P(None, "freq", "lat", "lon"),
        P(None, "freq", "lat", "lon"),
        P("lat", "lon"),
        P("lat", "lon"),
        P("lat", "lon"),
    )
    return jax.shard_map(
        local, mesh=mesh, in_specs=placed, out_specs=P(None, "freq", "lat", "lon"), check_vma=False
    )
```

```python
import math

import jax
import jax.numpy as jnp
import ml_dtypes
import numpy as np
from jax import lax
from jax.experimental import pallas as pl
from jax.experimental.pallas import tpu as pltpu
from jax.sharding import PartitionSpec as P

NCON = 16
NTIME = 256
LANES = 128
SUB = 8

LINEAR_DRAG = 0.5
GRAVITY = 1.0
OMEGA_STEP = 0.25
SPEED_SOFT = 0.01
VMEM_BYTES = 48 * 1024 * 1024
CHUNK_SHARES = (16, 46, 35)
SHARE_UNITS = 128
LOOP_TILES = 8
PACK_COST = 16384
AHEAD = 4
LATE_WEIGHT = 2048


def split_table():
    sample = np.arange(NTIME)[:, None]
    harmonic = np.arange(1, NCON + 1)[None, :]
    phase = (sample * harmonic % NTIME) * (2.0 * math.pi / NTIME)
    table = np.stack([np.cos(phase), np.sin(phase)], axis=2).reshape(NTIME, 2 * NCON)
    table = table.astype(np.float32)
    high = table.astype(ml_dtypes.bfloat16)
    low = (table - high.astype(np.float32)).astype(ml_dtypes.bfloat16)
    return high, low


def split_value(value):
    high = value.astype(jnp.bfloat16)
    low = (value - high.astype(jnp.float32)).astype(jnp.bfloat16)
    return high, low


def friction_kernel(groups, coefs, chunk_tiles, place_ref, synth_ref, analyse_ref, *refs):
    parts = len(chunk_tiles)
    tiles = sum(chunk_tiles)
    out_refs, token_ref = refs[groups * parts : -1], refs[-1]
    token_ref[...] = jnp.zeros_like(token_ref)
    columns = 2 * NCON

    def block(flow_refs, first, at, count):
        tile = first + at
        loaded = []
        for source in range(groups):
            several = [flow_refs[source][at + i] for i in range(count)]
            loaded.append(jnp.concatenate(several, axis=1))
        series = []
        for field in range(4):
            rows = slice(field * coefs, (field + 1) * coefs)
            values = jnp.concatenate([part[rows] for part in loaded], axis=0)
            high, low = split_value(values)
            operand = jnp.concatenate([high, low, high], axis=0)
            series.append(
                jnp.dot(synth_ref[0], operand, preferred_element_type=jnp.float32)
            )
        base_east, base_north, step_east, step_north = series
        square = base_east * base_east + base_north * base_north + SPEED_SOFT
        inverse = lax.rsqrt(square)
        speed = square * inverse
        projected = (base_east * step_east + base_north * step_north) * inverse
        forces = (
            speed * step_east + base_east * projected,
            speed * step_north + base_north * projected,
        )
        mean = jnp.sum(speed, axis=0, keepdims=True) * (1.0 / NTIME)
        analysed = []
        for force in forces:
            high, low = split_value(force)
            both = jnp.dot(analyse_ref[0], high, preferred_element_type=jnp.float32)
            rest = jnp.dot(
                analyse_ref[0, :columns, :], low, preferred_element_type=jnp.float32
            )
            analysed.append(both[:columns] + both[columns:] + rest)
        for part in range(count):
            lanes = slice(part * LANES, (part + 1) * LANES)
            for target in range(groups):
                rows = slice(target * coefs, (target + 1) * coefs)
                values = jnp.concatenate(
                    [analysed[0][rows, lanes], analysed[1][rows, lanes]], axis=0
                )
                start = pl.multiple_of((tile + part) * 2 * coefs, SUB)
                out_refs[target][pl.ds(start, 2 * coefs), :] = values
                at = tiles * 2 * coefs + tile + part
                out_refs[target][pl.ds(at, 1), :] = mean[:, lanes]

    first = 0
    for part, here in enumerate(chunk_tiles):
        flow_refs = refs[part * groups : (part + 1) * groups]

        def body(step, carry, flow_refs=flow_refs, first=first):
            block(flow_refs, first, step * 2, 2)
            return carry

        lax.fori_loop(0, here // 2, body, 0)
        if here % 2:
            block(flow_refs, first, here - 1, 1)
        first += here


def placed_tables(groups, coefs):
    high, low = split_table()
    synth, analyse = [], []
    for member in range(groups):
        sources = [(member - step) % groups for step in range(groups)]
        targets = [(member + step) % groups for step in range(groups)]
        source = np.concatenate([np.arange(coefs) + m * coefs for m in sources])
        target = np.concatenate([np.arange(coefs) + m * coefs for m in targets])
        synth.append(np.concatenate([high[:, source], high[:, source], low[:, source]], axis=1))
        both = np.concatenate([high[:, target].T, low[:, target].T], axis=0)
        analyse.append((both.astype(np.float32) * (2.0 / NTIME)).astype(ml_dtypes.bfloat16))
    return np.stack(synth), np.stack(analyse)


def piece_rows(tiles, coefs):
    return tiles * 2 * coefs + -(-tiles // SUB) * SUB


def friction_call(place, flows, coefs, weight):
    groups = len(flows[0])
    chunk_tiles = [chunk[0].shape[0] for chunk in flows]
    tiles = sum(chunk_tiles)
    synth, analyse = placed_tables(groups, coefs)
    cells = groups * tiles * LANES
    out_shape = (piece_rows(tiles, coefs), LANES)
    grid_spec = pltpu.PrefetchScalarGridSpec(
        num_scalar_prefetch=1,
        grid=(1,),
        in_specs=[
            pl.BlockSpec((1,) + synth.shape[1:], lambda i, place: (place[0], 0, 0)),
            pl.BlockSpec((1,) + analyse.shape[1:], lambda i, place: (place[0], 0, 0)),
        ]
        + [
            pl.BlockSpec(block.shape, lambda i, place: (0, 0, 0))
            for chunk in flows
            for block in chunk
        ],
        out_specs=[pl.BlockSpec(out_shape, lambda i, place: (0, 0))] * groups
        + [pl.BlockSpec((SUB, LANES), lambda i, place: (0, 0))],
    )
    return pl.pallas_call(
        lambda *refs: friction_kernel(groups, coefs, chunk_tiles, *refs),
        out_shape=[jax.ShapeDtypeStruct(out_shape, jnp.float32)] * groups
        + [jax.ShapeDtypeStruct((SUB, LANES), jnp.int32)],
        grid_spec=grid_spec,
        compiler_params=pltpu.CompilerParams(vmem_limit_bytes=VMEM_BYTES),
        cost_estimate=pl.CostEstimate(
            flops=cells * NTIME * weight, bytes_accessed=0, transcendentals=0
        ),
        name="friction",
    )(place, jnp.asarray(synth), jnp.asarray(analyse), *[b for chunk in flows for b in chunk])


def index_kernel(wet_ref, index_ref, place_ref, offset_ref, scratch):
    blocks = scratch.shape[0]
    rows, cols = wet_ref.shape
    at = 0
    for row in range(0, rows, SUB):
        for col in range(0, cols, LANES):
            part = wet_ref[row : row + SUB, col : col + LANES]
            scratch[at : at + SUB, :] = jnp.where(part != 0, 1.0, 0.0)
            at += SUB
    wet = scratch[...].astype(jnp.bfloat16)
    earlier = lax.broadcasted_iota(jnp.int32, (LANES, LANES), 0)
    later = lax.broadcasted_iota(jnp.int32, (LANES, LANES), 1)
    before = jnp.where(earlier < later, 1.0, 0.0).astype(jnp.bfloat16)
    ones = jnp.ones((LANES, LANES), jnp.bfloat16)
    rank = jnp.dot(wet, before, preferred_element_type=jnp.float32)
    count = jnp.dot(wet, ones, preferred_element_type=jnp.float32)
    low = lax.broadcasted_iota(jnp.int32, (blocks, blocks), 0)
    high = lax.broadcasted_iota(jnp.int32, (blocks, blocks), 1)
    summing = jnp.where(high < low, 1.0, 0.0).astype(jnp.bfloat16)
    offset = jnp.dot(summing, count.astype(jnp.bfloat16), preferred_element_type=jnp.float32)
    lane = lax.broadcasted_iota(jnp.int32, (blocks, LANES), 1)
    rank = rank.astype(jnp.int32)
    held = jnp.where(scratch[...] > 0.5, lane + LANES * (lane - rank), 0)
    for bit in range(7):
        step = 1 << bit
        coming = pltpu.roll(held, LANES - step, 1)
        moves = (coming >> (7 + bit)) & 1
        stays = 1 - ((held >> (7 + bit)) & 1)
        held = jnp.where(moves == 1, coming, held * stays)
    source = held & (LANES - 1)
    shift = offset.astype(jnp.int32) & (LANES - 1)
    index_ref[...] = jnp.take_along_axis(
        source, (lane - shift) & (LANES - 1), axis=1, mode="promise_in_bounds"
    )
    place_ref[...] = shift + rank
    eye = jnp.where(earlier == later, 1.0, 0.0)
    cubes = offset.reshape(blocks // LANES, LANES, LANES)
    table = jnp.sum(cubes * eye[None], axis=1)
    total = offset[blocks - 1 : blocks] + count[blocks - 1 : blocks]
    offset_ref[: blocks // LANES, :] = table.astype(jnp.int32)
    offset_ref[blocks // LANES : blocks // LANES + 1, :] = total.astype(jnp.int32)


def index_call(wet_mask):
    rows, cols = wet_mask.shape
    blocks = rows * cols // LANES
    table = -(-(blocks // LANES + 1) // SUB) * SUB
    return pl.pallas_call(
        index_kernel,
        out_shape=[
            jax.ShapeDtypeStruct((blocks, LANES), jnp.int32),
            jax.ShapeDtypeStruct((blocks, LANES), jnp.int32),
            jax.ShapeDtypeStruct((table, LANES), jnp.int32),
        ],
        scratch_shapes=[pltpu.VMEM((blocks, LANES), jnp.float32)],
        compiler_params=pltpu.CompilerParams(vmem_limit_bytes=VMEM_BYTES),
        name="index",
    )(wet_mask)


def pack_kernel(groups, coefs, tiles, waited, params_ref, offset_ref, index_ref, base_ref, step_ref, *refs):
    refs = refs[waited:]
    out_refs = refs[:groups]
    token_ref, held, stage, in_sem, out_sem = refs[groups:]
    token_ref[...] = jnp.zeros_like(token_ref)
    lane_tiles = held.shape[1]
    per_block = SUB * lane_tiles
    row_blocks = index_ref.shape[0] // per_block
    count = groups * tiles
    first_tile = params_ref[1]
    low = first_tile * LANES
    high = low + count * LANES

    def offset_of(block):
        return offset_ref[block >> 7, block & (LANES - 1)]

    begin = jnp.int32(0)
    end = jnp.int32(0)
    for block in range(row_blocks):
        begin += (offset_of((block + 1) * per_block) <= low).astype(jnp.int32)
        end += (offset_of(block * per_block) < high).astype(jnp.int32)
    end = jnp.maximum(end, begin)

    def copies(block):
        slot = lax.rem(block, AHEAD)
        rows = pl.ds(pl.multiple_of(block * SUB, SUB), SUB)
        started = []
        for lane_tile in range(lane_tiles):
            lanes = pl.ds(lane_tile * LANES, LANES)
            landing = held.at[slot, lane_tile]
            started.append(
                pltpu.make_async_copy(
                    base_ref.at[:, :, rows, lanes],
                    landing.at[pl.ds(0, 2)],
                    in_sem.at[slot, 2 * lane_tile],
                )
            )
            started.append(
                pltpu.make_async_copy(
                    step_ref.at[pl.ds(1, 2), :, rows, lanes],
                    landing.at[pl.ds(2, 2)],
                    in_sem.at[slot, 2 * lane_tile + 1],
                )
            )
        return started

    for step in range(AHEAD - 1):

        @pl.when(begin + step < end)
        def _():
            for copy in copies(begin + step):
                copy.start()

    lane = lax.broadcasted_iota(jnp.int32, (coefs, LANES), 1)

    def place_of(offset):
        return jnp.clip((offset >> 7) - first_tile + 1, 0, count + 1)

    def body(block, current):
        @pl.when(block + AHEAD - 1 < end)
        def _():
            for copy in copies(block + AHEAD - 1):
                copy.start()

        for copy in copies(block):
            copy.wait()
        slot = lax.rem(block, AHEAD)
        for lane_tile in range(lane_tiles):
            fields = [
                held.at[slot, lane_tile, field].reshape(coefs * SUB, LANES) for field in range(4)
            ]
            start = block * per_block + lane_tile * SUB
            index = index_ref[pl.ds(pl.multiple_of(start, SUB), SUB), :]
            following = offset_of(start)
            for r in range(SUB):
                offset = following
                following = offset_of(start + r + 1)
                shift = offset & (LANES - 1)
                crossing = (following >> 7) > (offset >> 7)
                source = jnp.broadcast_to(index[r : r + 1], (coefs, LANES))
                to = place_of(offset)
                renewed = []
                for field in range(4):
                    got = jnp.take_along_axis(
                        fields[field][pl.ds(r, coefs, stride=SUB), :],
                        source,
                        axis=1,
                        mode="promise_in_bounds",
                    )
                    full = jnp.where(lane >= shift, got, current[field])
                    stage[to, field * coefs : (field + 1) * coefs, :] = full
                    renewed.append(jnp.where(crossing, got, full))
                current = tuple(renewed)
        return current

    zero = jnp.zeros((coefs, LANES), jnp.float32)
    current = lax.fori_loop(begin, end, body, (zero,) * 4)
    last = place_of(offset_of(end * per_block))
    for field in range(4):
        stage[last, field * coefs : (field + 1) * coefs, :] = current[field]
    outs = []
    for step in range(groups):
        member = lax.rem(params_ref[0] + step, groups)
        outs.append(
            pltpu.make_async_copy(
                stage.at[pl.ds(1 + member * tiles, tiles)], out_refs[step], out_sem.at[step]
            )
        )
    for copy in outs:
        copy.start()
    for copy in outs:
        copy.wait()


def pack_call(params, offset, index, base_flow, direction, groups, tiles, waited):
    coefs, _, columns = direction.shape[1:]
    shape = (tiles, 4 * coefs, LANES)
    anywhere = pl.BlockSpec(memory_space=pl.ANY)
    grid_spec = pltpu.PrefetchScalarGridSpec(
        num_scalar_prefetch=2,
        grid=(1,),
        in_specs=[pl.BlockSpec(index.shape, lambda i, p, o: (0, 0))]
        + [anywhere] * (2 + len(waited)),
        out_specs=[anywhere] * groups + [pl.BlockSpec((SUB, LANES), lambda i, p, o: (0, 0))],
        scratch_shapes=[
            pltpu.VMEM((AHEAD, columns // LANES, 4, coefs, SUB, LANES), jnp.float32),
            pltpu.VMEM((groups * tiles + 2, 4 * coefs, LANES), jnp.float32),
            pltpu.SemaphoreType.DMA((AHEAD, 2 * (columns // LANES))),
            pltpu.SemaphoreType.DMA((groups,)),
        ],
    )
    return pl.pallas_call(
        lambda *refs: pack_kernel(groups, coefs, tiles, len(waited), *refs),
        out_shape=[jax.ShapeDtypeStruct(shape, jnp.float32)] * groups
        + [jax.ShapeDtypeStruct((SUB, LANES), jnp.int32)],
        grid_spec=grid_spec,
        compiler_params=pltpu.CompilerParams(vmem_limit_bytes=VMEM_BYTES),
        cost_estimate=pl.CostEstimate(
            flops=0, bytes_accessed=groups * tiles * coefs * PACK_COST, transcendentals=0
        ),
        name="pack",
    )(params, offset, index, base_flow, direction, *waited)


def prepare_kernel(coefs, scalars_ref, *refs):
    (here_ref, prev_ref, next_ref, wet_ref, wet_prev_ref, wet_next_ref, depth_ref, depth_prev_ref,
     above_ref, below_ref, slab_ref, out_ref, token_ref) = refs
    token_ref[...] = jnp.zeros_like(token_ref)
    columns = here_ref.shape[-1]
    row_block = pl.program_id(0)
    at_top = row_block == 0
    at_bottom = row_block == pl.num_programs(0) - 1
    wet = wet_ref[...].astype(jnp.float32)
    wet_prev = wet_prev_ref[SUB - 1 :, :].astype(jnp.float32)
    wet_next = wet_next_ref[:1, :].astype(jnp.float32)
    depth = depth_ref[...]
    depth_prev = depth_prev_ref[SUB - 1 :, :]
    lane = lax.broadcasted_iota(jnp.int32, (SUB, columns), 1)
    sub = lax.broadcasted_iota(jnp.int32, (SUB, columns), 0)
    row = (row_block * SUB + sub).astype(jnp.float32)
    rotation = 0.5 + (row + scalars_ref[0] + 0.5) * scalars_ref[1]

    def wide(slab):
        return jnp.concatenate([slab] * (columns // LANES), axis=1)

    def west(value, slab):
        return jnp.where(lane == 0, wide(slab), pltpu.roll(value, 1, 1))

    def east_of(value, slab):
        return jnp.where(lane == columns - 1, wide(slab), pltpu.roll(value, columns - 1, 1))

    def above(value, edge):
        return jnp.where(sub == 0, edge, pltpu.roll(value, 1, 0))

    def below(value, edge):
        return jnp.where(sub == SUB - 1, edge, pltpu.roll(value, SUB - 1, 0))

    for k in range(coefs // 2):
        angular = scalars_ref[2 + k]
        inverse_angular = 1.0 / (angular + jnp.zeros((SUB, columns), jnp.float32))
        planes = [
            [here_ref[p, 2 * k + part] * wet for p in range(3)] for part in range(2)
        ]
        for part in range(2):
            c = 2 * k + part
            height, east, north = planes[part]
            other = planes[1 - part]
            signed = angular if part == 0 else -angular
            east_flux = depth * east
            north_flux = depth * north
            north_edge = prev_ref[0, c, SUB - 1 :, :] * wet_prev
            flux_edge = jnp.where(at_top, above_ref[1, c : c + 1], north_edge * depth_prev)
            north_edge = jnp.where(at_top, above_ref[0, c : c + 1], north_edge)
            height_edge = jnp.where(
                at_bottom, below_ref[0, c : c + 1], next_ref[0, c, :1, :] * wet_next
            )
            east_edge = jnp.where(
                at_bottom, below_ref[1, c : c + 1], next_ref[1, c, :1, :] * wet_next
            )
            north_up = above(north, north_edge)
            east_down = below(east, east_edge)
            res_height = (
                signed * other[0]
                + east_flux
                - west(east_flux, slab_ref[2, c])
                + north_flux
                - above(north_flux, flux_edge)
            )
            north_mean = 0.25 * (
                north
                + east_of(north, slab_ref[4, c])
                + north_up
                + east_of(north_up, slab_ref[5, c])
            )
            east_mean = 0.25 * (
                east
                + west(east, slab_ref[0, c])
                + east_down
                + west(east_down, slab_ref[1, c])
            )
            res_east = (
                signed * other[1]
                + LINEAR_DRAG * east
                - rotation * north_mean
                + GRAVITY * (east_of(height, slab_ref[3, c]) - height)
            )
            res_north = (
                signed * other[2]
                + LINEAR_DRAG * north
                + rotation * east_mean
                + GRAVITY * (below(height, height_edge) - height)
            )
            if part == 0:
                out_ref[0, c + 1] = res_height * wet * inverse_angular
            else:
                out_ref[0, c - 1] = -res_height * wet * inverse_angular
            out_ref[1, c] = res_east * wet
            out_ref[2, c] = res_north * wet


def prepare_call(scalars, direction, wet_mask, depth, above, below, slabs):
    _, coefs, rows, columns = direction.shape
    last = rows // SUB - 1

    def before(i):
        return jnp.maximum(i - 1, 0)

    def after(i):
        return jnp.minimum(i + 1, last)

    planes = pl.BlockSpec((3, coefs, SUB, columns), lambda i: (0, 0, i, 0))
    flat = (SUB, columns)
    edge = pl.BlockSpec((2, coefs, columns), lambda i: (0, 0, 0))
    return pl.pallas_call(
        lambda *refs: prepare_kernel(coefs, *refs),
        out_shape=[
            jax.ShapeDtypeStruct(direction.shape, jnp.float32),
            jax.ShapeDtypeStruct((SUB, LANES), jnp.int32),
        ],
        grid=(rows // SUB,),
        in_specs=[
            pl.BlockSpec(memory_space=pltpu.SMEM),
            planes,
            pl.BlockSpec((1, coefs, SUB, columns), lambda i: (2, 0, before(i), 0)),
            pl.BlockSpec((2, coefs, SUB, columns), lambda i: (0, 0, after(i), 0)),
            pl.BlockSpec(flat, lambda i: (i, 0)),
            pl.BlockSpec(flat, lambda i: (before(i), 0)),
            pl.BlockSpec(flat, lambda i: (after(i), 0)),
            pl.BlockSpec(flat, lambda i: (i, 0)),
            pl.BlockSpec(flat, lambda i: (before(i), 0)),
            edge,
            edge,
            pl.BlockSpec((6, coefs, SUB, LANES), lambda i: (0, 0, i, 0)),
        ],
        out_specs=[planes, pl.BlockSpec((SUB, LANES), lambda i: (0, 0))],
        compiler_params=pltpu.CompilerParams(vmem_limit_bytes=VMEM_BYTES),
        cost_estimate=pl.CostEstimate(
            flops=rows * columns * coefs, bytes_accessed=0, transcendentals=0
        ),
        name="prepare",
    )(
        scalars, direction, direction, direction, wet_mask, wet_mask, wet_mask, depth, depth,
        above, below, slabs,
    )


def finish_kernel(coefs, lane_tiles, row_block, first_ref, offset_ref, table_ref, scalars_ref, back, spread_ref, refs):
    wet_ref, drag_ref, cell_ref, east_ref, north_ref, east_out, north_out = refs
    columns = lane_tiles * LANES
    wet = wet_ref[...].astype(jnp.float32)
    drag = drag_ref[...]
    sub = lax.broadcasted_iota(jnp.int32, (SUB, columns), 0)
    row = (row_block * SUB + sub).astype(jnp.float32)
    rotation = 0.5 + (row + scalars_ref[0] + 0.5) * scalars_ref[1]

    def gathered(here, after, index, over):
        first = jnp.take_along_axis(here, index, axis=1, mode="promise_in_bounds")
        second = jnp.take_along_axis(after, index, axis=1, mode="promise_in_bounds")
        return jnp.where(over, second, first)

    speed = []
    for lane_tile in range(lane_tiles):
        places = cell_ref[lane_tile * SUB : (lane_tile + 1) * SUB, :]
        turned = spread_ref.at[lane_tile].reshape(2 * coefs * SUB, LANES)
        speeds = [[], []]
        for r in range(SUB):
            at = (row_block * lane_tiles + lane_tile) * SUB + r
            tile = offset_ref[at >> 7, at & (LANES - 1)] >> 7
            found = []
            for which in range(2):
                start = pl.multiple_of(table_ref[first_ref[1] * 2, tile + which], SUB)
                found.append(back[pl.ds(start, 2 * coefs), :])
                start = table_ref[first_ref[1] * 2 + 1, tile + which]
                speeds[which].append(back[pl.ds(start, 1), :])
            place = jnp.broadcast_to(places[r : r + 1], (2 * coefs, LANES))
            turned[pl.ds(r, 2 * coefs, stride=SUB), :] = gathered(
                found[0], found[1], place & (LANES - 1), place >= LANES
            )
        speed.append(
            gathered(
                jnp.concatenate(speeds[0], axis=0),
                jnp.concatenate(speeds[1], axis=0),
                places & (LANES - 1),
                places >= LANES,
            )
        )
    is_wet = wet > 0.5
    friction = [
        jnp.where(
            is_wet,
            jnp.concatenate([spread_ref[n, index] for n in range(lane_tiles)], axis=1) * drag,
            0.0,
        )
        for index in range(2 * coefs)
    ]
    speed = jnp.where(is_wet, jnp.concatenate(speed, axis=1), 0.0)
    real_rate = drag * speed + LINEAR_DRAG
    for k in range(coefs // 2):
        angular = scalars_ref[2 + k]
        cos_at, sin_at = 2 * k, 2 * k + 1
        det_real = real_rate * real_rate - angular * angular + rotation * rotation
        det_imag = 2.0 * real_rate * angular
        inverse_norm = 1.0 / (det_real * det_real + det_imag * det_imag)
        inv_real = det_real * inverse_norm
        inv_imag = -det_imag * inverse_norm
        east_re = east_ref[0, cos_at] + friction[cos_at]
        east_im = -(east_ref[0, sin_at] + friction[sin_at])
        north_re = north_ref[0, cos_at] + friction[coefs + cos_at]
        north_im = -(north_ref[0, sin_at] + friction[coefs + sin_at])
        num_east_re = real_rate * east_re - angular * east_im + rotation * north_re
        num_east_im = real_rate * east_im + angular * east_re + rotation * north_im
        num_north_re = -rotation * east_re + real_rate * north_re - angular * north_im
        num_north_im = -rotation * east_im + real_rate * north_im + angular * north_re
        east_out[0, cos_at] = num_east_re * inv_real - num_east_im * inv_imag
        east_out[0, sin_at] = -(num_east_re * inv_imag + num_east_im * inv_real)
        north_out[0, cos_at] = num_north_re * inv_real - num_north_im * inv_imag
        north_out[0, sin_at] = -(num_north_re * inv_imag + num_north_im * inv_real)


def finish_call(first, offset, table, scalars, arrays, pieces, rows, result, groups, early):
    _, coefs, _, columns = result.shape
    lane_tiles = columns // LANES

    def kernel(first_ref, offset_ref, table_ref, scalars_ref, *refs):
        array_refs = refs[:3]
        piece_refs = refs[4:-4]
        out_ref, back, spread_ref, sem = refs[-4:]
        first = first_ref[0]
        count = first_ref[2]

        @pl.when(count > 0)
        def _():
            at = 0
            copies = []
            for n, piece in enumerate(piece_refs):
                rows = piece.shape[0]
                copy = pltpu.make_async_copy(piece, back.at[pl.ds(at, rows)], sem.at[n])
                needed = True
                if n < early[0]:
                    source = lax.rem(first_ref[1] + groups - n % groups, groups)
                    needed = source >= groups - early[1]
                elif n >= early[0] + groups:
                    needed = first_ref[3] > 0
                copies.append((copy, needed))
                at += rows

            def each(act):
                for copy, needed in copies:
                    if needed is True:
                        act(copy)
                    else:
                        pl.when(needed)(lambda copy=copy: act(copy))

            each(lambda copy: copy.start())

            def body(*block_refs):
                @pl.when(pl.program_id(0) == 0)
                def _():
                    each(lambda copy: copy.wait())

                finish_kernel(
                    coefs, lane_tiles, first + pl.program_id(0), first_ref, offset_ref,
                    table_ref, scalars_ref, back, spread_ref, block_refs,
                )

            deep = pl.Buffered(3)

            def flat(rows, width):
                return pl.BlockSpec(
                    (rows, width), lambda i: (first + i, 0), pipeline_mode=deep
                )

            def plane(p, mode):
                return pl.BlockSpec(
                    (1, coefs, SUB, columns), lambda i: (p, 0, first + i, 0), pipeline_mode=mode
                )

            pltpu.emit_pipeline(
                body,
                grid=(count,),
                in_specs=[
                    flat(SUB, columns),
                    flat(SUB, columns),
                    flat(SUB * lane_tiles, LANES),
                    plane(1, deep),
                    plane(2, deep),
                ],
                out_specs=[plane(1, None), plane(2, None)],
            )(*array_refs, out_ref, out_ref, out_ref, out_ref)

    anywhere = pl.BlockSpec(memory_space=pl.ANY)
    scalar = pl.BlockSpec(memory_space=pltpu.SMEM)
    operands = [first, offset, table, scalars] + list(arrays) + [result] + pieces
    return pl.pallas_call(
        kernel,
        out_shape=jax.ShapeDtypeStruct(result.shape, jnp.float32),
        in_specs=[scalar] * 4 + [anywhere] * (4 + len(pieces)),
        out_specs=anywhere,
        scratch_shapes=[
            pltpu.VMEM((rows, LANES), jnp.float32),
            pltpu.VMEM((lane_tiles, 2 * coefs, SUB, LANES), jnp.float32),
            pltpu.SemaphoreType.DMA((len(pieces),)),
        ],
        input_output_aliases={7: 0},
        compiler_params=pltpu.CompilerParams(vmem_limit_bytes=VMEM_BYTES),
        cost_estimate=pl.CostEstimate(
            flops=0, bytes_accessed=8 * SUB * columns * coefs * 36, transcendentals=0
        ),
        name="finish",
    )(*operands)


def shifted(block, axis, step, wrap):
    count = lax.axis_size(axis)
    pairs = [
        (i, (i + step) % count) for i in range(count) if wrap or 0 <= i + step < count
    ]
    return lax.ppermute(block, axis, pairs)


def edge_kernel(coefs, east_ref, height_ref, north_ref, last_ref, first_ref, wet_ref, depth_ref, *refs):
    up_ref, down_ref, right_ref, left_ref = refs[-4:]
    rows, columns = wet_ref.shape
    wet = wet_ref[...].astype(jnp.float32)
    end = slice(columns - LANES, columns)
    wet_end = wet[:, end]
    wet_start = wet[:, :LANES]
    depth_end = depth_ref[:, end]
    wet_last = wet[rows - 1 :, :]
    depth_last = depth_ref[rows - 1 :, :]
    for c in range(coefs):
        at = slice(c, c + 1)
        north_row = last_ref[0, c, SUB - 1 :, :] * wet_last
        up_ref[0, at, :] = north_row
        up_ref[1, at, :] = north_row * depth_last
        down_ref[0, at, :] = first_ref[0, c, :1, :] * wet[:1, :]
        down_ref[1, at, :] = first_ref[1, c, :1, :] * wet[:1, :]
        east = east_ref[0, c] * wet_end
        right_ref[0, at, :] = jnp.transpose(east)[LANES - 1 :, :]
        right_ref[1, at, :] = jnp.transpose(east * depth_end)[LANES - 1 :, :]
        left_ref[0, at, :] = jnp.transpose(height_ref[0, c] * wet_start)[:1, :]
        left_ref[1, at, :] = jnp.transpose(north_ref[0, c] * wet_start)[:1, :]


def edge_call(direction, wet_mask, depth, waited):
    _, coefs, rows, columns = direction.shape
    last_tile = columns // LANES - 1
    last_block = rows // SUB - 1
    tall = (1, coefs, rows, LANES)
    whole = pl.BlockSpec((rows, columns), lambda i: (0, 0))
    row_out = (2, coefs, columns)
    col_out = (2, coefs, rows)
    shapes = [row_out, row_out, col_out, col_out]
    return pl.pallas_call(
        lambda *refs: edge_kernel(coefs, *refs),
        out_shape=[jax.ShapeDtypeStruct(shape, jnp.float32) for shape in shapes],
        grid=(1,),
        in_specs=[
            pl.BlockSpec(tall, lambda i: (1, 0, 0, last_tile)),
            pl.BlockSpec(tall, lambda i: (0, 0, 0, 0)),
            pl.BlockSpec(tall, lambda i: (2, 0, 0, 0)),
            pl.BlockSpec((1, coefs, SUB, columns), lambda i: (2, 0, last_block, 0)),
            pl.BlockSpec((2, coefs, SUB, columns), lambda i: (0, 0, 0, 0)),
            whole,
            whole,
        ]
        + [pl.BlockSpec(memory_space=pl.ANY)] * len(waited),
        out_specs=[pl.BlockSpec(shape, lambda i: (0, 0, 0)) for shape in shapes],
        compiler_params=pltpu.CompilerParams(vmem_limit_bytes=VMEM_BYTES),
        cost_estimate=pl.CostEstimate(
            flops=rows * columns, bytes_accessed=0, transcendentals=0
        ),
        name="edges",
    )(direction, direction, direction, direction, direction, wet_mask, depth, *waited)


def halo(direction, wet_mask, depth, waited):
    up, down, right, left = edge_call(direction, wet_mask, depth, waited)
    above = shifted(up, "lat", 1, False)
    below = shifted(down, "lat", -1, False)
    east_below = jnp.concatenate([right[0, :, 1:], below[1, :, -1:]], axis=1)
    north_above = jnp.concatenate([above[0, :, :1], left[1, :, :-1]], axis=1)
    to_right = jnp.stack([right[0], east_below, right[1]])
    to_left = jnp.stack([left[0], left[1], north_above])
    cols = jnp.concatenate(
        [shifted(to_right, "lon", 1, True), shifted(to_left, "lon", -1, True)], axis=0
    )
    slabs = jnp.broadcast_to(cols[:, :, :, None], cols.shape + (LANES,))
    return above, below, slabs


def spread_out(blocks):
    return [
        block if step == 0 else shifted(block, "freq", step, True)
        for step, block in enumerate(blocks)
    ]


def tile_table(groups, coefs, back_chunks, blocks):
    table = np.zeros((2 * groups, blocks + LANES), np.int32)
    for member in range(groups):
        tile = 0
        row = 0
        for chunk_tiles in back_chunks:
            together = sum(chunk_tiles)
            before = 0
            for tiles in chunk_tiles:
                for band in range(groups):
                    start = row + (member - band) % groups * piece_rows(together, coefs)
                    for i in range(before, before + tiles):
                        if tile < blocks:
                            table[2 * member, tile] = start + i * 2 * coefs
                            table[2 * member + 1, tile] = start + together * 2 * coefs + i
                        tile += 1
                before += tiles
            row += groups * piece_rows(together, coefs)
    return table


def local(direction, base_flow, water_depth, drag_factor, wet_mask):
    coefs, tile_rows, tile_cols = direction.shape[1:]
    groups = lax.axis_size("freq")
    member = lax.axis_index("freq")
    lat_place = lax.axis_index("lat")
    total_rows = tile_rows * lax.axis_size("lat")
    lane_tiles = tile_cols // LANES
    angular = OMEGA_STEP * (
        member * (coefs // 2) + jnp.arange(coefs // 2, dtype=jnp.int32) + 1
    ).astype(jnp.float32)
    row_start = (lat_place * tile_rows).astype(jnp.float32)
    scalars = jnp.concatenate(
        [jnp.stack([row_start, jnp.float32(1.0 / total_rows)]), angular]
    )
    place = jnp.reshape(member, (1,)).astype(jnp.int32)
    blocks = tile_rows * lane_tiles
    row_blocks = tile_rows // SUB
    chunk_tiles = [share * blocks // (groups * SHARE_UNITS) for share in CHUNK_SHARES]
    fixed = groups * sum(chunk_tiles)
    steps = -(-(blocks - fixed) // (groups * LOOP_TILES))
    back_chunks = [chunk_tiles[:-1], chunk_tiles[-1:]]
    table = jnp.asarray(
        tile_table(groups, coefs, back_chunks + [[LOOP_TILES]] * steps, blocks)
    )
    index, cells, offset = index_call(wet_mask)
    offsets = offset.reshape(-1)
    ends = offsets[SUB * lane_tiles : blocks + 1 : SUB * lane_tiles]

    def packed(first_tile, tiles, token, waited=()):
        params = jnp.stack([place[0], first_tile + token])
        *flows, token = pack_call(
            params, offset, index, base_flow, direction, groups, tiles, waited
        )
        return spread_out(flows), token[0, 0]

    def through(flows, token, weight):
        *back, token = friction_call(place + token, flows, coefs, weight)
        return spread_out(back), token[0, 0]

    flows = []
    tile = 0
    token = jnp.int32(0)
    for tiles in chunk_tiles[:-1]:
        flow, token = packed(tile, tiles, token)
        flows.append(flow)
        tile += groups * tiles

    loop_cells = groups * LOOP_TILES * LANES
    beyond = offsets[blocks] + token - fixed * LANES
    loops = jnp.maximum(beyond + loop_cells - 1, 0) // loop_cells

    def more(state):
        done, held = state
        flow, _ = packed(fixed + done * groups * LOOP_TILES, LOOP_TILES, 0)
        back, _ = through([flow], 0, 1)
        held = lax.dynamic_update_slice_in_dim(
            held, jnp.concatenate(back, axis=0)[None], done, 0
        )
        return done + 1, held

    rows = groups * piece_rows(LOOP_TILES, coefs)
    extra = jnp.zeros((steps, rows, LANES), jnp.float32)
    done, extra = lax.while_loop(lambda state: state[0] < loops, more, (jnp.int32(0), extra))

    token = token + jnp.minimum(done, 0)
    flows.append(packed(tile, chunk_tiles[-1], token)[0])
    above, below, slabs = halo(direction, wet_mask, water_depth, flows[0][1:] + flows[-1][:1])
    result, prepared = prepare_call(
        scalars, direction, wet_mask, water_depth, above, below, slabs
    )
    back, token = through(flows[:-1], prepared[0, 0], 1)
    backs = [back]
    back, token = through(flows[-1:], token, LATE_WEIGHT)
    backs.append(back)

    arrays = (wet_mask, drag_factor, cells)
    pieces = []
    back_rows = rows * steps
    back_rows += groups * sum(piece_rows(sum(several), coefs) for several in back_chunks)
    begin = jnp.int32(0)
    tile = 0
    for last, several in enumerate(back_chunks):
        pieces += backs[last]
        tile += groups * sum(several)
        if last:
            end = jnp.int32(row_blocks)
            pieces.append(extra.reshape(-1, LANES))
        else:
            end = jnp.sum((ends <= tile * LANES).astype(jnp.int32))
        first = jnp.stack([begin, place[0], end - begin, loops])
        result = finish_call(
            first, offset, table, scalars, arrays, list(pieces), back_rows, result, groups,
            (groups, -(-SUB * lane_tiles // chunk_tiles[-2])) if last else (0, 0),
        )
        begin = end
    return result


def solution(mesh):
    placed = (
        P(None, "freq", "lat", "lon"),
        P(None, "freq", "lat", "lon"),
        P("lat", "lon"),
        P("lat", "lon"),
        P("lat", "lon"),
    )
    return jax.shard_map(
        local, mesh=mesh, in_specs=placed, out_specs=P(None, "freq", "lat", "lon"), check_vma=False
    )
```
